32 devices in a mesh: grp: 2 (over y), frm: 4 (over z), row: 2 (over x), sub: 2 (over core).
Axes of the slice: x: 2, y: 2, z: 4, core: 2. Of those that a mesh axis runs over, the one named last changes fastest.
Arguments:
- signal: bfloat16 [64, 65536], P('row', ('grp', 'frm', 'sub')), parts along dimension 1, may hold values from -6 to 6
- w_start: float32 [2560, 32], P('row'), may hold values from 0.02 to 0.4
- h_start: float32 [32, 65536], P(None, ('grp', 'frm', 'sub')), parts along dimension 1, may hold values from 0.02 to 0.4
Outputs:
- synergies: float32 [5120, 32], P(('grp', 'row')), parts along dimension 0
- activations: float32 [32, 65536], P(None, ('grp', 'frm', 'sub')), parts along dimension 1
The draws below stay inside these ranges and needn't reach their ends.
There are 2 independent parts, one for each index of `grp`. The reference program is written for one: setup_inputs(seed, part) draws one part's arguments, and reference() takes and returns one part's arrays. A program takes and returns all parts, laid end to end along the dimension named above; an argument that names none is the same for every part. Nothing has to cross between parts.
All inputs are finite; a program needn't handle non-finite values.
Results may differ from the reference program's by a relative error of at most 0.0019.
Values may be sent and summed in bfloat16 or wider, within the bound.
No kernel may reach another device: no remote copies, remote signals or barrier semaphores. Data moves between devices by JAX's collectives and lax.ppermute only.
A program may use at most 128 MiB of HBM per device.

```python
import math
import jax
import jax.numpy as jnp
from jax import lax

C = 64
NF = 40
RANK = 32
TAPS = 128
ITERS = 2
FR_DEV = 4096
FRAMES = 32768
ROWS = 2560


def shard_levels(key, extent, split, least, largest):
    factor_of, own = 1.0, jax.random.fold_in(key, 6)
    for axis_at, blocks in split:
        steps = jnp.exp(jax.random.uniform(jax.random.fold_in(own, axis_at), (blocks,), jnp.float32, least / len(split), largest / len(split)))
        factor_of = factor_of * jnp.repeat(steps, extent[axis_at] // blocks).reshape([-1 if axis == axis_at else 1 for axis in range(len(extent))])
    return factor_of


def noise(own_key, extent, spread, reach, shards=(), kind=jnp.bfloat16):
    result = spread * jax.random.normal(own_key, extent, jnp.float32)
    if shards:
        result = result * shard_levels(own_key, extent, shards, -0.22, 0.18)
    return jnp.clip(result, -reach, reach).astype(kind)


def setup_inputs(seed: int = 0, part: int = 0) -> dict:
    arg_keys = jax.random.split(jax.random.key(seed), 4)
    part_keys = jax.random.split(jax.random.fold_in(arg_keys[3], part), 4)
    return {
        "signal": noise(part_keys[0], (C, FRAMES), 1.0, 6.0, ((0, 2), (1, 8))),
        "w_start": jnp.clip(jnp.exp(math.log(0.4) - 2.9957323 * jax.random.uniform(arg_keys[1], (ROWS, RANK), jnp.float32) ** shard_levels(arg_keys[1], (ROWS, RANK), ((0, 2),), -0.2, 0.2)), 0.02, 0.4),
        "h_start": jnp.clip(jnp.exp(math.log(0.4) - 2.9957323 * jax.random.uniform(part_keys[2], (RANK, FRAMES), jnp.float32) ** shard_levels(part_keys[2], (RANK, FRAMES), ((1, 8),), -0.2, 0.2)), 0.02, 0.4),
    }


def morlet(offsets):
    level = jnp.arange(NF, dtype=jnp.float32) / (NF - 1)
    freq = 2.0 * jnp.power(12.0, level)
    sigma = 7.0 / (2.0 * math.pi * freq)
    all_times = (jnp.arange(TAPS, dtype=jnp.float32) - TAPS // 2) / 50.0
    all_env = jnp.exp(-all_times[None, :] ** 2 / (2.0 * sigma[:, None] ** 2))
    scale = 1.0 / jnp.sqrt(lax.optimization_barrier(jnp.sum(all_env * all_env, axis=1)))
    extra = (1,) * offsets.ndim
    freq_b = freq.reshape((NF,) + extra)
    sigma_b = sigma.reshape((NF,) + extra)
    scale_b = scale.reshape((NF,) + extra)
    times = (offsets - TAPS // 2) / 50.0
    env = jnp.exp(-times ** 2 / (2.0 * sigma_b ** 2)) * scale_b
    phase = 2.0 * math.pi * freq_b * times
    return jnp.stack([env * jnp.cos(phase), env * jnp.sin(phase)])

def reference(signal, w_start, h_start):
    kernel = morlet(jnp.arange(TAPS, dtype=jnp.float32)).astype(jnp.bfloat16)
    kernel_f = kernel.astype(jnp.float32)
    half_span = TAPS // 2
    padded = jnp.pad(signal, ((0, 0), (half_span, half_span)))
    nblocks = FRAMES // FR_DEV
    window_idx = jnp.arange(FR_DEV, dtype=jnp.int32)[:, None] + jnp.arange(TAPS, dtype=jnp.int32)[None, :]
    high = lax.Precision.HIGHEST

    def spectra_block(index):
        segment = lax.dynamic_slice_in_dim(padded, (index * FR_DEV).astype(jnp.int32), FR_DEV + TAPS, 1)
        windows = segment[:, window_idx].astype(jnp.float32)
        coeffs = jnp.einsum('ctk,pfk->cpft', windows, kernel_f)
        power_grid = coeffs[:, 0] ** 2 + coeffs[:, 1] ** 2
        return power_grid.reshape(C * NF, FR_DEV).astype(jnp.bfloat16)
    synergies = w_start
    activations = h_start
    for update in range(ITERS):
        synergies_low = synergies.astype(jnp.bfloat16)
        gram_sum = jnp.dot(synergies.T, synergies, precision=high)

        def scan_step(carry, index):
            crossed, h_gram = carry
            spectra = spectra_block(index)
            summed = jnp.dot(synergies_low.T, spectra, preferred_element_type=jnp.float32)
            old_block = lax.dynamic_slice_in_dim(activations, (index * FR_DEV).astype(jnp.int32), FR_DEV, 1)
            new_block = old_block * summed / jnp.dot(gram_sum, old_block, precision=high)
            block_low = new_block.astype(jnp.bfloat16)
            crossed = crossed + jnp.dot(spectra, block_low.T, preferred_element_type=jnp.float32)
            h_gram = h_gram + jnp.dot(new_block, new_block.T, precision=high)
            return ((crossed, h_gram), new_block)
        start_carry = (jnp.zeros((C * NF, RANK), jnp.float32), jnp.zeros((RANK, RANK), jnp.float32))
        (crossed, h_gram), new_blocks = lax.scan(scan_step, start_carry, jnp.arange(nblocks, dtype=jnp.int32))
        activations = new_blocks.transpose(1, 0, 2).reshape(RANK, FRAMES)
        synergies = synergies * crossed / jnp.dot(synergies, h_gram, precision=high)
    return (synergies, activations)
```

```python
import functools
import math

import jax
import jax.numpy as jnp
import ml_dtypes
import numpy as np
from jax import lax
from jax.experimental import pallas as pl
from jax.experimental.pallas import tpu as pltpu
from jax.sharding import PartitionSpec as P

NF = 40
TAPS = 128
HALF = TAPS // 2
GROUP = 4
GROUPS = NF // GROUP
F32 = jnp.float32
BF16 = jnp.bfloat16
HIGH = lax.Precision.HIGHEST
NT = (((1,), (1,)), ((), ()))
VMEM_LIMIT = 56 * 1024 * 1024


def wavelets():
    f = np.float32
    level = np.arange(NF, dtype=f) / f(NF - 1)
    freq = f(2.0) * np.power(f(12.0), level)
    sigma = f(7.0) / (f(2.0 * math.pi) * freq)
    times = (np.arange(TAPS, dtype=f) - f(HALF)) / f(50.0)
    env = np.exp(-(times[None, :] ** 2) / (f(2.0) * sigma[:, None] ** 2))
    scale = f(1.0) / np.sqrt(np.sum(env * env, axis=1))
    env = env * scale[:, None]
    phase = f(2.0 * math.pi) * freq[:, None] * times[None, :]
    return np.stack([env * np.cos(phase), env * np.sin(phase)]).astype(ml_dtypes.bfloat16)


def toeplitz():
    kernel = wavelets()
    table = np.zeros((NF, 2 * TAPS, 2 * TAPS), ml_dtypes.bfloat16)
    for at in range(TAPS):
        for part in range(2):
            table[:, at : at + TAPS, part * TAPS + at] = kernel[part]
    return table


def split_two(value):
    top = value.astype(BF16)
    return top, (value - top.astype(F32)).astype(BF16)


def joined(message, at, rank):
    return message[:, at : at + rank].astype(F32) + message[:, at + rank : at + 2 * rank].astype(F32)


def pack(out_ref, main, gram):
    rank, size = main.shape
    top, rest = split_two(gram)
    out_ref[:, :size] = main.astype(BF16)
    out_ref[:, size : size + rank] = top
    out_ref[:, size + rank : size + 2 * rank] = rest


def prepare_kernel(w_ref, msg_ref, gram_ref):
    w = w_ref[...]
    gram = lax.dot_general(w, w, NT, precision=HIGH, preferred_element_type=F32)
    gram_ref[...] = gram
    pack(msg_ref, w, gram)


def group_rows(s_scr, g, pair, rows, cl):
    halves = []
    for blk in (2 * pair, 2 * pair + 1):
        parts = [
            s_scr[pl.ds(g * GROUP, GROUP), blk, x * cl : (x + 1) * cl, :].reshape(GROUP * cl, TAPS)
            for x in range(rows)
        ]
        halves.append(jnp.concatenate(parts, axis=0))
    return jnp.concatenate(halves, axis=1)


def add_crossed(s_scr, wg, num_scr, g, pairs, rows, cl):
    for pair in range(pairs):
        cols = slice(2 * TAPS * pair, 2 * TAPS * (pair + 1))
        num_scr[:, cols] += jnp.dot(wg, group_rows(s_scr, g, pair, rows, cl), preferred_element_type=F32)


def finish_update(old, gram, num_scr, s_scr, p_scr, h_out, own_ref, own_gram_ref, msg_refs, rows, subs, cl):
    rank, frames = old.shape
    pairs = frames // (2 * TAPS)
    per_sub = GROUPS // subs
    new = old * num_scr[...] / jnp.dot(gram, old, precision=HIGH, preferred_element_type=F32)
    h_out[...] = new
    low = new.astype(BF16)
    h_gram = lax.dot_general(new, new, NT, precision=HIGH, preferred_element_type=F32)
    wide = GROUP * cl
    for g in range(GROUPS):
        acc = jnp.zeros((rank, rows * wide), F32)
        for pair in range(pairs):
            cols = slice(2 * TAPS * pair, 2 * TAPS * (pair + 1))
            acc = acc + lax.dot_general(
                low[:, cols], group_rows(s_scr, g, pair, rows, cl), NT, preferred_element_type=F32
            )
        at = (g % per_sub) * wide
        for x in range(rows):
            p_scr[x, g // per_sub, :, at : at + wide] = acc[:, x * wide : (x + 1) * wide]
    x_me, c_me = lax.axis_index("row"), lax.axis_index("sub")
    own_ref[...] = p_scr[x_me, c_me]
    own_gram_ref[...] = h_gram
    at = 0
    for dx in range(rows):
        for dc in range(subs):
            if dx or dc:
                pack(msg_refs[at], p_scr[lax.rem(x_me + dx, rows), lax.rem(c_me + dc, subs)], h_gram)
                at += 1


def first_kernel(rows, subs, cl, blocks, *refs):
    refs = list(refs)
    sig_refs = [refs.pop(0) for _ in range(rows)]
    halo_refs = [refs.pop(0) for _ in range(rows)]
    w_refs = [refs.pop(0) for _ in range(rows)]
    gram_ref, h_ref, tab_ref = refs.pop(0), refs.pop(0), refs.pop(0)
    s_hbm, h_out, own_ref, own_gram_ref = (refs.pop(0) for _ in range(4))
    msg_refs = [refs.pop(0) for _ in range(rows * subs - 1)]
    xp_scr, x_scr, w_scr, s_scr, num_scr, p_scr, sems = refs
    rank = h_ref.shape[0]
    frames = blocks * TAPS
    wide = GROUP * cl
    g = pl.program_id(0)
    x_me = lax.axis_index("row")

    @pl.when(g == 0)
    def _():
        for shift in range(rows):
            owner = lax.rem(x_me + rows - shift, rows)
            xp_scr[owner] = sig_refs[shift][...]
            for at in range(GROUPS):
                w_scr[at, owner] = w_refs[shift][:, at * wide : (at + 1) * wide]

        @pl.when(x_me == 0)
        def _():
            for at in range(rows):
                xp_scr[at, :, :HALF] = halo_refs[at][...]

        @pl.when(x_me == rows - 1)
        def _():
            for at in range(rows):
                xp_scr[rows - 1 - at, :, frames + HALF :] = halo_refs[at][...]

        for blk in range(blocks):
            for x in range(rows):
                x_scr[blk, x * cl : (x + 1) * cl, :] = xp_scr[x, :, blk * TAPS : (blk + 2) * TAPS]
        num_scr[...] = jnp.zeros_like(num_scr)

    for at in range(GROUP):
        co = jnp.dot(x_scr[...].reshape(blocks * rows * cl, 2 * TAPS), tab_ref[at], preferred_element_type=F32)
        power = co[:, :TAPS] * co[:, :TAPS] + co[:, TAPS:] * co[:, TAPS:]
        s_scr[g * GROUP + at] = power.astype(BF16).reshape(blocks, rows * cl, TAPS)

    def copy_out(at):
        span = pl.ds(at * GROUP, GROUP)
        return pltpu.make_async_copy(s_scr.at[span], s_hbm.at[span], sems.at[at])

    copy_out(g).start()
    wg = jnp.concatenate([w_scr[g, x] for x in range(rows)], axis=1)
    add_crossed(s_scr, wg, num_scr, g, blocks // 2, rows, cl)

    @pl.when(g == GROUPS - 1)
    def _():
        gram = gram_ref[...]
        for shift in range(1, rows):
            gram = gram + joined(w_refs[shift], NF * cl, rank)
        old = h_ref[:, pl.ds(pl.multiple_of(x_me * frames, TAPS), frames)]
        finish_update(old, gram, num_scr, s_scr, p_scr, h_out, own_ref, own_gram_ref, msg_refs, rows, subs, cl)
        for at in range(GROUPS):
            copy_out(at).wait()


def later_kernel(rows, subs, cl, blocks, *refs):
    refs = list(refs)
    w_refs = [refs.pop(0) for _ in range(rows * subs)]
    h_ref, s_hbm = refs.pop(0), refs.pop(0)
    h_out, own_ref, own_gram_ref = (refs.pop(0) for _ in range(3))
    msg_refs = [refs.pop(0) for _ in range(rows * subs - 1)]
    w_scr, s_scr, num_scr, p_scr, sems = refs
    rank = h_ref.shape[0]
    per_sub = GROUPS // subs
    wide = GROUP * cl
    x_me, c_me = lax.axis_index("row"), lax.axis_index("sub")

    def copy_in(at):
        span = pl.ds(at * GROUP, GROUP)
        return pltpu.make_async_copy(s_hbm.at[span], s_scr.at[span], sems.at[at])

    for at in range(GROUPS):
        copy_in(at).start()
    gram = jnp.zeros((rank, rank), F32)
    at = 0
    for dx in range(rows):
        for dc in range(subs):
            x_of, c_of = lax.rem(x_me + rows - dx, rows), lax.rem(c_me + subs - dc, subs)
            for part in range(per_sub):
                w_scr[c_of, part, x_of] = w_refs[at][:, part * wide : (part + 1) * wide]
            gram = gram + joined(w_refs[at], per_sub * wide, rank)
            at += 1
    num_scr[...] = jnp.zeros_like(num_scr)
    for g in range(GROUPS):
        copy_in(g).wait()
        wg = jnp.concatenate([w_scr[g // per_sub, g % per_sub, x] for x in range(rows)], axis=1)
        add_crossed(s_scr, wg, num_scr, g, blocks // 2, rows, cl)
    finish_update(h_ref[...], gram, num_scr, s_scr, p_scr, h_out, own_ref, own_gram_ref, msg_refs, rows, subs, cl)


def partial_kernel(*refs):
    own_ref, own_gram_ref, *msg_refs, out_ref = refs
    rank, size = own_ref.shape
    total, gram = own_ref[...], own_gram_ref[...]
    for ref in msg_refs:
        total = total + ref[:, :size].astype(F32)
        gram = gram + joined(ref, size, rank)
    pack(out_ref, total, gram)


def update_kernel(count, w_ref, *refs):
    msg_refs, (new_ref, out_ref, scr) = refs[:count], refs[count:]
    rank, size = new_ref.shape
    z_me = lax.axis_index("frm")
    for shift in range(count):
        scr[lax.rem(z_me + count - shift, count)] = msg_refs[shift][...]
    total, gram = scr[0, :, :size].astype(F32), joined(scr[0], size, rank)
    for at in range(1, count):
        total = total + scr[at, :, :size].astype(F32)
        gram = gram + joined(scr[at], size, rank)
    w = w_ref[lax.axis_index("sub")] if len(w_ref.shape) == 3 else w_ref[...]
    new = w * total / jnp.dot(gram, w, precision=HIGH, preferred_element_type=F32)
    new_ref[...] = new
    pack(out_ref, new, lax.dot_general(new, new, NT, precision=HIGH, preferred_element_type=F32))


def call(kernel, args, outs, scratch=(), grid=None, in_specs=None, out_specs=None):
    whole = pl.BlockSpec(memory_space=pltpu.VMEM)
    extra = {} if grid is None else {"grid": grid}
    return pl.pallas_call(
        kernel,
        out_shape=[jax.ShapeDtypeStruct(*out) for out in outs],
        in_specs=in_specs or [whole] * len(args),
        out_specs=out_specs or [whole] * len(outs),
        scratch_shapes=list(scratch),
        compiler_params=pltpu.CompilerParams(vmem_limit_bytes=VMEM_LIMIT),
        **extra,
    )(*args)


def shards(signal, w_start, h_start):
    rows, subs, frms = (lax.axis_size(axis) for axis in ("row", "sub", "frm"))
    x_me = lax.axis_index("row")
    cl, window = signal.shape
    rank = w_start.shape[1]
    frames = window // rows
    blocks = frames // TAPS
    chans = rows * cl
    size = NF * cl // subs
    line = frms * subs

    def row_shift(value, shift):
        return lax.ppermute(value, "row", [(i, (i + shift) % rows) for i in range(rows)])

    def quad_shift(value, dx, dc):
        pairs = [
            (x * subs + c, ((x + dx) % rows) * subs + (c + dc) % subs) for x in range(rows) for c in range(subs)
        ]
        return lax.ppermute(value, ("row", "sub"), pairs)

    def place(x, at):
        return (at // subs * rows + x) * subs + at % subs

    others = [(dx, dc) for dx in range(rows) for dc in range(subs) if dx or dc]

    padded = jnp.pad(signal, ((0, 0), (HALF, HALF)))

    def part_for(target):
        return lax.dynamic_slice_in_dim(padded, target * frames, frames + TAPS, 1)

    sig = [part_for(x_me)]
    for shift in range(1, rows):
        sig.append(row_shift(part_for((x_me + shift) % rows), shift))
    tail, head = signal[:, window - HALF :], signal[:, :HALF]
    halos = []
    for at in range(rows):
        to_next = [(place(at, i), place(0, i + 1)) for i in range(line - 1)]
        to_prev = [(place(rows - 1 - at, i + 1), place(rows - 1, i)) for i in range(line - 1)]
        halos.append(lax.ppermute(jnp.where(x_me == at, tail, head), ("frm", "row", "sub"), to_next + to_prev))

    w_cols = w_start.reshape(cl, NF, rank).transpose(2, 1, 0).reshape(rank, NF * cl)
    w_msg, w_gram = call(
        prepare_kernel, [w_cols], [((rank, NF * cl + 2 * rank), BF16), ((rank, rank), F32)]
    )
    w_msgs = [w_msg] + [row_shift(w_msg, shift) for shift in range(1, rows)]
    w_own = w_cols.reshape(rank, subs, size).transpose(1, 0, 2)

    msg = ((rank, size + 2 * rank), BF16)
    tail_outs = [((rank, frames), F32), ((rank, size), F32), ((rank, rank), F32)] + [msg] * len(others)
    s_shape = (NF, blocks, chans, TAPS)

    def fixed(shape):
        return pl.BlockSpec(shape, lambda g: (0,) * len(shape))

    table = jnp.asarray(toeplitz())
    args = sig + halos + w_msgs + [w_gram, h_start]
    spec = [fixed(a.shape) for a in args] + [pl.BlockSpec((GROUP, 2 * TAPS, 2 * TAPS), lambda g: (g, 0, 0))]
    tail_scratch = [
        pltpu.VMEM(s_shape, BF16),
        pltpu.VMEM((rank, frames), F32),
        pltpu.VMEM((rows, subs, rank, size), F32),
        pltpu.SemaphoreType.DMA((GROUPS,)),
    ]
    spectra, activations, own, own_gram, *msgs = call(
        functools.partial(first_kernel, rows, subs, cl, blocks),
        args + [table],
        [(s_shape, BF16)] + tail_outs,
        [
            pltpu.VMEM((rows, cl, frames + TAPS), BF16),
            pltpu.VMEM((blocks, chans, 2 * TAPS), BF16),
            pltpu.VMEM((GROUPS, rows, rank, GROUP * cl), BF16),
        ]
        + tail_scratch,
        (GROUPS,),
        spec,
        [pl.BlockSpec(memory_space=pl.ANY)] + [fixed(out[0]) for out in tail_outs],
    )

    def reduced(own, own_gram, msgs, w):
        got = [quad_shift(m, dx, dc) for m, (dx, dc) in zip(msgs, others)]
        (part,) = call(partial_kernel, [own, own_gram] + got, [msg])
        parts = [part] + [
            lax.ppermute(part, "frm", [(i, (i + shift) % frms) for i in range(frms)]) for shift in range(1, frms)
        ]
        return call(
            functools.partial(update_kernel, frms),
            [w] + parts,
            [((rank, size), F32), msg],
            [pltpu.VMEM((frms,) + msg[0], BF16)],
        )

    w_piece, w_msg = reduced(own, own_gram, msgs, w_own)
    w_msgs = [w_msg] + [quad_shift(w_msg, dx, dc) for dx, dc in others]
    whole = pl.BlockSpec(memory_space=pltpu.VMEM)
    activations, own, own_gram, *msgs = call(
        functools.partial(later_kernel, rows, subs, cl, blocks),
        w_msgs + [activations, spectra],
        tail_outs,
        [pltpu.VMEM((subs, GROUPS // subs, rows, rank, GROUP * cl), BF16)] + tail_scratch,
        in_specs=[whole] * (len(w_msgs) + 1) + [pl.BlockSpec(memory_space=pl.ANY)],
    )
    w_piece, _ = reduced(own, own_gram, msgs, w_piece)

    c_me = lax.axis_index("sub")
    full = jnp.zeros((subs, rank, size), F32)
    for dc in range(subs):
        got = w_piece if dc == 0 else lax.ppermute(w_piece, "sub", [(i, (i + dc) % subs) for i in range(subs)])
        full = lax.dynamic_update_slice(full, got[None], ((c_me + subs - dc) % subs, 0, 0))
    synergies = full.reshape(subs, rank, NF // subs, cl).transpose(3, 0, 2, 1).reshape(NF * cl, rank)

    wide = jnp.zeros((rank, window), F32)
    for shift in range(rows):
        got = activations if shift == 0 else row_shift(activations, shift)
        wide = lax.dynamic_update_slice(wide, got, (0, (x_me + rows - shift) % rows * frames))
    return (synergies, wide)


def solution(mesh):
    placed = (P("row", ("grp", "frm", "sub")), P("row", None), P(None, ("grp", "frm", "sub")))
    return jax.shard_map(
        shards,
        mesh=mesh,
        in_specs=placed,
        out_specs=(P(("grp", "row"), None), P(None, ("grp", "frm", "sub"))),
        check_vma=False,
    )
```

```python
import functools
import math

import jax
import jax.numpy as jnp
import ml_dtypes
import numpy as np
from jax import lax
from jax.experimental import pallas as pl
from jax.experimental.pallas import tpu as pltpu
from jax.sharding import PartitionSpec as P

NF = 40
TAPS = 128
HALF = TAPS // 2
GROUP = 4
GROUPS = NF // GROUP
F32 = jnp.float32
BF16 = jnp.bfloat16
HIGH = lax.Precision.HIGHEST
NT = (((1,), (1,)), ((), ()))
MIB = 1024 * 1024


def wavelets():
    f = np.float32
    level = np.arange(NF, dtype=f) / f(NF - 1)
    freq = f(2.0) * np.power(f(12.0), level)
    sigma = f(7.0) / (f(2.0 * math.pi) * freq)
    times = (np.arange(TAPS, dtype=f) - f(HALF)) / f(50.0)
    env = np.exp(-(times[None, :] ** 2) / (f(2.0) * sigma[:, None] ** 2))
    scale = f(1.0) / np.sqrt(np.sum(env * env, axis=1))
    env = env * scale[:, None]
    phase = f(2.0 * math.pi) * freq[:, None] * times[None, :]
    return np.stack([env * np.cos(phase), env * np.sin(phase)]).astype(ml_dtypes.bfloat16)


def toeplitz():
    kernel = wavelets()
    table = np.zeros((NF, 2 * TAPS, 2 * TAPS), ml_dtypes.bfloat16)
    for at in range(TAPS):
        for part in range(2):
            table[:, at : at + TAPS, part * TAPS + at] = kernel[part]
    return table


def split_two(value):
    top = value.astype(BF16)
    return top, (value - top.astype(F32)).astype(BF16)


def joined(message, at, rank):
    return message[:, at : at + rank].astype(F32) + message[:, at + rank : at + 2 * rank].astype(F32)


def pack(out_ref, main, gram):
    rank, size = main.shape
    top, rest = split_two(gram)
    out_ref[:, :size] = main.astype(BF16)
    out_ref[:, size : size + rank] = top
    out_ref[:, size + rank : size + 2 * rank] = rest


def prepare_kernel(w_ref, msg_ref, gram_ref):
    w = w_ref[...]
    gram = lax.dot_general(w, w, NT, precision=HIGH, preferred_element_type=F32)
    gram_ref[...] = gram
    pack(msg_ref, w, gram)


def group_rows(s_scr, g, pair, rows, cl):
    halves = []
    for blk in (2 * pair, 2 * pair + 1):
        parts = [
            s_scr[pl.ds(g * GROUP, GROUP), blk, x * cl : (x + 1) * cl, :].reshape(GROUP * cl, TAPS)
            for x in range(rows)
        ]
        halves.append(jnp.concatenate(parts, axis=0))
    return jnp.concatenate(halves, axis=1)


def add_crossed(s_scr, wg, num_scr, g, pairs, rows, cl):
    for pair in range(pairs):
        cols = slice(2 * TAPS * pair, 2 * TAPS * (pair + 1))
        num_scr[:, cols] += jnp.dot(wg, group_rows(s_scr, g, pair, rows, cl), preferred_element_type=F32)


def finish_update(old, gram, num_scr, s_scr, p_scr, h_out, own_ref, own_gram_ref, msg_refs, rows, subs, cl):
    rank, frames = old.shape
    pairs = frames // (2 * TAPS)
    per_sub = GROUPS // subs
    new = old * num_scr[...] / jnp.dot(gram, old, precision=HIGH, preferred_element_type=F32)
    h_out[...] = new
    low = new.astype(BF16)
    h_gram = lax.dot_general(new, new, NT, precision=HIGH, preferred_element_type=F32)
    wide = GROUP * cl
    for g in range(GROUPS):
        acc = jnp.zeros((rank, rows * wide), F32)
        for pair in range(pairs):
            cols = slice(2 * TAPS * pair, 2 * TAPS * (pair + 1))
            acc = acc + lax.dot_general(
                low[:, cols], group_rows(s_scr, g, pair, rows, cl), NT, preferred_element_type=F32
            )
        at = (g % per_sub) * wide
        for x in range(rows):
            p_scr[x, g // per_sub, :, at : at + wide] = acc[:, x * wide : (x + 1) * wide]
    x_me, c_me = lax.axis_index("row"), lax.axis_index("sub")
    own_ref[...] = p_scr[x_me, c_me]
    own_gram_ref[...] = h_gram
    at = 0
    for dx in range(rows):
        for dc in range(subs):
            if dx or dc:
                pack(msg_refs[at], p_scr[lax.rem(x_me + dx, rows), lax.rem(c_me + dc, subs)], h_gram)
                at += 1


def first_kernel(rows, subs, cl, blocks, *refs):
    refs = list(refs)
    sig_refs = [refs.pop(0) for _ in range(rows)]
    halo_refs = [refs.pop(0) for _ in range(rows)]
    w_refs = [refs.pop(0) for _ in range(rows)]
    gram_ref, h_ref, tab_ref = refs.pop(0), refs.pop(0), refs.pop(0)
    s_hbm, h_out, own_ref, own_gram_ref = (refs.pop(0) for _ in range(4))
    msg_refs = [refs.pop(0) for _ in range(rows * subs - 1)]
    xp_scr, x_scr, w_scr, s_scr, num_scr, p_scr, sems = refs
    rank = h_ref.shape[0]
    frames = blocks * TAPS
    wide = GROUP * cl
    g = pl.program_id(0)
    x_me = lax.axis_index("row")

    @pl.when(g == 0)
    def _():
        for shift in range(rows):
            owner = lax.rem(x_me + rows - shift, rows)
            xp_scr[owner] = sig_refs[shift][...]
            for at in range(GROUPS):
                w_scr[at, owner] = w_refs[shift][:, at * wide : (at + 1) * wide]

        @pl.when(x_me == 0)
        def _():
            for at in range(rows):
                xp_scr[at, :, :HALF] = halo_refs[at][...]

        @pl.when(x_me == rows - 1)
        def _():
            for at in range(rows):
                xp_scr[rows - 1 - at, :, frames + HALF :] = halo_refs[at][...]

        for blk in range(blocks):
            for x in range(rows):
                x_scr[blk, x * cl : (x + 1) * cl, :] = xp_scr[x, :, blk * TAPS : (blk + 2) * TAPS]
        num_scr[...] = jnp.zeros_like(num_scr)

    for at in range(GROUP):
        co = jnp.dot(x_scr[...].reshape(blocks * rows * cl, 2 * TAPS), tab_ref[at], preferred_element_type=F32)
        power = co[:, :TAPS] * co[:, :TAPS] + co[:, TAPS:] * co[:, TAPS:]
        s_scr[g * GROUP + at] = power.astype(BF16).reshape(blocks, rows * cl, TAPS)

    def copy_out(at):
        span = pl.ds(at * GROUP, GROUP)
        return pltpu.make_async_copy(s_scr.at[span], s_hbm.at[span], sems.at[at])

    copy_out(g).start()
    wg = jnp.concatenate([w_scr[g, x] for x in range(rows)], axis=1)
    add_crossed(s_scr, wg, num_scr, g, blocks // 2, rows, cl)

    @pl.when(g == GROUPS - 1)
    def _():
        gram = gram_ref[...]
        for shift in range(1, rows):
            gram = gram + joined(w_refs[shift], NF * cl, rank)
        old = h_ref[:, pl.ds(pl.multiple_of(x_me * frames, TAPS), frames)]
        finish_update(old, gram, num_scr, s_scr, p_scr, h_out, own_ref, own_gram_ref, msg_refs, rows, subs, cl)
        for at in range(GROUPS):
            copy_out(at).wait()


def later_kernel(rows, subs, cl, blocks, *refs):
    refs = list(refs)
    w_refs = [refs.pop(0) for _ in range(rows * subs)]
    h_ref, s_hbm = refs.pop(0), refs.pop(0)
    h_out, own_ref, own_gram_ref = (refs.pop(0) for _ in range(3))
    msg_refs = [refs.pop(0) for _ in range(rows * subs - 1)]
    w_scr, s_scr, num_scr, p_scr, sems = refs
    rank = h_ref.shape[0]
    per_sub = GROUPS // subs
    wide = GROUP * cl
    x_me, c_me = lax.axis_index("row"), lax.axis_index("sub")

    def copy_in(at):
        span = pl.ds(at * GROUP, GROUP)
        return pltpu.make_async_copy(s_hbm.at[span], s_scr.at[span], sems.at[at])

    for at in range(GROUPS):
        copy_in(at).start()
    gram = jnp.zeros((rank, rank), F32)
    at = 0
    for dx in range(rows):
        for dc in range(subs):
            x_of, c_of = lax.rem(x_me + rows - dx, rows), lax.rem(c_me + subs - dc, subs)
            for part in range(per_sub):
                w_scr[c_of, part, x_of] = w_refs[at][:, part * wide : (part + 1) * wide]
            gram = gram + joined(w_refs[at], per_sub * wide, rank)
            at += 1
    num_scr[...] = jnp.zeros_like(num_scr)
    for g in range(GROUPS):
        copy_in(g).wait()
        wg = jnp.concatenate([w_scr[g // per_sub, g % per_sub, x] for x in range(rows)], axis=1)
        add_crossed(s_scr, wg, num_scr, g, blocks // 2, rows, cl)
    finish_update(h_ref[...], gram, num_scr, s_scr, p_scr, h_out, own_ref, own_gram_ref, msg_refs, rows, subs, cl)


def partial_kernel(*refs):
    own_ref, own_gram_ref, *msg_refs, out_ref = refs
    rank, size = own_ref.shape
    total, gram = own_ref[...], own_gram_ref[...]
    for ref in msg_refs:
        total = total + ref[:, :size].astype(F32)
        gram = gram + joined(ref, size, rank)
    pack(out_ref, total, gram)


def update_kernel(count, w_ref, *refs):
    msg_refs, (new_ref, out_ref, scr) = refs[:count], refs[count:]
    rank, size = new_ref.shape
    z_me = lax.axis_index("frm")
    for shift in range(count):
        scr[lax.rem(z_me + count - shift, count)] = msg_refs[shift][...]
    total, gram = scr[0, :, :size].astype(F32), joined(scr[0], size, rank)
    for at in range(1, count):
        total = total + scr[at, :, :size].astype(F32)
        gram = gram + joined(scr[at], size, rank)
    w = w_ref[lax.axis_index("sub")] if len(w_ref.shape) == 3 else w_ref[...]
    new = w * total / jnp.dot(gram, w, precision=HIGH, preferred_element_type=F32)
    new_ref[...] = new
    pack(out_ref, new, lax.dot_general(new, new, NT, precision=HIGH, preferred_element_type=F32))


def call(kernel, args, outs, scratch=(), grid=None, in_specs=None, out_specs=None, limit=4):
    whole = pl.BlockSpec(memory_space=pltpu.VMEM)
    extra = {} if grid is None else {"grid": grid}
    return pl.pallas_call(
        kernel,
        out_shape=[jax.ShapeDtypeStruct(*out) for out in outs],
        in_specs=in_specs or [whole] * len(args),
        out_specs=out_specs or [whole] * len(outs),
        scratch_shapes=list(scratch),
        compiler_params=pltpu.CompilerParams(vmem_limit_bytes=limit * MIB),
        **extra,
    )(*args)


def shards(signal, w_start, h_start):
    rows, subs, frms = (lax.axis_size(axis) for axis in ("row", "sub", "frm"))
    x_me = lax.axis_index("row")
    cl, window = signal.shape
    rank = w_start.shape[1]
    frames = window // rows
    blocks = frames // TAPS
    chans = rows * cl
    size = NF * cl // subs
    line = frms * subs

    def row_shift(value, shift):
        return lax.ppermute(value, "row", [(i, (i + shift) % rows) for i in range(rows)])

    def quad_shift(value, dx, dc):
        pairs = [
            (x * subs + c, ((x + dx) % rows) * subs + (c + dc) % subs) for x in range(rows) for c in range(subs)
        ]
        return lax.ppermute(value, ("row", "sub"), pairs)

    def place(x, at):
        return (at // subs * rows + x) * subs + at % subs

    others = [(dx, dc) for dx in range(rows) for dc in range(subs) if dx or dc]

    padded = jnp.pad(signal, ((0, 0), (HALF, HALF)))

    def part_for(target):
        return lax.dynamic_slice_in_dim(padded, target * frames, frames + TAPS, 1)

    sig = [part_for(x_me)]
    for shift in range(1, rows):
        sig.append(row_shift(part_for((x_me + shift) % rows), shift))
    tail, head = signal[:, window - HALF :], signal[:, :HALF]
    halos = []
    for at in range(rows):
        to_next = [(place(at, i), place(0, i + 1)) for i in range(line - 1)]
        to_prev = [(place(rows - 1 - at, i + 1), place(rows - 1, i)) for i in range(line - 1)]
        halos.append(lax.ppermute(jnp.where(x_me == at, tail, head), ("frm", "row", "sub"), to_next + to_prev))

    w_cols = w_start.reshape(cl, NF, rank).transpose(2, 1, 0).reshape(rank, NF * cl)
    w_msg, w_gram = call(
        prepare_kernel, [w_cols], [((rank, NF * cl + 2 * rank), BF16), ((rank, rank), F32)]
    )
    w_msgs = [w_msg] + [row_shift(w_msg, shift) for shift in range(1, rows)]
    w_own = w_cols.reshape(rank, subs, size).transpose(1, 0, 2)

    msg = ((rank, size + 2 * rank), BF16)
    tail_outs = [((rank, frames), F32), ((rank, size), F32), ((rank, rank), F32)] + [msg] * len(others)
    s_shape = (NF, blocks, chans, TAPS)

    def fixed(shape):
        return pl.BlockSpec(shape, lambda g: (0,) * len(shape))

    table = jnp.asarray(toeplitz())
    args = sig + halos + w_msgs + [w_gram, h_start]
    spec = [fixed(a.shape) for a in args] + [pl.BlockSpec((GROUP, 2 * TAPS, 2 * TAPS), lambda g: (g, 0, 0))]
    tail_scratch = [
        pltpu.VMEM(s_shape, BF16),
        pltpu.VMEM((rank, frames), F32),
        pltpu.VMEM((rows, subs, rank, size), F32),
        pltpu.SemaphoreType.DMA((GROUPS,)),
    ]
    spectra, activations, own, own_gram, *msgs = call(
        functools.partial(first_kernel, rows, subs, cl, blocks),
        args + [table],
        [(s_shape, BF16)] + tail_outs,
        [
            pltpu.VMEM((rows, cl, frames + TAPS), BF16),
            pltpu.VMEM((blocks, chans, 2 * TAPS), BF16),
            pltpu.VMEM((GROUPS, rows, rank, GROUP * cl), BF16),
        ]
        + tail_scratch,
        (GROUPS,),
        spec,
        [pl.BlockSpec(memory_space=pl.ANY)] + [fixed(out[0]) for out in tail_outs],
        limit=26,
    )

    def reduced(own, own_gram, msgs, w):
        got = [quad_shift(m, dx, dc) for m, (dx, dc) in zip(msgs, others)]
        (part,) = call(partial_kernel, [own, own_gram] + got, [msg])
        parts = [part] + [
            lax.ppermute(part, "frm", [(i, (i + shift) % frms) for i in range(frms)]) for shift in range(1, frms)
        ]
        return call(
            functools.partial(update_kernel, frms),
            [w] + parts,
            [((rank, size), F32), msg],
            [pltpu.VMEM((frms,) + msg[0], BF16)],
        )

    w_piece, w_msg = reduced(own, own_gram, msgs, w_own)
    w_msgs = [w_msg] + [quad_shift(w_msg, dx, dc) for dx, dc in others]
    whole = pl.BlockSpec(memory_space=pltpu.VMEM)
    activations, own, own_gram, *msgs = call(
        functools.partial(later_kernel, rows, subs, cl, blocks),
        w_msgs + [activations, spectra],
        tail_outs,
        [pltpu.VMEM((subs, GROUPS // subs, rows, rank, GROUP * cl), BF16)] + tail_scratch,
        in_specs=[whole] * (len(w_msgs) + 1) + [pl.BlockSpec(memory_space=pl.ANY)],
        limit=20,
    )
    w_piece, _ = reduced(own, own_gram, msgs, w_piece)

    c_me = lax.axis_index("sub")
    full = jnp.zeros((subs, rank, size), F32)
    for dc in range(subs):
        got = w_piece if dc == 0 else lax.ppermute(w_piece, "sub", [(i, (i + dc) % subs) for i in range(subs)])
        full = lax.dynamic_update_slice(full, got[None], ((c_me + subs - dc) % subs, 0, 0))
    synergies = full.reshape(subs, rank, NF // subs, cl).transpose(3, 0, 2, 1).reshape(NF * cl, rank)

    wide = jnp.zeros((rank, window), F32)
    for shift in range(rows):
        got = activations if shift == 0 else row_shift(activations, shift)
        wide = lax.dynamic_update_slice(wide, got, (0, (x_me + rows - shift) % rows * frames))
    return (synergies, wide)


def solution(mesh):
    placed = (P("row", ("grp", "frm", "sub")), P("row", None), P(None, ("grp", "frm", "sub")))
    return jax.shard_map(
        shards,
        mesh=mesh,
        in_specs=placed,
        out_specs=(P(("grp", "row"), None), P(None, ("grp", "frm", "sub"))),
        check_vma=False,
    )
```

```python
import functools
import math

import jax
import jax.numpy as jnp
import ml_dtypes
import numpy as np
from jax import lax
from jax.experimental import pallas as pl
from jax.experimental.pallas import tpu as pltpu
from jax.sharding import PartitionSpec as P

NF = 40
TAPS = 128
HALF = TAPS // 2
GROUP = 4
GROUPS = NF // GROUP
F32 = jnp.float32
BF16 = jnp.bfloat16
HIGH = lax.Precision.HIGHEST
NT = (((1,), (1,)), ((), ()))
MIB = 1024 * 1024


def wavelets():
    f = np.float32
    level = np.arange(NF, dtype=f) / f(NF - 1)
    freq = f(2.0) * np.power(f(12.0), level)
    sigma = f(7.0) / (f(2.0 * math.pi) * freq)
    times = (np.arange(TAPS, dtype=f) - f(HALF)) / f(50.0)
    env = np.exp(-(times[None, :] ** 2) / (f(2.0) * sigma[:, None] ** 2))
    scale = f(1.0) / np.sqrt(np.sum(env * env, axis=1))
    env = env * scale[:, None]
    phase = f(2.0 * math.pi) * freq[:, None] * times[None, :]
    return np.stack([env * np.cos(phase), env * np.sin(phase)]).astype(ml_dtypes.bfloat16)


def toeplitz():
    kernel = wavelets()
    table = np.zeros((NF, 2 * TAPS, 2 * TAPS), ml_dtypes.bfloat16)
    for at in range(TAPS):
        for part in range(2):
            table[:, at : at + TAPS, part * TAPS + at] = kernel[part]
    return table


def split_two(value):
    top = value.astype(BF16)
    return top, (value - top.astype(F32)).astype(BF16)


def joined(message, at, rank):
    return message[:, at : at + rank].astype(F32) + message[:, at + rank : at + 2 * rank].astype(F32)


def pack(out_ref, main, gram):
    rank, size = main.shape
    top, rest = split_two(gram)
    out_ref[:, :size] = main.astype(BF16)
    out_ref[:, size : size + rank] = top
    out_ref[:, size + rank : size + 2 * rank] = rest


def prepare_kernel(w_ref, msg_ref, gram_ref):
    w = w_ref[...]
    gram = lax.dot_general(w, w, NT, precision=HIGH, preferred_element_type=F32)
    gram_ref[...] = gram
    pack(msg_ref, w, gram)


def group_rows(s_ref, g, pair, rows, cl):
    halves = []
    for blk in (2 * pair, 2 * pair + 1):
        parts = [
            s_ref[g * GROUP : (g + 1) * GROUP, blk, x * cl : (x + 1) * cl, :].reshape(GROUP * cl, TAPS)
            for x in range(rows)
        ]
        halves.append(jnp.concatenate(parts, axis=0))
    return jnp.concatenate(halves, axis=1)


def finish_update(old, gram, w_scr, num_scr, s_ref, p_scr, h_out, own_ref, own_gram_ref, msg_refs, rows, subs, cl):
    rank, frames = old.shape
    pairs = frames // (2 * TAPS)
    per_sub = GROUPS // subs
    wide = GROUP * cl
    for pair in range(pairs):
        acc = jnp.zeros((rank, 2 * TAPS), F32)
        for g in range(GROUPS):
            wg = jnp.concatenate([w_scr[g // per_sub, g % per_sub, x] for x in range(rows)], axis=1)
            acc = acc + jnp.dot(wg, group_rows(s_ref, g, pair, rows, cl), preferred_element_type=F32)
        num_scr[:, 2 * TAPS * pair : 2 * TAPS * (pair + 1)] = acc
    new = old * num_scr[...] / jnp.dot(gram, old, precision=HIGH, preferred_element_type=F32)
    h_out[...] = new
    low = new.astype(BF16)
    h_gram = lax.dot_general(new, new, NT, precision=HIGH, preferred_element_type=F32)
    for g in range(GROUPS):
        acc = jnp.zeros((rank, rows * wide), F32)
        for pair in range(pairs):
            cols = slice(2 * TAPS * pair, 2 * TAPS * (pair + 1))
            acc = acc + lax.dot_general(
                low[:, cols], group_rows(s_ref, g, pair, rows, cl), NT, preferred_element_type=F32
            )
        at = (g % per_sub) * wide
        for x in range(rows):
            p_scr[g // per_sub, x, :, at : at + wide] = acc[:, x * wide : (x + 1) * wide]
    c_me = lax.axis_index("sub")
    size = per_sub * wide
    own_ref[...] = p_scr[c_me]
    own_gram_ref[...] = h_gram
    for dc in range(1, subs):
        ref = msg_refs[dc - 1]
        ref[:, :, :size] = p_scr[lax.rem(c_me + dc, subs)]
        for x in range(rows):
            ref[x, :, size:] = h_gram


def first_kernel(rows, subs, cl, blocks, *refs):
    refs = list(refs)
    sig_hbm, h_hbm, tab_hbm, order_hbm = (refs.pop(0) for _ in range(4))
    sig_refs = [refs.pop(0) for _ in range(rows - 1)]
    halo_ref, w_ref, gram_ref = (refs.pop(0) for _ in range(3))
    w_msgs = [refs.pop(0) for _ in range(rows - 1)]
    s_ref, w_out, h_out, own_ref, own_gram_ref = (refs.pop(0) for _ in range(5))
    msg_refs = [refs.pop(0) for _ in range(subs - 1)]
    sig_scr, old_scr, tab_scr, order_scr, xp_scr, x_scr, w_scr, num_scr, p_scr, sems, tab_sems = refs
    rank, frames = old_scr.shape
    window = sig_hbm.shape[1]
    width = sig_scr.shape[1]
    per_sub = GROUPS // subs
    wide = GROUP * cl
    x_me, c_me = lax.axis_index("row"), lax.axis_index("sub")
    depth = tab_scr.shape[0]

    def tab_copy(g):
        slot = lax.rem(g, depth)
        return pltpu.make_async_copy(tab_hbm.at[pl.ds(g * GROUP, GROUP)], tab_scr.at[slot], tab_sems.at[slot])

    begin = pl.multiple_of(jnp.clip(x_me * frames - TAPS, 0, window - width), TAPS)
    sig_copy = pltpu.make_async_copy(sig_hbm.at[:, pl.ds(begin, width)], sig_scr, sems.at[0])
    old_copy = pltpu.make_async_copy(
        h_hbm.at[:, pl.ds(pl.multiple_of(x_me * frames, TAPS), frames)], old_scr, sems.at[1]
    )
    order_copy = pltpu.make_async_copy(order_hbm, order_scr, sems.at[2])
    sig_copy.start()
    for g in range(depth - 1):
        tab_copy(g).start()
    old_copy.start()
    order_copy.start()
    sig_copy.wait()

    def place(source, owner):
        @pl.when(x_me == 0)
        def _():
            xp_scr[owner, :, HALF:] = source[:, : frames + HALF]

        @pl.when(x_me == rows - 1)
        def _():
            skip = width - frames - HALF
            xp_scr[owner, :, : frames + HALF] = source[:, skip:]

        if rows > 2:

            @pl.when((x_me > 0) & (x_me < rows - 1))
            def _():
                xp_scr[owner] = source[:, HALF : HALF + frames + TAPS]

    place(sig_scr, x_me)
    for shift in range(1, rows):
        place(sig_refs[shift - 1], lax.rem(x_me + rows - shift, rows))

    @pl.when(x_me == 0)
    def _():
        for at in range(rows):
            xp_scr[rows - 1 - at, :, :HALF] = halo_ref[at * cl : (at + 1) * cl, HALF:]

    @pl.when(x_me == rows - 1)
    def _():
        for at in range(rows):
            xp_scr[(rows - at) % rows, :, frames + HALF :] = halo_ref[at * cl : (at + 1) * cl, :HALF]

    for blk in range(blocks):
        for x in range(rows):
            x_scr[blk, x * cl : (x + 1) * cl, :] = xp_scr[x, :, blk * TAPS : (blk + 2) * TAPS]

    def convolve(g, carry):
        tab_copy(g).wait()

        @pl.when(g + depth - 1 < GROUPS)
        def _():
            tab_copy(g + depth - 1).start()

        for at in range(GROUP):
            co = jnp.dot(
                x_scr[...].reshape(blocks * rows * cl, 2 * TAPS),
                tab_scr[lax.rem(g, depth), at],
                preferred_element_type=F32,
            )
            power = co[:, :TAPS] * co[:, :TAPS] + co[:, TAPS:] * co[:, TAPS:]
            s_ref[g * GROUP + at] = power.astype(BF16).reshape(blocks, rows * cl, TAPS)
        return carry

    lax.fori_loop(0, GROUPS, convolve, 0)

    order_copy.wait()
    w = w_ref[...]
    top = w.astype(BF16)
    rest = w - top.astype(F32)
    middle = rest.astype(BF16)
    terms = [top, middle, (rest - middle.astype(F32)).astype(BF16)] + [ref[:, : NF * cl] for ref in w_msgs]
    moved = jnp.dot(jnp.concatenate(terms, axis=0), order_scr[...], preferred_element_type=F32)
    for at in range(GROUPS):
        cols = slice(at * wide, (at + 1) * wide)
        w_scr[at // per_sub, at % per_sub, x_me] = moved[:rank, cols].astype(BF16)
        for shift in range(1, rows):
            owner = lax.rem(x_me + rows - shift, rows)
            line = (shift + 2) * rank
            w_scr[at // per_sub, at % per_sub, owner] = moved[line : line + rank, cols].astype(BF16)
    whole = moved[:rank] + (moved[rank : 2 * rank] + moved[2 * rank : 3 * rank])
    size = per_sub * wide
    for c in range(subs):

        @pl.when(c_me == c)
        def _():
            w_out[...] = whole[:, c * size : (c + 1) * size]

    gram = gram_ref[...]
    for ref in w_msgs:
        gram = gram + joined(ref, NF * cl, rank)
    old_copy.wait()
    finish_update(
        old_scr[...], gram, w_scr, num_scr, s_ref, p_scr, h_out, own_ref, own_gram_ref, msg_refs, rows, subs, cl
    )


def later_kernel(rows, subs, cl, blocks, *refs):
    refs = list(refs)
    w_refs = [refs.pop(0) for _ in range(rows * subs)]
    h_ref, s_ref = refs.pop(0), refs.pop(0)
    h_out, own_ref, own_gram_ref = (refs.pop(0) for _ in range(3))
    msg_refs = [refs.pop(0) for _ in range(subs - 1)]
    w_scr, num_scr, p_scr = refs
    rank = h_ref.shape[0]
    per_sub = GROUPS // subs
    wide = GROUP * cl
    x_me, c_me = lax.axis_index("row"), lax.axis_index("sub")
    gram = jnp.zeros((rank, rank), F32)
    at = 0
    for dx in range(rows):
        for dc in range(subs):
            x_of, c_of = lax.rem(x_me + rows - dx, rows), lax.rem(c_me + subs - dc, subs)
            for part in range(per_sub):
                w_scr[c_of, part, x_of] = w_refs[at][:, part * wide : (part + 1) * wide]
            gram = gram + joined(w_refs[at], per_sub * wide, rank)
            at += 1
    finish_update(
        h_ref[...], gram, w_scr, num_scr, s_ref, p_scr, h_out, own_ref, own_gram_ref, msg_refs, rows, subs, cl
    )


def core_kernel(rows, subs, *refs):
    own_ref, own_gram_ref, *refs = refs
    msg_refs, refs = refs[: subs - 1], refs[subs - 1 :]
    out_ref, gram_ref, *out_msgs, scr = refs
    size = own_ref.shape[2]
    total, gram = own_ref[...], own_gram_ref[...]
    for ref in msg_refs:
        total = total + ref[:, :, :size]
        gram = gram + ref[0, :, size:]
    scr[...] = total
    gram_ref[...] = gram
    x_me = lax.axis_index("row")
    out_ref[...] = scr[x_me]
    for dx in range(1, rows):
        pack(out_msgs[dx - 1], scr[lax.rem(x_me + dx, rows)], gram)


def row_kernel(*refs):
    own_ref, own_gram_ref, *msg_refs, out_ref = refs
    rank, size = own_ref.shape
    total, gram = own_ref[...], own_gram_ref[...]
    for ref in msg_refs:
        total = total + ref[:, :size].astype(F32)
        gram = gram + joined(ref, size, rank)
    pack(out_ref, total, gram)


def summed(z_me, count, msg_refs, scr, rank, size):
    for shift in range(count):
        scr[partner(z_me, shift, count)] = msg_refs[shift][...]
    total, gram = scr[0, :, :size].astype(F32), joined(scr[0], size, rank)
    for at in range(1, count):
        total = total + scr[at, :, :size].astype(F32)
        gram = gram + joined(scr[at], size, rank)
    return total, gram


def partner(place, shift, count):
    if count & (count - 1):
        return (place + count - shift) % count
    return place ^ shift


def update_kernel(count, w_ref, *refs):
    msg_refs, (new_ref, out_ref, scr) = refs[:count], refs[count:]
    rank, size = new_ref.shape
    total, gram = summed(lax.axis_index("frm"), count, msg_refs, scr, rank, size)
    w = w_ref[...]
    new = w * total / jnp.dot(gram, w, precision=HIGH, preferred_element_type=F32)
    new_ref[...] = new
    pack(out_ref, new, lax.dot_general(new, new, NT, precision=HIGH, preferred_element_type=F32))


def last_kernel(count, w_ref, order_ref, *refs):
    msg_refs, (out_ref, scr) = refs[:count], refs[count:]
    rank, size = w_ref.shape
    total, gram = summed(lax.axis_index("frm"), count, msg_refs, scr, rank, size)
    w = w_ref[...]
    new = w * total / jnp.dot(gram, w, precision=HIGH, preferred_element_type=F32)
    top = new.astype(BF16)
    rest = new - top.astype(F32)
    middle = rest.astype(BF16)
    terms = jnp.concatenate([top, middle, (rest - middle.astype(F32)).astype(BF16)], axis=0)
    for c in range(order_ref.shape[1] // size):

        @pl.when(lax.axis_index("sub") == c)
        def _():
            moved = lax.dot_general(
                terms, order_ref[:, c * size : (c + 1) * size], NT, preferred_element_type=F32
            )
            out_ref[...] = moved[:rank] + (moved[rank : 2 * rank] + moved[2 * rank :])


def join_kernel(rows, *refs):
    own_refs, (out_ref, sems) = refs[:rows], refs[rows:]
    frames = own_refs[0].shape[1]
    x_me = lax.axis_index("row")
    copies = []
    for shift in range(rows):
        begin = pl.multiple_of(lax.rem(x_me + rows - shift, rows) * frames, TAPS)
        copies.append(pltpu.make_async_copy(own_refs[shift], out_ref.at[:, pl.ds(begin, frames)], sems.at[shift]))
    for copy in copies:
        copy.start()
    for copy in copies:
        copy.wait()


def call(kernel, args, outs, scratch=(), in_specs=None, out_specs=None, limit=4):
    whole = pl.BlockSpec(memory_space=pltpu.VMEM)
    return pl.pallas_call(
        kernel,
        out_shape=[jax.ShapeDtypeStruct(*out) if isinstance(out, tuple) else out for out in outs],
        in_specs=in_specs or [whole] * len(args),
        out_specs=out_specs or [whole] * len(outs),
        scratch_shapes=list(scratch),
        compiler_params=pltpu.CompilerParams(vmem_limit_bytes=limit * MIB),
    )(*args)


def reorder(cl):
    order = np.zeros((cl, NF, NF, cl), ml_dtypes.bfloat16)
    chans, freqs = np.meshgrid(np.arange(cl), np.arange(NF), indexing="ij")
    order[chans, freqs, freqs, chans] = 1
    return order.reshape(cl * NF, NF * cl)


def shards(signal, w_start, h_start):
    rows, subs, frms = (lax.axis_size(axis) for axis in ("row", "sub", "frm"))
    x_me = lax.axis_index("row")
    cl, window = signal.shape
    rank = w_start.shape[1]
    frames = window // rows
    blocks = frames // TAPS
    chans = rows * cl
    size = NF * cl // subs
    line = frms * subs
    width = frames + (TAPS if rows == 2 else 2 * TAPS)
    anywhere = pl.BlockSpec(memory_space=pl.ANY)
    whole = pl.BlockSpec(memory_space=pltpu.VMEM)

    def hbm(value):
        return pltpu.with_memory_space_constraint(value, pltpu.HBM)

    def vmem(value):
        return pltpu.with_memory_space_constraint(value, pltpu.VMEM)

    def row_shift(value, shift):
        return lax.ppermute(value, "row", [(i, (i + shift) % rows) for i in range(rows)])

    def sub_shift(value, shift):
        return lax.ppermute(value, "sub", [(i, (i + shift) % subs) for i in range(subs)])

    def frm_shift(value, shift):
        return lax.ppermute(value, "frm", [(partner(i, shift, frms), i) for i in range(frms)])

    def place(x, at):
        return (at // subs * rows + x) * subs + at % subs

    def begin(target):
        return jnp.clip(target * frames - TAPS, 0, window - width)

    sig = [
        row_shift(lax.dynamic_slice_in_dim(signal, begin((x_me + shift) % rows), width, 1), shift)
        for shift in range(1, rows)
    ]
    edge = jnp.where(x_me == 0, 0, window - TAPS)
    got_edge = jnp.where(x_me == 0, 0, width - TAPS)
    ends = [lax.dynamic_slice_in_dim(signal, edge, TAPS, 1)]
    ends += [lax.dynamic_slice_in_dim(part, got_edge, TAPS, 1) for part in sig]
    pairs = [(place(rows - 1, i), place(0, i + 1)) for i in range(line - 1)]
    halo = lax.ppermute(
        jnp.concatenate(ends, axis=0), ("frm", "row", "sub"), pairs + [(b, a) for a, b in pairs]
    )

    w_cols = w_start.T
    w_msg, w_gram = call(
        prepare_kernel, [w_cols], [((rank, NF * cl + 2 * rank), BF16), ((rank, rank), F32)]
    )
    w_msgs = [row_shift(w_msg, shift) for shift in range(1, rows)]

    msg = ((rank, size + 2 * rank), BF16)
    piece = ((rank, size), F32)
    tail_outs = [((rank, frames), F32), ((rows,) + piece[0], F32), ((rank, rank), F32)]
    tail_outs += [((rows, rank, size + rank), F32)] * (subs - 1)
    tail_scratch = [
        pltpu.VMEM((subs, GROUPS // subs, rows, rank, GROUP * cl), BF16),
        pltpu.VMEM((rank, frames), F32),
        pltpu.VMEM((subs, rows) + piece[0], F32),
    ]
    order = jnp.asarray(reorder(cl))
    held = [hbm(signal), hbm(h_start), hbm(jnp.asarray(toeplitz())), hbm(order)]
    rest = sig + [halo, w_cols, w_gram] + w_msgs
    spectra, w_piece, activations, own, own_gram, *msgs = call(
        functools.partial(first_kernel, rows, subs, cl, blocks),
        held + rest,
        [pltpu.VMEM((NF, blocks, chans, TAPS), BF16), piece] + tail_outs,
        [
            pltpu.VMEM((cl, width), BF16),
            pltpu.VMEM((rank, frames), F32),
            pltpu.VMEM((3, GROUP, 2 * TAPS, 2 * TAPS), BF16),
            pltpu.VMEM(order.shape, BF16),
            pltpu.VMEM((rows, cl, frames + TAPS), BF16),
            pltpu.VMEM((blocks, chans, 2 * TAPS), BF16),
        ]
        + tail_scratch
        + [pltpu.SemaphoreType.DMA((3,)), pltpu.SemaphoreType.DMA((3,))],
        in_specs=[anywhere] * len(held) + [whole] * len(rest),
        limit=24,
    )

    def gathered(own, own_gram, msgs):
        got = [sub_shift(m, dc + 1) for dc, m in enumerate(msgs)]
        part, gram, *outs = call(
            functools.partial(core_kernel, rows, subs),
            [own, own_gram] + got,
            [piece, ((rank, rank), F32)] + [msg] * (rows - 1),
            [pltpu.VMEM((rows,) + piece[0], F32)],
        )
        got = [row_shift(m, dx + 1) for dx, m in enumerate(outs)]
        (part,) = call(row_kernel, [part, gram] + got, [msg])
        return [part] + [frm_shift(part, shift) for shift in range(1, frms)]

    piled = [pltpu.VMEM((frms,) + msg[0], BF16)]
    w_piece, w_msg = call(
        functools.partial(update_kernel, frms), [w_piece] + gathered(own, own_gram, msgs), [piece, msg], piled
    )
    w_msgs = []
    for dx in range(rows):
        base = row_shift(w_msg, dx) if dx else w_msg
        w_msgs += [base] + [sub_shift(base, dc) for dc in range(1, subs)]
    activations, own, own_gram, *msgs = call(
        functools.partial(later_kernel, rows, subs, cl, blocks),
        w_msgs + [activations, vmem(spectra)],
        tail_outs,
        tail_scratch,
        limit=8,
    )
    (part,) = call(
        functools.partial(last_kernel, frms),
        [w_piece, vmem(order)] + gathered(own, own_gram, msgs),
        [((rank, NF * cl), F32)],
        piled,
    )
    synergies = part
    for dc in range(1, subs):
        synergies = synergies + sub_shift(part, dc)

    (wide,) = call(
        functools.partial(join_kernel, rows),
        [activations] + [row_shift(activations, shift) for shift in range(1, rows)],
        [pltpu.HBM((rank, window), F32)],
        [pltpu.SemaphoreType.DMA((rows,))],
        in_specs=[anywhere] * rows,
        out_specs=[anywhere],
    )
    return (synergies.T, wide)


def solution(mesh):
    placed = (P("row", ("grp", "frm", "sub")), P("row", None), P(None, ("grp", "frm", "sub")))
    return jax.shard_map(
        shards,
        mesh=mesh,
        in_specs=placed,
        out_specs=(P(("grp", "row"), None), P(None, ("grp", "frm", "sub"))),
        check_vma=False,
    )
```

```python
import functools
import math

import jax
import jax.numpy as jnp
import ml_dtypes
import numpy as np
from jax import lax
from jax.experimental import pallas as pl
from jax.experimental.pallas import tpu as pltpu
from jax.sharding import PartitionSpec as P

NF = 40
TAPS = 128
HALF = TAPS // 2
GROUP = 4
GROUPS = NF // GROUP
F32 = jnp.float32
BF16 = jnp.bfloat16
HIGH = lax.Precision.HIGHEST
NT = (((1,), (1,)), ((), ()))
MIB = 1024 * 1024


def wavelets():
    f = np.float32
    level = np.arange(NF, dtype=f) / f(NF - 1)
    freq = f(2.0) * np.power(f(12.0), level)
    sigma = f(7.0) / (f(2.0 * math.pi) * freq)
    times = (np.arange(TAPS, dtype=f) - f(HALF)) / f(50.0)
    env = np.exp(-(times[None, :] ** 2) / (f(2.0) * sigma[:, None] ** 2))
    scale = f(1.0) / np.sqrt(np.sum(env * env, axis=1))
    env = env * scale[:, None]
    phase = f(2.0 * math.pi) * freq[:, None] * times[None, :]
    return np.stack([env * np.cos(phase), env * np.sin(phase)]).astype(ml_dtypes.bfloat16)


def toeplitz():
    kernel = wavelets()
    table = np.zeros((NF, 2 * TAPS, 2 * TAPS), ml_dtypes.bfloat16)
    for at in range(TAPS):
        for part in range(2):
            table[:, at : at + TAPS, part * TAPS + at] = kernel[part]
    return table


def split_two(value):
    top = value.astype(BF16)
    return top, (value - top.astype(F32)).astype(BF16)


def joined(message, at, rank):
    return message[:, at : at + rank].astype(F32) + message[:, at + rank : at + 2 * rank].astype(F32)


def pack(out_ref, main, gram):
    rank, size = main.shape
    top, rest = split_two(gram)
    out_ref[:, :size] = main.astype(BF16)
    out_ref[:, size : size + rank] = top
    out_ref[:, size + rank : size + 2 * rank] = rest


def prepare_kernel(w_ref, *refs):
    msg_ref, gram_ref = refs[-2:]
    w = w_ref[...]
    gram = lax.dot_general(w, w, NT, precision=HIGH, preferred_element_type=F32)
    gram_ref[...] = gram
    pack(msg_ref, w, gram)


def group_rows(s_ref, g, pair, rows, cl):
    halves = []
    for blk in (2 * pair, 2 * pair + 1):
        parts = [
            s_ref[pl.ds(g * GROUP, GROUP), blk, x * cl : (x + 1) * cl, :].reshape(GROUP * cl, TAPS)
            for x in range(rows)
        ]
        halves.append(jnp.concatenate(parts, axis=0))
    return jnp.concatenate(halves, axis=1)


def crossed(low, s_ref, core, out_ref, rows, subs, cl):
    per_sub = GROUPS // subs
    wide = GROUP * cl
    for part in range(per_sub):
        acc = jnp.zeros((low.shape[0], rows * wide), F32)
        for pair in range(low.shape[1] // (2 * TAPS)):
            cols = slice(2 * TAPS * pair, 2 * TAPS * (pair + 1))
            spectra = group_rows(s_ref, core * per_sub + part, pair, rows, cl)
            acc = acc + lax.dot_general(low[:, cols], spectra, NT, preferred_element_type=F32)
        for x in range(rows):
            out_ref[x, :, part * wide : (part + 1) * wide] = acc[:, x * wide : (x + 1) * wide]


def new_activations(old, gram, w_scr, num_scr, s_ref, h_out, h_gram_ref, msg_refs, rows, subs, cl):
    rank, frames = old.shape
    per_sub = GROUPS // subs
    for pair in range(frames // (2 * TAPS)):
        acc = jnp.zeros((rank, 2 * TAPS), F32)
        for g in range(GROUPS):
            wg = jnp.concatenate([w_scr[g // per_sub, g % per_sub, x] for x in range(rows)], axis=1)
            acc = acc + jnp.dot(wg, group_rows(s_ref, g, pair, rows, cl), preferred_element_type=F32)
        num_scr[:, 2 * TAPS * pair : 2 * TAPS * (pair + 1)] = acc
    new = old * num_scr[...] / jnp.dot(gram, old, precision=HIGH, preferred_element_type=F32)
    h_out[...] = new
    h_gram = lax.dot_general(new, new, NT, precision=HIGH, preferred_element_type=F32)
    h_gram_ref[...] = h_gram
    size = per_sub * GROUP * cl
    c_me = lax.axis_index("sub")
    for dc in range(1, subs):
        ref = msg_refs[dc - 1]
        crossed(new.astype(BF16), s_ref, lax.rem(c_me + dc, subs), ref, rows, subs, cl)
        for x in range(rows):
            ref[x, :, size:] = h_gram


def own_kernel(rows, subs, cl, h_ref, s_ref, out_ref):
    crossed(h_ref[...].astype(BF16), s_ref, lax.axis_index("sub"), out_ref, rows, subs, cl)


def spectra_kernel(rows, cl, blocks, *refs):
    refs = list(refs)
    sig_hbm, h_hbm, w_hbm, tab_hbm, order_hbm = (refs.pop(0) for _ in range(5))
    sig_refs = [refs.pop(0) for _ in range(rows - 1)]
    halo_refs = [refs.pop(0) for _ in range(rows)]
    s_ref, old_ref, w_ref, order_ref = (refs.pop(0) for _ in range(4))
    sig_scr, tab_scr, xp_scr, x_scr, sems, tab_sems = refs
    frames = old_ref.shape[1]
    window = sig_hbm.shape[1]
    width = sig_scr.shape[1]
    x_me = lax.axis_index("row")
    depth = tab_scr.shape[0]

    def tab_copy(g):
        slot = lax.rem(g, depth)
        return pltpu.make_async_copy(tab_hbm.at[pl.ds(g * GROUP, GROUP)], tab_scr.at[slot], tab_sems.at[slot])

    begin = pl.multiple_of(jnp.clip(x_me * frames - TAPS, 0, window - width), TAPS)
    sig_copy = pltpu.make_async_copy(sig_hbm.at[:, pl.ds(begin, width)], sig_scr, sems.at[0])
    mine = pl.ds(pl.multiple_of(x_me * frames, TAPS), frames)
    later = [
        pltpu.make_async_copy(h_hbm.at[:, mine], old_ref, sems.at[1]),
        pltpu.make_async_copy(w_hbm, w_ref, sems.at[2]),
        pltpu.make_async_copy(order_hbm, order_ref, sems.at[3]),
    ]
    sig_copy.start()
    for g in range(depth - 1):
        tab_copy(g).start()
    for copy in later:
        copy.start()

    def place(source, owner):
        @pl.when(x_me == 0)
        def _():
            xp_scr[owner, :, HALF:] = source[:, : frames + HALF]

        @pl.when(x_me == rows - 1)
        def _():
            skip = width - frames - HALF
            xp_scr[owner, :, : frames + HALF] = source[:, skip:]

        if rows > 2:

            @pl.when((x_me > 0) & (x_me < rows - 1))
            def _():
                xp_scr[owner] = source[:, HALF : HALF + frames + TAPS]

    for shift in range(1, rows):
        place(sig_refs[shift - 1], lax.rem(x_me + rows - shift, rows))
    sig_copy.wait()
    place(sig_scr, x_me)

    @pl.when(x_me == 0)
    def _():
        for at in range(rows):
            xp_scr[at, :, :HALF] = halo_refs[at][:, HALF:]

    @pl.when(x_me == rows - 1)
    def _():
        for at in range(rows):
            xp_scr[rows - 1 - at, :, frames + HALF :] = halo_refs[at][:, :HALF]

    for blk in range(blocks):
        for x in range(rows):
            x_scr[blk, x * cl : (x + 1) * cl, :] = xp_scr[x, :, blk * TAPS : (blk + 2) * TAPS]

    def convolve(g, carry):
        tab_copy(g).wait()

        @pl.when(g + depth - 1 < GROUPS)
        def _():
            tab_copy(g + depth - 1).start()

        for at in range(GROUP):
            co = jnp.dot(
                x_scr[...].reshape(blocks * rows * cl, 2 * TAPS),
                tab_scr[lax.rem(g, depth), at],
                preferred_element_type=F32,
            )
            power = co[:, :TAPS] * co[:, :TAPS] + co[:, TAPS:] * co[:, TAPS:]
            s_ref[g * GROUP + at] = power.astype(BF16).reshape(blocks, rows * cl, TAPS)
        return carry

    lax.fori_loop(0, GROUPS, convolve, 0)
    for copy in later:
        copy.wait()


def first_kernel(rows, subs, cl, *refs):
    refs = list(refs)
    w_ref, gram_ref = (refs.pop(0) for _ in range(2))
    w_msgs = [refs.pop(0) for _ in range(rows - 1)]
    order_ref, h_ref, s_ref = (refs.pop(0) for _ in range(3))
    w_out, h_out, h_gram_ref = (refs.pop(0) for _ in range(3))
    msg_refs, (w_scr, num_scr) = refs[: subs - 1], refs[subs - 1 :]
    rank = h_ref.shape[0]
    per_sub = GROUPS // subs
    wide = GROUP * cl
    x_me, c_me = lax.axis_index("row"), lax.axis_index("sub")
    w = w_ref[...]
    top = w.astype(BF16)
    rest = w - top.astype(F32)
    middle = rest.astype(BF16)
    terms = [top, middle, (rest - middle.astype(F32)).astype(BF16)] + [ref[:, : NF * cl] for ref in w_msgs]
    moved = jnp.dot(jnp.concatenate(terms, axis=0), order_ref[...], preferred_element_type=F32)
    for at in range(GROUPS):
        cols = slice(at * wide, (at + 1) * wide)
        w_scr[at // per_sub, at % per_sub, x_me] = moved[:rank, cols].astype(BF16)
        for shift in range(1, rows):
            owner = lax.rem(x_me + rows - shift, rows)
            line = (shift + 2) * rank
            w_scr[at // per_sub, at % per_sub, owner] = moved[line : line + rank, cols].astype(BF16)
    whole = moved[:rank] + (moved[rank : 2 * rank] + moved[2 * rank : 3 * rank])
    size = per_sub * wide
    for c in range(subs):

        @pl.when(c_me == c)
        def _():
            w_out[...] = whole[:, c * size : (c + 1) * size]

    gram = gram_ref[...]
    for ref in w_msgs:
        gram = gram + joined(ref, NF * cl, rank)
    new_activations(h_ref[...], gram, w_scr, num_scr, s_ref, h_out, h_gram_ref, msg_refs, rows, subs, cl)


def later_kernel(rows, subs, cl, *refs):
    refs = list(refs)
    w_refs = [refs.pop(0) for _ in range(rows * subs)]
    h_ref, s_ref = refs.pop(0), refs.pop(0)
    h_out, h_gram_ref = (refs.pop(0) for _ in range(2))
    msg_refs, (w_scr, num_scr) = refs[: subs - 1], refs[subs - 1 :]
    rank = h_ref.shape[0]
    per_sub = GROUPS // subs
    wide = GROUP * cl
    x_me, c_me = lax.axis_index("row"), lax.axis_index("sub")
    gram = jnp.zeros((rank, rank), F32)
    at = 0
    for dx in range(rows):
        for dc in range(subs):
            x_of, c_of = lax.rem(x_me + rows - dx, rows), lax.rem(c_me + subs - dc, subs)
            for part in range(per_sub):
                w_scr[c_of, part, x_of] = w_refs[at][:, part * wide : (part + 1) * wide]
            gram = gram + joined(w_refs[at], per_sub * wide, rank)
            at += 1
    new_activations(h_ref[...], gram, w_scr, num_scr, s_ref, h_out, h_gram_ref, msg_refs, rows, subs, cl)


def core_kernel(rows, subs, *refs):
    own_ref, own_gram_ref, *refs = refs
    msg_refs, refs = refs[: subs - 1], refs[subs - 1 :]
    out_ref, gram_ref, *out_msgs, scr = refs
    size = own_ref.shape[2]
    total, gram = own_ref[...], own_gram_ref[...]
    for ref in msg_refs:
        total = total + ref[:, :, :size]
        gram = gram + ref[0, :, size:]
    scr[...] = total
    gram_ref[...] = gram
    x_me = lax.axis_index("row")
    out_ref[...] = scr[x_me]
    for dx in range(1, rows):
        pack(out_msgs[dx - 1], scr[lax.rem(x_me + dx, rows)], gram)


def row_kernel(*refs):
    own_ref, own_gram_ref, *msg_refs, out_ref = refs
    rank, size = own_ref.shape
    total, gram = own_ref[...], own_gram_ref[...]
    for ref in msg_refs:
        total = total + ref[:, :size].astype(F32)
        gram = gram + joined(ref, size, rank)
    pack(out_ref, total, gram)


def summed(z_me, count, msg_refs, scr, rank, size):
    for shift in range(count):
        scr[partner(z_me, shift, count)] = msg_refs[shift][...]
    total, gram = scr[0, :, :size].astype(F32), joined(scr[0], size, rank)
    for at in range(1, count):
        total = total + scr[at, :, :size].astype(F32)
        gram = gram + joined(scr[at], size, rank)
    return total, gram


def partner(place, shift, count):
    if count & (count - 1):
        return (place + count - shift) % count
    return place ^ shift


def update_kernel(count, w_ref, *refs):
    msg_refs, (new_ref, out_ref, scr) = refs[:count], refs[count:]
    rank, size = new_ref.shape
    total, gram = summed(lax.axis_index("frm"), count, msg_refs, scr, rank, size)
    w = w_ref[...]
    new = w * total / jnp.dot(gram, w, precision=HIGH, preferred_element_type=F32)
    new_ref[...] = new
    pack(out_ref, new, lax.dot_general(new, new, NT, precision=HIGH, preferred_element_type=F32))


def last_kernel(count, w_ref, order_ref, *refs):
    msg_refs, (out_ref, scr) = refs[:count], refs[count:]
    rank, size = w_ref.shape
    total, gram = summed(lax.axis_index("frm"), count, msg_refs, scr, rank, size)
    w = w_ref[...]
    new = w * total / jnp.dot(gram, w, precision=HIGH, preferred_element_type=F32)
    top = new.astype(BF16)
    rest = new - top.astype(F32)
    middle = rest.astype(BF16)
    terms = jnp.concatenate([top, middle, (rest - middle.astype(F32)).astype(BF16)], axis=0)
    for c in range(order_ref.shape[1] // size):

        @pl.when(lax.axis_index("sub") == c)
        def _():
            moved = lax.dot_general(
                terms, order_ref[:, c * size : (c + 1) * size], NT, preferred_element_type=F32
            )
            out_ref[...] = moved[:rank] + (moved[rank : 2 * rank] + moved[2 * rank :])


def join_kernel(rows, subs, *refs):
    act_refs, parts, (syn_ref, out_ref, scr, sems) = refs[:rows], refs[rows : rows + subs], refs[rows + subs :]
    frames = act_refs[0].shape[1]
    x_me = lax.axis_index("row")
    copies = []
    for shift in range(rows):
        begin = pl.multiple_of(lax.rem(x_me + rows - shift, rows) * frames, TAPS)
        copies.append(pltpu.make_async_copy(act_refs[shift], out_ref.at[:, pl.ds(begin, frames)], sems.at[shift]))
    for copy in copies:
        copy.start()
    total = parts[0][...]
    for part in parts[1:]:
        total = total + part[...]
    scr[...] = total
    copies.append(pltpu.make_async_copy(scr, syn_ref, sems.at[rows]))
    copies[-1].start()
    for copy in copies:
        copy.wait()


def call(kernel, args, outs, scratch=(), in_specs=None, out_specs=None, limit=4, cost=None):
    whole = pl.BlockSpec(memory_space=pltpu.VMEM)
    if cost is not None:
        cost = pl.CostEstimate(flops=cost, bytes_accessed=0, transcendentals=0)
    return pl.pallas_call(
        kernel,
        out_shape=[jax.ShapeDtypeStruct(*out) if isinstance(out, tuple) else out for out in outs],
        in_specs=in_specs or [whole] * len(args),
        out_specs=out_specs or [whole] * len(outs),
        scratch_shapes=list(scratch),
        compiler_params=pltpu.CompilerParams(vmem_limit_bytes=limit * MIB),
        cost_estimate=cost,
    )(*args)


def reorder(cl):
    order = np.zeros((cl, NF, NF, cl), ml_dtypes.bfloat16)
    chans, freqs = np.meshgrid(np.arange(cl), np.arange(NF), indexing="ij")
    order[chans, freqs, freqs, chans] = 1
    return order.reshape(cl * NF, NF * cl)


def shards(signal, w_start, h_start):
    rows, subs, frms = (lax.axis_size(axis) for axis in ("row", "sub", "frm"))
    x_me = lax.axis_index("row")
    cl, window = signal.shape
    rank = w_start.shape[1]
    frames = window // rows
    blocks = frames // TAPS
    chans = rows * cl
    size = NF * cl // subs
    line = frms * subs
    width = frames + (TAPS if rows == 2 else 2 * TAPS)
    anywhere = pl.BlockSpec(memory_space=pl.ANY)
    whole = pl.BlockSpec(memory_space=pltpu.VMEM)

    def hbm(value):
        return pltpu.with_memory_space_constraint(value, pltpu.HBM)

    def vmem(value):
        return pltpu.with_memory_space_constraint(value, pltpu.VMEM)

    def row_shift(value, shift):
        return lax.ppermute(value, "row", [(i, (i + shift) % rows) for i in range(rows)])

    def sub_shift(value, shift):
        return lax.ppermute(value, "sub", [(i, (i + shift) % subs) for i in range(subs)])

    def frm_shift(value, shift):
        return lax.ppermute(value, "frm", [(partner(i, shift, frms), i) for i in range(frms)])

    def place(x, at):
        return (at // subs * rows + x) * subs + at % subs

    def begin(target):
        return jnp.clip(target * frames - TAPS, 0, window - width)

    sig = [
        row_shift(lax.dynamic_slice_in_dim(signal, begin((x_me + shift) % rows), width, 1), shift)
        for shift in range(1, rows)
    ]
    tail, head = signal[:, window - TAPS :], signal[:, :TAPS]
    halos = [None] * rows
    for at in reversed(range(rows)):
        to_next = [(place(at, i), place(0, i + 1)) for i in range(line - 1)]
        to_prev = [(place(rows - 1 - at, i + 1), place(rows - 1, i)) for i in range(line - 1)]
        halos[at] = lax.ppermute(jnp.where(x_me == at, tail, head), ("frm", "row", "sub"), to_next + to_prev)

    w_cols = w_start.T
    w_msg, w_gram = call(
        prepare_kernel,
        [w_cols] + sig,
        [((rank, NF * cl + 2 * rank), BF16), ((rank, rank), F32)],
        in_specs=[whole] + [anywhere] * len(sig),
    )
    w_msgs = [row_shift(w_msg, shift) for shift in range(1, rows)]

    msg = ((rank, size + 2 * rank), BF16)
    piece = ((rank, size), F32)
    update_outs = [((rank, frames), F32), ((rank, rank), F32)]
    update_outs += [((rows, rank, size + rank), F32)] * (subs - 1)
    update_scratch = [
        pltpu.VMEM((subs, GROUPS // subs, rows, rank, GROUP * cl), BF16),
        pltpu.VMEM((rank, frames), F32),
    ]
    order = jnp.asarray(reorder(cl))
    held = [hbm(signal), hbm(h_start), hbm(w_cols), hbm(jnp.asarray(toeplitz())), hbm(order)]
    macs = NF * chans * frames * rank
    spectra, old, w_own, order = call(
        functools.partial(spectra_kernel, rows, cl, blocks),
        held + sig + halos,
        [
            pltpu.VMEM((NF, blocks, chans, TAPS), BF16),
            pltpu.VMEM((rank, frames), F32),
            pltpu.VMEM((rank, NF * cl), F32),
            pltpu.VMEM(order.shape, BF16),
        ],
        [
            pltpu.VMEM((cl, width), BF16),
            pltpu.VMEM((3, GROUP, 2 * TAPS, 2 * TAPS), BF16),
            pltpu.VMEM((rows, cl, frames + TAPS), BF16),
            pltpu.VMEM((blocks, chans, 2 * TAPS), BF16),
            pltpu.SemaphoreType.DMA((4,)),
            pltpu.SemaphoreType.DMA((3,)),
        ],
        in_specs=[anywhere] * len(held) + [whole] * (len(sig) + len(halos)),
        limit=12,
        cost=2 * NF * chans * frames * 4 * TAPS,
    )
    spectra, order = vmem(spectra), vmem(order)

    def gathered(activations, h_gram, msgs):
        got = [sub_shift(m, dc + 1) for dc, m in enumerate(msgs)]
        (own,) = call(
            functools.partial(own_kernel, rows, subs, cl),
            [activations, spectra],
            [((rows,) + piece[0], F32)],
            cost=16 * macs // subs,
        )
        part, gram, *outs = call(
            functools.partial(core_kernel, rows, subs),
            [own, h_gram] + got,
            [piece, ((rank, rank), F32)] + [msg] * (rows - 1),
            [pltpu.VMEM((rows,) + piece[0], F32)],
        )
        got = [row_shift(m, dx + 1) for dx, m in enumerate(outs)]
        (part,) = call(row_kernel, [part, gram] + got, [msg])
        return [part] + [frm_shift(part, shift) for shift in range(1, frms)]

    w_piece, activations, h_gram, *msgs = call(
        functools.partial(first_kernel, rows, subs, cl),
        [vmem(w_own), w_gram] + w_msgs + [order, vmem(old), spectra],
        [piece] + update_outs,
        update_scratch,
        limit=8,
    )
    piled = [pltpu.VMEM((frms,) + msg[0], BF16)]
    w_piece, w_msg = call(
        functools.partial(update_kernel, frms),
        [w_piece] + gathered(activations, h_gram, msgs),
        [piece, msg],
        piled,
    )
    w_msgs = []
    for dx in range(rows):
        base = row_shift(w_msg, dx) if dx else w_msg
        w_msgs += [base] + [sub_shift(base, dc) for dc in range(1, subs)]
    activations, h_gram, *msgs = call(
        functools.partial(later_kernel, rows, subs, cl),
        w_msgs + [activations, spectra],
        update_outs,
        update_scratch,
        limit=8,
    )
    parts = gathered(activations, h_gram, msgs)
    activations, parts[0] = lax.optimization_barrier((activations, parts[0]))
    sides = [activations] + [row_shift(activations, shift) for shift in range(1, rows)]
    (part,) = call(
        functools.partial(last_kernel, frms), [w_piece, order] + parts, [((rank, NF * cl), F32)], piled
    )
    synergies, wide = call(
        functools.partial(join_kernel, rows, subs),
        sides + [part] + [sub_shift(part, dc) for dc in range(1, subs)],
        [pltpu.HBM((rank, NF * cl), F32), pltpu.HBM((rank, window), F32)],
        [pltpu.VMEM((rank, NF * cl), F32), pltpu.SemaphoreType.DMA((rows + 1,))],
        in_specs=[anywhere] * rows + [whole] * subs,
        out_specs=[anywhere] * 2,
    )
    return (synergies.T, wide)


def solution(mesh):
    placed = (P("row", ("grp", "frm", "sub")), P("row", None), P(None, ("grp", "frm", "sub")))
    return jax.shard_map(
        shards,
        mesh=mesh,
        in_specs=placed,
        out_specs=(P(("grp", "row"), None), P(None, ("grp", "frm", "sub"))),
        check_vma=False,
    )
```

```python
import functools
import math

import jax
import jax.numpy as jnp
import ml_dtypes
import numpy as np
from jax import lax
from jax.experimental import pallas as pl
from jax.experimental.pallas import tpu as pltpu
from jax.sharding import PartitionSpec as P

NF = 40
TAPS = 128
HALF = TAPS // 2
GROUP = 4
GROUPS = NF // GROUP
F32 = jnp.float32
BF16 = jnp.bfloat16
HIGH = lax.Precision.HIGHEST
NT = (((1,), (1,)), ((), ()))
MIB = 1024 * 1024


def wavelets():
    f = np.float32
    level = np.arange(NF, dtype=f) / f(NF - 1)
    freq = f(2.0) * np.power(f(12.0), level)
    sigma = f(7.0) / (f(2.0 * math.pi) * freq)
    times = (np.arange(TAPS, dtype=f) - f(HALF)) / f(50.0)
    env = np.exp(-(times[None, :] ** 2) / (f(2.0) * sigma[:, None] ** 2))
    scale = f(1.0) / np.sqrt(np.sum(env * env, axis=1))
    env = env * scale[:, None]
    phase = f(2.0 * math.pi) * freq[:, None] * times[None, :]
    return np.stack([env * np.cos(phase), env * np.sin(phase)]).astype(ml_dtypes.bfloat16)


def toeplitz():
    kernel = wavelets()
    table = np.zeros((NF, 2 * TAPS, 2 * TAPS), ml_dtypes.bfloat16)
    for at in range(TAPS):
        for part in range(2):
            table[:, at : at + TAPS, part * TAPS + at] = kernel[part]
    return table


def split_two(value):
    top = value.astype(BF16)
    return top, (value - top.astype(F32)).astype(BF16)


def joined(message, at, rank):
    return message[:, at : at + rank].astype(F32) + message[:, at + rank : at + 2 * rank].astype(F32)


def pack(out_ref, main, gram):
    rank, size = main.shape
    top, rest = split_two(gram)
    out_ref[:, :size] = main.astype(BF16)
    out_ref[:, size : size + rank] = top
    out_ref[:, size + rank : size + 2 * rank] = rest


def fetch_kernel(w_hbm, h_hbm, tab_hbm, order_hbm, *refs):
    w_ref, old_ref, tab_ref, order_ref, msg_ref, gram_ref, sems = refs[-7:]
    frames = old_ref.shape[1]
    mine = pl.ds(pl.multiple_of(lax.axis_index("row") * frames, TAPS), frames)
    copies = [
        pltpu.make_async_copy(w_hbm, w_ref, sems.at[0]),
        pltpu.make_async_copy(tab_hbm, tab_ref, sems.at[1]),
        pltpu.make_async_copy(h_hbm.at[:, mine], old_ref, sems.at[2]),
        pltpu.make_async_copy(order_hbm, order_ref, sems.at[3]),
    ]
    for copy in copies:
        copy.start()
    copies[0].wait()
    w = w_ref[...]
    gram = lax.dot_general(w, w, NT, precision=HIGH, preferred_element_type=F32)
    gram_ref[...] = gram
    pack(msg_ref, w, gram)
    for copy in copies[1:]:
        copy.wait()


def cut_edges_kernel(rows, sig_hbm, *refs):
    out_refs, sems = refs[:rows], refs[rows]
    window, x_me = sig_hbm.shape[1], lax.axis_index("row")
    copies = []
    for at in range(rows):
        begin = pl.multiple_of(jnp.where(x_me == at, window - TAPS, 0), TAPS)
        copies.append(pltpu.make_async_copy(sig_hbm.at[:, pl.ds(begin, TAPS)], out_refs[at], sems.at[at]))
    for copy in copies:
        copy.start()
    for copy in copies:
        copy.wait()


def cut_signal_kernel(rows, frames, sig_hbm, *refs):
    out_refs, sems = refs[-rows - 1 : -1], refs[-1]
    window, x_me = sig_hbm.shape[1], lax.axis_index("row")
    width = out_refs[0].shape[1]
    copies = []
    for shift in range(rows):
        target = lax.rem(x_me + shift, rows)
        begin = pl.multiple_of(jnp.clip(target * frames - TAPS, 0, window - width), TAPS)
        copies.append(pltpu.make_async_copy(sig_hbm.at[:, pl.ds(begin, width)], out_refs[shift], sems.at[shift]))
    for copy in copies:
        copy.start()
    for copy in copies:
        copy.wait()


def pair_rows(s_ref, span, pair, x, cl):
    halves = [s_ref[span, blk, x].reshape(-1, TAPS) for blk in (2 * pair, 2 * pair + 1)]
    return jnp.concatenate(halves, axis=1)


def group_rows(s_ref, g, pair, rows, cl):
    span = slice(g * GROUP, (g + 1) * GROUP)
    return jnp.concatenate([pair_rows(s_ref, span, pair, x, cl) for x in range(rows)], axis=0)


def crossed(low, s_ref, x, core, subs, cl):
    count = NF // subs
    span = pl.ds(core * count, count)
    acc = jnp.zeros((low.shape[0], count * cl), F32)
    for pair in range(low.shape[1] // (2 * TAPS)):
        cols = slice(2 * TAPS * pair, 2 * TAPS * (pair + 1))
        acc = acc + lax.dot_general(
            low[:, cols], pair_rows(s_ref, span, pair, x, cl), NT, preferred_element_type=F32
        )
    return acc


def others_of(rows, subs):
    return [(dx, dc) for dx in range(1, rows) for dc in range(1, subs)]


def new_activations(old, gram, w_scr, num_scr, s_ref, h_out, h_gram_ref, msg_refs, rows, subs, cl):
    rank, frames = old.shape
    per_sub = GROUPS // subs
    for pair in range(frames // (2 * TAPS)):
        acc = jnp.zeros((rank, 2 * TAPS), F32)
        for g in range(GROUPS):
            wg = jnp.concatenate([w_scr[g // per_sub, g % per_sub, x] for x in range(rows)], axis=1)
            acc = acc + jnp.dot(wg, group_rows(s_ref, g, pair, rows, cl), preferred_element_type=F32)
        num_scr[:, 2 * TAPS * pair : 2 * TAPS * (pair + 1)] = acc
    new = old * num_scr[...] / jnp.dot(gram, old, precision=HIGH, preferred_element_type=F32)
    h_out[...] = new
    h_gram = lax.dot_general(new, new, NT, precision=HIGH, preferred_element_type=F32)
    h_gram_ref[...] = h_gram
    size = per_sub * GROUP * cl
    x_me, c_me = lax.axis_index("row"), lax.axis_index("sub")
    for ref, (dx, dc) in zip(msg_refs, others_of(rows, subs)):
        ref[:, :size] = crossed(
            new.astype(BF16), s_ref, lax.rem(x_me + dx, rows), lax.rem(c_me + dc, subs), subs, cl
        )
        ref[:, size:] = h_gram


def products_kernel(places, rows, subs, cl, h_ref, s_ref, *refs):
    x_me, c_me = lax.axis_index("row"), lax.axis_index("sub")
    low = h_ref[...].astype(BF16)
    for ref, (dx, dc) in zip(refs[len(refs) - len(places) :], places):
        ref[...] = crossed(low, s_ref, lax.rem(x_me + dx, rows), lax.rem(c_me + dc, subs), subs, cl)


def spectra_kernel(rows, cl, blocks, *refs):
    refs = list(refs)
    sig_refs = [refs.pop(0) for _ in range(rows)]
    halo_refs = [refs.pop(0) for _ in range(rows)]
    tab_ref, s_ref, xp_scr, x_scr = refs
    frames = blocks * TAPS
    width = sig_refs[0].shape[1]
    x_me = lax.axis_index("row")

    def place(source, owner):
        @pl.when(x_me == 0)
        def _():
            xp_scr[owner, :, HALF:] = source[:, : frames + HALF]

        @pl.when(x_me == rows - 1)
        def _():
            skip = width - frames - HALF
            xp_scr[owner, :, : frames + HALF] = source[:, skip:]

        if rows > 2:

            @pl.when((x_me > 0) & (x_me < rows - 1))
            def _():
                xp_scr[owner] = source[:, HALF : HALF + frames + TAPS]

    for shift in range(rows):
        place(sig_refs[shift], lax.rem(x_me + rows - shift, rows))

    @pl.when(x_me == 0)
    def _():
        for at in range(rows):
            xp_scr[at, :, :HALF] = halo_refs[at][:, HALF:]

    @pl.when(x_me == rows - 1)
    def _():
        for at in range(rows):
            xp_scr[rows - 1 - at, :, frames + HALF :] = halo_refs[at][:, :HALF]

    for blk in range(blocks):
        for x in range(rows):
            x_scr[blk, x * cl : (x + 1) * cl, :] = xp_scr[x, :, blk * TAPS : (blk + 2) * TAPS]

    def convolve(g, carry):
        for at in range(GROUP):
            co = jnp.dot(
                x_scr[...].reshape(blocks * rows * cl, 2 * TAPS),
                tab_ref[g * GROUP + at],
                preferred_element_type=F32,
            )
            power = co[:, :TAPS] * co[:, :TAPS] + co[:, TAPS:] * co[:, TAPS:]
            s_ref[g * GROUP + at] = power.astype(BF16).reshape(blocks, rows, cl, TAPS)
        return carry

    lax.fori_loop(0, GROUPS, convolve, 0)


def first_kernel(rows, subs, cl, *refs):
    refs = list(refs)
    w_ref, gram_ref = (refs.pop(0) for _ in range(2))
    w_msgs = [refs.pop(0) for _ in range(rows - 1)]
    order_ref, h_ref, s_ref = (refs.pop(0) for _ in range(3))
    w_out, h_out, h_gram_ref = (refs.pop(0) for _ in range(3))
    msg_refs, (w_scr, num_scr) = refs[:-2], refs[-2:]
    rank = h_ref.shape[0]
    per_sub = GROUPS // subs
    wide = GROUP * cl
    x_me, c_me = lax.axis_index("row"), lax.axis_index("sub")
    w = w_ref[...]
    top = w.astype(BF16)
    rest = w - top.astype(F32)
    middle = rest.astype(BF16)
    terms = [top, middle, (rest - middle.astype(F32)).astype(BF16)] + [ref[:, : NF * cl] for ref in w_msgs]
    moved = jnp.dot(jnp.concatenate(terms, axis=0), order_ref[...], preferred_element_type=F32)
    for at in range(GROUPS):
        cols = slice(at * wide, (at + 1) * wide)
        w_scr[at // per_sub, at % per_sub, x_me] = moved[:rank, cols].astype(BF16)
        for shift in range(1, rows):
            owner = lax.rem(x_me + rows - shift, rows)
            line = (shift + 2) * rank
            w_scr[at // per_sub, at % per_sub, owner] = moved[line : line + rank, cols].astype(BF16)
    whole = moved[:rank] + (moved[rank : 2 * rank] + moved[2 * rank : 3 * rank])
    size = per_sub * wide
    for c in range(subs):

        @pl.when(c_me == c)
        def _():
            w_out[...] = whole[:, c * size : (c + 1) * size]

    gram = gram_ref[...]
    for ref in w_msgs:
        gram = gram + joined(ref, NF * cl, rank)
    new_activations(h_ref[...], gram, w_scr, num_scr, s_ref, h_out, h_gram_ref, msg_refs, rows, subs, cl)


def later_kernel(rows, subs, cl, *refs):
    refs = list(refs)
    w_refs = [refs.pop(0) for _ in range(rows * subs)]
    h_ref, s_ref = refs.pop(0), refs.pop(0)
    h_out, h_gram_ref = (refs.pop(0) for _ in range(2))
    msg_refs, (w_scr, num_scr) = refs[:-2], refs[-2:]
    rank = h_ref.shape[0]
    per_sub = GROUPS // subs
    wide = GROUP * cl
    x_me, c_me = lax.axis_index("row"), lax.axis_index("sub")
    gram = jnp.zeros((rank, rank), F32)
    at = 0
    for dx in range(rows):
        for dc in range(subs):
            x_of, c_of = lax.rem(x_me + rows - dx, rows), lax.rem(c_me + subs - dc, subs)
            for part in range(per_sub):
                w_scr[c_of, part, x_of] = w_refs[at][:, part * wide : (part + 1) * wide]
            gram = gram + joined(w_refs[at], per_sub * wide, rank)
            at += 1
    new_activations(h_ref[...], gram, w_scr, num_scr, s_ref, h_out, h_gram_ref, msg_refs, rows, subs, cl)


def core_kernel(count, rank, *refs):
    own_refs, gram_ref, got_refs = refs[:count], refs[count], refs[count + 1 : -count - 1]
    out_refs, total_ref = refs[-count - 1 : -1], refs[-1]
    size = own_refs[0].shape[1]
    each = len(got_refs) // count
    gram = gram_ref[...]
    for ref in got_refs[:each]:
        gram = gram + ref[:, size:]
    total_ref[...] = gram
    for at in range(count):
        total = own_refs[at][...]
        for ref in got_refs[at * each : (at + 1) * each]:
            total = total + ref[:, :size]
        pack(out_refs[at], total, gram)


def row_kernel(subs, own_ref, gram_ref, *refs):
    core_refs, msg_refs, out_ref = refs[: subs - 1], refs[subs - 1 : -1], refs[-1]
    rank, size = own_ref.shape
    total, gram = own_ref[...], gram_ref[...]
    for ref in core_refs:
        total = total + ref[...]
    for ref in msg_refs:
        total = total + ref[:, :size].astype(F32)
        gram = gram + joined(ref, size, rank)
    pack(out_ref, total, gram)


def summed(z_me, count, msg_refs, scr, rank, size):
    for shift in range(count):
        scr[partner(z_me, shift, count)] = msg_refs[shift][...]
    total, gram = scr[0, :, :size].astype(F32), joined(scr[0], size, rank)
    for at in range(1, count):
        total = total + scr[at, :, :size].astype(F32)
        gram = gram + joined(scr[at], size, rank)
    return total, gram


def partner(place, shift, count):
    if count & (count - 1):
        return (place + count - shift) % count
    return place ^ shift


def update_kernel(count, w_ref, *refs):
    msg_refs, (new_ref, out_ref, scr) = refs[:count], refs[count:]
    rank, size = new_ref.shape
    total, gram = summed(lax.axis_index("frm"), count, msg_refs, scr, rank, size)
    w = w_ref[...]
    new = w * total / jnp.dot(gram, w, precision=HIGH, preferred_element_type=F32)
    new_ref[...] = new
    pack(out_ref, new, lax.dot_general(new, new, NT, precision=HIGH, preferred_element_type=F32))


def last_kernel(count, w_ref, order_ref, *refs):
    msg_refs, (out_ref, scr) = refs[:count], refs[count:]
    rank, size = w_ref.shape
    total, gram = summed(lax.axis_index("frm"), count, msg_refs, scr, rank, size)
    w = w_ref[...]
    new = w * total / jnp.dot(gram, w, precision=HIGH, preferred_element_type=F32)
    top = new.astype(BF16)
    rest = new - top.astype(F32)
    middle = rest.astype(BF16)
    terms = jnp.concatenate([top, middle, (rest - middle.astype(F32)).astype(BF16)], axis=0)
    for c in range(order_ref.shape[1] // size):

        @pl.when(lax.axis_index("sub") == c)
        def _():
            moved = lax.dot_general(
                terms, order_ref[:, c * size : (c + 1) * size], NT, preferred_element_type=F32
            )
            out_ref[...] = moved[:rank] + (moved[rank : 2 * rank] + moved[2 * rank :])


def join_kernel(rows, subs, *refs):
    act_refs, parts, (syn_ref, out_ref, scr, sems) = refs[:rows], refs[rows : rows + subs], refs[rows + subs :]
    frames = act_refs[0].shape[1]
    x_me = lax.axis_index("row")
    copies = []
    for shift in range(rows):
        begin = pl.multiple_of(lax.rem(x_me + rows - shift, rows) * frames, TAPS)
        copies.append(pltpu.make_async_copy(act_refs[shift], out_ref.at[:, pl.ds(begin, frames)], sems.at[shift]))
    for copy in copies:
        copy.start()
    total = parts[0][...]
    for part in parts[1:]:
        total = total + part[...]
    scr[...] = total
    copies.append(pltpu.make_async_copy(scr, syn_ref, sems.at[rows]))
    copies[-1].start()
    for copy in copies:
        copy.wait()


def call(kernel, args, outs, scratch=(), in_specs=None, out_specs=None, limit=4, cost=None):
    whole = pl.BlockSpec(memory_space=pltpu.VMEM)
    if cost is not None:
        cost = pl.CostEstimate(flops=cost, bytes_accessed=0, transcendentals=0)
    return pl.pallas_call(
        kernel,
        out_shape=[jax.ShapeDtypeStruct(*out) if isinstance(out, tuple) else out for out in outs],
        in_specs=in_specs or [whole] * len(args),
        out_specs=out_specs or [whole] * len(outs),
        scratch_shapes=list(scratch),
        compiler_params=pltpu.CompilerParams(vmem_limit_bytes=limit * MIB),
        cost_estimate=cost,
    )(*args)


def reorder(cl):
    order = np.zeros((cl, NF, NF, cl), ml_dtypes.bfloat16)
    chans, freqs = np.meshgrid(np.arange(cl), np.arange(NF), indexing="ij")
    order[chans, freqs, freqs, chans] = 1
    return order.reshape(cl * NF, NF * cl)


def shards(signal, w_start, h_start):
    rows, subs, frms = (lax.axis_size(axis) for axis in ("row", "sub", "frm"))
    x_me = lax.axis_index("row")
    cl, window = signal.shape
    rank = w_start.shape[1]
    frames = window // rows
    blocks = frames // TAPS
    chans = rows * cl
    size = NF * cl // subs
    line = frms * subs
    width = frames + (TAPS if rows == 2 else 2 * TAPS)
    anywhere = pl.BlockSpec(memory_space=pl.ANY)
    whole = pl.BlockSpec(memory_space=pltpu.VMEM)

    def hbm(value):
        return pltpu.with_memory_space_constraint(value, pltpu.HBM)

    def vmem(value):
        return pltpu.with_memory_space_constraint(value, pltpu.VMEM)

    def row_shift(value, shift):
        return lax.ppermute(value, "row", [(i, (i + shift) % rows) for i in range(rows)])

    def sub_shift(value, shift):
        return lax.ppermute(value, "sub", [(i, (i + shift) % subs) for i in range(subs)])

    def frm_shift(value, shift):
        return lax.ppermute(value, "frm", [(partner(i, shift, frms), i) for i in range(frms)])

    def place(x, at):
        return (at // subs * rows + x) * subs + at % subs

    edges = call(
        functools.partial(cut_edges_kernel, rows),
        [hbm(signal)],
        [((cl, TAPS), BF16)] * rows,
        [pltpu.SemaphoreType.DMA((rows,))],
        in_specs=[anywhere],
    )
    halos = [None] * rows
    for at in reversed(range(rows)):
        to_next = [(place(at, i), place(0, i + 1)) for i in range(line - 1)]
        to_prev = [(place(rows - 1 - at, i + 1), place(rows - 1, i)) for i in range(line - 1)]
        halos[at] = lax.ppermute(edges[at], ("frm", "row", "sub"), to_next + to_prev)
    own_sig, *out_sigs = call(
        functools.partial(cut_signal_kernel, rows, frames),
        [hbm(signal)] + list(edges),
        [((cl, width), BF16)] * rows,
        [pltpu.SemaphoreType.DMA((rows,))],
        in_specs=[anywhere] * (rows + 1),
    )
    sig = [own_sig] + [row_shift(part, shift + 1) for shift, part in enumerate(out_sigs)]

    msg = ((rank, size + 2 * rank), BF16)
    piece = ((rank, size), F32)
    update_outs = [((rank, frames), F32), ((rank, rank), F32)]
    update_outs += [((rank, size + rank), F32)] * ((rows - 1) * (subs - 1))
    update_scratch = [
        pltpu.VMEM((subs, GROUPS // subs, rows, rank, GROUP * cl), BF16),
        pltpu.VMEM((rank, frames), F32),
    ]
    table, order = jnp.asarray(toeplitz()), jnp.asarray(reorder(cl))
    w_own, old, table, order, w_msg, w_gram = call(
        fetch_kernel,
        [hbm(w_start.T), hbm(h_start), hbm(table), hbm(order), own_sig],
        [
            pltpu.VMEM((rank, NF * cl), F32),
            pltpu.VMEM((rank, frames), F32),
            pltpu.VMEM(table.shape, BF16),
            pltpu.VMEM(order.shape, BF16),
            ((rank, NF * cl + 2 * rank), BF16),
            ((rank, rank), F32),
        ],
        [pltpu.SemaphoreType.DMA((4,))],
        in_specs=[anywhere] * 5,
        cost=2 * 10**9,
    )
    w_msgs = [row_shift(w_msg, shift) for shift in range(1, rows)]
    order = vmem(order)
    (spectra,) = call(
        functools.partial(spectra_kernel, rows, cl, blocks),
        sig + halos + [vmem(table)],
        [pltpu.VMEM((NF, blocks, rows, cl, TAPS), BF16)],
        [pltpu.VMEM((rows, cl, frames + TAPS), BF16), pltpu.VMEM((blocks, chans, 2 * TAPS), BF16)],
        limit=8,
        cost=2 * NF * chans * frames * 4 * TAPS,
    )
    spectra = vmem(spectra)

    def products(places, activations, after):
        return call(
            functools.partial(products_kernel, places, rows, subs, cl),
            [activations, spectra] + after,
            [piece] * len(places),
            in_specs=[whole] * 2 + [anywhere] * len(after),
            cost=1 if after else 16 * NF * cl * frames * rank // subs * len(places),
        )

    def gathered(activations, h_gram, msgs):
        got = [sub_shift(m, dc) for m, (_, dc) in zip(msgs, others_of(rows, subs))]
        out_places = [(dx, 0) for dx in range(1, rows)]
        own = products(out_places, activations, [])
        *outs, gram = call(
            functools.partial(core_kernel, rows - 1, rank),
            list(own) + [h_gram] + got,
            [msg] * (rows - 1) + [((rank, rank), F32)],
        )
        from_rows = [row_shift(m, dx + 1) for dx, m in enumerate(outs)]
        for_cores = products([(0, dc) for dc in range(1, subs)], activations, outs)
        from_cores = [sub_shift(m, dc + 1) for dc, m in enumerate(for_cores)]
        (own,) = products([(0, 0)], activations, list(for_cores))
        (part,) = call(functools.partial(row_kernel, subs), [own, gram] + from_cores + from_rows, [msg])
        return [part] + [frm_shift(part, shift) for shift in range(1, frms)]

    w_piece, activations, h_gram, *msgs = call(
        functools.partial(first_kernel, rows, subs, cl),
        [vmem(w_own), w_gram] + w_msgs + [order, vmem(old), spectra],
        [piece] + update_outs,
        update_scratch,
        limit=8,
    )
    piled = [pltpu.VMEM((frms,) + msg[0], BF16)]
    w_piece, w_msg = call(
        functools.partial(update_kernel, frms),
        [w_piece] + gathered(activations, h_gram, msgs),
        [piece, msg],
        piled,
    )
    w_msgs = []
    for dx in range(rows):
        base = row_shift(w_msg, dx) if dx else w_msg
        w_msgs += [base] + [sub_shift(base, dc) for dc in range(1, subs)]
    activations, h_gram, *msgs = call(
        functools.partial(later_kernel, rows, subs, cl),
        w_msgs + [activations, spectra],
        update_outs,
        update_scratch,
        limit=8,
    )
    parts = gathered(activations, h_gram, msgs)
    activations, parts[0] = lax.optimization_barrier((activations, parts[0]))
    sides = [activations] + [row_shift(activations, shift) for shift in range(1, rows)]
    (part,) = call(
        functools.partial(last_kernel, frms), [w_piece, order] + parts, [((rank, NF * cl), F32)], piled
    )
    synergies, wide = call(
        functools.partial(join_kernel, rows, subs),
        sides + [part] + [sub_shift(part, dc) for dc in range(1, subs)],
        [pltpu.HBM((rank, NF * cl), F32), pltpu.HBM((rank, window), F32)],
        [pltpu.VMEM((rank, NF * cl), F32), pltpu.SemaphoreType.DMA((rows + 1,))],
        in_specs=[anywhere] * rows + [whole] * subs,
        out_specs=[anywhere] * 2,
    )
    return (synergies.T, wide)


def solution(mesh):
    placed = (P("row", ("grp", "frm", "sub")), P("row", None), P(None, ("grp", "frm", "sub")))
    return jax.shard_map(
        shards,
        mesh=mesh,
        in_specs=placed,
        out_specs=(P(("grp", "row"), None), P(None, ("grp", "frm", "sub"))),
        check_vma=False,
    )
```

```python
import functools
import math

import jax
import jax.numpy as jnp
import ml_dtypes
import numpy as np
from jax import lax
from jax.experimental import pallas as pl
from jax.experimental.pallas import tpu as pltpu
from jax.sharding import PartitionSpec as P

NF = 40
TAPS = 128
HALF = TAPS // 2
GROUP = 4
GROUPS = NF // GROUP
F32 = jnp.float32
BF16 = jnp.bfloat16
HIGH = lax.Precision.HIGHEST
NT = (((1,), (1,)), ((), ()))
MIB = 1024 * 1024


def wavelets():
    f = np.float32
    level = np.arange(NF, dtype=f) / f(NF - 1)
    freq = f(2.0) * np.power(f(12.0), level)
    sigma = f(7.0) / (f(2.0 * math.pi) * freq)
    times = (np.arange(TAPS, dtype=f) - f(HALF)) / f(50.0)
    env = np.exp(-(times[None, :] ** 2) / (f(2.0) * sigma[:, None] ** 2))
    scale = f(1.0) / np.sqrt(np.sum(env * env, axis=1))
    env = env * scale[:, None]
    phase = f(2.0 * math.pi) * freq[:, None] * times[None, :]
    return np.stack([env * np.cos(phase), env * np.sin(phase)]).astype(ml_dtypes.bfloat16)


def toeplitz():
    kernel = wavelets()
    table = np.zeros((NF, 2 * TAPS, 2 * TAPS), ml_dtypes.bfloat16)
    for at in range(TAPS):
        for part in range(2):
            table[:, at : at + TAPS, part * TAPS + at] = kernel[part]
    return table


def split_two(value):
    top = value.astype(BF16)
    return top, (value - top.astype(F32)).astype(BF16)


def joined(message, at, rank):
    return message[:, at : at + rank].astype(F32) + message[:, at + rank : at + 2 * rank].astype(F32)


def pack(out_ref, main, gram):
    rank, size = main.shape
    top, rest = split_two(gram)
    out_ref[:, :size] = main.astype(BF16)
    out_ref[:, size : size + rank] = top
    out_ref[:, size + rank : size + 2 * rank] = rest


def fetch_kernel(w_hbm, h_hbm, order_hbm, *refs):
    piece_ref, msg_ref, gram_ref, old_ref, order_ref, w_scr, sems = refs[-7:]
    frames = old_ref.shape[1]
    size = piece_ref.shape[1]
    mine = pl.ds(pl.multiple_of(lax.axis_index("row") * frames, TAPS), frames)
    copies = [
        pltpu.make_async_copy(w_hbm, w_scr, sems.at[0]),
        pltpu.make_async_copy(order_hbm, order_ref, sems.at[1]),
        pltpu.make_async_copy(h_hbm.at[:, mine], old_ref, sems.at[2]),
    ]
    for copy in copies:
        copy.start()
    copies[0].wait()
    w = w_scr[...]
    rank = w.shape[0]
    gram = lax.dot_general(w, w, NT, precision=HIGH, preferred_element_type=F32)
    gram_ref[...] = gram
    terms = three_terms(w)
    copies[1].wait()
    moved = jnp.dot(terms, order_ref[...], preferred_element_type=F32)
    whole = moved[:rank] + (moved[rank : 2 * rank] + moved[2 * rank :])
    for c in range(w.shape[1] // size):

        @pl.when(lax.axis_index("sub") == c)
        def _():
            piece_ref[...] = whole[:, c * size : (c + 1) * size]

    pack(msg_ref, whole, gram)
    copies[2].wait()


def table_kernel(tab_hbm, *refs):
    tab_ref, sem = refs[-2:]
    copy = pltpu.make_async_copy(tab_hbm, tab_ref, sem)
    copy.start()
    copy.wait()


def three_terms(value):
    top = value.astype(BF16)
    rest = value - top.astype(F32)
    middle = rest.astype(BF16)
    return jnp.concatenate([top, middle, (rest - middle.astype(F32)).astype(BF16)], axis=0)


def edges_kernel(rows, sig_ref, *refs):
    got_refs, out_ref = refs[: rows - 1], refs[rows - 1]
    cl, width = sig_ref.shape
    x_me = lax.axis_index("row")
    for at, ref in enumerate((sig_ref,) + tuple(got_refs)):

        @pl.when(x_me == 0)
        def _():
            out_ref[at * cl : (at + 1) * cl, :] = ref[:, :TAPS]

        @pl.when(x_me > 0)
        def _():
            out_ref[at * cl : (at + 1) * cl, :] = ref[:, width - TAPS :]


def cut_signal_kernel(rows, frames, sig_hbm, *refs):
    out_refs, sems = refs[-rows - 1 : -1], refs[-1]
    window, x_me = sig_hbm.shape[1], lax.axis_index("row")
    width = out_refs[0].shape[1]
    copies = []
    for shift in range(rows):
        target = lax.rem(x_me + shift, rows)
        begin = pl.multiple_of(jnp.clip(target * frames - TAPS, 0, window - width), TAPS)
        copies.append(pltpu.make_async_copy(sig_hbm.at[:, pl.ds(begin, width)], out_refs[shift], sems.at[shift]))
    for copy in copies:
        copy.start()
    for copy in copies:
        copy.wait()


def pair_rows(s_ref, span, pair, x, cl):
    halves = [s_ref[span, blk, x].reshape(-1, TAPS) for blk in (2 * pair, 2 * pair + 1)]
    return jnp.concatenate(halves, axis=1)


def numerators(parts, s_ref, num_ref, cl):
    for pair in range(num_ref.shape[1] // (2 * TAPS)):
        terms = [
            jnp.dot(w, pair_rows(s_ref, slice(None), pair, x, cl), preferred_element_type=F32) for w, x in parts
        ]
        num_ref[:, 2 * TAPS * pair : 2 * TAPS * (pair + 1)] = functools.reduce(jnp.add, terms)


def crossed(low, s_ref, x, core, subs, cl):
    count = NF // subs
    span = pl.ds(core * count, count)
    acc = jnp.zeros((low.shape[0], count * cl), F32)
    for pair in range(low.shape[1] // (2 * TAPS)):
        cols = slice(2 * TAPS * pair, 2 * TAPS * (pair + 1))
        acc = acc + lax.dot_general(
            low[:, cols], pair_rows(s_ref, span, pair, x, cl), NT, preferred_element_type=F32
        )
    return acc


def others_of(rows, subs):
    return [(dx, dc) for dx in range(1, rows) for dc in range(1, subs)]


def new_activations(old, gram, above, s_ref, h_out, h_gram_ref, msg_refs, rows, subs, cl):
    new = old * above / jnp.dot(gram, old, precision=HIGH, preferred_element_type=F32)
    h_out[...] = new
    h_gram = lax.dot_general(new, new, NT, precision=HIGH, preferred_element_type=F32)
    h_gram_ref[...] = h_gram
    size = NF // subs * cl
    x_me, c_me = lax.axis_index("row"), lax.axis_index("sub")
    for ref, (dx, dc) in zip(msg_refs, others_of(rows, subs)):
        ref[:, :size] = crossed(
            new.astype(BF16), s_ref, lax.rem(x_me + dx, rows), lax.rem(c_me + dc, subs), subs, cl
        )
        ref[:, size:] = h_gram


def products_kernel(places, rows, subs, cl, h_ref, s_ref, *refs):
    x_me, c_me = lax.axis_index("row"), lax.axis_index("sub")
    low = h_ref[...].astype(BF16)
    for ref, (dx, dc) in zip(refs[len(refs) - len(places) :], places):
        ref[...] = crossed(low, s_ref, lax.rem(x_me + dx, rows), lax.rem(c_me + dc, subs), subs, cl)


def spectra_kernel(rows, cl, blocks, *refs):
    refs = list(refs)
    sig_refs = [refs.pop(0) for _ in range(rows)]
    halo_ref, tab_ref, s_ref, xp_scr, x_scr = refs
    frames = blocks * TAPS
    width = sig_refs[0].shape[1]
    x_me = lax.axis_index("row")

    def place(source, owner):
        @pl.when(x_me == 0)
        def _():
            xp_scr[owner, :, HALF:] = source[:, : frames + HALF]

        @pl.when(x_me == rows - 1)
        def _():
            skip = width - frames - HALF
            xp_scr[owner, :, : frames + HALF] = source[:, skip:]

        if rows > 2:

            @pl.when((x_me > 0) & (x_me < rows - 1))
            def _():
                xp_scr[owner] = source[:, HALF : HALF + frames + TAPS]

    for shift in range(rows):
        place(sig_refs[shift], lax.rem(x_me + rows - shift, rows))

    @pl.when(x_me == 0)
    def _():
        for at in range(rows):
            xp_scr[rows - 1 - at, :, :HALF] = halo_ref[at * cl : (at + 1) * cl, HALF:]

    @pl.when(x_me == rows - 1)
    def _():
        for at in range(rows):
            xp_scr[(rows - at) % rows, :, frames + HALF :] = halo_ref[at * cl : (at + 1) * cl, :HALF]

    for blk in range(blocks):
        for x in range(rows):
            x_scr[blk, x * cl : (x + 1) * cl, :] = xp_scr[x, :, blk * TAPS : (blk + 2) * TAPS]

    def convolve(g, carry):
        for at in range(GROUP):
            co = jnp.dot(
                x_scr[...].reshape(blocks * rows * cl, 2 * TAPS),
                tab_ref[g * GROUP + at],
                preferred_element_type=F32,
            )
            power = co[:, :TAPS] * co[:, :TAPS] + co[:, TAPS:] * co[:, TAPS:]
            s_ref[g * GROUP + at] = power.astype(BF16).reshape(blocks, rows, cl, TAPS)
        return carry

    lax.fori_loop(0, GROUPS, convolve, 0)


def first_kernel(rows, subs, cl, *refs):
    refs = list(refs)
    w_refs = [refs.pop(0) for _ in range(rows)]
    h_ref, s_ref, h_out, h_gram_ref = (refs.pop(0) for _ in range(4))
    msg_refs, num_scr = refs[:-1], refs[-1]
    x_me = lax.axis_index("row")
    parts, gram = [], jnp.zeros(h_gram_ref.shape, F32)
    for shift, ref in enumerate(w_refs):
        parts.append((ref[:, : NF * cl], lax.rem(x_me + rows - shift, rows)))
        gram = gram + joined(ref, NF * cl, h_ref.shape[0])
    numerators(parts, s_ref, num_scr, cl)
    new_activations(h_ref[...], gram, num_scr[...], s_ref, h_out, h_gram_ref, msg_refs, rows, subs, cl)


def row_parts(rows, subs, cl, w_refs, w_scr, shifts):
    x_me, c_me = lax.axis_index("row"), lax.axis_index("sub")
    size = NF // subs * cl
    parts = []
    for line, dx in enumerate(shifts):
        for dc in range(subs):
            w_scr[line, lax.rem(c_me + subs - dc, subs)] = w_refs[line * subs + dc][:, :size]
        w = jnp.concatenate([w_scr[line, c] for c in range(subs)], axis=1)
        parts.append((w, lax.rem(x_me + rows - dx, rows)))
    return parts


def early_kernel(rows, subs, cl, *refs):
    w_refs, (s_ref, num_ref, w_scr) = refs[:subs], refs[subs:]
    numerators(row_parts(rows, subs, cl, w_refs, w_scr, [0]), s_ref, num_ref, cl)


def later_kernel(rows, subs, cl, *refs):
    refs = list(refs)
    w_refs = [refs.pop(0) for _ in range(rows * subs)]
    early_ref, h_ref, s_ref, h_out, h_gram_ref = (refs.pop(0) for _ in range(5))
    msg_refs, (w_scr, num_scr) = refs[:-2], refs[-2:]
    gram = jnp.zeros(h_gram_ref.shape, F32)
    for ref in w_refs:
        gram = gram + joined(ref, NF // subs * cl, h_ref.shape[0])
    above = early_ref[...]
    if rows > 1:
        numerators(row_parts(rows, subs, cl, w_refs[subs:], w_scr, list(range(1, rows))), s_ref, num_scr, cl)
        above = above + num_scr[...]
    new_activations(h_ref[...], gram, above, s_ref, h_out, h_gram_ref, msg_refs, rows, subs, cl)


def core_kernel(count, rank, *refs):
    own_refs, gram_ref, got_refs = refs[:count], refs[count], refs[count + 1 : -count - 1]
    out_refs, total_ref = refs[-count - 1 : -1], refs[-1]
    size = own_refs[0].shape[1]
    each = len(got_refs) // count
    gram = gram_ref[...]
    for ref in got_refs[:each]:
        gram = gram + ref[:, size:]
    total_ref[...] = gram
    for at in range(count):
        total = own_refs[at][...]
        for ref in got_refs[at * each : (at + 1) * each]:
            total = total + ref[:, :size]
        pack(out_refs[at], total, gram)


def row_kernel(subs, own_ref, gram_ref, *refs):
    core_refs, msg_refs, out_ref = refs[: subs - 1], refs[subs - 1 : -1], refs[-1]
    rank, size = own_ref.shape
    total, gram = own_ref[...], gram_ref[...]
    for ref in core_refs:
        total = total + ref[...]
    for ref in msg_refs:
        total = total + ref[:, :size].astype(F32)
        gram = gram + joined(ref, size, rank)
    pack(out_ref, total, gram)


def summed(z_me, count, msg_refs, scr, rank, size):
    for shift in range(count):
        scr[partner(z_me, shift, count)] = msg_refs[shift][...]
    total, gram = scr[0, :, :size].astype(F32), joined(scr[0], size, rank)
    for at in range(1, count):
        total = total + scr[at, :, :size].astype(F32)
        gram = gram + joined(scr[at], size, rank)
    return total, gram


def partner(place, shift, count):
    if count & (count - 1):
        return (place + count - shift) % count
    return place ^ shift


def update_kernel(count, w_ref, *refs):
    msg_refs, (new_ref, out_ref, scr) = refs[:count], refs[count:]
    rank, size = new_ref.shape
    total, gram = summed(lax.axis_index("frm"), count, msg_refs, scr, rank, size)
    w = w_ref[...]
    new = w * total / jnp.dot(gram, w, precision=HIGH, preferred_element_type=F32)
    new_ref[...] = new
    pack(out_ref, new, lax.dot_general(new, new, NT, precision=HIGH, preferred_element_type=F32))


def last_kernel(count, w_ref, order_ref, *refs):
    msg_refs, (out_ref, scr) = refs[:count], refs[count:]
    rank, size = w_ref.shape
    total, gram = summed(lax.axis_index("frm"), count, msg_refs, scr, rank, size)
    w = w_ref[...]
    new = w * total / jnp.dot(gram, w, precision=HIGH, preferred_element_type=F32)
    terms = three_terms(new)
    for c in range(order_ref.shape[1] // size):

        @pl.when(lax.axis_index("sub") == c)
        def _():
            moved = lax.dot_general(
                terms, order_ref[:, c * size : (c + 1) * size], NT, preferred_element_type=F32
            )
            out_ref[...] = moved[:rank] + (moved[rank : 2 * rank] + moved[2 * rank :])


def join_kernel(rows, subs, *refs):
    act_refs, parts, (syn_ref, out_ref, scr, sems) = refs[:rows], refs[rows : rows + subs], refs[rows + subs :]
    frames = act_refs[0].shape[1]
    x_me = lax.axis_index("row")
    copies = []
    for shift in range(rows):
        begin = pl.multiple_of(lax.rem(x_me + rows - shift, rows) * frames, TAPS)
        copies.append(pltpu.make_async_copy(act_refs[shift], out_ref.at[:, pl.ds(begin, frames)], sems.at[shift]))
    for copy in copies:
        copy.start()
    total = parts[0][...]
    for part in parts[1:]:
        total = total + part[...]
    scr[...] = total
    copies.append(pltpu.make_async_copy(scr, syn_ref, sems.at[rows]))
    copies[-1].start()
    for copy in copies:
        copy.wait()


def call(kernel, args, outs, scratch=(), in_specs=None, out_specs=None, limit=4, cost=None):
    whole = pl.BlockSpec(memory_space=pltpu.VMEM)
    if cost is not None:
        cost = pl.CostEstimate(flops=cost, bytes_accessed=0, transcendentals=0)
    return pl.pallas_call(
        kernel,
        out_shape=[jax.ShapeDtypeStruct(*out) if isinstance(out, tuple) else out for out in outs],
        in_specs=in_specs or [whole] * len(args),
        out_specs=out_specs or [whole] * len(outs),
        scratch_shapes=list(scratch),
        compiler_params=pltpu.CompilerParams(vmem_limit_bytes=limit * MIB),
        cost_estimate=cost,
    )(*args)


def reorder(cl):
    order = np.zeros((cl, NF, NF, cl), ml_dtypes.bfloat16)
    chans, freqs = np.meshgrid(np.arange(cl), np.arange(NF), indexing="ij")
    order[chans, freqs, freqs, chans] = 1
    return order.reshape(cl * NF, NF * cl)


def shards(signal, w_start, h_start):
    rows, subs, frms = (lax.axis_size(axis) for axis in ("row", "sub", "frm"))
    x_me = lax.axis_index("row")
    cl, window = signal.shape
    rank = w_start.shape[1]
    frames = window // rows
    blocks = frames // TAPS
    chans = rows * cl
    size = NF * cl // subs
    line = frms * subs
    width = frames + (TAPS if rows == 2 else 2 * TAPS)
    anywhere = pl.BlockSpec(memory_space=pl.ANY)
    whole = pl.BlockSpec(memory_space=pltpu.VMEM)

    def hbm(value):
        return pltpu.with_memory_space_constraint(value, pltpu.HBM)

    def vmem(value):
        return pltpu.with_memory_space_constraint(value, pltpu.VMEM)

    def row_shift(value, shift):
        return lax.ppermute(value, "row", [(i, (i + shift) % rows) for i in range(rows)])

    def sub_shift(value, shift):
        return lax.ppermute(value, "sub", [(i, (i + shift) % subs) for i in range(subs)])

    def frm_shift(value, shift):
        return lax.ppermute(value, "frm", [(partner(i, shift, frms), i) for i in range(frms)])

    def place(x, at):
        return (at // subs * rows + x) * subs + at % subs

    own_sig, *out_sigs = call(
        functools.partial(cut_signal_kernel, rows, frames),
        [hbm(signal)],
        [((cl, width), BF16)] * rows,
        [pltpu.SemaphoreType.DMA((rows,))],
        in_specs=[anywhere],
    )
    sig = [own_sig] + [row_shift(part, shift + 1) for shift, part in enumerate(out_sigs)]
    (edge,) = call(functools.partial(edges_kernel, rows), sig, [((chans, TAPS), BF16)])
    pairs = [(place(rows - 1, i), place(0, i + 1)) for i in range(line - 1)]
    halo = lax.ppermute(edge, ("frm", "row", "sub"), pairs + [(b, a) for a, b in pairs])

    msg = ((rank, size + 2 * rank), BF16)
    piece = ((rank, size), F32)
    update_outs = [((rank, frames), F32), ((rank, rank), F32)]
    update_outs += [((rank, size + rank), F32)] * ((rows - 1) * (subs - 1))
    table, order = jnp.asarray(toeplitz()), jnp.asarray(reorder(cl))
    w_piece, w_msg, w_gram, old, order = call(
        fetch_kernel,
        [hbm(w_start.T), hbm(h_start), hbm(order), own_sig],
        [
            piece,
            ((rank, NF * cl + 2 * rank), BF16),
            ((rank, rank), F32),
            pltpu.VMEM((rank, frames), F32),
            pltpu.VMEM(order.shape, BF16),
        ],
        [pltpu.VMEM((rank, NF * cl), F32), pltpu.SemaphoreType.DMA((3,))],
        in_specs=[anywhere] * 4,
        cost=2 * 10**9,
    )
    w_msgs = [w_msg] + [row_shift(w_msg, shift) for shift in range(1, rows)]
    order = vmem(order)
    (table,) = call(
        table_kernel,
        [hbm(table), edge],
        [pltpu.VMEM(table.shape, BF16)],
        [pltpu.SemaphoreType.DMA],
        in_specs=[anywhere] * 2,
        cost=2 * 10**9,
    )
    (spectra,) = call(
        functools.partial(spectra_kernel, rows, cl, blocks),
        sig + [halo, vmem(table)],
        [pltpu.VMEM((NF, blocks, rows, cl, TAPS), BF16)],
        [pltpu.VMEM((rows, cl, frames + TAPS), BF16), pltpu.VMEM((blocks, chans, 2 * TAPS), BF16)],
        limit=8,
        cost=2 * NF * chans * frames * 4 * TAPS,
    )
    spectra = vmem(spectra)

    def products(places, activations, after):
        return call(
            functools.partial(products_kernel, places, rows, subs, cl),
            [activations, spectra] + after,
            [piece] * len(places),
            in_specs=[whole] * 2 + [anywhere] * len(after),
            cost=1 if after else 16 * NF * cl * frames * rank // subs * len(places),
        )

    def gathered(activations, h_gram, msgs):
        got = [sub_shift(m, dc) for m, (_, dc) in zip(msgs, others_of(rows, subs))]
        places = [(dx, 0) for dx in range(1, rows)] + [(0, dc) for dc in range(1, subs)]
        formed = products(places, activations, [])
        for_rows, for_cores = formed[: rows - 1], formed[rows - 1 :]
        from_cores = [sub_shift(m, dc + 1) for dc, m in enumerate(for_cores)]
        *outs, gram = call(
            functools.partial(core_kernel, rows - 1, rank),
            list(for_rows) + [h_gram] + got,
            [msg] * (rows - 1) + [((rank, rank), F32)],
        )
        from_rows = [row_shift(m, dx + 1) for dx, m in enumerate(outs)]
        (own,) = products([(0, 0)], activations, outs)
        (part,) = call(functools.partial(row_kernel, subs), [own, gram] + from_cores + from_rows, [msg])
        return [part] + [frm_shift(part, shift) for shift in range(1, frms)]

    activations, h_gram, *msgs = call(
        functools.partial(first_kernel, rows, subs, cl),
        w_msgs + [vmem(old), spectra],
        update_outs,
        [pltpu.VMEM((rank, frames), F32)],
        limit=8,
    )
    piled = [pltpu.VMEM((frms,) + msg[0], BF16)]
    w_piece, w_msg = call(
        functools.partial(update_kernel, frms),
        [w_piece] + gathered(activations, h_gram, msgs),
        [piece, msg],
        piled,
    )
    w_msgs = [w_msg] + [sub_shift(w_msg, dc) for dc in range(1, subs)]
    w_pieces = pltpu.VMEM((rows, subs, rank, size), BF16)
    (early,) = call(
        functools.partial(early_kernel, rows, subs, cl),
        w_msgs + [spectra],
        [((rank, frames), F32)],
        [w_pieces],
        cost=16 * NF * cl * frames * rank,
    )
    from_rows = [row_shift(w_msg, dx) for dx in range(1, rows)]
    *from_rows, early = lax.optimization_barrier((*from_rows, early))
    for base in from_rows:
        w_msgs += [base] + [sub_shift(base, dc) for dc in range(1, subs)]
    activations, h_gram, *msgs = call(
        functools.partial(later_kernel, rows, subs, cl),
        w_msgs + [early, activations, spectra],
        update_outs,
        [w_pieces, pltpu.VMEM((rank, frames), F32)],
        limit=8,
    )
    parts = gathered(activations, h_gram, msgs)
    activations, parts[0] = lax.optimization_barrier((activations, parts[0]))
    sides = [activations] + [row_shift(activations, shift) for shift in range(1, rows)]
    (part,) = call(
        functools.partial(last_kernel, frms), [w_piece, order] + parts, [((rank, NF * cl), F32)], piled
    )
    synergies, wide = call(
        functools.partial(join_kernel, rows, subs),
        sides + [part] + [sub_shift(part, dc) for dc in range(1, subs)],
        [pltpu.HBM((rank, NF * cl), F32), pltpu.HBM((rank, window), F32)],
        [pltpu.VMEM((rank, NF * cl), F32), pltpu.SemaphoreType.DMA((rows + 1,))],
        in_specs=[anywhere] * rows + [whole] * subs,
        out_specs=[anywhere] * 2,
    )
    return (synergies.T, wide)


def solution(mesh):
    placed = (P("row", ("grp", "frm", "sub")), P("row", None), P(None, ("grp", "frm", "sub")))
    return jax.shard_map(
        shards,
        mesh=mesh,
        in_specs=placed,
        out_specs=(P(("grp", "row"), None), P(None, ("grp", "frm", "sub"))),
        check_vma=False,
    )
```

```python
import functools
import math

import jax
import jax.numpy as jnp
import ml_dtypes
import numpy as np
from jax import lax
from jax.experimental import pallas as pl
from jax.experimental.pallas import tpu as pltpu
from jax.sharding import PartitionSpec as P

NF = 40
TAPS = 128
HALF = TAPS // 2
GROUP = 4
GROUPS = NF // GROUP
F32 = jnp.float32
BF16 = jnp.bfloat16
HIGH = lax.Precision.HIGHEST
NT = (((1,), (1,)), ((), ()))
MIB = 1024 * 1024


def wavelets():
    f = np.float32
    level = np.arange(NF, dtype=f) / f(NF - 1)
    freq = f(2.0) * np.power(f(12.0), level)
    sigma = f(7.0) / (f(2.0 * math.pi) * freq)
    times = (np.arange(TAPS, dtype=f) - f(HALF)) / f(50.0)
    env = np.exp(-(times[None, :] ** 2) / (f(2.0) * sigma[:, None] ** 2))
    scale = f(1.0) / np.sqrt(np.sum(env * env, axis=1))
    env = env * scale[:, None]
    phase = f(2.0 * math.pi) * freq[:, None] * times[None, :]
    return np.stack([env * np.cos(phase), env * np.sin(phase)]).astype(ml_dtypes.bfloat16)


def toeplitz():
    kernel = wavelets()
    table = np.zeros((NF, 2 * TAPS, 2 * TAPS), ml_dtypes.bfloat16)
    for at in range(TAPS):
        for part in range(2):
            table[:, at : at + TAPS, part * TAPS + at] = kernel[part]
    return table


def split_two(value):
    top = value.astype(BF16)
    return top, (value - top.astype(F32)).astype(BF16)


def joined(message, at, rank):
    return message[:, at : at + rank].astype(F32) + message[:, at + rank : at + 2 * rank].astype(F32)


def pack(out_ref, main, gram):
    rank, size = main.shape
    top, rest = split_two(gram)
    out_ref[:, :size] = main.astype(BF16)
    out_ref[:, size : size + rank] = top
    out_ref[:, size + rank : size + 2 * rank] = rest


def fetch_kernel(w_hbm, h_hbm, order_hbm, tab_hbm, *refs):
    piece_ref, whole_ref, gram_ref, old_ref, order_ref, tab_ref, w_scr, sems = refs[-8:]
    frames = old_ref.shape[1]
    size = piece_ref.shape[1]
    mine = pl.ds(pl.multiple_of(lax.axis_index("row") * frames, TAPS), frames)
    copies = [
        pltpu.make_async_copy(w_hbm, w_scr, sems.at[0]),
        pltpu.make_async_copy(order_hbm, order_ref, sems.at[1]),
        pltpu.make_async_copy(tab_hbm, tab_ref, sems.at[2]),
        pltpu.make_async_copy(h_hbm.at[:, mine], old_ref, sems.at[3]),
    ]
    for copy in copies:
        copy.start()
    copies[0].wait()
    w = w_scr[...]
    rank = w.shape[0]
    gram = lax.dot_general(w, w, NT, precision=HIGH, preferred_element_type=F32)
    gram_ref[...] = gram
    terms = three_terms(w)
    copies[1].wait()
    moved = jnp.dot(terms, order_ref[...], preferred_element_type=F32)
    whole = moved[:rank] + (moved[rank : 2 * rank] + moved[2 * rank :])
    for c in range(w.shape[1] // size):

        @pl.when(lax.axis_index("sub") == c)
        def _():
            piece_ref[...] = whole[:, c * size : (c + 1) * size]

    whole_ref[...] = whole
    copies[2].wait()
    copies[3].wait()


def pack_kernel(w_ref, gram_ref, *refs):
    pack(refs[-1], w_ref[...], gram_ref[...])


def three_terms(value):
    top = value.astype(BF16)
    rest = value - top.astype(F32)
    middle = rest.astype(BF16)
    return jnp.concatenate([top, middle, (rest - middle.astype(F32)).astype(BF16)], axis=0)


def edges_kernel(rows, sig_ref, *refs):
    got_refs, out_ref = refs[: rows - 1], refs[rows - 1]
    cl, width = sig_ref.shape
    x_me = lax.axis_index("row")
    for at, ref in enumerate((sig_ref,) + tuple(got_refs)):

        @pl.when(x_me == 0)
        def _():
            out_ref[at * cl : (at + 1) * cl, :] = ref[:, :TAPS]

        @pl.when(x_me > 0)
        def _():
            out_ref[at * cl : (at + 1) * cl, :] = ref[:, width - TAPS :]


def cut_signal_kernel(rows, frames, sig_hbm, *refs):
    out_refs, sems = refs[-rows - 1 : -1], refs[-1]
    window, x_me = sig_hbm.shape[1], lax.axis_index("row")
    width = out_refs[0].shape[1]
    copies = []
    for shift in range(rows):
        target = lax.rem(x_me + shift, rows)
        begin = pl.multiple_of(jnp.clip(target * frames - TAPS, 0, window - width), TAPS)
        copies.append(pltpu.make_async_copy(sig_hbm.at[:, pl.ds(begin, width)], out_refs[shift], sems.at[shift]))
    for copy in copies:
        copy.start()
    for copy in copies:
        copy.wait()


def pair_rows(s_ref, span, pair, x, cl):
    halves = [s_ref[span, blk, x].reshape(-1, TAPS) for blk in (2 * pair, 2 * pair + 1)]
    return jnp.concatenate(halves, axis=1)


def numerators(parts, s_ref, num_ref, cl):
    for pair in range(num_ref.shape[1] // (2 * TAPS)):
        terms = [
            jnp.dot(w, pair_rows(s_ref, slice(None), pair, x, cl), preferred_element_type=F32) for w, x in parts
        ]
        num_ref[:, 2 * TAPS * pair : 2 * TAPS * (pair + 1)] = functools.reduce(jnp.add, terms)


def crossed(low, s_ref, x, core, subs, cl):
    count = NF // subs
    span = pl.ds(core * count, count)
    acc = jnp.zeros((low.shape[0], count * cl), F32)
    for pair in range(low.shape[1] // (2 * TAPS)):
        cols = slice(2 * TAPS * pair, 2 * TAPS * (pair + 1))
        acc = acc + lax.dot_general(
            low[:, cols], pair_rows(s_ref, span, pair, x, cl), NT, preferred_element_type=F32
        )
    return acc


def others_of(rows, subs):
    return [(dx, dc) for dx in range(1, rows) for dc in range(1, subs)]


def new_activations(old, gram, above, s_ref, h_out, h_gram_ref, msg_refs, rows, subs, cl):
    new = old * above / jnp.dot(gram, old, precision=HIGH, preferred_element_type=F32)
    h_out[...] = new
    h_gram = lax.dot_general(new, new, NT, precision=HIGH, preferred_element_type=F32)
    h_gram_ref[...] = h_gram
    size = NF // subs * cl
    x_me, c_me = lax.axis_index("row"), lax.axis_index("sub")
    for ref, (dx, dc) in zip(msg_refs, others_of(rows, subs)):
        ref[:, :size] = crossed(
            new.astype(BF16), s_ref, lax.rem(x_me + dx, rows), lax.rem(c_me + dc, subs), subs, cl
        )
        ref[:, size:] = h_gram


def products_kernel(places, rows, subs, cl, h_ref, s_ref, *refs):
    x_me, c_me = lax.axis_index("row"), lax.axis_index("sub")
    low = h_ref[...].astype(BF16)
    for ref, (dx, dc) in zip(refs[len(refs) - len(places) :], places):
        ref[...] = crossed(low, s_ref, lax.rem(x_me + dx, rows), lax.rem(c_me + dc, subs), subs, cl)


def spectra_kernel(rows, cl, blocks, *refs):
    refs = list(refs)
    sig_refs = [refs.pop(0) for _ in range(rows)]
    halo_ref, tab_ref, s_ref, xp_scr, x_scr = refs
    frames = blocks * TAPS
    width = sig_refs[0].shape[1]
    x_me = lax.axis_index("row")

    def place(source, owner):
        @pl.when(x_me == 0)
        def _():
            xp_scr[owner, :, HALF:] = source[:, : frames + HALF]

        @pl.when(x_me == rows - 1)
        def _():
            skip = width - frames - HALF
            xp_scr[owner, :, : frames + HALF] = source[:, skip:]

        if rows > 2:

            @pl.when((x_me > 0) & (x_me < rows - 1))
            def _():
                xp_scr[owner] = source[:, HALF : HALF + frames + TAPS]

    for shift in range(rows):
        place(sig_refs[shift], lax.rem(x_me + rows - shift, rows))

    @pl.when(x_me == 0)
    def _():
        for at in range(rows):
            xp_scr[rows - 1 - at, :, :HALF] = halo_ref[at * cl : (at + 1) * cl, HALF:]

    @pl.when(x_me == rows - 1)
    def _():
        for at in range(rows):
            xp_scr[(rows - at) % rows, :, frames + HALF :] = halo_ref[at * cl : (at + 1) * cl, :HALF]

    for blk in range(blocks):
        for x in range(rows):
            x_scr[blk, x * cl : (x + 1) * cl, :] = xp_scr[x, :, blk * TAPS : (blk + 2) * TAPS]

    def convolve(g, carry):
        for at in range(GROUP):
            co = jnp.dot(
                x_scr[...].reshape(blocks * rows * cl, 2 * TAPS),
                tab_ref[g * GROUP + at],
                preferred_element_type=F32,
            )
            power = co[:, :TAPS] * co[:, :TAPS] + co[:, TAPS:] * co[:, TAPS:]
            s_ref[g * GROUP + at] = power.astype(BF16).reshape(blocks, rows, cl, TAPS)
        return carry

    lax.fori_loop(0, GROUPS, convolve, 0)


def first_kernel(rows, subs, cl, *refs):
    refs = list(refs)
    w_refs = [refs.pop(0) for _ in range(rows)]
    h_ref, s_ref, h_out, h_gram_ref = (refs.pop(0) for _ in range(4))
    msg_refs, num_scr = refs[:-1], refs[-1]
    x_me = lax.axis_index("row")
    parts, gram = [], jnp.zeros(h_gram_ref.shape, F32)
    for shift, ref in enumerate(w_refs):
        parts.append((ref[:, : NF * cl], lax.rem(x_me + rows - shift, rows)))
        gram = gram + joined(ref, NF * cl, h_ref.shape[0])
    numerators(parts, s_ref, num_scr, cl)
    new_activations(h_ref[...], gram, num_scr[...], s_ref, h_out, h_gram_ref, msg_refs, rows, subs, cl)


def row_parts(rows, subs, cl, w_refs, w_scr, shifts):
    x_me, c_me = lax.axis_index("row"), lax.axis_index("sub")
    size = NF // subs * cl
    parts = []
    for line, dx in enumerate(shifts):
        for dc in range(subs):
            w_scr[line, lax.rem(c_me + subs - dc, subs)] = w_refs[line * subs + dc][:, :size]
        w = jnp.concatenate([w_scr[line, c] for c in range(subs)], axis=1)
        parts.append((w, lax.rem(x_me + rows - dx, rows)))
    return parts


def early_kernel(rows, subs, cl, *refs):
    w_refs, (s_ref, num_ref, w_scr) = refs[:subs], refs[subs:]
    numerators(row_parts(rows, subs, cl, w_refs, w_scr, [0]), s_ref, num_ref, cl)


def later_kernel(rows, subs, cl, *refs):
    refs = list(refs)
    w_refs = [refs.pop(0) for _ in range(rows * subs)]
    early_ref, h_ref, s_ref, h_out, h_gram_ref = (refs.pop(0) for _ in range(5))
    msg_refs, (w_scr, num_scr) = refs[:-2], refs[-2:]
    gram = jnp.zeros(h_gram_ref.shape, F32)
    for ref in w_refs:
        gram = gram + joined(ref, NF // subs * cl, h_ref.shape[0])
    above = early_ref[...]
    if rows > 1:
        numerators(row_parts(rows, subs, cl, w_refs[subs:], w_scr, list(range(1, rows))), s_ref, num_scr, cl)
        above = above + num_scr[...]
    new_activations(h_ref[...], gram, above, s_ref, h_out, h_gram_ref, msg_refs, rows, subs, cl)


def core_kernel(count, rank, *refs):
    own_refs, gram_ref, got_refs = refs[:count], refs[count], refs[count + 1 : -count - 1]
    out_refs, total_ref = refs[-count - 1 : -1], refs[-1]
    size = own_refs[0].shape[1]
    each = len(got_refs) // count
    gram = gram_ref[...]
    for ref in got_refs[:each]:
        gram = gram + ref[:, size:]
    total_ref[...] = gram
    for at in range(count):
        total = own_refs[at][...]
        for ref in got_refs[at * each : (at + 1) * each]:
            total = total + ref[:, :size]
        pack(out_refs[at], total, gram)


def row_kernel(subs, own_ref, gram_ref, *refs):
    core_refs, msg_refs, out_ref = refs[: subs - 1], refs[subs - 1 : -1], refs[-1]
    rank, size = own_ref.shape
    total, gram = own_ref[...], gram_ref[...]
    for ref in core_refs:
        total = total + ref[...]
    for ref in msg_refs:
        total = total + ref[:, :size].astype(F32)
        gram = gram + joined(ref, size, rank)
    pack(out_ref, total, gram)


def summed(z_me, count, msg_refs, scr, rank, size):
    for shift in range(count):
        scr[partner(z_me, shift, count)] = msg_refs[shift][...]
    total, gram = scr[0, :, :size].astype(F32), joined(scr[0], size, rank)
    for at in range(1, count):
        total = total + scr[at, :, :size].astype(F32)
        gram = gram + joined(scr[at], size, rank)
    return total, gram


def partner(place, shift, count):
    if count & (count - 1):
        return (place + count - shift) % count
    return place ^ shift


def update_kernel(count, w_ref, *refs):
    msg_refs, (new_ref, out_ref, scr) = refs[:count], refs[count:]
    rank, size = new_ref.shape
    total, gram = summed(lax.axis_index("frm"), count, msg_refs, scr, rank, size)
    w = w_ref[...]
    new = w * total / jnp.dot(gram, w, precision=HIGH, preferred_element_type=F32)
    new_ref[...] = new
    pack(out_ref, new, lax.dot_general(new, new, NT, precision=HIGH, preferred_element_type=F32))


def last_kernel(count, w_ref, order_ref, *refs):
    msg_refs, (out_ref, scr) = refs[:count], refs[count:]
    rank, size = w_ref.shape
    total, gram = summed(lax.axis_index("frm"), count, msg_refs, scr, rank, size)
    w = w_ref[...]
    new = w * total / jnp.dot(gram, w, precision=HIGH, preferred_element_type=F32)
    terms = three_terms(new)
    for c in range(order_ref.shape[1] // size):

        @pl.when(lax.axis_index("sub") == c)
        def _():
            moved = lax.dot_general(
                terms, order_ref[:, c * size : (c + 1) * size], NT, preferred_element_type=F32
            )
            out_ref[...] = moved[:rank] + (moved[rank : 2 * rank] + moved[2 * rank :])


def join_kernel(rows, subs, *refs):
    act_refs, parts, (syn_ref, out_ref, scr, sems) = refs[:rows], refs[rows : rows + subs], refs[rows + subs :]
    frames = act_refs[0].shape[1]
    x_me = lax.axis_index("row")
    copies = []
    for shift in range(rows):
        begin = pl.multiple_of(lax.rem(x_me + rows - shift, rows) * frames, TAPS)
        copies.append(pltpu.make_async_copy(act_refs[shift], out_ref.at[:, pl.ds(begin, frames)], sems.at[shift]))
    for copy in copies:
        copy.start()
    total = parts[0][...]
    for part in parts[1:]:
        total = total + part[...]
    scr[...] = total
    copies.append(pltpu.make_async_copy(scr, syn_ref, sems.at[rows]))
    copies[-1].start()
    for copy in copies:
        copy.wait()


def call(kernel, args, outs, scratch=(), in_specs=None, out_specs=None, limit=4, cost=None):
    whole = pl.BlockSpec(memory_space=pltpu.VMEM)
    if cost is not None:
        cost = pl.CostEstimate(flops=cost, bytes_accessed=0, transcendentals=0)
    return pl.pallas_call(
        kernel,
        out_shape=[jax.ShapeDtypeStruct(*out) if isinstance(out, tuple) else out for out in outs],
        in_specs=in_specs or [whole] * len(args),
        out_specs=out_specs or [whole] * len(outs),
        scratch_shapes=list(scratch),
        compiler_params=pltpu.CompilerParams(vmem_limit_bytes=limit * MIB),
        cost_estimate=cost,
    )(*args)


def reorder(cl):
    order = np.zeros((cl, NF, NF, cl), ml_dtypes.bfloat16)
    chans, freqs = np.meshgrid(np.arange(cl), np.arange(NF), indexing="ij")
    order[chans, freqs, freqs, chans] = 1
    return order.reshape(cl * NF, NF * cl)


def shards(signal, w_start, h_start):
    rows, subs, frms = (lax.axis_size(axis) for axis in ("row", "sub", "frm"))
    x_me = lax.axis_index("row")
    cl, window = signal.shape
    rank = w_start.shape[1]
    frames = window // rows
    blocks = frames // TAPS
    chans = rows * cl
    size = NF * cl // subs
    line = frms * subs
    width = frames + (TAPS if rows == 2 else 2 * TAPS)
    anywhere = pl.BlockSpec(memory_space=pl.ANY)
    whole = pl.BlockSpec(memory_space=pltpu.VMEM)

    def hbm(value):
        return pltpu.with_memory_space_constraint(value, pltpu.HBM)

    def vmem(value):
        return pltpu.with_memory_space_constraint(value, pltpu.VMEM)

    def row_shift(value, shift):
        return lax.ppermute(value, "row", [(i, (i + shift) % rows) for i in range(rows)])

    def sub_shift(value, shift):
        return lax.ppermute(value, "sub", [(i, (i + shift) % subs) for i in range(subs)])

    def frm_shift(value, shift):
        return lax.ppermute(value, "frm", [(partner(i, shift, frms), i) for i in range(frms)])

    def place(x, at):
        return (at // subs * rows + x) * subs + at % subs

    own_sig, *out_sigs = call(
        functools.partial(cut_signal_kernel, rows, frames),
        [hbm(signal)],
        [((cl, width), BF16)] * rows,
        [pltpu.SemaphoreType.DMA((rows,))],
        in_specs=[anywhere],
    )
    sig = [own_sig] + [row_shift(part, shift + 1) for shift, part in enumerate(out_sigs)]
    (edge,) = call(functools.partial(edges_kernel, rows), sig, [((chans, TAPS), BF16)])
    pairs = [(place(rows - 1, i), place(0, i + 1)) for i in range(line - 1)]
    halo = lax.ppermute(edge, ("frm", "row", "sub"), pairs + [(b, a) for a, b in pairs])

    msg = ((rank, size + 2 * rank), BF16)
    piece = ((rank, size), F32)
    update_outs = [((rank, frames), F32), ((rank, rank), F32)]
    update_outs += [((rank, size + rank), F32)] * ((rows - 1) * (subs - 1))
    table, order = jnp.asarray(toeplitz()), jnp.asarray(reorder(cl))
    w_piece, w_whole, w_gram, old, order, table = call(
        fetch_kernel,
        [hbm(w_start.T), hbm(h_start), hbm(order), hbm(table), own_sig],
        [
            piece,
            ((rank, NF * cl), F32),
            ((rank, rank), F32),
            pltpu.VMEM((rank, frames), F32),
            pltpu.VMEM(order.shape, BF16),
            pltpu.VMEM(table.shape, BF16),
        ],
        [pltpu.VMEM((rank, NF * cl), F32), pltpu.SemaphoreType.DMA((4,))],
        in_specs=[anywhere] * 5,
        cost=2 * 10**9,
    )
    (w_msg,) = call(
        pack_kernel,
        [w_whole, w_gram, edge],
        [((rank, NF * cl + 2 * rank), BF16)],
        in_specs=[whole, whole, anywhere],
    )
    w_msgs = [w_msg] + [row_shift(w_msg, shift) for shift in range(1, rows)]
    order = vmem(order)
    (spectra,) = call(
        functools.partial(spectra_kernel, rows, cl, blocks),
        sig + [halo, vmem(table)],
        [pltpu.VMEM((NF, blocks, rows, cl, TAPS), BF16)],
        [pltpu.VMEM((rows, cl, frames + TAPS), BF16), pltpu.VMEM((blocks, chans, 2 * TAPS), BF16)],
        limit=8,
        cost=2 * NF * chans * frames * 4 * TAPS,
    )
    spectra = vmem(spectra)

    def products(places, activations, after):
        return call(
            functools.partial(products_kernel, places, rows, subs, cl),
            [activations, spectra] + after,
            [piece] * len(places),
            in_specs=[whole] * 2 + [anywhere] * len(after),
            cost=1 if after else 16 * NF * cl * frames * rank // subs * len(places),
        )

    def gathered(activations, h_gram, msgs):
        got = [sub_shift(m, dc) for m, (_, dc) in zip(msgs, others_of(rows, subs))]
        places = [(dx, 0) for dx in range(1, rows)] + [(0, dc) for dc in range(1, subs)]
        formed = products(places, activations, [])
        for_rows, for_cores = formed[: rows - 1], formed[rows - 1 :]
        from_cores = [sub_shift(m, dc + 1) for dc, m in enumerate(for_cores)]
        *outs, gram = call(
            functools.partial(core_kernel, rows - 1, rank),
            list(for_rows) + [h_gram] + got,
            [msg] * (rows - 1) + [((rank, rank), F32)],
        )
        from_rows = [row_shift(m, dx + 1) for dx, m in enumerate(outs)]
        (own,) = products([(0, 0)], activations, outs)
        (part,) = call(functools.partial(row_kernel, subs), [own, gram] + from_cores + from_rows, [msg])
        return [part] + [frm_shift(part, shift) for shift in range(1, frms)]

    activations, h_gram, *msgs = call(
        functools.partial(first_kernel, rows, subs, cl),
        w_msgs + [vmem(old), spectra],
        update_outs,
        [pltpu.VMEM((rank, frames), F32)],
        limit=8,
    )
    piled = [pltpu.VMEM((frms,) + msg[0], BF16)]
    w_piece, w_msg = call(
        functools.partial(update_kernel, frms),
        [w_piece] + gathered(activations, h_gram, msgs),
        [piece, msg],
        piled,
    )
    w_msgs = [w_msg] + [sub_shift(w_msg, dc) for dc in range(1, subs)]
    w_pieces = pltpu.VMEM((rows, subs, rank, size), BF16)
    (early,) = call(
        functools.partial(early_kernel, rows, subs, cl),
        w_msgs + [spectra],
        [((rank, frames), F32)],
        [w_pieces],
        cost=16 * NF * cl * frames * rank,
    )
    from_rows = [row_shift(w_msg, dx) for dx in range(1, rows)]
    *from_rows, early = lax.optimization_barrier((*from_rows, early))
    for base in from_rows:
        w_msgs += [base] + [sub_shift(base, dc) for dc in range(1, subs)]
    activations, h_gram, *msgs = call(
        functools.partial(later_kernel, rows, subs, cl),
        w_msgs + [early, activations, spectra],
        update_outs,
        [w_pieces, pltpu.VMEM((rank, frames), F32)],
        limit=8,
    )
    parts = gathered(activations, h_gram, msgs)
    activations, parts[0] = lax.optimization_barrier((activations, parts[0]))
    sides = [activations] + [row_shift(activations, shift) for shift in range(1, rows)]
    (part,) = call(
        functools.partial(last_kernel, frms), [w_piece, order] + parts, [((rank, NF * cl), F32)], piled
    )
    synergies, wide = call(
        functools.partial(join_kernel, rows, subs),
        sides + [part] + [sub_shift(part, dc) for dc in range(1, subs)],
        [pltpu.HBM((rank, NF * cl), F32), pltpu.HBM((rank, window), F32)],
        [pltpu.VMEM((rank, NF * cl), F32), pltpu.SemaphoreType.DMA((rows + 1,))],
        in_specs=[anywhere] * rows + [whole] * subs,
        out_specs=[anywhere] * 2,
    )
    return (synergies.T, wide)


def solution(mesh):
    placed = (P("row", ("grp", "frm", "sub")), P("row", None), P(None, ("grp", "frm", "sub")))
    return jax.shard_map(
        shards,
        mesh=mesh,
        in_specs=placed,
        out_specs=(P(("grp", "row"), None), P(None, ("grp", "frm", "sub"))),
        check_vma=False,
    )
```

```python
import functools
import math

import jax
import jax.numpy as jnp
import ml_dtypes
import numpy as np
from jax import lax
from jax.experimental import pallas as pl
from jax.experimental.pallas import tpu as pltpu
from jax.sharding import PartitionSpec as P

NF = 40
TAPS = 128
HALF = TAPS // 2
GROUP = 4
GROUPS = NF // GROUP
F32 = jnp.float32
BF16 = jnp.bfloat16
HIGH = lax.Precision.HIGHEST
NT = (((1,), (1,)), ((), ()))
MIB = 1024 * 1024


def wavelets():
    f = np.float32
    level = np.arange(NF, dtype=f) / f(NF - 1)
    freq = f(2.0) * np.power(f(12.0), level)
    sigma = f(7.0) / (f(2.0 * math.pi) * freq)
    times = (np.arange(TAPS, dtype=f) - f(HALF)) / f(50.0)
    env = np.exp(-(times[None, :] ** 2) / (f(2.0) * sigma[:, None] ** 2))
    scale = f(1.0) / np.sqrt(np.sum(env * env, axis=1))
    env = env * scale[:, None]
    phase = f(2.0 * math.pi) * freq[:, None] * times[None, :]
    return np.stack([env * np.cos(phase), env * np.sin(phase)]).astype(ml_dtypes.bfloat16)


def toeplitz():
    kernel = wavelets()
    table = np.zeros((NF, 2 * TAPS, 2 * TAPS), ml_dtypes.bfloat16)
    for at in range(TAPS):
        for part in range(2):
            table[:, at : at + TAPS, part * TAPS + at] = kernel[part]
    return table


def split_two(value):
    top = value.astype(BF16)
    return top, (value - top.astype(F32)).astype(BF16)


def joined(message, at, rank):
    return message[:, at : at + rank].astype(F32) + message[:, at + rank : at + 2 * rank].astype(F32)


def pack(out_ref, main, gram):
    rank, size = main.shape
    top, rest = split_two(gram)
    out_ref[:, :size] = main.astype(BF16)
    out_ref[:, size : size + rank] = top
    out_ref[:, size + rank : size + 2 * rank] = rest


def reorder_kernel(w_ref, order_ref, *refs):
    piece_ref, msg_ref = refs[-2:]
    w = w_ref[...]
    rank, size = piece_ref.shape
    gram = lax.dot_general(w, w, NT, precision=HIGH, preferred_element_type=F32)
    moved = jnp.dot(three_terms(w), order_ref[...], preferred_element_type=F32)
    whole = moved[:rank] + (moved[rank : 2 * rank] + moved[2 * rank :])
    for c in range(w.shape[1] // size):

        @pl.when(lax.axis_index("sub") == c)
        def _():
            piece_ref[...] = whole[:, c * size : (c + 1) * size]

    pack(msg_ref, whole, gram)


def three_terms(value):
    top = value.astype(BF16)
    rest = value - top.astype(F32)
    middle = rest.astype(BF16)
    return jnp.concatenate([top, middle, (rest - middle.astype(F32)).astype(BF16)], axis=0)


def edges_kernel(rows, sig_ref, *refs):
    got_refs, out_ref = refs[: rows - 1], refs[-1]
    cl, width = sig_ref.shape
    x_me = lax.axis_index("row")
    for at, ref in enumerate((sig_ref,) + tuple(got_refs)):

        @pl.when(x_me == 0)
        def _():
            out_ref[at * cl : (at + 1) * cl, :] = ref[:, :TAPS]

        @pl.when(x_me > 0)
        def _():
            out_ref[at * cl : (at + 1) * cl, :] = ref[:, width - TAPS :]


def cut_signal_kernel(rows, frames, sig_hbm, *refs):
    out_refs, sems = refs[-rows - 1 : -1], refs[-1]
    window, x_me = sig_hbm.shape[1], lax.axis_index("row")
    width = out_refs[0].shape[1]
    copies = []
    for shift in range(rows):
        target = lax.rem(x_me + shift, rows)
        begin = pl.multiple_of(jnp.clip(target * frames - TAPS, 0, window - width), TAPS)
        copies.append(pltpu.make_async_copy(sig_hbm.at[:, pl.ds(begin, width)], out_refs[shift], sems.at[shift]))
    for copy in copies:
        copy.start()
    for copy in copies:
        copy.wait()


def pair_rows(s_ref, span, pair, x, cl):
    halves = [s_ref[span, blk, x].reshape(-1, TAPS) for blk in (2 * pair, 2 * pair + 1)]
    return jnp.concatenate(halves, axis=1)


def numerators(parts, s_ref, num_ref, cl):
    for pair in range(num_ref.shape[1] // (2 * TAPS)):
        terms = [
            jnp.dot(w, pair_rows(s_ref, slice(None), pair, x, cl), preferred_element_type=F32) for w, x in parts
        ]
        num_ref[:, 2 * TAPS * pair : 2 * TAPS * (pair + 1)] = functools.reduce(jnp.add, terms)


def crossed(low, s_ref, x, core, subs, cl):
    count = NF // subs
    span = pl.ds(core * count, count)
    acc = jnp.zeros((low.shape[0], count * cl), F32)
    for pair in range(low.shape[1] // (2 * TAPS)):
        cols = slice(2 * TAPS * pair, 2 * TAPS * (pair + 1))
        acc = acc + lax.dot_general(
            low[:, cols], pair_rows(s_ref, span, pair, x, cl), NT, preferred_element_type=F32
        )
    return acc


def others_of(rows, subs):
    return [(dx, dc) for dx in range(1, rows) for dc in range(1, subs)]


def new_activations(old, gram, above, s_ref, h_out, h_gram_ref, msg_refs, rows, subs, cl):
    new = old * above / jnp.dot(gram, old, precision=HIGH, preferred_element_type=F32)
    h_out[...] = new
    h_gram = lax.dot_general(new, new, NT, precision=HIGH, preferred_element_type=F32)
    h_gram_ref[...] = h_gram
    size = NF // subs * cl
    x_me, c_me = lax.axis_index("row"), lax.axis_index("sub")
    for ref, (dx, dc) in zip(msg_refs, others_of(rows, subs)):
        ref[:, :size] = crossed(
            new.astype(BF16), s_ref, lax.rem(x_me + dx, rows), lax.rem(c_me + dc, subs), subs, cl
        )
        ref[:, size:] = h_gram


def products_kernel(places, rows, subs, cl, h_ref, s_ref, *refs):
    x_me, c_me = lax.axis_index("row"), lax.axis_index("sub")
    low = h_ref[...].astype(BF16)
    for ref, (dx, dc) in zip(refs[len(refs) - len(places) :], places):
        ref[...] = crossed(low, s_ref, lax.rem(x_me + dx, rows), lax.rem(c_me + dc, subs), subs, cl)


def place_signal(source, target, rows, frames):
    x_me = lax.axis_index("row")
    width = source.shape[1]

    @pl.when(x_me == 0)
    def _():
        target[:, HALF:] = source[:, : frames + HALF]

    @pl.when(x_me == rows - 1)
    def _():
        target[:, : frames + HALF] = source[:, width - frames - HALF :]

    if rows > 2:

        @pl.when((x_me > 0) & (x_me < rows - 1))
        def _():
            target[...] = source[:, HALF : HALF + frames + TAPS]


def power_of(x_ref, table):
    co = jnp.dot(x_ref[...], table, preferred_element_type=F32)
    return (co[:, :TAPS] * co[:, :TAPS] + co[:, TAPS:] * co[:, TAPS:]).astype(BF16)


def own_spectra_kernel(rows, sig_ref, w_hbm, h_hbm, order_hbm, tab_hbm, *refs):
    s_ref, w_ref, old_ref, order_ref, tab_ref, xp_scr, x_scr, sems, tab_sems = refs
    _, blocks, _, cl, _ = s_ref.shape
    frames = blocks * TAPS
    x_me = lax.axis_index("row")
    mine = pl.ds(pl.multiple_of(x_me * frames, TAPS), frames)

    def tab_copy(g):
        span = pl.ds(g * GROUP, GROUP)
        return pltpu.make_async_copy(tab_hbm.at[span], tab_ref.at[span], tab_sems.at[g])

    later = [
        pltpu.make_async_copy(w_hbm, w_ref, sems.at[0]),
        pltpu.make_async_copy(order_hbm, order_ref, sems.at[1]),
        pltpu.make_async_copy(h_hbm.at[:, mine], old_ref, sems.at[2]),
    ]
    for g in range(GROUPS):
        tab_copy(g).start()
    for copy in later:
        copy.start()
    place_signal(sig_ref, xp_scr, rows, frames)
    first = jnp.where(x_me == 0, 1, 0)
    for at in range(blocks - 1):
        begin = pl.multiple_of((first + at) * TAPS, TAPS)
        x_scr[at * cl : (at + 1) * cl, :] = xp_scr[:, pl.ds(begin, 2 * TAPS)]

    def convolve(g, carry):
        tab_copy(g).wait()
        for at in range(GROUP):
            f = g * GROUP + at
            s_ref[f, pl.ds(first, blocks - 1), x_me] = power_of(x_scr, tab_ref[f]).reshape(blocks - 1, cl, TAPS)
        return carry

    lax.fori_loop(0, GROUPS, convolve, 0)
    for copy in later:
        copy.wait()


def other_spectra_kernel(rows, halo_ref, tab_ref, *refs):
    sig_refs, (_, s_ref, xp_scr, x_scr) = refs[:rows], refs[rows:]
    _, blocks, _, cl, _ = s_ref.shape
    frames = blocks * TAPS
    x_me = lax.axis_index("row")
    owners = [lax.rem(x_me + rows - shift, rows) for shift in range(rows)]
    for shift in range(rows):
        place_signal(sig_refs[shift], xp_scr.at[owners[shift]], rows, frames)

    @pl.when(x_me == 0)
    def _():
        for at in range(rows):
            xp_scr[rows - 1 - at, :, :HALF] = halo_ref[at * cl : (at + 1) * cl, HALF:]

    @pl.when(x_me == rows - 1)
    def _():
        for at in range(rows):
            xp_scr[(rows - at) % rows, :, frames + HALF :] = halo_ref[at * cl : (at + 1) * cl, :HALF]

    outer = jnp.where(x_me == 0, 0, blocks - 1)
    begin = pl.multiple_of(outer * TAPS, TAPS)
    x_scr[:cl, :] = xp_scr[x_me, :, pl.ds(begin, 2 * TAPS)]
    for shift in range(1, rows):
        for blk in range(blocks):
            at = cl * (1 + (shift - 1) * blocks + blk)
            x_scr[at : at + cl, :] = xp_scr[owners[shift], :, blk * TAPS : (blk + 2) * TAPS]

    def convolve(g, carry):
        for at in range(GROUP):
            f = g * GROUP + at
            power = power_of(x_scr, tab_ref[f])
            s_ref[f, outer, x_me] = power[:cl]
            for shift in range(1, rows):
                line = cl * (1 + (shift - 1) * blocks)
                s_ref[f, :, owners[shift]] = power[line : line + blocks * cl].reshape(blocks, cl, TAPS)
        return carry

    lax.fori_loop(0, GROUPS, convolve, 0)


def first_kernel(rows, subs, cl, *refs):
    refs = list(refs)
    w_refs = [refs.pop(0) for _ in range(rows)]
    h_ref, s_ref, h_out, h_gram_ref = (refs.pop(0) for _ in range(4))
    msg_refs, num_scr = refs[:-1], refs[-1]
    x_me = lax.axis_index("row")
    parts, gram = [], jnp.zeros(h_gram_ref.shape, F32)
    for shift, ref in enumerate(w_refs):
        parts.append((ref[:, : NF * cl], lax.rem(x_me + rows - shift, rows)))
        gram = gram + joined(ref, NF * cl, h_ref.shape[0])
    numerators(parts, s_ref, num_scr, cl)
    new_activations(h_ref[...], gram, num_scr[...], s_ref, h_out, h_gram_ref, msg_refs, rows, subs, cl)


def row_parts(rows, subs, cl, w_refs, w_scr, shifts):
    x_me, c_me = lax.axis_index("row"), lax.axis_index("sub")
    size = NF // subs * cl
    parts = []
    for line, dx in enumerate(shifts):
        for dc in range(subs):
            w_scr[line, lax.rem(c_me + subs - dc, subs)] = w_refs[line * subs + dc][:, :size]
        w = jnp.concatenate([w_scr[line, c] for c in range(subs)], axis=1)
        parts.append((w, lax.rem(x_me + rows - dx, rows)))
    return parts


def early_kernel(rows, subs, cl, *refs):
    w_refs, (s_ref, num_ref, w_scr) = refs[:subs], refs[subs:]
    numerators(row_parts(rows, subs, cl, w_refs, w_scr, [0]), s_ref, num_ref, cl)


def later_kernel(rows, subs, cl, *refs):
    refs = list(refs)
    w_refs = [refs.pop(0) for _ in range(rows * subs)]
    early_ref, h_ref, s_ref, h_out, h_gram_ref = (refs.pop(0) for _ in range(5))
    msg_refs, (w_scr, num_scr) = refs[:-2], refs[-2:]
    gram = jnp.zeros(h_gram_ref.shape, F32)
    for ref in w_refs:
        gram = gram + joined(ref, NF // subs * cl, h_ref.shape[0])
    above = early_ref[...]
    if rows > 1:
        numerators(row_parts(rows, subs, cl, w_refs[subs:], w_scr, list(range(1, rows))), s_ref, num_scr, cl)
        above = above + num_scr[...]
    new_activations(h_ref[...], gram, above, s_ref, h_out, h_gram_ref, msg_refs, rows, subs, cl)


def core_kernel(count, rank, *refs):
    own_refs, gram_ref, got_refs = refs[:count], refs[count], refs[count + 1 : -count - 1]
    out_refs, total_ref = refs[-count - 1 : -1], refs[-1]
    size = own_refs[0].shape[1]
    each = len(got_refs) // count
    gram = gram_ref[...]
    for ref in got_refs[:each]:
        gram = gram + ref[:, size:]
    total_ref[...] = gram
    for at in range(count):
        total = own_refs[at][...]
        for ref in got_refs[at * each : (at + 1) * each]:
            total = total + ref[:, :size]
        pack(out_refs[at], total, gram)


def row_kernel(subs, own_ref, gram_ref, *refs):
    core_refs, msg_refs, out_ref = refs[: subs - 1], refs[subs - 1 : -1], refs[-1]
    rank, size = own_ref.shape
    total, gram = own_ref[...], gram_ref[...]
    for ref in core_refs:
        total = total + ref[...]
    for ref in msg_refs:
        total = total + ref[:, :size].astype(F32)
        gram = gram + joined(ref, size, rank)
    pack(out_ref, total, gram)


def summed(z_me, count, msg_refs, scr, rank, size):
    for shift in range(count):
        scr[partner(z_me, shift, count)] = msg_refs[shift][...]
    total, gram = scr[0, :, :size].astype(F32), joined(scr[0], size, rank)
    for at in range(1, count):
        total = total + scr[at, :, :size].astype(F32)
        gram = gram + joined(scr[at], size, rank)
    return total, gram


def partner(place, shift, count):
    if count & (count - 1):
        return (place + count - shift) % count
    return place ^ shift


def update_kernel(count, w_ref, *refs):
    msg_refs, (new_ref, out_ref, scr) = refs[:count], refs[count:]
    rank, size = new_ref.shape
    total, gram = summed(lax.axis_index("frm"), count, msg_refs, scr, rank, size)
    w = w_ref[...]
    new = w * total / jnp.dot(gram, w, precision=HIGH, preferred_element_type=F32)
    new_ref[...] = new
    pack(out_ref, new, lax.dot_general(new, new, NT, precision=HIGH, preferred_element_type=F32))


def last_kernel(count, w_ref, order_ref, *refs):
    msg_refs, (out_ref, scr) = refs[:count], refs[count:]
    rank, size = w_ref.shape
    total, gram = summed(lax.axis_index("frm"), count, msg_refs, scr, rank, size)
    w = w_ref[...]
    new = w * total / jnp.dot(gram, w, precision=HIGH, preferred_element_type=F32)
    terms = three_terms(new)
    for c in range(order_ref.shape[1] // size):

        @pl.when(lax.axis_index("sub") == c)
        def _():
            moved = lax.dot_general(
                terms, order_ref[:, c * size : (c + 1) * size], NT, preferred_element_type=F32
            )
            out_ref[...] = moved[:rank] + (moved[rank : 2 * rank] + moved[2 * rank :])


def join_kernel(rows, subs, *refs):
    act_refs, parts, (syn_ref, out_ref, scr, sems) = refs[:rows], refs[rows : rows + subs], refs[rows + subs :]
    frames = act_refs[0].shape[1]
    x_me = lax.axis_index("row")
    copies = []
    for shift in range(rows):
        begin = pl.multiple_of(lax.rem(x_me + rows - shift, rows) * frames, TAPS)
        copies.append(pltpu.make_async_copy(act_refs[shift], out_ref.at[:, pl.ds(begin, frames)], sems.at[shift]))
    for copy in copies:
        copy.start()
    total = parts[0][...]
    for part in parts[1:]:
        total = total + part[...]
    scr[...] = total
    copies.append(pltpu.make_async_copy(scr, syn_ref, sems.at[rows]))
    copies[-1].start()
    for copy in copies:
        copy.wait()


def call(kernel, args, outs, scratch=(), in_specs=None, out_specs=None, limit=4, cost=None, aliases=None):
    whole = pl.BlockSpec(memory_space=pltpu.VMEM)
    if cost is not None:
        cost = pl.CostEstimate(flops=cost, bytes_accessed=0, transcendentals=0)
    return pl.pallas_call(
        kernel,
        out_shape=[jax.ShapeDtypeStruct(*out) if isinstance(out, tuple) else out for out in outs],
        in_specs=in_specs or [whole] * len(args),
        out_specs=out_specs or [whole] * len(outs),
        scratch_shapes=list(scratch),
        compiler_params=pltpu.CompilerParams(vmem_limit_bytes=limit * MIB),
        cost_estimate=cost,
        input_output_aliases=aliases or {},
    )(*args)


def reorder(cl):
    order = np.zeros((cl, NF, NF, cl), ml_dtypes.bfloat16)
    chans, freqs = np.meshgrid(np.arange(cl), np.arange(NF), indexing="ij")
    order[chans, freqs, freqs, chans] = 1
    return order.reshape(cl * NF, NF * cl)


def shards(signal, w_start, h_start):
    rows, subs, frms = (lax.axis_size(axis) for axis in ("row", "sub", "frm"))
    x_me = lax.axis_index("row")
    cl, window = signal.shape
    rank = w_start.shape[1]
    frames = window // rows
    blocks = frames // TAPS
    chans = rows * cl
    size = NF * cl // subs
    line = frms * subs
    width = frames + (TAPS if rows == 2 else 2 * TAPS)
    anywhere = pl.BlockSpec(memory_space=pl.ANY)
    whole = pl.BlockSpec(memory_space=pltpu.VMEM)

    def hbm(value):
        return pltpu.with_memory_space_constraint(value, pltpu.HBM)

    def vmem(value):
        return pltpu.with_memory_space_constraint(value, pltpu.VMEM)

    def row_shift(value, shift):
        return lax.ppermute(value, "row", [(i, (i + shift) % rows) for i in range(rows)])

    def sub_shift(value, shift):
        return lax.ppermute(value, "sub", [(i, (i + shift) % subs) for i in range(subs)])

    def frm_shift(value, shift):
        return lax.ppermute(value, "frm", [(partner(i, shift, frms), i) for i in range(frms)])

    def place(x, at):
        return (at // subs * rows + x) * subs + at % subs

    own_sig, *out_sigs = call(
        functools.partial(cut_signal_kernel, rows, frames),
        [hbm(signal)],
        [((cl, width), BF16)] * rows,
        [pltpu.SemaphoreType.DMA((rows,))],
        in_specs=[anywhere],
    )
    sig = [own_sig] + [row_shift(part, shift + 1) for shift, part in enumerate(out_sigs)]
    msg = ((rank, size + 2 * rank), BF16)
    piece = ((rank, size), F32)
    update_outs = [((rank, frames), F32), ((rank, rank), F32)]
    update_outs += [((rank, size + rank), F32)] * ((rows - 1) * (subs - 1))
    table, order = jnp.asarray(toeplitz()), jnp.asarray(reorder(cl))
    half_done, w_own, old, order, table = call(
        functools.partial(own_spectra_kernel, rows),
        [own_sig, hbm(w_start.T), hbm(h_start), hbm(order), hbm(table)],
        [
            pltpu.VMEM((NF, blocks, rows, cl, TAPS), BF16),
            pltpu.VMEM((rank, NF * cl), F32),
            pltpu.VMEM((rank, frames), F32),
            pltpu.VMEM(order.shape, BF16),
            pltpu.VMEM(table.shape, BF16),
        ],
        [
            pltpu.VMEM((cl, frames + TAPS), BF16),
            pltpu.VMEM(((blocks - 1) * cl, 2 * TAPS), BF16),
            pltpu.SemaphoreType.DMA((3,)),
            pltpu.SemaphoreType.DMA((GROUPS,)),
        ],
        in_specs=[whole] + [anywhere] * 4,
        limit=8,
        cost=2 * NF * cl * frames * 4 * TAPS,
    )
    order = vmem(order)
    (edge,) = call(
        functools.partial(edges_kernel, rows),
        sig + [vmem(half_done)],
        [((chans, TAPS), BF16)],
        in_specs=[whole] * rows + [anywhere],
    )
    pairs = [(place(rows - 1, i), place(0, i + 1)) for i in range(line - 1)]
    halo = lax.ppermute(edge, ("frm", "row", "sub"), pairs + [(b, a) for a, b in pairs])
    w_piece, w_msg = call(
        reorder_kernel,
        [vmem(w_own), order, edge],
        [piece, ((rank, NF * cl + 2 * rank), BF16)],
        in_specs=[whole, whole, anywhere],
    )
    w_msgs = [w_msg] + [row_shift(w_msg, shift) for shift in range(1, rows)]
    (spectra,) = call(
        functools.partial(other_spectra_kernel, rows),
        [halo, vmem(table)] + sig + [vmem(half_done)],
        [pltpu.VMEM((NF, blocks, rows, cl, TAPS), BF16)],
        [
            pltpu.VMEM((rows, cl, frames + TAPS), BF16),
            pltpu.VMEM((((rows - 1) * blocks + 1) * cl, 2 * TAPS), BF16),
        ],
        in_specs=[whole] * (rows + 2) + [anywhere],
        limit=8,
        cost=2 * NF * chans * frames * 4 * TAPS,
        aliases={rows + 2: 0},
    )
    spectra = vmem(spectra)

    def products(places, activations, after):
        return call(
            functools.partial(products_kernel, places, rows, subs, cl),
            [activations, spectra] + after,
            [piece] * len(places),
            in_specs=[whole] * 2 + [anywhere] * len(after),
            cost=1 if after else 16 * NF * cl * frames * rank // subs * len(places),
        )

    def gathered(activations, h_gram, msgs):
        got = [sub_shift(m, dc) for m, (_, dc) in zip(msgs, others_of(rows, subs))]
        places = [(dx, 0) for dx in range(1, rows)] + [(0, dc) for dc in range(1, subs)]
        formed = products(places, activations, [])
        for_rows, for_cores = formed[: rows - 1], formed[rows - 1 :]
        from_cores = [sub_shift(m, dc + 1) for dc, m in enumerate(for_cores)]
        *outs, gram = call(
            functools.partial(core_kernel, rows - 1, rank),
            list(for_rows) + [h_gram] + got,
            [msg] * (rows - 1) + [((rank, rank), F32)],
        )
        from_rows = [row_shift(m, dx + 1) for dx, m in enumerate(outs)]
        (own,) = products([(0, 0)], activations, outs)
        (part,) = call(functools.partial(row_kernel, subs), [own, gram] + from_cores + from_rows, [msg])
        return [part] + [frm_shift(part, shift) for shift in range(1, frms)]

    activations, h_gram, *msgs = call(
        functools.partial(first_kernel, rows, subs, cl),
        w_msgs + [vmem(old), spectra],
        update_outs,
        [pltpu.VMEM((rank, frames), F32)],
        limit=8,
    )
    piled = [pltpu.VMEM((frms,) + msg[0], BF16)]
    w_piece, w_msg = call(
        functools.partial(update_kernel, frms),
        [w_piece] + gathered(activations, h_gram, msgs),
        [piece, msg],
        piled,
    )
    w_msgs = [w_msg] + [sub_shift(w_msg, dc) for dc in range(1, subs)]
    w_pieces = pltpu.VMEM((rows, subs, rank, size), BF16)
    (early,) = call(
        functools.partial(early_kernel, rows, subs, cl),
        w_msgs + [spectra],
        [((rank, frames), F32)],
        [w_pieces],
        cost=16 * NF * cl * frames * rank,
    )
    from_rows = [row_shift(w_msg, dx) for dx in range(1, rows)]
    *from_rows, early = lax.optimization_barrier((*from_rows, early))
    for base in from_rows:
        w_msgs += [base] + [sub_shift(base, dc) for dc in range(1, subs)]
    activations, h_gram, *msgs = call(
        functools.partial(later_kernel, rows, subs, cl),
        w_msgs + [early, activations, spectra],
        update_outs,
        [w_pieces, pltpu.VMEM((rank, frames), F32)],
        limit=8,
    )
    parts = gathered(activations, h_gram, msgs)
    activations, parts[0] = lax.optimization_barrier((activations, parts[0]))
    sides = [activations] + [row_shift(activations, shift) for shift in range(1, rows)]
    (part,) = call(
        functools.partial(last_kernel, frms), [w_piece, order] + parts, [((rank, NF * cl), F32)], piled
    )
    synergies, wide = call(
        functools.partial(join_kernel, rows, subs),
        sides + [part] + [sub_shift(part, dc) for dc in range(1, subs)],
        [pltpu.HBM((rank, NF * cl), F32), pltpu.HBM((rank, window), F32)],
        [pltpu.VMEM((rank, NF * cl), F32), pltpu.SemaphoreType.DMA((rows + 1,))],
        in_specs=[anywhere] * rows + [whole] * subs,
        out_specs=[anywhere] * 2,
    )
    return (synergies.T, wide)


def solution(mesh):
    placed = (P("row", ("grp", "frm", "sub")), P("row", None), P(None, ("grp", "frm", "sub")))
    return jax.shard_map(
        shards,
        mesh=mesh,
        in_specs=placed,
        out_specs=(P(("grp", "row"), None), P(None, ("grp", "frm", "sub"))),
        check_vma=False,
    )
```

```python
import functools
import math

import jax
import jax.numpy as jnp
import ml_dtypes
import numpy as np
from jax import lax
from jax.experimental import pallas as pl
from jax.experimental.pallas import tpu as pltpu
from jax.sharding import PartitionSpec as P

NF = 40
TAPS = 128
HALF = TAPS // 2
GROUP = 8
GROUPS = NF // GROUP
F32 = jnp.float32
BF16 = jnp.bfloat16
HIGH = lax.Precision.HIGHEST
NT = (((1,), (1,)), ((), ()))
MIB = 1024 * 1024


def wavelets():
    f = np.float32
    level = np.arange(NF, dtype=f) / f(NF - 1)
    freq = f(2.0) * np.power(f(12.0), level)
    sigma = f(7.0) / (f(2.0 * math.pi) * freq)
    times = (np.arange(TAPS, dtype=f) - f(HALF)) / f(50.0)
    env = np.exp(-(times[None, :] ** 2) / (f(2.0) * sigma[:, None] ** 2))
    scale = f(1.0) / np.sqrt(np.sum(env * env, axis=1))
    env = env * scale[:, None]
    phase = f(2.0 * math.pi) * freq[:, None] * times[None, :]
    return np.stack([env * np.cos(phase), env * np.sin(phase)]).astype(ml_dtypes.bfloat16)


def toeplitz():
    kernel = wavelets()
    table = np.zeros((NF, 2 * TAPS, 2 * TAPS), ml_dtypes.bfloat16)
    for at in range(TAPS):
        for part in range(2):
            table[:, at : at + TAPS, part * TAPS + at] = kernel[part]
    return table


def split_two(value):
    top = value.astype(BF16)
    return top, (value - top.astype(F32)).astype(BF16)


def joined(message, at, rank):
    return message[:, at : at + rank].astype(F32) + message[:, at + rank : at + 2 * rank].astype(F32)


def pack(out_ref, main, gram):
    rank, size = main.shape
    top, rest = split_two(gram)
    out_ref[:, :size] = main.astype(BF16)
    out_ref[:, size : size + rank] = top
    out_ref[:, size + rank : size + 2 * rank] = rest


def reorder_kernel(w_ref, order_ref, *refs):
    piece_ref, msg_ref = refs[-2:]
    w = w_ref[...]
    rank, size = piece_ref.shape
    gram = lax.dot_general(w, w, NT, precision=HIGH, preferred_element_type=F32)
    moved = jnp.dot(three_terms(w), order_ref[...], preferred_element_type=F32)
    whole = moved[:rank] + (moved[rank : 2 * rank] + moved[2 * rank :])
    for c in range(w.shape[1] // size):

        @pl.when(lax.axis_index("sub") == c)
        def _():
            piece_ref[...] = whole[:, c * size : (c + 1) * size]

    pack(msg_ref, whole, gram)


def three_terms(value):
    top = value.astype(BF16)
    rest = value - top.astype(F32)
    middle = rest.astype(BF16)
    return jnp.concatenate([top, middle, (rest - middle.astype(F32)).astype(BF16)], axis=0)


def edges_kernel(rows, sig_ref, *refs):
    got_refs, out_ref = refs[: rows - 1], refs[-1]
    cl, width = sig_ref.shape
    x_me = lax.axis_index("row")
    for at, ref in enumerate((sig_ref,) + tuple(got_refs)):

        @pl.when(x_me == 0)
        def _():
            out_ref[at * cl : (at + 1) * cl, :] = ref[:, :TAPS]

        @pl.when(x_me > 0)
        def _():
            out_ref[at * cl : (at + 1) * cl, :] = ref[:, width - TAPS :]


def cut_signal_kernel(rows, frames, sig_hbm, *refs):
    out_refs, sems = refs[-rows - 1 : -1], refs[-1]
    window, x_me = sig_hbm.shape[1], lax.axis_index("row")
    width = out_refs[0].shape[1]
    copies = []
    for shift in range(rows):
        target = lax.rem(x_me + shift, rows)
        begin = pl.multiple_of(jnp.clip(target * frames - TAPS, 0, window - width), TAPS)
        copies.append(pltpu.make_async_copy(sig_hbm.at[:, pl.ds(begin, width)], out_refs[shift], sems.at[shift]))
    for copy in copies:
        copy.start()
    for copy in copies:
        copy.wait()


def pair_rows(s_ref, span, pair, x, cl):
    halves = [s_ref[span, blk, x].reshape(-1, TAPS) for blk in (2 * pair, 2 * pair + 1)]
    return jnp.concatenate(halves, axis=1)


def numerators(parts, s_ref, num_ref, cl):
    for pair in range(num_ref.shape[1] // (2 * TAPS)):
        terms = [
            jnp.dot(w, pair_rows(s_ref, slice(None), pair, x, cl), preferred_element_type=F32) for w, x in parts
        ]
        num_ref[:, 2 * TAPS * pair : 2 * TAPS * (pair + 1)] = functools.reduce(jnp.add, terms)


def crossed(low, s_ref, places, subs, cl):
    count = NF // subs
    acc = jnp.zeros((low.shape[0], len(places) * count * cl), F32)
    for pair in range(low.shape[1] // (2 * TAPS)):
        cols = slice(2 * TAPS * pair, 2 * TAPS * (pair + 1))
        parts = [pair_rows(s_ref, pl.ds(core * count, count), pair, x, cl) for x, core in places]
        acc = acc + lax.dot_general(
            low[:, cols], jnp.concatenate(parts, axis=0), NT, preferred_element_type=F32
        )
    return acc


def others_of(rows, subs):
    return [(dx, dc) for dx in range(1, rows) for dc in range(1, subs)]


def new_activations(old, gram, above, s_ref, h_out, h_gram_ref, msg_refs, rows, subs, cl):
    new = old * above / jnp.dot(gram, old, precision=HIGH, preferred_element_type=F32)
    h_out[...] = new
    h_gram = lax.dot_general(new, new, NT, precision=HIGH, preferred_element_type=F32)
    h_gram_ref[...] = h_gram
    size = NF // subs * cl
    x_me, c_me = lax.axis_index("row"), lax.axis_index("sub")
    for ref, (dx, dc) in zip(msg_refs, others_of(rows, subs)):
        target = (lax.rem(x_me + dx, rows), lax.rem(c_me + dc, subs))
        ref[:, :size] = crossed(new.astype(BF16), s_ref, [target], subs, cl)
        ref[:, size:] = h_gram


def products_kernel(places, rows, subs, cl, h_ref, s_ref, *refs):
    x_me, c_me = lax.axis_index("row"), lax.axis_index("sub")
    low = h_ref[...].astype(BF16)
    targets = [(lax.rem(x_me + dx, rows), lax.rem(c_me + dc, subs)) for dx, dc in places]
    acc = crossed(low, s_ref, targets, subs, cl)
    size = acc.shape[1] // len(places)
    for at, ref in enumerate(refs[len(refs) - len(places) :]):
        ref[...] = acc[:, at * size : (at + 1) * size]


def place_signal(source, target, rows, frames):
    x_me = lax.axis_index("row")
    width = source.shape[1]

    @pl.when(x_me == 0)
    def _():
        target[:, HALF:] = source[:, : frames + HALF]

    @pl.when(x_me == rows - 1)
    def _():
        target[:, : frames + HALF] = source[:, width - frames - HALF :]

    if rows > 2:

        @pl.when((x_me > 0) & (x_me < rows - 1))
        def _():
            target[...] = source[:, HALF : HALF + frames + TAPS]


def power_of(x_ref, table):
    co = jnp.dot(x_ref[...], table, preferred_element_type=F32)
    return (co[:, :TAPS] * co[:, :TAPS] + co[:, TAPS:] * co[:, TAPS:]).astype(BF16)


def own_spectra_kernel(rows, sig_ref, w_hbm, h_hbm, order_hbm, tab_hbm, *refs):
    s_ref, w_ref, old_ref, order_ref, tab_ref, xp_scr, x_scr, sems, tab_sems = refs
    _, blocks, _, cl, _ = s_ref.shape
    frames = blocks * TAPS
    x_me = lax.axis_index("row")
    mine = pl.ds(pl.multiple_of(x_me * frames, TAPS), frames)

    def tab_copy(g):
        span = pl.ds(g * GROUP, GROUP)
        return pltpu.make_async_copy(tab_hbm.at[span], tab_ref.at[span], tab_sems.at[g])

    later = [
        pltpu.make_async_copy(w_hbm, w_ref, sems.at[0]),
        pltpu.make_async_copy(order_hbm, order_ref, sems.at[1]),
        pltpu.make_async_copy(h_hbm.at[:, mine], old_ref, sems.at[2]),
    ]
    for g in range(GROUPS):
        tab_copy(g).start()
    for copy in later:
        copy.start()
    place_signal(sig_ref, xp_scr, rows, frames)
    first = jnp.where(x_me == 0, 1, 0)
    for at in range(blocks - 1):
        begin = pl.multiple_of((first + at) * TAPS, TAPS)
        x_scr[at * cl : (at + 1) * cl, :] = xp_scr[:, pl.ds(begin, 2 * TAPS)]

    def convolve(g, carry):
        tab_copy(g).wait()
        for at in range(GROUP):
            f = g * GROUP + at
            s_ref[f, pl.ds(first, blocks - 1), x_me] = power_of(x_scr, tab_ref[f]).reshape(blocks - 1, cl, TAPS)
        return carry

    lax.fori_loop(0, GROUPS, convolve, 0)
    for copy in later:
        copy.wait()


def other_spectra_kernel(rows, halo_ref, tab_ref, *refs):
    sig_refs, (_, s_ref, xp_scr, x_scr) = refs[:rows], refs[rows:]
    _, blocks, _, cl, _ = s_ref.shape
    frames = blocks * TAPS
    x_me = lax.axis_index("row")
    owners = [lax.rem(x_me + rows - shift, rows) for shift in range(rows)]
    for shift in range(rows):
        place_signal(sig_refs[shift], xp_scr.at[owners[shift]], rows, frames)

    @pl.when(x_me == 0)
    def _():
        for at in range(rows):
            xp_scr[rows - 1 - at, :, :HALF] = halo_ref[at * cl : (at + 1) * cl, HALF:]

    @pl.when(x_me == rows - 1)
    def _():
        for at in range(rows):
            xp_scr[(rows - at) % rows, :, frames + HALF :] = halo_ref[at * cl : (at + 1) * cl, :HALF]

    outer = jnp.where(x_me == 0, 0, blocks - 1)
    begin = pl.multiple_of(outer * TAPS, TAPS)
    x_scr[:cl, :] = xp_scr[x_me, :, pl.ds(begin, 2 * TAPS)]
    for shift in range(1, rows):
        for blk in range(blocks):
            at = cl * (1 + (shift - 1) * blocks + blk)
            x_scr[at : at + cl, :] = xp_scr[owners[shift], :, blk * TAPS : (blk + 2) * TAPS]

    def convolve(g, carry):
        for at in range(GROUP):
            f = g * GROUP + at
            power = power_of(x_scr, tab_ref[f])
            s_ref[f, outer, x_me] = power[:cl]
            for shift in range(1, rows):
                line = cl * (1 + (shift - 1) * blocks)
                s_ref[f, :, owners[shift]] = power[line : line + blocks * cl].reshape(blocks, cl, TAPS)
        return carry

    lax.fori_loop(0, GROUPS, convolve, 0)


def first_kernel(rows, subs, cl, *refs):
    refs = list(refs)
    w_refs = [refs.pop(0) for _ in range(rows)]
    h_ref, s_ref, h_out, h_gram_ref = (refs.pop(0) for _ in range(4))
    msg_refs, num_scr = refs[:-1], refs[-1]
    x_me = lax.axis_index("row")
    parts, gram = [], jnp.zeros(h_gram_ref.shape, F32)
    for shift, ref in enumerate(w_refs):
        parts.append((ref[:, : NF * cl], lax.rem(x_me + rows - shift, rows)))
        gram = gram + joined(ref, NF * cl, h_ref.shape[0])
    numerators(parts, s_ref, num_scr, cl)
    new_activations(h_ref[...], gram, num_scr[...], s_ref, h_out, h_gram_ref, msg_refs, rows, subs, cl)


def row_parts(rows, subs, cl, w_refs, w_scr, shifts):
    x_me, c_me = lax.axis_index("row"), lax.axis_index("sub")
    size = NF // subs * cl
    parts = []
    for line, dx in enumerate(shifts):
        for dc in range(subs):
            w_scr[line, lax.rem(c_me + subs - dc, subs)] = w_refs[line * subs + dc][:, :size]
        w = jnp.concatenate([w_scr[line, c] for c in range(subs)], axis=1)
        parts.append((w, lax.rem(x_me + rows - dx, rows)))
    return parts


def early_kernel(rows, subs, cl, *refs):
    w_refs, (s_ref, num_ref, w_scr) = refs[:subs], refs[subs:]
    numerators(row_parts(rows, subs, cl, w_refs, w_scr, [0]), s_ref, num_ref, cl)


def later_kernel(rows, subs, cl, *refs):
    refs = list(refs)
    w_refs = [refs.pop(0) for _ in range(rows * subs)]
    early_ref, h_ref, s_ref, h_out, h_gram_ref = (refs.pop(0) for _ in range(5))
    msg_refs, (w_scr, num_scr) = refs[:-2], refs[-2:]
    gram = jnp.zeros(h_gram_ref.shape, F32)
    for ref in w_refs:
        gram = gram + joined(ref, NF // subs * cl, h_ref.shape[0])
    above = early_ref[...]
    if rows > 1:
        numerators(row_parts(rows, subs, cl, w_refs[subs:], w_scr, list(range(1, rows))), s_ref, num_scr, cl)
        above = above + num_scr[...]
    new_activations(h_ref[...], gram, above, s_ref, h_out, h_gram_ref, msg_refs, rows, subs, cl)


def core_kernel(count, rank, *refs):
    own_refs, gram_ref, got_refs = refs[:count], refs[count], refs[count + 1 : -count - 1]
    out_refs, total_ref = refs[-count - 1 : -1], refs[-1]
    size = own_refs[0].shape[1]
    each = len(got_refs) // count
    gram = gram_ref[...]
    for ref in got_refs[:each]:
        gram = gram + ref[:, size:]
    total_ref[...] = gram
    for at in range(count):
        total = own_refs[at][...]
        for ref in got_refs[at * each : (at + 1) * each]:
            total = total + ref[:, :size]
        pack(out_refs[at], total, gram)


def row_kernel(subs, own_ref, gram_ref, *refs):
    core_refs, msg_refs, out_ref = refs[: subs - 1], refs[subs - 1 : -1], refs[-1]
    rank, size = own_ref.shape
    total, gram = own_ref[...], gram_ref[...]
    for ref in core_refs:
        total = total + ref[...]
    for ref in msg_refs:
        total = total + ref[:, :size].astype(F32)
        gram = gram + joined(ref, size, rank)
    pack(out_ref, total, gram)


def summed(z_me, count, msg_refs, scr, rank, size):
    for shift in range(count):
        scr[partner(z_me, shift, count)] = msg_refs[shift][...]
    total, gram = scr[0, :, :size].astype(F32), joined(scr[0], size, rank)
    for at in range(1, count):
        total = total + scr[at, :, :size].astype(F32)
        gram = gram + joined(scr[at], size, rank)
    return total, gram


def partner(place, shift, count):
    if count & (count - 1):
        return (place + count - shift) % count
    return place ^ shift


def update_kernel(count, w_ref, *refs):
    msg_refs, (new_ref, out_ref, scr) = refs[:count], refs[count:]
    rank, size = new_ref.shape
    total, gram = summed(lax.axis_index("frm"), count, msg_refs, scr, rank, size)
    w = w_ref[...]
    new = w * total / jnp.dot(gram, w, precision=HIGH, preferred_element_type=F32)
    new_ref[...] = new
    pack(out_ref, new, lax.dot_general(new, new, NT, precision=HIGH, preferred_element_type=F32))


def last_kernel(count, w_ref, order_ref, *refs):
    msg_refs, (out_ref, scr) = refs[:count], refs[count:]
    rank, size = w_ref.shape
    total, gram = summed(lax.axis_index("frm"), count, msg_refs, scr, rank, size)
    w = w_ref[...]
    new = w * total / jnp.dot(gram, w, precision=HIGH, preferred_element_type=F32)
    terms = three_terms(new)
    for c in range(order_ref.shape[1] // size):

        @pl.when(lax.axis_index("sub") == c)
        def _():
            moved = lax.dot_general(
                terms, order_ref[:, c * size : (c + 1) * size], NT, preferred_element_type=F32
            )
            out_ref[...] = moved[:rank] + (moved[rank : 2 * rank] + moved[2 * rank :])


def join_kernel(rows, *refs):
    act_refs, (out_ref, sems) = refs[:rows], refs[rows:]
    frames = act_refs[0].shape[1]
    x_me = lax.axis_index("row")
    copies = []
    for shift in range(rows):
        begin = pl.multiple_of(lax.rem(x_me + rows - shift, rows) * frames, TAPS)
        copies.append(pltpu.make_async_copy(act_refs[shift], out_ref.at[:, pl.ds(begin, frames)], sems.at[shift]))
    for copy in copies:
        copy.start()
    for copy in copies:
        copy.wait()


def sum_kernel(*refs):
    parts, (out_ref, scr, sem) = refs[:-3], refs[-3:]
    total = parts[0][...]
    for part in parts[1:]:
        total = total + part[...]
    scr[...] = total
    copy = pltpu.make_async_copy(scr, out_ref, sem)
    copy.start()
    copy.wait()


def call(kernel, args, outs, scratch=(), in_specs=None, out_specs=None, limit=4, cost=None, aliases=None):
    whole = pl.BlockSpec(memory_space=pltpu.VMEM)
    if cost is not None:
        cost = pl.CostEstimate(flops=cost, bytes_accessed=0, transcendentals=0)
    return pl.pallas_call(
        kernel,
        out_shape=[jax.ShapeDtypeStruct(*out) if isinstance(out, tuple) else out for out in outs],
        in_specs=in_specs or [whole] * len(args),
        out_specs=out_specs or [whole] * len(outs),
        scratch_shapes=list(scratch),
        compiler_params=pltpu.CompilerParams(vmem_limit_bytes=limit * MIB),
        cost_estimate=cost,
        input_output_aliases=aliases or {},
    )(*args)


def reorder(cl):
    order = np.zeros((cl, NF, NF, cl), ml_dtypes.bfloat16)
    chans, freqs = np.meshgrid(np.arange(cl), np.arange(NF), indexing="ij")
    order[chans, freqs, freqs, chans] = 1
    return order.reshape(cl * NF, NF * cl)


def shards(signal, w_start, h_start):
    rows, subs, frms = (lax.axis_size(axis) for axis in ("row", "sub", "frm"))
    x_me = lax.axis_index("row")
    cl, window = signal.shape
    rank = w_start.shape[1]
    frames = window // rows
    blocks = frames // TAPS
    chans = rows * cl
    size = NF * cl // subs
    line = frms * subs
    width = frames + (TAPS if rows == 2 else 2 * TAPS)
    anywhere = pl.BlockSpec(memory_space=pl.ANY)
    whole = pl.BlockSpec(memory_space=pltpu.VMEM)

    def hbm(value):
        return pltpu.with_memory_space_constraint(value, pltpu.HBM)

    def vmem(value):
        return pltpu.with_memory_space_constraint(value, pltpu.VMEM)

    def row_shift(value, shift):
        return lax.ppermute(value, "row", [(i, (i + shift) % rows) for i in range(rows)])

    def sub_shift(value, shift):
        return lax.ppermute(value, "sub", [(i, (i + shift) % subs) for i in range(subs)])

    def frm_shift(value, shift):
        return lax.ppermute(value, "frm", [(partner(i, shift, frms), i) for i in range(frms)])

    def place(x, at):
        return (at // subs * rows + x) * subs + at % subs

    own_sig, *out_sigs = call(
        functools.partial(cut_signal_kernel, rows, frames),
        [hbm(signal)],
        [((cl, width), BF16)] * rows,
        [pltpu.SemaphoreType.DMA((rows,))],
        in_specs=[anywhere],
    )
    sig = [own_sig] + [row_shift(part, shift + 1) for shift, part in enumerate(out_sigs)]
    msg = ((rank, size + 2 * rank), BF16)
    piece = ((rank, size), F32)
    update_outs = [((rank, frames), F32), ((rank, rank), F32)]
    update_outs += [((rank, size + rank), F32)] * ((rows - 1) * (subs - 1))
    table, order = jnp.asarray(toeplitz()), jnp.asarray(reorder(cl))
    half_done, w_own, old, order, table = call(
        functools.partial(own_spectra_kernel, rows),
        [own_sig, hbm(w_start.T), hbm(h_start), hbm(order), hbm(table)],
        [
            pltpu.VMEM((NF, blocks, rows, cl, TAPS), BF16),
            pltpu.VMEM((rank, NF * cl), F32),
            pltpu.VMEM((rank, frames), F32),
            pltpu.VMEM(order.shape, BF16),
            pltpu.VMEM(table.shape, BF16),
        ],
        [
            pltpu.VMEM((cl, frames + TAPS), BF16),
            pltpu.VMEM(((blocks - 1) * cl, 2 * TAPS), BF16),
            pltpu.SemaphoreType.DMA((3,)),
            pltpu.SemaphoreType.DMA((GROUPS,)),
        ],
        in_specs=[whole] + [anywhere] * 4,
        limit=8,
        cost=2 * NF * cl * frames * 4 * TAPS,
    )
    order = vmem(order)
    (edge,) = call(
        functools.partial(edges_kernel, rows),
        sig + [vmem(half_done)],
        [((chans, TAPS), BF16)],
        in_specs=[whole] * rows + [anywhere],
    )
    pairs = [(place(rows - 1, i), place(0, i + 1)) for i in range(line - 1)]
    halo = lax.ppermute(edge, ("frm", "row", "sub"), pairs + [(b, a) for a, b in pairs])
    w_piece, w_msg = call(
        reorder_kernel,
        [vmem(w_own), order, edge],
        [piece, ((rank, NF * cl + 2 * rank), BF16)],
        in_specs=[whole, whole, anywhere],
    )
    w_msgs = [w_msg] + [row_shift(w_msg, shift) for shift in range(1, rows)]
    (spectra,) = call(
        functools.partial(other_spectra_kernel, rows),
        [halo, vmem(table)] + sig + [vmem(half_done)],
        [pltpu.VMEM((NF, blocks, rows, cl, TAPS), BF16)],
        [
            pltpu.VMEM((rows, cl, frames + TAPS), BF16),
            pltpu.VMEM((((rows - 1) * blocks + 1) * cl, 2 * TAPS), BF16),
        ],
        in_specs=[whole] * (rows + 2) + [anywhere],
        limit=8,
        cost=2 * NF * chans * frames * 4 * TAPS,
        aliases={rows + 2: 0},
    )
    spectra = vmem(spectra)

    def products(places, activations, after):
        return call(
            functools.partial(products_kernel, places, rows, subs, cl),
            [activations, spectra] + after,
            [piece] * len(places),
            in_specs=[whole] * 2 + [anywhere] * len(after),
            cost=1 if after else 16 * NF * cl * frames * rank // subs * len(places),
        )

    def gathered(activations, h_gram, msgs):
        got = [sub_shift(m, dc) for m, (_, dc) in zip(msgs, others_of(rows, subs))]
        places = [(dx, 0) for dx in range(1, rows)] + [(0, dc) for dc in range(1, subs)]
        formed = products(places, activations, [])
        for_rows, for_cores = formed[: rows - 1], formed[rows - 1 :]
        from_cores = [sub_shift(m, dc + 1) for dc, m in enumerate(for_cores)]
        *outs, gram = call(
            functools.partial(core_kernel, rows - 1, rank),
            list(for_rows) + [h_gram] + got,
            [msg] * (rows - 1) + [((rank, rank), F32)],
        )
        from_rows = [row_shift(m, dx + 1) for dx, m in enumerate(outs)]
        (own,) = products([(0, 0)], activations, outs)
        (part,) = call(functools.partial(row_kernel, subs), [own, gram] + from_cores + from_rows, [msg])
        return [part] + [frm_shift(part, shift) for shift in range(1, frms)]

    activations, h_gram, *msgs = call(
        functools.partial(first_kernel, rows, subs, cl),
        w_msgs + [vmem(old), spectra],
        update_outs,
        [pltpu.VMEM((rank, frames), F32)],
        limit=8,
    )
    piled = [pltpu.VMEM((frms,) + msg[0], BF16)]
    w_piece, w_msg = call(
        functools.partial(update_kernel, frms),
        [w_piece] + gathered(activations, h_gram, msgs),
        [piece, msg],
        piled,
    )
    w_msgs = [w_msg] + [sub_shift(w_msg, dc) for dc in range(1, subs)]
    w_pieces = pltpu.VMEM((rows, subs, rank, size), BF16)
    (early,) = call(
        functools.partial(early_kernel, rows, subs, cl),
        w_msgs + [spectra],
        [((rank, frames), F32)],
        [w_pieces],
        cost=16 * NF * cl * frames * rank,
    )
    from_rows = [row_shift(w_msg, dx) for dx in range(1, rows)]
    *from_rows, early = lax.optimization_barrier((*from_rows, early))
    for base in from_rows:
        w_msgs += [base] + [sub_shift(base, dc) for dc in range(1, subs)]
    activations, h_gram, *msgs = call(
        functools.partial(later_kernel, rows, subs, cl),
        w_msgs + [early, activations, spectra],
        update_outs,
        [w_pieces, pltpu.VMEM((rank, frames), F32)],
        limit=8,
    )
    parts = gathered(activations, h_gram, msgs)
    activations, parts[0] = lax.optimization_barrier((activations, parts[0]))
    sides = [activations] + [row_shift(activations, shift) for shift in range(1, rows)]
    (part,) = call(
        functools.partial(last_kernel, frms), [w_piece, order] + parts, [((rank, NF * cl), F32)], piled
    )
    (wide,) = call(
        functools.partial(join_kernel, rows),
        sides,
        [pltpu.HBM((rank, window), F32)],
        [pltpu.SemaphoreType.DMA((rows,))],
        in_specs=[anywhere] * rows,
        out_specs=[anywhere],
    )
    (synergies,) = call(
        sum_kernel,
        [part] + [sub_shift(part, dc) for dc in range(1, subs)],
        [pltpu.HBM((rank, NF * cl), F32)],
        [pltpu.VMEM((rank, NF * cl), F32), pltpu.SemaphoreType.DMA],
        out_specs=[anywhere],
    )
    return (synergies.T, wide)


def solution(mesh):
    placed = (P("row", ("grp", "frm", "sub")), P("row", None), P(None, ("grp", "frm", "sub")))
    return jax.shard_map(
        shards,
        mesh=mesh,
        in_specs=placed,
        out_specs=(P(("grp", "row"), None), P(None, ("grp", "frm", "sub"))),
        check_vma=False,
    )
```

```python
import functools
import math

import jax
import jax.numpy as jnp
import ml_dtypes
import numpy as np
from jax import lax
from jax.experimental import pallas as pl
from jax.experimental.pallas import tpu as pltpu
from jax.sharding import PartitionSpec as P

NF = 40
TAPS = 128
HALF = TAPS // 2
GROUP = 8
GROUPS = NF // GROUP
F32 = jnp.float32
BF16 = jnp.bfloat16
HIGH = lax.Precision.HIGHEST
NT = (((1,), (1,)), ((), ()))
MIB = 1024 * 1024


def wavelets():
    f = np.float32
    level = np.arange(NF, dtype=f) / f(NF - 1)
    freq = f(2.0) * np.power(f(12.0), level)
    sigma = f(7.0) / (f(2.0 * math.pi) * freq)
    times = (np.arange(TAPS, dtype=f) - f(HALF)) / f(50.0)
    env = np.exp(-(times[None, :] ** 2) / (f(2.0) * sigma[:, None] ** 2))
    scale = f(1.0) / np.sqrt(np.sum(env * env, axis=1))
    env = env * scale[:, None]
    phase = f(2.0 * math.pi) * freq[:, None] * times[None, :]
    return np.stack([env * np.cos(phase), env * np.sin(phase)]).astype(ml_dtypes.bfloat16)


def toeplitz():
    kernel = wavelets()
    table = np.zeros((NF, 2 * TAPS, 2 * TAPS), ml_dtypes.bfloat16)
    for at in range(TAPS):
        for part in range(2):
            table[:, at : at + TAPS, part * TAPS + at] = kernel[part]
    return table


def split_two(value):
    top = value.astype(BF16)
    return top, (value - top.astype(F32)).astype(BF16)


def joined(message, at, rank):
    return message[:, at : at + rank].astype(F32) + message[:, at + rank : at + 2 * rank].astype(F32)


def pack(out_ref, main, gram):
    rank, size = main.shape
    top, rest = split_two(gram)
    out_ref[:, :size] = main.astype(BF16)
    out_ref[:, size : size + rank] = top
    out_ref[:, size + rank : size + 2 * rank] = rest


def reorder_kernel(w_ref, order_ref, *refs):
    piece_ref, msg_ref = refs[-2:]
    w = w_ref[...]
    rank, size = piece_ref.shape
    gram = lax.dot_general(w, w, NT, precision=HIGH, preferred_element_type=F32)
    moved = jnp.dot(three_terms(w), order_ref[...], preferred_element_type=F32)
    whole = moved[:rank] + (moved[rank : 2 * rank] + moved[2 * rank :])
    for c in range(w.shape[1] // size):

        @pl.when(lax.axis_index("sub") == c)
        def _():
            piece_ref[...] = whole[:, c * size : (c + 1) * size]

    pack(msg_ref, whole, gram)


def three_terms(value):
    top = value.astype(BF16)
    rest = value - top.astype(F32)
    middle = rest.astype(BF16)
    return jnp.concatenate([top, middle, (rest - middle.astype(F32)).astype(BF16)], axis=0)


def edges_kernel(rows, sig_ref, *refs):
    got_refs, out_ref = refs[: rows - 1], refs[-1]
    cl, width = sig_ref.shape
    x_me = lax.axis_index("row")
    for at, ref in enumerate((sig_ref,) + tuple(got_refs)):

        @pl.when(x_me == 0)
        def _():
            out_ref[at * cl : (at + 1) * cl, :] = ref[:, :TAPS]

        @pl.when(x_me > 0)
        def _():
            out_ref[at * cl : (at + 1) * cl, :] = ref[:, width - TAPS :]


def cut_signal_kernel(rows, frames, sig_hbm, *refs):
    out_refs, sems = refs[-rows - 1 : -1], refs[-1]
    window, x_me = sig_hbm.shape[1], lax.axis_index("row")
    width = out_refs[0].shape[1]
    copies = []
    for shift in range(rows):
        target = lax.rem(x_me + shift, rows)
        begin = pl.multiple_of(jnp.clip(target * frames - TAPS, 0, window - width), TAPS)
        copies.append(pltpu.make_async_copy(sig_hbm.at[:, pl.ds(begin, width)], out_refs[shift], sems.at[shift]))
    for copy in copies:
        copy.start()
    for copy in copies:
        copy.wait()


def pair_rows(s_ref, span, pair, x, cl):
    halves = [s_ref[span, blk, x].reshape(-1, TAPS) for blk in (2 * pair, 2 * pair + 1)]
    return jnp.concatenate(halves, axis=1)


def numerators(parts, s_ref, num_ref, cl):
    for pair in range(num_ref.shape[1] // (2 * TAPS)):
        terms = [
            jnp.dot(w, pair_rows(s_ref, slice(None), pair, x, cl), preferred_element_type=F32) for w, x in parts
        ]
        num_ref[:, 2 * TAPS * pair : 2 * TAPS * (pair + 1)] = functools.reduce(jnp.add, terms)


def crossed(low, s_ref, places, subs, cl):
    count = NF // subs
    acc = jnp.zeros((low.shape[0], len(places) * count * cl), F32)
    for pair in range(low.shape[1] // (2 * TAPS)):
        cols = slice(2 * TAPS * pair, 2 * TAPS * (pair + 1))
        parts = [pair_rows(s_ref, pl.ds(core * count, count), pair, x, cl) for x, core in places]
        acc = acc + lax.dot_general(
            low[:, cols], jnp.concatenate(parts, axis=0), NT, preferred_element_type=F32
        )
    return acc


def others_of(rows, subs):
    return [(dx, dc) for dx in range(1, rows) for dc in range(1, subs)]


def new_activations(old, gram, above, s_ref, h_out, h_gram_ref, msg_refs, rows, subs, cl):
    new = old * above / jnp.dot(gram, old, precision=HIGH, preferred_element_type=F32)
    h_out[...] = new
    h_gram = lax.dot_general(new, new, NT, precision=HIGH, preferred_element_type=F32)
    h_gram_ref[...] = h_gram
    size = NF // subs * cl
    x_me, c_me = lax.axis_index("row"), lax.axis_index("sub")
    for ref, (dx, dc) in zip(msg_refs, others_of(rows, subs)):
        target = (lax.rem(x_me + dx, rows), lax.rem(c_me + dc, subs))
        ref[:, :size] = crossed(new.astype(BF16), s_ref, [target], subs, cl)
        ref[:, size:] = h_gram


def products_kernel(places, rows, subs, cl, h_ref, s_ref, *refs):
    x_me, c_me = lax.axis_index("row"), lax.axis_index("sub")
    low = h_ref[...].astype(BF16)
    targets = [(lax.rem(x_me + dx, rows), lax.rem(c_me + dc, subs)) for dx, dc in places]
    acc = crossed(low, s_ref, targets, subs, cl)
    size = acc.shape[1] // len(places)
    for at, ref in enumerate(refs[len(refs) - len(places) :]):
        ref[...] = acc[:, at * size : (at + 1) * size]


def place_signal(source, target, rows, frames):
    x_me = lax.axis_index("row")
    width = source.shape[1]

    @pl.when(x_me == 0)
    def _():
        target[:, HALF:] = source[:, : frames + HALF]

    @pl.when(x_me == rows - 1)
    def _():
        target[:, : frames + HALF] = source[:, width - frames - HALF :]

    if rows > 2:

        @pl.when((x_me > 0) & (x_me < rows - 1))
        def _():
            target[...] = source[:, HALF : HALF + frames + TAPS]


def power_of(x_ref, table):
    co = jnp.dot(x_ref[...], table, preferred_element_type=F32)
    return (co[:, :TAPS] * co[:, :TAPS] + co[:, TAPS:] * co[:, TAPS:]).astype(BF16)


def own_spectra_kernel(rows, sig_ref, w_hbm, h_hbm, order_hbm, tab_hbm, *refs):
    s_ref, w_ref, old_ref, order_ref, tab_ref, xp_scr, x_scr, sems, tab_sems = refs
    _, blocks, _, cl, _ = s_ref.shape
    frames = blocks * TAPS
    x_me = lax.axis_index("row")
    mine = pl.ds(pl.multiple_of(x_me * frames, TAPS), frames)

    def tab_copy(g):
        span = pl.ds(g * GROUP, GROUP)
        return pltpu.make_async_copy(tab_hbm.at[span], tab_ref.at[span], tab_sems.at[g])

    later = [
        pltpu.make_async_copy(w_hbm, w_ref, sems.at[0]),
        pltpu.make_async_copy(order_hbm, order_ref, sems.at[1]),
        pltpu.make_async_copy(h_hbm.at[:, mine], old_ref, sems.at[2]),
    ]
    for g in range(GROUPS):
        tab_copy(g).start()
    for copy in later:
        copy.start()
    place_signal(sig_ref, xp_scr, rows, frames)
    first = jnp.where(x_me == 0, 1, 0)
    for at in range(blocks - 1):
        begin = pl.multiple_of((first + at) * TAPS, TAPS)
        x_scr[at * cl : (at + 1) * cl, :] = xp_scr[:, pl.ds(begin, 2 * TAPS)]

    for f in range(NF):
        if f % GROUP == 0:
            tab_copy(f // GROUP).wait()
        s_ref[f, pl.ds(first, blocks - 1), x_me] = power_of(x_scr, tab_ref[f]).reshape(blocks - 1, cl, TAPS)
    for copy in later:
        copy.wait()


def other_spectra_kernel(rows, halo_ref, tab_ref, *refs):
    sig_refs, (_, s_ref, xp_scr, x_scr) = refs[:rows], refs[rows:]
    _, blocks, _, cl, _ = s_ref.shape
    frames = blocks * TAPS
    x_me = lax.axis_index("row")
    owners = [lax.rem(x_me + rows - shift, rows) for shift in range(rows)]
    for shift in range(rows):
        place_signal(sig_refs[shift], xp_scr.at[owners[shift]], rows, frames)

    @pl.when(x_me == 0)
    def _():
        for at in range(rows):
            xp_scr[rows - 1 - at, :, :HALF] = halo_ref[at * cl : (at + 1) * cl, HALF:]

    @pl.when(x_me == rows - 1)
    def _():
        for at in range(rows):
            xp_scr[(rows - at) % rows, :, frames + HALF :] = halo_ref[at * cl : (at + 1) * cl, :HALF]

    outer = jnp.where(x_me == 0, 0, blocks - 1)
    begin = pl.multiple_of(outer * TAPS, TAPS)
    x_scr[:cl, :] = xp_scr[x_me, :, pl.ds(begin, 2 * TAPS)]
    for shift in range(1, rows):
        for blk in range(blocks):
            at = cl * (1 + (shift - 1) * blocks + blk)
            x_scr[at : at + cl, :] = xp_scr[owners[shift], :, blk * TAPS : (blk + 2) * TAPS]

    for f in range(NF):
        power = power_of(x_scr, tab_ref[f])
        s_ref[f, outer, x_me] = power[:cl]
        for shift in range(1, rows):
            line = cl * (1 + (shift - 1) * blocks)
            s_ref[f, :, owners[shift]] = power[line : line + blocks * cl].reshape(blocks, cl, TAPS)


def first_kernel(rows, subs, cl, *refs):
    refs = list(refs)
    w_refs = [refs.pop(0) for _ in range(rows)]
    h_ref, s_ref, h_out, h_gram_ref = (refs.pop(0) for _ in range(4))
    msg_refs, num_scr = refs[:-1], refs[-1]
    x_me = lax.axis_index("row")
    parts, gram = [], jnp.zeros(h_gram_ref.shape, F32)
    for shift, ref in enumerate(w_refs):
        parts.append((ref[:, : NF * cl], lax.rem(x_me + rows - shift, rows)))
        gram = gram + joined(ref, NF * cl, h_ref.shape[0])
    numerators(parts, s_ref, num_scr, cl)
    new_activations(h_ref[...], gram, num_scr[...], s_ref, h_out, h_gram_ref, msg_refs, rows, subs, cl)


def row_parts(rows, subs, cl, w_refs, w_scr, shifts):
    x_me, c_me = lax.axis_index("row"), lax.axis_index("sub")
    size = NF // subs * cl
    parts = []
    for line, dx in enumerate(shifts):
        for dc in range(subs):
            w_scr[line, lax.rem(c_me + subs - dc, subs)] = w_refs[line * subs + dc][:, :size]
        w = jnp.concatenate([w_scr[line, c] for c in range(subs)], axis=1)
        parts.append((w, lax.rem(x_me + rows - dx, rows)))
    return parts


def early_kernel(rows, subs, cl, *refs):
    w_refs, (s_ref, num_ref, w_scr) = refs[:subs], refs[subs:]
    numerators(row_parts(rows, subs, cl, w_refs, w_scr, [0]), s_ref, num_ref, cl)


def later_kernel(rows, subs, cl, *refs):
    refs = list(refs)
    w_refs = [refs.pop(0) for _ in range(rows * subs)]
    early_ref, h_ref, s_ref, h_out, h_gram_ref = (refs.pop(0) for _ in range(5))
    msg_refs, (w_scr, num_scr) = refs[:-2], refs[-2:]
    gram = jnp.zeros(h_gram_ref.shape, F32)
    for ref in w_refs:
        gram = gram + joined(ref, NF // subs * cl, h_ref.shape[0])
    above = early_ref[...]
    if rows > 1:
        numerators(row_parts(rows, subs, cl, w_refs[subs:], w_scr, list(range(1, rows))), s_ref, num_scr, cl)
        above = above + num_scr[...]
    new_activations(h_ref[...], gram, above, s_ref, h_out, h_gram_ref, msg_refs, rows, subs, cl)


def core_kernel(count, rank, *refs):
    own_refs, gram_ref, got_refs = refs[:count], refs[count], refs[count + 1 : -count - 1]
    out_refs, total_ref = refs[-count - 1 : -1], refs[-1]
    size = own_refs[0].shape[1]
    each = len(got_refs) // count
    gram = gram_ref[...]
    for ref in got_refs[:each]:
        gram = gram + ref[:, size:]
    total_ref[...] = gram
    for at in range(count):
        total = own_refs[at][...]
        for ref in got_refs[at * each : (at + 1) * each]:
            total = total + ref[:, :size]
        pack(out_refs[at], total, gram)


def row_kernel(subs, own_ref, gram_ref, *refs):
    core_refs, msg_refs, out_ref = refs[: subs - 1], refs[subs - 1 : -1], refs[-1]
    rank, size = own_ref.shape
    total, gram = own_ref[...], gram_ref[...]
    for ref in core_refs:
        total = total + ref[...]
    for ref in msg_refs:
        total = total + ref[:, :size].astype(F32)
        gram = gram + joined(ref, size, rank)
    pack(out_ref, total, gram)


def summed(z_me, count, msg_refs, scr, rank, size):
    for shift in range(count):
        scr[partner(z_me, shift, count)] = msg_refs[shift][...]
    total, gram = scr[0, :, :size].astype(F32), joined(scr[0], size, rank)
    for at in range(1, count):
        total = total + scr[at, :, :size].astype(F32)
        gram = gram + joined(scr[at], size, rank)
    return total, gram


def partner(place, shift, count):
    if count & (count - 1):
        return (place + count - shift) % count
    return place ^ shift


def update_kernel(count, w_ref, *refs):
    msg_refs, (new_ref, out_ref, scr) = refs[:count], refs[count:]
    rank, size = new_ref.shape
    total, gram = summed(lax.axis_index("frm"), count, msg_refs, scr, rank, size)
    w = w_ref[...]
    new = w * total / jnp.dot(gram, w, precision=HIGH, preferred_element_type=F32)
    new_ref[...] = new
    pack(out_ref, new, lax.dot_general(new, new, NT, precision=HIGH, preferred_element_type=F32))


def last_kernel(count, w_ref, order_ref, *refs):
    msg_refs, (out_ref, scr) = refs[:count], refs[count:]
    rank, size = w_ref.shape
    total, gram = summed(lax.axis_index("frm"), count, msg_refs, scr, rank, size)
    w = w_ref[...]
    new = w * total / jnp.dot(gram, w, precision=HIGH, preferred_element_type=F32)
    terms = three_terms(new)
    for c in range(order_ref.shape[1] // size):

        @pl.when(lax.axis_index("sub") == c)
        def _():
            moved = lax.dot_general(
                terms, order_ref[:, c * size : (c + 1) * size], NT, preferred_element_type=F32
            )
            out_ref[...] = moved[:rank] + (moved[rank : 2 * rank] + moved[2 * rank :])


def join_kernel(rows, *refs):
    act_refs, (out_ref, sems) = refs[:rows], refs[rows:]
    frames = act_refs[0].shape[1]
    x_me = lax.axis_index("row")
    copies = []
    for shift in range(rows):
        begin = pl.multiple_of(lax.rem(x_me + rows - shift, rows) * frames, TAPS)
        copies.append(pltpu.make_async_copy(act_refs[shift], out_ref.at[:, pl.ds(begin, frames)], sems.at[shift]))
    for copy in copies:
        copy.start()
    for copy in copies:
        copy.wait()


def sum_kernel(_, *refs):
    parts, (out_ref, scr, sem) = refs[:-3], refs[-3:]
    total = parts[0][...]
    for part in parts[1:]:
        total = total + part[...]
    scr[...] = total
    copy = pltpu.make_async_copy(scr, out_ref, sem)
    copy.start()
    copy.wait()


def call(kernel, args, outs, scratch=(), in_specs=None, out_specs=None, limit=4, cost=None, aliases=None):
    whole = pl.BlockSpec(memory_space=pltpu.VMEM)
    if cost is not None:
        cost = pl.CostEstimate(flops=cost, bytes_accessed=0, transcendentals=0)
    return pl.pallas_call(
        kernel,
        out_shape=[jax.ShapeDtypeStruct(*out) if isinstance(out, tuple) else out for out in outs],
        in_specs=in_specs or [whole] * len(args),
        out_specs=out_specs or [whole] * len(outs),
        scratch_shapes=list(scratch),
        compiler_params=pltpu.CompilerParams(vmem_limit_bytes=limit * MIB),
        cost_estimate=cost,
        input_output_aliases=aliases or {},
    )(*args)


def reorder(cl):
    order = np.zeros((cl, NF, NF, cl), ml_dtypes.bfloat16)
    chans, freqs = np.meshgrid(np.arange(cl), np.arange(NF), indexing="ij")
    order[chans, freqs, freqs, chans] = 1
    return order.reshape(cl * NF, NF * cl)


def shards(signal, w_start, h_start):
    rows, subs, frms = (lax.axis_size(axis) for axis in ("row", "sub", "frm"))
    x_me = lax.axis_index("row")
    cl, window = signal.shape
    rank = w_start.shape[1]
    frames = window // rows
    blocks = frames // TAPS
    chans = rows * cl
    size = NF * cl // subs
    line = frms * subs
    width = frames + (TAPS if rows == 2 else 2 * TAPS)
    anywhere = pl.BlockSpec(memory_space=pl.ANY)
    whole = pl.BlockSpec(memory_space=pltpu.VMEM)

    def hbm(value):
        return pltpu.with_memory_space_constraint(value, pltpu.HBM)

    def vmem(value):
        return pltpu.with_memory_space_constraint(value, pltpu.VMEM)

    def row_shift(value, shift):
        return lax.ppermute(value, "row", [(i, (i + shift) % rows) for i in range(rows)])

    def sub_shift(value, shift):
        return lax.ppermute(value, "sub", [(i, (i + shift) % subs) for i in range(subs)])

    def frm_shift(value, shift):
        return lax.ppermute(value, "frm", [(partner(i, shift, frms), i) for i in range(frms)])

    def place(x, at):
        return (at // subs * rows + x) * subs + at % subs

    own_sig, *out_sigs = call(
        functools.partial(cut_signal_kernel, rows, frames),
        [hbm(signal)],
        [((cl, width), BF16)] * rows,
        [pltpu.SemaphoreType.DMA((rows,))],
        in_specs=[anywhere],
    )
    sig = [own_sig] + [row_shift(part, shift + 1) for shift, part in enumerate(out_sigs)]
    msg = ((rank, size + 2 * rank), BF16)
    piece = ((rank, size), F32)
    update_outs = [((rank, frames), F32), ((rank, rank), F32)]
    update_outs += [((rank, size + rank), F32)] * ((rows - 1) * (subs - 1))
    table, order = jnp.asarray(toeplitz()), jnp.asarray(reorder(cl))
    half_done, w_own, old, order, table = call(
        functools.partial(own_spectra_kernel, rows),
        [own_sig, hbm(w_start.T), hbm(h_start), hbm(order), hbm(table)],
        [
            pltpu.VMEM((NF, blocks, rows, cl, TAPS), BF16),
            pltpu.VMEM((rank, NF * cl), F32),
            pltpu.VMEM((rank, frames), F32),
            pltpu.VMEM(order.shape, BF16),
            pltpu.VMEM(table.shape, BF16),
        ],
        [
            pltpu.VMEM((cl, frames + TAPS), BF16),
            pltpu.VMEM(((blocks - 1) * cl, 2 * TAPS), BF16),
            pltpu.SemaphoreType.DMA((3,)),
            pltpu.SemaphoreType.DMA((GROUPS,)),
        ],
        in_specs=[whole] + [anywhere] * 4,
        limit=8,
        cost=2 * NF * cl * frames * 4 * TAPS,
    )
    order = vmem(order)
    (edge,) = call(
        functools.partial(edges_kernel, rows),
        sig + [vmem(half_done)],
        [((chans, TAPS), BF16)],
        in_specs=[whole] * rows + [anywhere],
    )
    pairs = [(place(rows - 1, i), place(0, i + 1)) for i in range(line - 1)]
    halo = lax.ppermute(edge, ("frm", "row", "sub"), pairs + [(b, a) for a, b in pairs])
    w_piece, w_msg = call(
        reorder_kernel,
        [vmem(w_own), order, edge],
        [piece, ((rank, NF * cl + 2 * rank), BF16)],
        in_specs=[whole, whole, anywhere],
    )
    w_msgs = [w_msg] + [row_shift(w_msg, shift) for shift in range(1, rows)]
    (spectra,) = call(
        functools.partial(other_spectra_kernel, rows),
        [halo, vmem(table)] + sig + [vmem(half_done)],
        [pltpu.VMEM((NF, blocks, rows, cl, TAPS), BF16)],
        [
            pltpu.VMEM((rows, cl, frames + TAPS), BF16),
            pltpu.VMEM((((rows - 1) * blocks + 1) * cl, 2 * TAPS), BF16),
        ],
        in_specs=[whole] * (rows + 2) + [anywhere],
        limit=8,
        cost=2 * NF * chans * frames * 4 * TAPS,
        aliases={rows + 2: 0},
    )
    spectra = vmem(spectra)

    def products(places, activations, after):
        return call(
            functools.partial(products_kernel, places, rows, subs, cl),
            [activations, spectra] + after,
            [piece] * len(places),
            in_specs=[whole] * 2 + [anywhere] * len(after),
            cost=1 if after else 16 * NF * cl * frames * rank // subs * len(places),
        )

    def gathered(activations, h_gram, msgs):
        got = [sub_shift(m, dc) for m, (_, dc) in zip(msgs, others_of(rows, subs))]
        places = [(dx, 0) for dx in range(1, rows)] + [(0, dc) for dc in range(1, subs)]
        formed = products(places, activations, [])
        for_rows, for_cores = formed[: rows - 1], formed[rows - 1 :]
        from_cores = [sub_shift(m, dc + 1) for dc, m in enumerate(for_cores)]
        *outs, gram = call(
            functools.partial(core_kernel, rows - 1, rank),
            list(for_rows) + [h_gram] + got,
            [msg] * (rows - 1) + [((rank, rank), F32)],
        )
        from_rows = [row_shift(m, dx + 1) for dx, m in enumerate(outs)]
        (own,) = products([(0, 0)], activations, outs)
        (part,) = call(functools.partial(row_kernel, subs), [own, gram] + from_cores + from_rows, [msg])
        return [part] + [frm_shift(part, shift) for shift in range(1, frms)]

    activations, h_gram, *msgs = call(
        functools.partial(first_kernel, rows, subs, cl),
        w_msgs + [vmem(old), spectra],
        update_outs,
        [pltpu.VMEM((rank, frames), F32)],
        limit=8,
    )
    piled = [pltpu.VMEM((frms,) + msg[0], BF16)]
    w_piece, w_msg = call(
        functools.partial(update_kernel, frms),
        [w_piece] + gathered(activations, h_gram, msgs),
        [piece, msg],
        piled,
    )
    w_msgs = [w_msg] + [sub_shift(w_msg, dc) for dc in range(1, subs)]
    w_pieces = pltpu.VMEM((rows, subs, rank, size), BF16)
    (early,) = call(
        functools.partial(early_kernel, rows, subs, cl),
        w_msgs + [spectra],
        [((rank, frames), F32)],
        [w_pieces],
        cost=16 * NF * cl * frames * rank,
    )
    from_rows = [row_shift(w_msg, dx) for dx in range(1, rows)]
    *from_rows, early = lax.optimization_barrier((*from_rows, early))
    for base in from_rows:
        w_msgs += [base] + [sub_shift(base, dc) for dc in range(1, subs)]
    activations, h_gram, *msgs = call(
        functools.partial(later_kernel, rows, subs, cl),
        w_msgs + [early, activations, spectra],
        update_outs,
        [w_pieces, pltpu.VMEM((rank, frames), F32)],
        limit=8,
    )
    parts = gathered(activations, h_gram, msgs)
    activations, parts[0] = lax.optimization_barrier((activations, parts[0]))
    sides = [activations] + [row_shift(activations, shift) for shift in range(1, rows)]
    (part,) = call(
        functools.partial(last_kernel, frms), [w_piece, order] + parts, [((rank, NF * cl), F32)], piled
    )
    (wide,) = call(
        functools.partial(join_kernel, rows),
        sides,
        [pltpu.HBM((rank, window), F32)],
        [pltpu.SemaphoreType.DMA((rows,))],
        in_specs=[anywhere] * rows,
        out_specs=[anywhere],
    )
    (synergies,) = call(
        sum_kernel,
        [wide, part] + [sub_shift(part, dc) for dc in range(1, subs)],
        [pltpu.HBM((rank, NF * cl), F32)],
        [pltpu.VMEM((rank, NF * cl), F32), pltpu.SemaphoreType.DMA],
        in_specs=[anywhere] + [whole] * subs,
        out_specs=[anywhere],
    )
    return (synergies.T, wide)


def solution(mesh):
    placed = (P("row", ("grp", "frm", "sub")), P("row", None), P(None, ("grp", "frm", "sub")))
    return jax.shard_map(
        shards,
        mesh=mesh,
        in_specs=placed,
        out_specs=(P(("grp", "row"), None), P(None, ("grp", "frm", "sub"))),
        check_vma=False,
    )
```

```python
import functools
import math

import jax
import jax.numpy as jnp
import ml_dtypes
import numpy as np
from jax import lax
from jax.experimental import pallas as pl
from jax.experimental.pallas import tpu as pltpu
from jax.sharding import PartitionSpec as P

NF = 40
TAPS = 128
HALF = TAPS // 2
LANES = 128
CUTS = (0, 2, 8, 16, 24, 32, NF)
F32 = jnp.float32
BF16 = jnp.bfloat16
HIGH = lax.Precision.HIGHEST
NT = (((1,), (1,)), ((), ()))
MIB = 1024 * 1024


def wavelets():
    f = np.float32
    level = np.arange(NF, dtype=f) / f(NF - 1)
    freq = f(2.0) * np.power(f(12.0), level)
    sigma = f(7.0) / (f(2.0 * math.pi) * freq)
    times = (np.arange(TAPS, dtype=f) - f(HALF)) / f(50.0)
    env = np.exp(-(times[None, :] ** 2) / (f(2.0) * sigma[:, None] ** 2))
    scale = f(1.0) / np.sqrt(np.sum(env * env, axis=1))
    env = env * scale[:, None]
    phase = f(2.0 * math.pi) * freq[:, None] * times[None, :]
    return np.stack([env * np.cos(phase), env * np.sin(phase)]).astype(ml_dtypes.bfloat16)


def toeplitz():
    kernel = wavelets()
    table = np.zeros((NF, 2 * TAPS, 2 * TAPS), ml_dtypes.bfloat16)
    for at in range(TAPS):
        for part in range(2):
            table[:, at : at + TAPS, part * TAPS + at] = kernel[part]
    return table


def split_two(value):
    top = value.astype(BF16)
    return top, (value - top.astype(F32)).astype(BF16)


def message(rank, size):
    return (rank * -(-size // LANES) + rank // 2, LANES)


def pack(out_ref, main, gram):
    rank, size = main.shape
    half = rank // 2
    for at in range(0, size, LANES):
        line = at // LANES * rank
        width = min(LANES, size - at)
        out_ref[line : line + rank, :width] = main[:, at : at + width].astype(BF16)
    top, rest = split_two(gram)
    terms = [top[:half], top[half:], rest[:half], rest[half:]]
    line = out_ref.shape[0] - half
    for at, term in enumerate(terms):
        out_ref[line:, at * rank : (at + 1) * rank] = term


def body(value, rank, size):
    parts = []
    for at in range(0, size, LANES):
        line = at // LANES * rank
        parts.append(value[line : line + rank, : min(LANES, size - at)])
    return jnp.concatenate(parts, axis=1)


def gram_of(value, rank):
    last = value[value.shape[0] - rank // 2 :, :].astype(F32)
    total = last[:, : 2 * rank] + last[:, 2 * rank : 4 * rank]
    return jnp.concatenate([total[:, :rank], total[:, rank:]], axis=0)


def reorder_kernel(w_ref, order_ref, *refs):
    piece_ref, msg_ref = refs[-2:]
    w = w_ref[...]
    rank, size = piece_ref.shape
    gram = lax.dot_general(w, w, NT, precision=HIGH, preferred_element_type=F32)
    moved = jnp.dot(three_terms(w), order_ref[...], preferred_element_type=F32)
    whole = moved[:rank] + (moved[rank : 2 * rank] + moved[2 * rank :])
    for c in range(w.shape[1] // size):

        @pl.when(lax.axis_index("sub") == c)
        def _():
            piece_ref[...] = whole[:, c * size : (c + 1) * size]

    pack(msg_ref, whole, gram)


def three_terms(value):
    top = value.astype(BF16)
    rest = value - top.astype(F32)
    middle = rest.astype(BF16)
    return jnp.concatenate([top, middle, (rest - middle.astype(F32)).astype(BF16)], axis=0)


def edges_kernel(rows, sig_ref, *refs):
    got_refs, out_ref = refs[: rows - 1], refs[-1]
    cl, width = sig_ref.shape
    x_me = lax.axis_index("row")
    for at, ref in enumerate((sig_ref,) + tuple(got_refs)):

        @pl.when(x_me == 0)
        def _():
            out_ref[at * cl : (at + 1) * cl, :] = ref[:, :TAPS]

        @pl.when(x_me > 0)
        def _():
            out_ref[at * cl : (at + 1) * cl, :] = ref[:, width - TAPS :]


def cut_signal_kernel(rows, frames, sig_hbm, *refs):
    out_refs, sems = refs[-rows - 1 : -1], refs[-1]
    window, x_me = sig_hbm.shape[1], lax.axis_index("row")
    width = out_refs[0].shape[1]
    copies = []
    for shift in range(rows):
        target = lax.rem(x_me + shift, rows)
        begin = pl.multiple_of(jnp.clip(target * frames - TAPS, 0, window - width), TAPS)
        copies.append(pltpu.make_async_copy(sig_hbm.at[:, pl.ds(begin, width)], out_refs[shift], sems.at[shift]))
    for copy in copies:
        copy.start()
    for copy in copies:
        copy.wait()


def pair_rows(s_ref, span, pair, x, cl):
    halves = [s_ref[span, blk, x].reshape(-1, TAPS) for blk in (2 * pair, 2 * pair + 1)]
    return jnp.concatenate(halves, axis=1)


def numerators(parts, s_ref, num_ref, cl):
    for pair in range(num_ref.shape[1] // (2 * TAPS)):
        terms = [
            jnp.dot(w, pair_rows(s_ref, slice(None), pair, x, cl), preferred_element_type=F32) for w, x in parts
        ]
        num_ref[:, 2 * TAPS * pair : 2 * TAPS * (pair + 1)] = functools.reduce(jnp.add, terms)


def crossed(low, s_ref, places, subs, cl):
    count = NF // subs
    acc = jnp.zeros((low.shape[0], len(places) * count * cl), F32)
    for pair in range(low.shape[1] // (2 * TAPS)):
        cols = slice(2 * TAPS * pair, 2 * TAPS * (pair + 1))
        parts = [pair_rows(s_ref, pl.ds(core * count, count), pair, x, cl) for x, core in places]
        acc = acc + lax.dot_general(
            low[:, cols], jnp.concatenate(parts, axis=0), NT, preferred_element_type=F32
        )
    return acc


def others_of(rows, subs):
    return [(dx, dc) for dx in range(1, rows) for dc in range(1, subs)]


def new_activations(old, gram, above, s_ref, h_out, h_gram_ref, msg_refs, rows, subs, cl):
    new = old * above / jnp.dot(gram, old, precision=HIGH, preferred_element_type=F32)
    h_out[...] = new
    h_gram = lax.dot_general(new, new, NT, precision=HIGH, preferred_element_type=F32)
    h_gram_ref[...] = h_gram
    size = NF // subs * cl
    x_me, c_me = lax.axis_index("row"), lax.axis_index("sub")
    for ref, (dx, dc) in zip(msg_refs, others_of(rows, subs)):
        target = (lax.rem(x_me + dx, rows), lax.rem(c_me + dc, subs))
        ref[:, :size] = crossed(new.astype(BF16), s_ref, [target], subs, cl)
        ref[:, size:] = h_gram


def products_kernel(places, rows, subs, cl, h_ref, s_ref, *refs):
    x_me, c_me = lax.axis_index("row"), lax.axis_index("sub")
    low = h_ref[...].astype(BF16)
    targets = [(lax.rem(x_me + dx, rows), lax.rem(c_me + dc, subs)) for dx, dc in places]
    acc = crossed(low, s_ref, targets, subs, cl)
    size = acc.shape[1] // len(places)
    for at, ref in enumerate(refs[len(refs) - len(places) :]):
        ref[...] = acc[:, at * size : (at + 1) * size]


def place_signal(source, target, rows, frames):
    x_me = lax.axis_index("row")
    width = source.shape[1]

    @pl.when(x_me == 0)
    def _():
        target[:, HALF:] = source[:, : frames + HALF]

    @pl.when(x_me == rows - 1)
    def _():
        target[:, : frames + HALF] = source[:, width - frames - HALF :]

    if rows > 2:

        @pl.when((x_me > 0) & (x_me < rows - 1))
        def _():
            target[...] = source[:, HALF : HALF + frames + TAPS]


def power_of(x_ref, table):
    co = jnp.dot(x_ref[...], table, preferred_element_type=F32)
    return (co[:, :TAPS] * co[:, :TAPS] + co[:, TAPS:] * co[:, TAPS:]).astype(BF16)


def own_spectra_kernel(rows, sig_ref, w_hbm, h_hbm, order_hbm, tab_hbm, *refs):
    s_ref, w_ref, old_ref, order_ref, tab_ref, xp_scr, x_scr, sems, tab_sems = refs
    _, blocks, _, cl, _ = s_ref.shape
    frames = blocks * TAPS
    x_me = lax.axis_index("row")
    mine = pl.ds(pl.multiple_of(x_me * frames, TAPS), frames)

    table = [
        pltpu.make_async_copy(tab_hbm.at[begin:end], tab_ref.at[begin:end], tab_sems.at[at])
        for at, (begin, end) in enumerate(zip(CUTS, CUTS[1:]))
    ]
    later = [
        pltpu.make_async_copy(w_hbm, w_ref, sems.at[0]),
        pltpu.make_async_copy(order_hbm, order_ref, sems.at[1]),
        pltpu.make_async_copy(h_hbm.at[:, mine], old_ref, sems.at[2]),
    ]
    for copy in table:
        copy.start()
    place_signal(sig_ref, xp_scr, rows, frames)
    first = jnp.where(x_me == 0, 1, 0)
    for at in range(blocks - 1):
        begin = pl.multiple_of((first + at) * TAPS, TAPS)
        x_scr[at * cl : (at + 1) * cl, :] = xp_scr[:, pl.ds(begin, 2 * TAPS)]

    for f in range(NF):
        if f in CUTS:
            table[CUTS.index(f)].wait()
        if f == CUTS[3]:
            for copy in later:
                copy.start()
        s_ref[f, pl.ds(first, blocks - 1), x_me] = power_of(x_scr, tab_ref[f]).reshape(blocks - 1, cl, TAPS)
    for copy in later:
        copy.wait()


def other_spectra_kernel(rows, halo_ref, tab_ref, *refs):
    sig_refs, (_, s_ref, xp_scr, x_scr) = refs[:rows], refs[rows:]
    _, blocks, _, cl, _ = s_ref.shape
    frames = blocks * TAPS
    x_me = lax.axis_index("row")
    owners = [lax.rem(x_me + rows - shift, rows) for shift in range(rows)]
    for shift in range(rows):
        place_signal(sig_refs[shift], xp_scr.at[owners[shift]], rows, frames)

    @pl.when(x_me == 0)
    def _():
        for at in range(rows):
            xp_scr[rows - 1 - at, :, :HALF] = halo_ref[at * cl : (at + 1) * cl, HALF:]

    @pl.when(x_me == rows - 1)
    def _():
        for at in range(rows):
            xp_scr[(rows - at) % rows, :, frames + HALF :] = halo_ref[at * cl : (at + 1) * cl, :HALF]

    outer = jnp.where(x_me == 0, 0, blocks - 1)
    begin = pl.multiple_of(outer * TAPS, TAPS)
    x_scr[:cl, :] = xp_scr[x_me, :, pl.ds(begin, 2 * TAPS)]
    for shift in range(1, rows):
        for blk in range(blocks):
            at = cl * (1 + (shift - 1) * blocks + blk)
            x_scr[at : at + cl, :] = xp_scr[owners[shift], :, blk * TAPS : (blk + 2) * TAPS]

    for f in range(NF):
        power = power_of(x_scr, tab_ref[f])
        s_ref[f, outer, x_me] = power[:cl]
        for shift in range(1, rows):
            line = cl * (1 + (shift - 1) * blocks)
            s_ref[f, :, owners[shift]] = power[line : line + blocks * cl].reshape(blocks, cl, TAPS)


def first_kernel(rows, subs, cl, *refs):
    refs = list(refs)
    w_refs = [refs.pop(0) for _ in range(rows)]
    h_ref, s_ref, h_out, h_gram_ref = (refs.pop(0) for _ in range(4))
    msg_refs, num_scr = refs[:-1], refs[-1]
    x_me = lax.axis_index("row")
    parts, gram = [], jnp.zeros(h_gram_ref.shape, F32)
    for shift, ref in enumerate(w_refs):
        parts.append((body(ref[...], h_ref.shape[0], NF * cl), lax.rem(x_me + rows - shift, rows)))
        gram = gram + gram_of(ref[...], h_ref.shape[0])
    numerators(parts, s_ref, num_scr, cl)
    new_activations(h_ref[...], gram, num_scr[...], s_ref, h_out, h_gram_ref, msg_refs, rows, subs, cl)


def row_parts(rows, subs, cl, w_refs, w_scr, shifts):
    x_me, c_me = lax.axis_index("row"), lax.axis_index("sub")
    size = NF // subs * cl
    parts = []
    for line, dx in enumerate(shifts):
        for dc in range(subs):
            piece = body(w_refs[line * subs + dc][...], w_scr.shape[2], size)
            w_scr[line, lax.rem(c_me + subs - dc, subs)] = piece
        w = jnp.concatenate([w_scr[line, c] for c in range(subs)], axis=1)
        parts.append((w, lax.rem(x_me + rows - dx, rows)))
    return parts


def early_kernel(rows, subs, cl, *refs):
    w_refs, (s_ref, num_ref, w_scr) = refs[:subs], refs[subs:]
    numerators(row_parts(rows, subs, cl, w_refs, w_scr, [0]), s_ref, num_ref, cl)


def later_kernel(rows, subs, cl, *refs):
    refs = list(refs)
    w_refs = [refs.pop(0) for _ in range(rows * subs)]
    early_ref, h_ref, s_ref, h_out, h_gram_ref = (refs.pop(0) for _ in range(5))
    msg_refs, (w_scr, num_scr) = refs[:-2], refs[-2:]
    gram = jnp.zeros(h_gram_ref.shape, F32)
    for ref in w_refs:
        gram = gram + gram_of(ref[...], h_ref.shape[0])
    above = early_ref[...]
    if rows > 1:
        numerators(row_parts(rows, subs, cl, w_refs[subs:], w_scr, list(range(1, rows))), s_ref, num_scr, cl)
        above = above + num_scr[...]
    new_activations(h_ref[...], gram, above, s_ref, h_out, h_gram_ref, msg_refs, rows, subs, cl)


def core_kernel(count, rank, *refs):
    own_refs, gram_ref, got_refs = refs[:count], refs[count], refs[count + 1 : -count - 1]
    out_refs, total_ref = refs[-count - 1 : -1], refs[-1]
    size = own_refs[0].shape[1]
    each = len(got_refs) // count
    gram = gram_ref[...]
    for ref in got_refs[:each]:
        gram = gram + ref[:, size:]
    total_ref[...] = gram
    for at in range(count):
        total = own_refs[at][...]
        for ref in got_refs[at * each : (at + 1) * each]:
            total = total + ref[:, :size]
        pack(out_refs[at], total, gram)


def row_kernel(subs, own_ref, gram_ref, *refs):
    core_refs, msg_refs, out_ref = refs[: subs - 1], refs[subs - 1 : -1], refs[-1]
    rank, size = own_ref.shape
    total, gram = own_ref[...], gram_ref[...]
    for ref in core_refs:
        total = total + ref[...]
    for ref in msg_refs:
        total = total + body(ref[...], rank, size).astype(F32)
        gram = gram + gram_of(ref[...], rank)
    pack(out_ref, total, gram)


def summed(z_me, count, msg_refs, scr, rank, size):
    for shift in range(count):
        scr[partner(z_me, shift, count)] = msg_refs[shift][...]
    total, gram = body(scr[0], rank, size).astype(F32), gram_of(scr[0], rank)
    for at in range(1, count):
        total = total + body(scr[at], rank, size).astype(F32)
        gram = gram + gram_of(scr[at], rank)
    return total, gram


def partner(place, shift, count):
    if count & (count - 1):
        return (place + count - shift) % count
    return place ^ shift


def update_kernel(count, w_ref, *refs):
    msg_refs, (new_ref, out_ref, scr) = refs[:count], refs[count:]
    rank, size = new_ref.shape
    total, gram = summed(lax.axis_index("frm"), count, msg_refs, scr, rank, size)
    w = w_ref[...]
    new = w * total / jnp.dot(gram, w, precision=HIGH, preferred_element_type=F32)
    new_ref[...] = new
    pack(out_ref, new, lax.dot_general(new, new, NT, precision=HIGH, preferred_element_type=F32))


def last_kernel(count, w_ref, order_ref, *refs):
    msg_refs, (out_ref, scr) = refs[:count], refs[count:]
    rank, size = w_ref.shape
    total, gram = summed(lax.axis_index("frm"), count, msg_refs, scr, rank, size)
    w = w_ref[...]
    new = w * total / jnp.dot(gram, w, precision=HIGH, preferred_element_type=F32)
    terms = three_terms(new)
    for c in range(order_ref.shape[1] // size):

        @pl.when(lax.axis_index("sub") == c)
        def _():
            moved = lax.dot_general(
                terms, order_ref[:, c * size : (c + 1) * size], NT, preferred_element_type=F32
            )
            out_ref[...] = moved[:rank] + (moved[rank : 2 * rank] + moved[2 * rank :])


def join_kernel(rows, *refs):
    act_refs, (out_ref, sems) = refs[:rows], refs[rows:]
    frames = act_refs[0].shape[1]
    x_me = lax.axis_index("row")
    copies = []
    for shift in range(rows):
        begin = pl.multiple_of(lax.rem(x_me + rows - shift, rows) * frames, TAPS)
        copies.append(pltpu.make_async_copy(act_refs[shift], out_ref.at[:, pl.ds(begin, frames)], sems.at[shift]))
    for copy in copies:
        copy.start()
    for copy in copies:
        copy.wait()


def sum_kernel(_, *refs):
    parts, (out_ref, scr, sem) = refs[:-3], refs[-3:]
    total = parts[0][...]
    for part in parts[1:]:
        total = total + part[...]
    scr[...] = total
    copy = pltpu.make_async_copy(scr, out_ref, sem)
    copy.start()
    copy.wait()


def call(kernel, args, outs, scratch=(), in_specs=None, out_specs=None, limit=4, cost=None, aliases=None):
    whole = pl.BlockSpec(memory_space=pltpu.VMEM)
    if cost is not None:
        cost = pl.CostEstimate(flops=cost, bytes_accessed=0, transcendentals=0)
    return pl.pallas_call(
        kernel,
        out_shape=[jax.ShapeDtypeStruct(*out) if isinstance(out, tuple) else out for out in outs],
        in_specs=in_specs or [whole] * len(args),
        out_specs=out_specs or [whole] * len(outs),
        scratch_shapes=list(scratch),
        compiler_params=pltpu.CompilerParams(vmem_limit_bytes=limit * MIB),
        cost_estimate=cost,
        input_output_aliases=aliases or {},
    )(*args)


def reorder(cl):
    order = np.zeros((cl, NF, NF, cl), ml_dtypes.bfloat16)
    chans, freqs = np.meshgrid(np.arange(cl), np.arange(NF), indexing="ij")
    order[chans, freqs, freqs, chans] = 1
    return order.reshape(cl * NF, NF * cl)


def shards(signal, w_start, h_start):
    rows, subs, frms = (lax.axis_size(axis) for axis in ("row", "sub", "frm"))
    x_me = lax.axis_index("row")
    cl, window = signal.shape
    rank = w_start.shape[1]
    frames = window // rows
    blocks = frames // TAPS
    chans = rows * cl
    size = NF * cl // subs
    line = frms * subs
    width = frames + (TAPS if rows == 2 else 2 * TAPS)
    anywhere = pl.BlockSpec(memory_space=pl.ANY)
    whole = pl.BlockSpec(memory_space=pltpu.VMEM)

    def hbm(value):
        return pltpu.with_memory_space_constraint(value, pltpu.HBM)

    def vmem(value):
        return pltpu.with_memory_space_constraint(value, pltpu.VMEM)

    def row_shift(value, shift):
        return lax.ppermute(value, "row", [(i, (i + shift) % rows) for i in range(rows)])

    def sub_shift(value, shift):
        return lax.ppermute(value, "sub", [(i, (i + shift) % subs) for i in range(subs)])

    def frm_shift(value, shift):
        return lax.ppermute(value, "frm", [(partner(i, shift, frms), i) for i in range(frms)])

    def place(x, at):
        return (at // subs * rows + x) * subs + at % subs

    own_sig, *out_sigs = call(
        functools.partial(cut_signal_kernel, rows, frames),
        [hbm(signal)],
        [((cl, width), BF16)] * rows,
        [pltpu.SemaphoreType.DMA((rows,))],
        in_specs=[anywhere],
    )
    sig = [own_sig] + [row_shift(part, shift + 1) for shift, part in enumerate(out_sigs)]
    msg = (message(rank, size), BF16)
    piece = ((rank, size), F32)
    update_outs = [((rank, frames), F32), ((rank, rank), F32)]
    update_outs += [((rank, size + rank), F32)] * ((rows - 1) * (subs - 1))
    table, order = jnp.asarray(toeplitz()), jnp.asarray(reorder(cl))
    half_done, w_own, old, order, table = call(
        functools.partial(own_spectra_kernel, rows),
        [own_sig, hbm(w_start.T), hbm(h_start), hbm(order), hbm(table)],
        [
            pltpu.VMEM((NF, blocks, rows, cl, TAPS), BF16),
            pltpu.VMEM((rank, NF * cl), F32),
            pltpu.VMEM((rank, frames), F32),
            pltpu.VMEM(order.shape, BF16),
            pltpu.VMEM(table.shape, BF16),
        ],
        [
            pltpu.VMEM((cl, frames + TAPS), BF16),
            pltpu.VMEM(((blocks - 1) * cl, 2 * TAPS), BF16),
            pltpu.SemaphoreType.DMA((3,)),
            pltpu.SemaphoreType.DMA((len(CUTS) - 1,)),
        ],
        in_specs=[whole] + [anywhere] * 4,
        limit=8,
        cost=2 * NF * cl * frames * 4 * TAPS,
    )
    order = vmem(order)
    (edge,) = call(
        functools.partial(edges_kernel, rows),
        sig + [vmem(half_done)],
        [((chans, TAPS), BF16)],
        in_specs=[whole] * rows + [anywhere],
    )
    pairs = [(place(rows - 1, i), place(0, i + 1)) for i in range(line - 1)]
    halo = lax.ppermute(edge, ("frm", "row", "sub"), pairs + [(b, a) for a, b in pairs])
    w_piece, w_msg = call(
        reorder_kernel,
        [vmem(w_own), order, edge],
        [piece, (message(rank, NF * cl), BF16)],
        in_specs=[whole, whole, anywhere],
    )
    w_msgs = [w_msg] + [row_shift(w_msg, shift) for shift in range(1, rows)]
    (spectra,) = call(
        functools.partial(other_spectra_kernel, rows),
        [halo, vmem(table)] + sig + [vmem(half_done)],
        [pltpu.VMEM((NF, blocks, rows, cl, TAPS), BF16)],
        [
            pltpu.VMEM((rows, cl, frames + TAPS), BF16),
            pltpu.VMEM((((rows - 1) * blocks + 1) * cl, 2 * TAPS), BF16),
        ],
        in_specs=[whole] * (rows + 2) + [anywhere],
        limit=8,
        cost=2 * NF * chans * frames * 4 * TAPS,
        aliases={rows + 2: 0},
    )
    spectra = vmem(spectra)

    def products(places, activations, after):
        return call(
            functools.partial(products_kernel, places, rows, subs, cl),
            [activations, spectra] + after,
            [piece] * len(places),
            in_specs=[whole] * 2 + [anywhere] * len(after),
            cost=1 if after else 16 * NF * cl * frames * rank // subs * len(places),
        )

    def gathered(activations, h_gram, msgs):
        got = [sub_shift(m, dc) for m, (_, dc) in zip(msgs, others_of(rows, subs))]
        places = [(dx, 0) for dx in range(1, rows)] + [(0, dc) for dc in range(1, subs)]
        formed = products(places, activations, [])
        for_rows, for_cores = formed[: rows - 1], formed[rows - 1 :]
        from_cores = [sub_shift(m, dc + 1) for dc, m in enumerate(for_cores)]
        *outs, gram = call(
            functools.partial(core_kernel, rows - 1, rank),
            list(for_rows) + [h_gram] + got,
            [msg] * (rows - 1) + [((rank, rank), F32)],
        )
        from_rows = [row_shift(m, dx + 1) for dx, m in enumerate(outs)]
        (own,) = products([(0, 0)], activations, outs)
        (part,) = call(functools.partial(row_kernel, subs), [own, gram] + from_cores + from_rows, [msg])
        return [part] + [frm_shift(part, shift) for shift in range(1, frms)]

    activations, h_gram, *msgs = call(
        functools.partial(first_kernel, rows, subs, cl),
        w_msgs + [vmem(old), spectra],
        update_outs,
        [pltpu.VMEM((rank, frames), F32)],
        limit=8,
    )
    piled = [pltpu.VMEM((frms,) + msg[0], BF16)]
    w_piece, w_msg = call(
        functools.partial(update_kernel, frms),
        [w_piece] + gathered(activations, h_gram, msgs),
        [piece, msg],
        piled,
    )
    w_msgs = [w_msg] + [sub_shift(w_msg, dc) for dc in range(1, subs)]
    w_pieces = pltpu.VMEM((rows, subs, rank, size), BF16)
    (early,) = call(
        functools.partial(early_kernel, rows, subs, cl),
        w_msgs + [spectra],
        [((rank, frames), F32)],
        [w_pieces],
        cost=16 * NF * cl * frames * rank,
    )
    from_rows = [row_shift(w_msg, dx) for dx in range(1, rows)]
    *from_rows, early = lax.optimization_barrier((*from_rows, early))
    for base in from_rows:
        w_msgs += [base] + [sub_shift(base, dc) for dc in range(1, subs)]
    activations, h_gram, *msgs = call(
        functools.partial(later_kernel, rows, subs, cl),
        w_msgs + [early, activations, spectra],
        update_outs,
        [w_pieces, pltpu.VMEM((rank, frames), F32)],
        limit=8,
    )
    parts = gathered(activations, h_gram, msgs)
    activations, parts[0] = lax.optimization_barrier((activations, parts[0]))
    sides = [activations] + [row_shift(activations, shift) for shift in range(1, rows)]
    (part,) = call(
        functools.partial(last_kernel, frms), [w_piece, order] + parts, [((rank, NF * cl), F32)], piled
    )
    (wide,) = call(
        functools.partial(join_kernel, rows),
        sides,
        [pltpu.HBM((rank, window), F32)],
        [pltpu.SemaphoreType.DMA((rows,))],
        in_specs=[anywhere] * rows,
        out_specs=[anywhere],
    )
    (synergies,) = call(
        sum_kernel,
        [hbm(wide), part] + [sub_shift(part, dc) for dc in range(1, subs)],
        [pltpu.HBM((rank, NF * cl), F32)],
        [pltpu.VMEM((rank, NF * cl), F32), pltpu.SemaphoreType.DMA],
        in_specs=[anywhere] + [whole] * subs,
        out_specs=[anywhere],
    )
    return (synergies.T, wide)


def solution(mesh):
    placed = (P("row", ("grp", "frm", "sub")), P("row", None), P(None, ("grp", "frm", "sub")))
    return jax.shard_map(
        shards,
        mesh=mesh,
        in_specs=placed,
        out_specs=(P(("grp", "row"), None), P(None, ("grp", "frm", "sub"))),
        check_vma=False,
    )
```

```python
import functools
import math

import jax
import jax.numpy as jnp
import ml_dtypes
import numpy as np
from jax import lax
from jax.experimental import pallas as pl
from jax.experimental.pallas import tpu as pltpu
from jax.sharding import PartitionSpec as P

NF = 40
TAPS = 128
HALF = TAPS // 2
LANES = 128
CUTS = (8, 16, 24, 32, NF)
AHEAD = CUTS[0]
F32 = jnp.float32
BF16 = jnp.bfloat16
HIGH = lax.Precision.HIGHEST
NT = (((1,), (1,)), ((), ()))
MIB = 1024 * 1024


def wavelets():
    f = np.float32
    level = np.arange(NF, dtype=f) / f(NF - 1)
    freq = f(2.0) * np.power(f(12.0), level)
    sigma = f(7.0) / (f(2.0 * math.pi) * freq)
    times = (np.arange(TAPS, dtype=f) - f(HALF)) / f(50.0)
    env = np.exp(-(times[None, :] ** 2) / (f(2.0) * sigma[:, None] ** 2))
    scale = f(1.0) / np.sqrt(np.sum(env * env, axis=1))
    env = env * scale[:, None]
    phase = f(2.0 * math.pi) * freq[:, None] * times[None, :]
    return np.stack([env * np.cos(phase), env * np.sin(phase)]).astype(ml_dtypes.bfloat16)


def toeplitz():
    kernel = wavelets()
    table = np.zeros((NF, 2 * TAPS, 2 * TAPS), ml_dtypes.bfloat16)
    for at in range(TAPS):
        for part in range(2):
            table[:, at : at + TAPS, part * TAPS + at] = kernel[part]
    return table


def split_two(value):
    top = value.astype(BF16)
    return top, (value - top.astype(F32)).astype(BF16)


def message(rank, size):
    return (rank * -(-size // LANES) + rank // 2, LANES)


def pack(out_ref, main, gram):
    rank, size = main.shape
    half = rank // 2
    for at in range(0, size, LANES):
        line = at // LANES * rank
        width = min(LANES, size - at)
        out_ref[line : line + rank, :width] = main[:, at : at + width].astype(BF16)
    top, rest = split_two(gram)
    terms = [top[:half], top[half:], rest[:half], rest[half:]]
    line = out_ref.shape[0] - half
    for at, term in enumerate(terms):
        out_ref[line:, at * rank : (at + 1) * rank] = term


def body(value, rank, size):
    parts = []
    for at in range(0, size, LANES):
        line = at // LANES * rank
        parts.append(value[line : line + rank, : min(LANES, size - at)])
    return jnp.concatenate(parts, axis=1)


def gram_of(value, rank):
    last = value[value.shape[0] - rank // 2 :, :].astype(F32)
    total = last[:, : 2 * rank] + last[:, 2 * rank : 4 * rank]
    return jnp.concatenate([total[:, :rank], total[:, rank:]], axis=0)


def reorder_kernel(w_ref, order_ref, *refs):
    piece_ref, msg_ref = refs[-2:]
    w = w_ref[...]
    rank, size = piece_ref.shape
    gram = lax.dot_general(w, w, NT, precision=HIGH, preferred_element_type=F32)
    moved = jnp.dot(three_terms(w), order_ref[...], preferred_element_type=F32)
    whole = moved[:rank] + (moved[rank : 2 * rank] + moved[2 * rank :])
    for c in range(w.shape[1] // size):

        @pl.when(lax.axis_index("sub") == c)
        def _():
            piece_ref[...] = whole[:, c * size : (c + 1) * size]

    pack(msg_ref, whole, gram)


def three_terms(value):
    top = value.astype(BF16)
    rest = value - top.astype(F32)
    middle = rest.astype(BF16)
    return jnp.concatenate([top, middle, (rest - middle.astype(F32)).astype(BF16)], axis=0)


def edges_kernel(rows, sig_ref, *refs):
    got_refs, out_ref = refs[: rows - 1], refs[-1]
    cl, width = sig_ref.shape
    x_me = lax.axis_index("row")
    for at, ref in enumerate((sig_ref,) + tuple(got_refs)):

        @pl.when(x_me == 0)
        def _():
            out_ref[at * cl : (at + 1) * cl, :] = ref[:, :TAPS]

        @pl.when(x_me > 0)
        def _():
            out_ref[at * cl : (at + 1) * cl, :] = ref[:, width - TAPS :]


def cut_kernel(rows, frames, sig_hbm, tab_hbm, *refs):
    out_refs, (tab_ref, sems) = refs[:rows], refs[rows:]
    window, x_me = sig_hbm.shape[1], lax.axis_index("row")
    width = out_refs[0].shape[1]
    copies = []
    for shift in reversed(range(rows)):
        target = lax.rem(x_me + shift, rows)
        begin = pl.multiple_of(jnp.clip(target * frames - TAPS, 0, window - width), TAPS)
        copies.append(pltpu.make_async_copy(sig_hbm.at[:, pl.ds(begin, width)], out_refs[shift], sems.at[shift]))
    copies.append(pltpu.make_async_copy(tab_hbm.at[:AHEAD], tab_ref, sems.at[rows]))
    for copy in copies:
        copy.start()
    for copy in copies:
        copy.wait()


def pair_rows(s_ref, span, pair, x, cl):
    halves = [s_ref[span, blk, x].reshape(-1, TAPS) for blk in (2 * pair, 2 * pair + 1)]
    return jnp.concatenate(halves, axis=1)


def numerators(parts, s_ref, num_ref, cl):
    for pair in range(num_ref.shape[1] // (2 * TAPS)):
        terms = [
            jnp.dot(w, pair_rows(s_ref, slice(None), pair, x, cl), preferred_element_type=F32) for w, x in parts
        ]
        num_ref[:, 2 * TAPS * pair : 2 * TAPS * (pair + 1)] = functools.reduce(jnp.add, terms)


def crossed(low, s_ref, places, subs, cl):
    count = NF // subs
    acc = jnp.zeros((low.shape[0], len(places) * count * cl), F32)
    for pair in range(low.shape[1] // (2 * TAPS)):
        cols = slice(2 * TAPS * pair, 2 * TAPS * (pair + 1))
        parts = [pair_rows(s_ref, pl.ds(core * count, count), pair, x, cl) for x, core in places]
        acc = acc + lax.dot_general(
            low[:, cols], jnp.concatenate(parts, axis=0), NT, preferred_element_type=F32
        )
    return acc


def others_of(rows, subs):
    return [(dx, dc) for dx in range(1, rows) for dc in range(1, subs)]


def new_activations(old, gram, above, s_ref, h_out, h_gram_ref, msg_refs, rows, subs, cl):
    new = old * above / jnp.dot(gram, old, precision=HIGH, preferred_element_type=F32)
    h_out[...] = new
    h_gram = lax.dot_general(new, new, NT, precision=HIGH, preferred_element_type=F32)
    h_gram_ref[...] = h_gram
    size = NF // subs * cl
    x_me, c_me = lax.axis_index("row"), lax.axis_index("sub")
    for ref, (dx, dc) in zip(msg_refs, others_of(rows, subs)):
        target = (lax.rem(x_me + dx, rows), lax.rem(c_me + dc, subs))
        ref[:, :size] = crossed(new.astype(BF16), s_ref, [target], subs, cl)
        ref[:, size:] = h_gram


def products_kernel(places, rows, subs, cl, h_ref, s_ref, *refs):
    x_me, c_me = lax.axis_index("row"), lax.axis_index("sub")
    low = h_ref[...].astype(BF16)
    targets = [(lax.rem(x_me + dx, rows), lax.rem(c_me + dc, subs)) for dx, dc in places]
    acc = crossed(low, s_ref, targets, subs, cl)
    size = acc.shape[1] // len(places)
    for at, ref in enumerate(refs[len(refs) - len(places) :]):
        ref[...] = acc[:, at * size : (at + 1) * size]


def place_signal(source, target, rows, frames):
    x_me = lax.axis_index("row")
    width = source.shape[1]

    @pl.when(x_me == 0)
    def _():
        target[:, HALF:] = source[:, : frames + HALF]

    @pl.when(x_me == rows - 1)
    def _():
        target[:, : frames + HALF] = source[:, width - frames - HALF :]

    if rows > 2:

        @pl.when((x_me > 0) & (x_me < rows - 1))
        def _():
            target[...] = source[:, HALF : HALF + frames + TAPS]


def power_of(x_ref, table):
    co = jnp.dot(x_ref[...], table, preferred_element_type=F32)
    return (co[:, :TAPS] * co[:, :TAPS] + co[:, TAPS:] * co[:, TAPS:]).astype(BF16)


def table_at(f, ahead_ref, tab_ref):
    return ahead_ref[f] if f < AHEAD else tab_ref[f - AHEAD]


def own_spectra_kernel(rows, sig_ref, ahead_ref, w_hbm, h_hbm, order_hbm, tab_hbm, *refs):
    s_ref, w_ref, old_ref, order_ref, tab_ref, xp_scr, x_scr, sems, tab_sems = refs
    _, blocks, _, cl, _ = s_ref.shape
    frames = blocks * TAPS
    x_me = lax.axis_index("row")
    mine = pl.ds(pl.multiple_of(x_me * frames, TAPS), frames)

    table = [
        pltpu.make_async_copy(tab_hbm.at[begin:end], tab_ref.at[begin - AHEAD : end - AHEAD], tab_sems.at[at])
        for at, (begin, end) in enumerate(zip(CUTS, CUTS[1:]))
    ]
    later = [
        pltpu.make_async_copy(w_hbm, w_ref, sems.at[0]),
        pltpu.make_async_copy(order_hbm, order_ref, sems.at[1]),
        pltpu.make_async_copy(h_hbm.at[:, mine], old_ref, sems.at[2]),
    ]
    for copy in table:
        copy.start()
    place_signal(sig_ref, xp_scr, rows, frames)
    first = jnp.where(x_me == 0, 1, 0)
    for at in range(blocks - 1):
        begin = pl.multiple_of((first + at) * TAPS, TAPS)
        x_scr[at * cl : (at + 1) * cl, :] = xp_scr[:, pl.ds(begin, 2 * TAPS)]

    for f in range(NF):
        if f in CUTS:
            table[CUTS.index(f)].wait()
        if f == CUTS[1]:
            for copy in later:
                copy.start()
        power = power_of(x_scr, table_at(f, ahead_ref, tab_ref))
        s_ref[f, pl.ds(first, blocks - 1), x_me] = power.reshape(blocks - 1, cl, TAPS)
    for copy in later:
        copy.wait()


def other_spectra_kernel(rows, halo_ref, ahead_ref, tab_ref, *refs):
    sig_refs, (s_ref, xp_scr, x_scr) = refs[:rows], refs[-3:]
    _, blocks, _, cl, _ = s_ref.shape
    frames = blocks * TAPS
    x_me = lax.axis_index("row")
    owners = [lax.rem(x_me + rows - shift, rows) for shift in range(rows)]
    for shift in range(rows):
        place_signal(sig_refs[shift], xp_scr.at[owners[shift]], rows, frames)

    @pl.when(x_me == 0)
    def _():
        for at in range(rows):
            xp_scr[rows - 1 - at, :, :HALF] = halo_ref[at * cl : (at + 1) * cl, HALF:]

    @pl.when(x_me == rows - 1)
    def _():
        for at in range(rows):
            xp_scr[(rows - at) % rows, :, frames + HALF :] = halo_ref[at * cl : (at + 1) * cl, :HALF]

    outer = jnp.where(x_me == 0, 0, blocks - 1)
    begin = pl.multiple_of(outer * TAPS, TAPS)
    x_scr[:cl, :] = xp_scr[x_me, :, pl.ds(begin, 2 * TAPS)]
    for shift in range(1, rows):
        for blk in range(blocks):
            at = cl * (1 + (shift - 1) * blocks + blk)
            x_scr[at : at + cl, :] = xp_scr[owners[shift], :, blk * TAPS : (blk + 2) * TAPS]

    for f in range(NF):
        power = power_of(x_scr, table_at(f, ahead_ref, tab_ref))
        s_ref[f, outer, x_me] = power[:cl]
        for shift in range(1, rows):
            line = cl * (1 + (shift - 1) * blocks)
            s_ref[f, :, owners[shift]] = power[line : line + blocks * cl].reshape(blocks, cl, TAPS)


def outer_pair(pairs):
    return jnp.where(lax.axis_index("row") == 0, 0, pairs - 1)


def pair_columns(pair):
    return pl.ds(pl.multiple_of(pair * 2 * TAPS, 2 * TAPS), 2 * TAPS)


def first_early_kernel(cl, w_ref, s_ref, num_ref):
    rank, frames = num_ref.shape
    pairs = frames // (2 * TAPS)
    x_me = lax.axis_index("row")
    w = body(w_ref[...], rank, NF * cl)
    num_ref[:, pair_columns(outer_pair(pairs))] = jnp.zeros((rank, 2 * TAPS), F32)
    for at in range(pairs - 1):
        pair = at + jnp.where(x_me == 0, 1, 0)
        rows_of = pair_rows(s_ref, slice(None), pair, x_me, cl)
        num_ref[:, pair_columns(pair)] = jnp.dot(w, rows_of, preferred_element_type=F32)


def first_kernel(rows, subs, cl, *refs):
    refs = list(refs)
    w_refs = [refs.pop(0) for _ in range(rows)]
    early_ref, h_ref, s_ref, h_out, h_gram_ref = (refs.pop(0) for _ in range(5))
    msg_refs, num_scr = refs[:-1], refs[-1]
    rank, frames = h_ref.shape
    x_me = lax.axis_index("row")
    parts, gram = [], jnp.zeros(h_gram_ref.shape, F32)
    for shift, ref in enumerate(w_refs):
        parts.append((body(ref[...], rank, NF * cl), lax.rem(x_me + rows - shift, rows)))
        gram = gram + gram_of(ref[...], rank)
    if rows > 1:
        numerators(parts[1:], s_ref, num_scr, cl)
    else:
        num_scr[...] = jnp.zeros_like(num_scr)
    outer = outer_pair(frames // (2 * TAPS))
    num_scr[:, pair_columns(outer)] += jnp.dot(
        parts[0][0], pair_rows(s_ref, slice(None), outer, x_me, cl), preferred_element_type=F32
    )
    above = early_ref[...] + num_scr[...]
    new_activations(h_ref[...], gram, above, s_ref, h_out, h_gram_ref, msg_refs, rows, subs, cl)


def row_parts(rows, subs, cl, w_refs, w_scr, shifts):
    x_me, c_me = lax.axis_index("row"), lax.axis_index("sub")
    size = NF // subs * cl
    parts = []
    for line, dx in enumerate(shifts):
        for dc in range(subs):
            piece = body(w_refs[line * subs + dc][...], w_scr.shape[2], size)
            w_scr[line, lax.rem(c_me + subs - dc, subs)] = piece
        w = jnp.concatenate([w_scr[line, c] for c in range(subs)], axis=1)
        parts.append((w, lax.rem(x_me + rows - dx, rows)))
    return parts


def early_kernel(rows, subs, cl, *refs):
    w_refs, (s_ref, num_ref, w_scr) = refs[:subs], refs[subs:]
    numerators(row_parts(rows, subs, cl, w_refs, w_scr, [0]), s_ref, num_ref, cl)


def later_kernel(rows, subs, cl, *refs):
    refs = list(refs)
    w_refs = [refs.pop(0) for _ in range(rows * subs)]
    early_ref, h_ref, s_ref, h_out, h_gram_ref = (refs.pop(0) for _ in range(5))
    msg_refs, (w_scr, num_scr) = refs[:-2], refs[-2:]
    gram = jnp.zeros(h_gram_ref.shape, F32)
    for ref in w_refs:
        gram = gram + gram_of(ref[...], h_ref.shape[0])
    above = early_ref[...]
    if rows > 1:
        numerators(row_parts(rows, subs, cl, w_refs[subs:], w_scr, list(range(1, rows))), s_ref, num_scr, cl)
        above = above + num_scr[...]
    new_activations(h_ref[...], gram, above, s_ref, h_out, h_gram_ref, msg_refs, rows, subs, cl)


def core_kernel(count, rank, *refs):
    own_refs, gram_ref, got_refs = refs[:count], refs[count], refs[count + 1 : -count - 1]
    out_refs, total_ref = refs[-count - 1 : -1], refs[-1]
    size = own_refs[0].shape[1]
    each = len(got_refs) // count
    gram = gram_ref[...]
    for ref in got_refs[:each]:
        gram = gram + ref[:, size:]
    total_ref[...] = gram
    for at in range(count):
        total = own_refs[at][...]
        for ref in got_refs[at * each : (at + 1) * each]:
            total = total + ref[:, :size]
        pack(out_refs[at], total, gram)


def row_kernel(subs, own_ref, gram_ref, *refs):
    core_refs, msg_refs, out_ref = refs[: subs - 1], refs[subs - 1 : -1], refs[-1]
    rank, size = own_ref.shape
    total, gram = own_ref[...], gram_ref[...]
    for ref in core_refs:
        total = total + ref[...]
    for ref in msg_refs:
        total = total + body(ref[...], rank, size).astype(F32)
        gram = gram + gram_of(ref[...], rank)
    pack(out_ref, total, gram)


def summed(z_me, count, msg_refs, scr, rank, size):
    for shift in range(count):
        scr[partner(z_me, shift, count)] = msg_refs[shift][...]
    total, gram = body(scr[0], rank, size).astype(F32), gram_of(scr[0], rank)
    for at in range(1, count):
        total = total + body(scr[at], rank, size).astype(F32)
        gram = gram + gram_of(scr[at], rank)
    return total, gram


def partner(place, shift, count):
    if count & (count - 1):
        return (place + count - shift) % count
    return place ^ shift


def update_kernel(count, w_ref, *refs):
    msg_refs, (new_ref, out_ref, scr) = refs[:count], refs[count:]
    rank, size = new_ref.shape
    total, gram = summed(lax.axis_index("frm"), count, msg_refs, scr, rank, size)
    w = w_ref[...]
    new = w * total / jnp.dot(gram, w, precision=HIGH, preferred_element_type=F32)
    new_ref[...] = new
    pack(out_ref, new, lax.dot_general(new, new, NT, precision=HIGH, preferred_element_type=F32))


def last_kernel(count, w_ref, order_ref, *refs):
    msg_refs, (out_ref, scr) = refs[:count], refs[count:]
    rank, size = w_ref.shape
    total, gram = summed(lax.axis_index("frm"), count, msg_refs, scr, rank, size)
    w = w_ref[...]
    new = w * total / jnp.dot(gram, w, precision=HIGH, preferred_element_type=F32)
    terms = three_terms(new)
    for c in range(order_ref.shape[1] // size):

        @pl.when(lax.axis_index("sub") == c)
        def _():
            moved = lax.dot_general(
                terms, order_ref[:, c * size : (c + 1) * size], NT, preferred_element_type=F32
            )
            out_ref[...] = moved[:rank] + (moved[rank : 2 * rank] + moved[2 * rank :])


def join_kernel(rows, *refs):
    act_refs, (out_ref, sems) = refs[:rows], refs[rows:]
    frames = act_refs[0].shape[1]
    x_me = lax.axis_index("row")
    copies = []
    for shift in range(rows):
        begin = pl.multiple_of(lax.rem(x_me + rows - shift, rows) * frames, TAPS)
        copies.append(pltpu.make_async_copy(act_refs[shift], out_ref.at[:, pl.ds(begin, frames)], sems.at[shift]))
    for copy in copies:
        copy.start()
    for copy in copies:
        copy.wait()


def sum_kernel(_, *refs):
    parts, (out_ref, scr, sem) = refs[:-3], refs[-3:]
    total = parts[0][...]
    for part in parts[1:]:
        total = total + part[...]
    scr[...] = total
    copy = pltpu.make_async_copy(scr, out_ref, sem)
    copy.start()
    copy.wait()


def call(kernel, args, outs, scratch=(), in_specs=None, out_specs=None, limit=4, cost=None, aliases=None):
    whole = pl.BlockSpec(memory_space=pltpu.VMEM)
    if cost is not None:
        cost = pl.CostEstimate(flops=cost, bytes_accessed=0, transcendentals=0)
    return pl.pallas_call(
        kernel,
        out_shape=[jax.ShapeDtypeStruct(*out) if isinstance(out, tuple) else out for out in outs],
        in_specs=in_specs or [whole] * len(args),
        out_specs=out_specs or [whole] * len(outs),
        scratch_shapes=list(scratch),
        compiler_params=pltpu.CompilerParams(vmem_limit_bytes=limit * MIB),
        cost_estimate=cost,
        input_output_aliases=aliases or {},
    )(*args)


def reorder(cl):
    order = np.zeros((cl, NF, NF, cl), ml_dtypes.bfloat16)
    chans, freqs = np.meshgrid(np.arange(cl), np.arange(NF), indexing="ij")
    order[chans, freqs, freqs, chans] = 1
    return order.reshape(cl * NF, NF * cl)


def shards(signal, w_start, h_start):
    rows, subs, frms = (lax.axis_size(axis) for axis in ("row", "sub", "frm"))
    x_me = lax.axis_index("row")
    cl, window = signal.shape
    rank = w_start.shape[1]
    frames = window // rows
    blocks = frames // TAPS
    chans = rows * cl
    size = NF * cl // subs
    line = frms * subs
    width = frames + (TAPS if rows == 2 else 2 * TAPS)
    anywhere = pl.BlockSpec(memory_space=pl.ANY)
    whole = pl.BlockSpec(memory_space=pltpu.VMEM)

    def hbm(value):
        return pltpu.with_memory_space_constraint(value, pltpu.HBM)

    def vmem(value):
        return pltpu.with_memory_space_constraint(value, pltpu.VMEM)

    def row_shift(value, shift):
        return lax.ppermute(value, "row", [(i, (i + shift) % rows) for i in range(rows)])

    def sub_shift(value, shift):
        return lax.ppermute(value, "sub", [(i, (i + shift) % subs) for i in range(subs)])

    def frm_shift(value, shift):
        return lax.ppermute(value, "frm", [(partner(i, shift, frms), i) for i in range(frms)])

    def place(x, at):
        return (at // subs * rows + x) * subs + at % subs

    table, order = hbm(jnp.asarray(toeplitz())), jnp.asarray(reorder(cl))
    *cuts, ahead = call(
        functools.partial(cut_kernel, rows, frames),
        [hbm(signal), table],
        [((cl, width), BF16)] * rows + [pltpu.VMEM((AHEAD,) + table.shape[1:], BF16)],
        [pltpu.SemaphoreType.DMA((rows + 1,))],
        in_specs=[anywhere] * 2,
    )
    own_sig, *out_sigs = cuts
    ahead = vmem(ahead)
    sig = [own_sig] + [row_shift(part, shift + 1) for shift, part in enumerate(out_sigs)]
    msg = (message(rank, size), BF16)
    piece = ((rank, size), F32)
    update_outs = [((rank, frames), F32), ((rank, rank), F32)]
    update_outs += [((rank, size + rank), F32)] * ((rows - 1) * (subs - 1))
    half_done, w_own, old, order, table = call(
        functools.partial(own_spectra_kernel, rows),
        [own_sig, ahead, hbm(w_start.T), hbm(h_start), hbm(order), table],
        [
            pltpu.VMEM((NF, blocks, rows, cl, TAPS), BF16),
            pltpu.VMEM((rank, NF * cl), F32),
            pltpu.VMEM((rank, frames), F32),
            pltpu.VMEM(order.shape, BF16),
            pltpu.VMEM((NF - AHEAD,) + table.shape[1:], BF16),
        ],
        [
            pltpu.VMEM((cl, frames + TAPS), BF16),
            pltpu.VMEM(((blocks - 1) * cl, 2 * TAPS), BF16),
            pltpu.SemaphoreType.DMA((3,)),
            pltpu.SemaphoreType.DMA((len(CUTS) - 1,)),
        ],
        in_specs=[whole] * 2 + [anywhere] * 4,
        limit=8,
        cost=2 * NF * cl * frames * 4 * TAPS,
    )
    order = vmem(order)
    (edge,) = call(
        functools.partial(edges_kernel, rows),
        sig + [vmem(half_done)],
        [((chans, TAPS), BF16)],
        in_specs=[whole] * rows + [anywhere],
    )
    pairs = [(place(rows - 1, i), place(0, i + 1)) for i in range(line - 1)]
    halo = lax.ppermute(edge, ("frm", "row", "sub"), pairs + [(b, a) for a, b in pairs])
    w_piece, w_msg = call(
        reorder_kernel,
        [vmem(w_own), order, edge],
        [piece, (message(rank, NF * cl), BF16)],
        in_specs=[whole, whole, anywhere],
    )
    w_msgs = [w_msg] + [row_shift(w_msg, shift) for shift in range(1, rows)]
    (early,) = call(
        functools.partial(first_early_kernel, cl),
        [w_msg, vmem(half_done)],
        [((rank, frames), F32)],
        cost=16 * NF * cl * frames * rank,
    )
    (spectra,) = call(
        functools.partial(other_spectra_kernel, rows),
        [halo, ahead, vmem(table)] + sig + [vmem(half_done), early],
        [pltpu.VMEM((NF, blocks, rows, cl, TAPS), BF16)],
        [
            pltpu.VMEM((rows, cl, frames + TAPS), BF16),
            pltpu.VMEM((((rows - 1) * blocks + 1) * cl, 2 * TAPS), BF16),
        ],
        in_specs=[whole] * (rows + 3) + [anywhere] * 2,
        limit=8,
        cost=2 * NF * chans * frames * 4 * TAPS,
        aliases={rows + 3: 0},
    )
    spectra = vmem(spectra)

    def products(places, activations, after):
        return call(
            functools.partial(products_kernel, places, rows, subs, cl),
            [activations, spectra] + after,
            [piece] * len(places),
            in_specs=[whole] * 2 + [anywhere] * len(after),
            cost=1 if after else 16 * NF * cl * frames * rank // subs * len(places),
        )

    def gathered(activations, h_gram, msgs):
        got = [sub_shift(m, dc) for m, (_, dc) in zip(msgs, others_of(rows, subs))]
        places = [(dx, 0) for dx in range(1, rows)] + [(0, dc) for dc in range(1, subs)]
        formed = products(places, activations, [])
        for_rows, for_cores = formed[: rows - 1], formed[rows - 1 :]
        from_cores = [sub_shift(m, dc + 1) for dc, m in enumerate(for_cores)]
        *outs, gram = call(
            functools.partial(core_kernel, rows - 1, rank),
            list(for_rows) + [h_gram] + got,
            [msg] * (rows - 1) + [((rank, rank), F32)],
        )
        from_rows = [row_shift(m, dx + 1) for dx, m in enumerate(outs)]
        (own,) = products([(0, 0)], activations, outs)
        (part,) = call(functools.partial(row_kernel, subs), [own, gram] + from_cores + from_rows, [msg])
        return [part] + [frm_shift(part, shift) for shift in range(1, frms)]

    activations, h_gram, *msgs = call(
        functools.partial(first_kernel, rows, subs, cl),
        w_msgs + [early, vmem(old), spectra],
        update_outs,
        [pltpu.VMEM((rank, frames), F32)],
        limit=8,
    )
    piled = [pltpu.VMEM((frms,) + msg[0], BF16)]
    w_piece, w_msg = call(
        functools.partial(update_kernel, frms),
        [w_piece] + gathered(activations, h_gram, msgs),
        [piece, msg],
        piled,
    )
    w_msgs = [w_msg] + [sub_shift(w_msg, dc) for dc in range(1, subs)]
    w_pieces = pltpu.VMEM((rows, subs, rank, size), BF16)
    (early,) = call(
        functools.partial(early_kernel, rows, subs, cl),
        w_msgs + [spectra],
        [((rank, frames), F32)],
        [w_pieces],
        cost=16 * NF * cl * frames * rank,
    )
    from_rows = [row_shift(w_msg, dx) for dx in range(1, rows)]
    *from_rows, early = lax.optimization_barrier((*from_rows, early))
    for base in from_rows:
        w_msgs += [base] + [sub_shift(base, dc) for dc in range(1, subs)]
    activations, h_gram, *msgs = call(
        functools.partial(later_kernel, rows, subs, cl),
        w_msgs + [early, activations, spectra],
        update_outs,
        [w_pieces, pltpu.VMEM((rank, frames), F32)],
        limit=8,
    )
    parts = gathered(activations, h_gram, msgs)
    activations, parts[0] = lax.optimization_barrier((activations, parts[0]))
    sides = [activations] + [row_shift(activations, shift) for shift in range(1, rows)]
    (part,) = call(
        functools.partial(last_kernel, frms), [w_piece, order] + parts, [((rank, NF * cl), F32)], piled
    )
    (wide,) = call(
        functools.partial(join_kernel, rows),
        sides,
        [pltpu.HBM((rank, window), F32)],
        [pltpu.SemaphoreType.DMA((rows,))],
        in_specs=[anywhere] * rows,
        out_specs=[anywhere],
    )
    (synergies,) = call(
        sum_kernel,
        [hbm(wide), part] + [sub_shift(part, dc) for dc in range(1, subs)],
        [pltpu.HBM((rank, NF * cl), F32)],
        [pltpu.VMEM((rank, NF * cl), F32), pltpu.SemaphoreType.DMA],
        in_specs=[anywhere] + [whole] * subs,
        out_specs=[anywhere],
    )
    return (synergies.T, wide)


def solution(mesh):
    placed = (P("row", ("grp", "frm", "sub")), P("row", None), P(None, ("grp", "frm", "sub")))
    return jax.shard_map(
        shards,
        mesh=mesh,
        in_specs=placed,
        out_specs=(P(("grp", "row"), None), P(None, ("grp", "frm", "sub"))),
        check_vma=False,
    )
```

```python
import functools
import math

import jax
import jax.numpy as jnp
import ml_dtypes
import numpy as np
from jax import lax
from jax.experimental import pallas as pl
from jax.experimental.pallas import tpu as pltpu
from jax.sharding import PartitionSpec as P

NF = 40
TAPS = 128
HALF = TAPS // 2
LANES = 128
CUTS = (8, 16, 24, 32, NF)
AHEAD = CUTS[0]
F32 = jnp.float32
BF16 = jnp.bfloat16
HIGH = lax.Precision.HIGHEST
NT = (((1,), (1,)), ((), ()))
MIB = 1024 * 1024


def wavelets():
    f = np.float32
    level = np.arange(NF, dtype=f) / f(NF - 1)
    freq = f(2.0) * np.power(f(12.0), level)
    sigma = f(7.0) / (f(2.0 * math.pi) * freq)
    times = (np.arange(TAPS, dtype=f) - f(HALF)) / f(50.0)
    env = np.exp(-(times[None, :] ** 2) / (f(2.0) * sigma[:, None] ** 2))
    scale = f(1.0) / np.sqrt(np.sum(env * env, axis=1))
    env = env * scale[:, None]
    phase = f(2.0 * math.pi) * freq[:, None] * times[None, :]
    return np.stack([env * np.cos(phase), env * np.sin(phase)]).astype(ml_dtypes.bfloat16)


def toeplitz():
    kernel = wavelets()
    table = np.zeros((NF, 2 * TAPS, 2 * TAPS), ml_dtypes.bfloat16)
    for at in range(TAPS):
        for part in range(2):
            table[:, at : at + TAPS, part * TAPS + at] = kernel[part]
    return table


def split_two(value):
    top = value.astype(BF16)
    return top, (value - top.astype(F32)).astype(BF16)


def message(rank, size):
    return (rank * -(-size // LANES) + rank // 2, LANES)


def pack(out_ref, main, gram):
    rank, size = main.shape
    half = rank // 2
    for at in range(0, size, LANES):
        line = at // LANES * rank
        width = min(LANES, size - at)
        out_ref[line : line + rank, :width] = main[:, at : at + width].astype(BF16)
    top, rest = split_two(gram)
    terms = [top[:half], top[half:], rest[:half], rest[half:]]
    line = out_ref.shape[0] - half
    for at, term in enumerate(terms):
        out_ref[line:, at * rank : (at + 1) * rank] = term


def body(value, rank, size):
    parts = []
    for at in range(0, size, LANES):
        line = at // LANES * rank
        parts.append(value[line : line + rank, : min(LANES, size - at)])
    return jnp.concatenate(parts, axis=1)


def gram_of(value, rank):
    last = value[value.shape[0] - rank // 2 :, :].astype(F32)
    total = last[:, : 2 * rank] + last[:, 2 * rank : 4 * rank]
    return jnp.concatenate([total[:, :rank], total[:, rank:]], axis=0)


def reorder_kernel(w_ref, order_ref, *refs):
    piece_ref, msg_ref = refs[-2:]
    w = w_ref[...]
    rank, size = piece_ref.shape
    gram = lax.dot_general(w, w, NT, precision=HIGH, preferred_element_type=F32)
    moved = jnp.dot(three_terms(w), order_ref[...], preferred_element_type=F32)
    whole = moved[:rank] + (moved[rank : 2 * rank] + moved[2 * rank :])
    for c in range(w.shape[1] // size):

        @pl.when(lax.axis_index("sub") == c)
        def _():
            piece_ref[...] = whole[:, c * size : (c + 1) * size]

    pack(msg_ref, whole, gram)


def three_terms(value):
    top = value.astype(BF16)
    rest = value - top.astype(F32)
    middle = rest.astype(BF16)
    return jnp.concatenate([top, middle, (rest - middle.astype(F32)).astype(BF16)], axis=0)


def edges_kernel(rows, sig_ref, *refs):
    got_refs, out_ref = refs[: rows - 1], refs[-1]
    cl, width = sig_ref.shape
    x_me = lax.axis_index("row")
    for at, ref in enumerate((sig_ref,) + tuple(got_refs)):

        @pl.when(x_me == 0)
        def _():
            out_ref[at * cl : (at + 1) * cl, :] = ref[:, :TAPS]

        @pl.when(x_me > 0)
        def _():
            out_ref[at * cl : (at + 1) * cl, :] = ref[:, width - TAPS :]


def cut_kernel(rows, frames, sig_hbm, tab_hbm, *refs):
    out_refs, (tab_ref, sems) = refs[:rows], refs[rows:]
    window, x_me = sig_hbm.shape[1], lax.axis_index("row")
    width = out_refs[0].shape[1]
    copies = []
    for shift in reversed(range(rows)):
        target = lax.rem(x_me + shift, rows)
        begin = pl.multiple_of(jnp.clip(target * frames - TAPS, 0, window - width), TAPS)
        copies.append(pltpu.make_async_copy(sig_hbm.at[:, pl.ds(begin, width)], out_refs[shift], sems.at[shift]))
    copies.append(pltpu.make_async_copy(tab_hbm.at[:AHEAD], tab_ref, sems.at[rows]))
    for copy in copies:
        copy.start()
    for copy in copies:
        copy.wait()


def pair_rows(s_ref, span, pair, x, cl):
    halves = [s_ref[span, blk, x].reshape(-1, TAPS) for blk in (2 * pair, 2 * pair + 1)]
    return jnp.concatenate(halves, axis=1)


def numerators(parts, s_ref, num_ref, cl):
    for pair in range(num_ref.shape[1] // (2 * TAPS)):
        terms = [
            jnp.dot(w, pair_rows(s_ref, slice(None), pair, x, cl), preferred_element_type=F32) for w, x in parts
        ]
        num_ref[:, 2 * TAPS * pair : 2 * TAPS * (pair + 1)] = functools.reduce(jnp.add, terms)


def crossed(low, s_ref, places, subs, cl):
    count = NF // subs
    acc = jnp.zeros((low.shape[0], len(places) * count * cl), F32)
    for pair in range(low.shape[1] // (2 * TAPS)):
        cols = slice(2 * TAPS * pair, 2 * TAPS * (pair + 1))
        parts = [pair_rows(s_ref, pl.ds(core * count, count), pair, x, cl) for x, core in places]
        acc = acc + lax.dot_general(
            low[:, cols], jnp.concatenate(parts, axis=0), NT, preferred_element_type=F32
        )
    return acc


def others_of(rows, subs):
    return [(dx, dc) for dx in range(1, rows) for dc in range(1, subs)]


def new_activations(old, gram, above, s_ref, h_out, h_gram_ref, msg_refs, rows, subs, cl):
    new = old * above / jnp.dot(gram, old, precision=HIGH, preferred_element_type=F32)
    h_out[...] = new
    h_gram = lax.dot_general(new, new, NT, precision=HIGH, preferred_element_type=F32)
    h_gram_ref[...] = h_gram
    size = NF // subs * cl
    x_me, c_me = lax.axis_index("row"), lax.axis_index("sub")
    for ref, (dx, dc) in zip(msg_refs, others_of(rows, subs)):
        target = (lax.rem(x_me + dx, rows), lax.rem(c_me + dc, subs))
        ref[:, :size] = crossed(new.astype(BF16), s_ref, [target], subs, cl)
        ref[:, size:] = h_gram


def products_kernel(places, rows, subs, cl, h_ref, s_ref, *refs):
    x_me, c_me = lax.axis_index("row"), lax.axis_index("sub")
    low = h_ref[...].astype(BF16)
    targets = [(lax.rem(x_me + dx, rows), lax.rem(c_me + dc, subs)) for dx, dc in places]
    acc = crossed(low, s_ref, targets, subs, cl)
    size = acc.shape[1] // len(places)
    for at, ref in enumerate(refs[len(refs) - len(places) :]):
        ref[...] = acc[:, at * size : (at + 1) * size]


def place_signal(source, target, rows, frames):
    x_me = lax.axis_index("row")
    width = source.shape[1]

    @pl.when(x_me == 0)
    def _():
        target[:, HALF:] = source[:, : frames + HALF]

    @pl.when(x_me == rows - 1)
    def _():
        target[:, : frames + HALF] = source[:, width - frames - HALF :]

    if rows > 2:

        @pl.when((x_me > 0) & (x_me < rows - 1))
        def _():
            target[...] = source[:, HALF : HALF + frames + TAPS]


def power_of(x_ref, table):
    co = jnp.dot(x_ref[...], table, preferred_element_type=F32)
    return (co[:, :TAPS] * co[:, :TAPS] + co[:, TAPS:] * co[:, TAPS:]).astype(BF16)


def table_at(f, ahead_ref, tab_ref):
    return ahead_ref[f] if f < AHEAD else tab_ref[f - AHEAD]


def own_spectra_kernel(rows, sig_ref, ahead_ref, w_hbm, h_hbm, order_hbm, tab_hbm, *refs):
    s_ref, w_ref, old_ref, order_ref, tab_ref, xp_scr, x_scr, sems, tab_sems = refs
    _, blocks, _, cl, _ = s_ref.shape
    frames = blocks * TAPS
    x_me = lax.axis_index("row")
    mine = pl.ds(pl.multiple_of(x_me * frames, TAPS), frames)

    table = [
        pltpu.make_async_copy(tab_hbm.at[begin:end], tab_ref.at[begin - AHEAD : end - AHEAD], tab_sems.at[at])
        for at, (begin, end) in enumerate(zip(CUTS, CUTS[1:]))
    ]
    later = [
        pltpu.make_async_copy(w_hbm, w_ref, sems.at[0]),
        pltpu.make_async_copy(order_hbm, order_ref, sems.at[1]),
        pltpu.make_async_copy(h_hbm.at[:, mine], old_ref, sems.at[2]),
    ]
    for copy in table:
        copy.start()
    place_signal(sig_ref, xp_scr, rows, frames)
    first = jnp.where(x_me == 0, 1, 0)
    for at in range(blocks - 1):
        begin = pl.multiple_of((first + at) * TAPS, TAPS)
        x_scr[at * cl : (at + 1) * cl, :] = xp_scr[:, pl.ds(begin, 2 * TAPS)]

    for f in range(NF):
        if f in CUTS:
            table[CUTS.index(f)].wait()
        if f == CUTS[1]:
            for copy in later:
                copy.start()
        power = power_of(x_scr, table_at(f, ahead_ref, tab_ref))
        s_ref[f, pl.ds(first, blocks - 1), x_me] = power.reshape(blocks - 1, cl, TAPS)
    for copy in later:
        copy.wait()


def other_spectra_kernel(rows, halo_ref, ahead_ref, tab_ref, *refs):
    sig_refs, (s_ref, xp_scr, x_scr) = refs[:rows], refs[-3:]
    _, blocks, _, cl, _ = s_ref.shape
    frames = blocks * TAPS
    x_me = lax.axis_index("row")
    owners = [lax.rem(x_me + rows - shift, rows) for shift in range(rows)]
    for shift in range(rows):
        place_signal(sig_refs[shift], xp_scr.at[owners[shift]], rows, frames)

    @pl.when(x_me == 0)
    def _():
        for at in range(rows):
            xp_scr[rows - 1 - at, :, :HALF] = halo_ref[at * cl : (at + 1) * cl, HALF:]

    @pl.when(x_me == rows - 1)
    def _():
        for at in range(rows):
            xp_scr[(rows - at) % rows, :, frames + HALF :] = halo_ref[at * cl : (at + 1) * cl, :HALF]

    outer = jnp.where(x_me == 0, 0, blocks - 1)
    begin = pl.multiple_of(outer * TAPS, TAPS)
    x_scr[:cl, :] = xp_scr[x_me, :, pl.ds(begin, 2 * TAPS)]
    for shift in range(1, rows):
        for blk in range(blocks):
            at = cl * (1 + (shift - 1) * blocks + blk)
            x_scr[at : at + cl, :] = xp_scr[owners[shift], :, blk * TAPS : (blk + 2) * TAPS]

    for f in range(NF):
        power = power_of(x_scr, table_at(f, ahead_ref, tab_ref))
        s_ref[f, outer, x_me] = power[:cl]
        for shift in range(1, rows):
            line = cl * (1 + (shift - 1) * blocks)
            s_ref[f, :, owners[shift]] = power[line : line + blocks * cl].reshape(blocks, cl, TAPS)


def outer_pair(pairs):
    return jnp.where(lax.axis_index("row") == 0, 0, pairs - 1)


def pair_columns(pair):
    return pl.ds(pl.multiple_of(pair * 2 * TAPS, 2 * TAPS), 2 * TAPS)


def first_early_kernel(cl, w_ref, s_ref, num_ref):
    rank, frames = num_ref.shape
    pairs = frames // (2 * TAPS)
    x_me = lax.axis_index("row")
    w = body(w_ref[...], rank, NF * cl)
    num_ref[:, pair_columns(outer_pair(pairs))] = jnp.zeros((rank, 2 * TAPS), F32)
    for at in range(pairs - 1):
        pair = at + jnp.where(x_me == 0, 1, 0)
        rows_of = pair_rows(s_ref, slice(None), pair, x_me, cl)
        num_ref[:, pair_columns(pair)] = jnp.dot(w, rows_of, preferred_element_type=F32)


def first_kernel(rows, subs, cl, *refs):
    refs = list(refs)
    w_refs = [refs.pop(0) for _ in range(rows)]
    early_ref, h_ref, s_ref, h_out, h_gram_ref = (refs.pop(0) for _ in range(5))
    msg_refs, num_scr = refs[:-1], refs[-1]
    rank, frames = h_ref.shape
    x_me = lax.axis_index("row")
    parts, gram = [], jnp.zeros(h_gram_ref.shape, F32)
    for shift, ref in enumerate(w_refs):
        parts.append((body(ref[...], rank, NF * cl), lax.rem(x_me + rows - shift, rows)))
        gram = gram + gram_of(ref[...], rank)
    if rows > 1:
        numerators(parts[1:], s_ref, num_scr, cl)
    else:
        num_scr[...] = jnp.zeros_like(num_scr)
    outer = outer_pair(frames // (2 * TAPS))
    num_scr[:, pair_columns(outer)] += jnp.dot(
        parts[0][0], pair_rows(s_ref, slice(None), outer, x_me, cl), preferred_element_type=F32
    )
    above = early_ref[...] + num_scr[...]
    new_activations(h_ref[...], gram, above, s_ref, h_out, h_gram_ref, msg_refs, rows, subs, cl)


def row_parts(rows, subs, cl, w_refs, w_scr, shifts):
    x_me, c_me = lax.axis_index("row"), lax.axis_index("sub")
    size = NF // subs * cl
    parts = []
    for line, dx in enumerate(shifts):
        for dc in range(subs):
            piece = body(w_refs[line * subs + dc][...], w_scr.shape[2], size)
            w_scr[line, lax.rem(c_me + subs - dc, subs)] = piece
        w = jnp.concatenate([w_scr[line, c] for c in range(subs)], axis=1)
        parts.append((w, lax.rem(x_me + rows - dx, rows)))
    return parts


def early_kernel(rows, subs, cl, *refs):
    w_refs, (s_ref, num_ref, w_scr) = refs[:subs], refs[subs:]
    numerators(row_parts(rows, subs, cl, w_refs, w_scr, [0]), s_ref, num_ref, cl)


def later_kernel(rows, subs, cl, *refs):
    refs = list(refs)
    w_refs = [refs.pop(0) for _ in range(rows * subs)]
    early_ref, h_ref, s_ref, h_out, h_gram_ref = (refs.pop(0) for _ in range(5))
    msg_refs, (w_scr, num_scr) = refs[:-2], refs[-2:]
    gram = jnp.zeros(h_gram_ref.shape, F32)
    for ref in w_refs:
        gram = gram + gram_of(ref[...], h_ref.shape[0])
    above = early_ref[...]
    if rows > 1:
        numerators(row_parts(rows, subs, cl, w_refs[subs:], w_scr, list(range(1, rows))), s_ref, num_scr, cl)
        above = above + num_scr[...]
    new_activations(h_ref[...], gram, above, s_ref, h_out, h_gram_ref, msg_refs, rows, subs, cl)


def core_kernel(count, rank, *refs):
    own_refs, gram_ref, got_refs = refs[:count], refs[count], refs[count + 1 : -count - 1]
    out_refs, total_ref = refs[-count - 1 : -1], refs[-1]
    size = own_refs[0].shape[1]
    each = len(got_refs) // count
    gram = gram_ref[...]
    for ref in got_refs[:each]:
        gram = gram + ref[:, size:]
    total_ref[...] = gram
    for at in range(count):
        total = own_refs[at][...]
        for ref in got_refs[at * each : (at + 1) * each]:
            total = total + ref[:, :size]
        pack(out_refs[at], total, gram)


def row_kernel(subs, own_ref, gram_ref, *refs):
    core_refs, msg_refs, out_ref = refs[: subs - 1], refs[subs - 1 : -1], refs[-1]
    rank, size = own_ref.shape
    total, gram = own_ref[...], gram_ref[...]
    for ref in core_refs:
        total = total + ref[...]
    for ref in msg_refs:
        total = total + body(ref[...], rank, size).astype(F32)
        gram = gram + gram_of(ref[...], rank)
    pack(out_ref, total, gram)


def summed(z_me, count, msg_refs, scr, rank, size):
    for at, shift in enumerate([0, *reversed(range(1, count))]):
        scr[partner(z_me, shift, count)] = msg_refs[at][...]
    total, gram = body(scr[0], rank, size).astype(F32), gram_of(scr[0], rank)
    for at in range(1, count):
        total = total + body(scr[at], rank, size).astype(F32)
        gram = gram + gram_of(scr[at], rank)
    return total, gram


def partner(place, shift, count):
    if count & (count - 1):
        return (place + count - shift) % count
    return place ^ shift


def update_kernel(count, w_ref, *refs):
    msg_refs, (new_ref, out_ref, scr) = refs[:count], refs[count:]
    rank, size = new_ref.shape
    total, gram = summed(lax.axis_index("frm"), count, msg_refs, scr, rank, size)
    w = w_ref[...]
    new = w * total / jnp.dot(gram, w, precision=HIGH, preferred_element_type=F32)
    new_ref[...] = new
    pack(out_ref, new, lax.dot_general(new, new, NT, precision=HIGH, preferred_element_type=F32))


def last_kernel(count, w_ref, order_ref, *refs):
    msg_refs, (out_ref, scr) = refs[:count], refs[count:]
    rank, size = w_ref.shape
    total, gram = summed(lax.axis_index("frm"), count, msg_refs, scr, rank, size)
    w = w_ref[...]
    new = w * total / jnp.dot(gram, w, precision=HIGH, preferred_element_type=F32)
    terms = three_terms(new)
    for c in range(order_ref.shape[1] // size):

        @pl.when(lax.axis_index("sub") == c)
        def _():
            moved = lax.dot_general(
                terms, order_ref[:, c * size : (c + 1) * size], NT, preferred_element_type=F32
            )
            out_ref[...] = moved[:rank] + (moved[rank : 2 * rank] + moved[2 * rank :])


def join_kernel(rows, *refs):
    act_refs, (out_ref, sems) = refs[:rows], refs[rows:]
    frames = act_refs[0].shape[1]
    x_me = lax.axis_index("row")
    copies = []
    for shift in range(rows):
        begin = pl.multiple_of(lax.rem(x_me + rows - shift, rows) * frames, TAPS)
        copies.append(pltpu.make_async_copy(act_refs[shift], out_ref.at[:, pl.ds(begin, frames)], sems.at[shift]))
    for copy in copies:
        copy.start()
    for copy in copies:
        copy.wait()


def sum_kernel(_, *refs):
    parts, (out_ref, scr, sem) = refs[:-3], refs[-3:]
    total = parts[0][...]
    for part in parts[1:]:
        total = total + part[...]
    scr[...] = total
    copy = pltpu.make_async_copy(scr, out_ref, sem)
    copy.start()
    copy.wait()


def call(kernel, args, outs, scratch=(), in_specs=None, out_specs=None, limit=4, cost=None, aliases=None):
    whole = pl.BlockSpec(memory_space=pltpu.VMEM)
    if cost is not None:
        cost = pl.CostEstimate(flops=cost, bytes_accessed=0, transcendentals=0)
    return pl.pallas_call(
        kernel,
        out_shape=[jax.ShapeDtypeStruct(*out) if isinstance(out, tuple) else out for out in outs],
        in_specs=in_specs or [whole] * len(args),
        out_specs=out_specs or [whole] * len(outs),
        scratch_shapes=list(scratch),
        compiler_params=pltpu.CompilerParams(vmem_limit_bytes=limit * MIB),
        cost_estimate=cost,
        input_output_aliases=aliases or {},
    )(*args)


def reorder(cl):
    order = np.zeros((cl, NF, NF, cl), ml_dtypes.bfloat16)
    chans, freqs = np.meshgrid(np.arange(cl), np.arange(NF), indexing="ij")
    order[chans, freqs, freqs, chans] = 1
    return order.reshape(cl * NF, NF * cl)


def shards(signal, w_start, h_start):
    rows, subs, frms = (lax.axis_size(axis) for axis in ("row", "sub", "frm"))
    x_me = lax.axis_index("row")
    cl, window = signal.shape
    rank = w_start.shape[1]
    frames = window // rows
    blocks = frames // TAPS
    chans = rows * cl
    size = NF * cl // subs
    line = frms * subs
    width = frames + (TAPS if rows == 2 else 2 * TAPS)
    anywhere = pl.BlockSpec(memory_space=pl.ANY)
    whole = pl.BlockSpec(memory_space=pltpu.VMEM)

    def hbm(value):
        return pltpu.with_memory_space_constraint(value, pltpu.HBM)

    def vmem(value):
        return pltpu.with_memory_space_constraint(value, pltpu.VMEM)

    def row_shift(value, shift):
        return lax.ppermute(value, "row", [(i, (i + shift) % rows) for i in range(rows)])

    def sub_shift(value, shift):
        return lax.ppermute(value, "sub", [(i, (i + shift) % subs) for i in range(subs)])

    def frm_shift(value, shift):
        return lax.ppermute(value, "frm", [(partner(i, shift, frms), i) for i in range(frms)])

    def place(x, at):
        return (at // subs * rows + x) * subs + at % subs

    table, order = hbm(jnp.asarray(toeplitz())), jnp.asarray(reorder(cl))
    *cuts, ahead = call(
        functools.partial(cut_kernel, rows, frames),
        [hbm(signal), table],
        [((cl, width), BF16)] * rows + [pltpu.VMEM((AHEAD,) + table.shape[1:], BF16)],
        [pltpu.SemaphoreType.DMA((rows + 1,))],
        in_specs=[anywhere] * 2,
    )
    own_sig, *out_sigs = cuts
    ahead = vmem(ahead)
    sig = [own_sig] + [row_shift(part, shift + 1) for shift, part in enumerate(out_sigs)]
    msg = (message(rank, size), BF16)
    piece = ((rank, size), F32)
    update_outs = [((rank, frames), F32), ((rank, rank), F32)]
    update_outs += [((rank, size + rank), F32)] * ((rows - 1) * (subs - 1))
    half_done, w_own, old, order, table = call(
        functools.partial(own_spectra_kernel, rows),
        [own_sig, ahead, hbm(w_start.T), hbm(h_start), hbm(order), table],
        [
            pltpu.VMEM((NF, blocks, rows, cl, TAPS), BF16),
            pltpu.VMEM((rank, NF * cl), F32),
            pltpu.VMEM((rank, frames), F32),
            pltpu.VMEM(order.shape, BF16),
            pltpu.VMEM((NF - AHEAD,) + table.shape[1:], BF16),
        ],
        [
            pltpu.VMEM((cl, frames + TAPS), BF16),
            pltpu.VMEM(((blocks - 1) * cl, 2 * TAPS), BF16),
            pltpu.SemaphoreType.DMA((3,)),
            pltpu.SemaphoreType.DMA((len(CUTS) - 1,)),
        ],
        in_specs=[whole] * 2 + [anywhere] * 4,
        limit=8,
        cost=2 * NF * cl * frames * 4 * TAPS,
    )
    order = vmem(order)
    (edge,) = call(
        functools.partial(edges_kernel, rows),
        sig + [vmem(half_done)],
        [((chans, TAPS), BF16)],
        in_specs=[whole] * rows + [anywhere],
    )
    pairs = [(place(rows - 1, i), place(0, i + 1)) for i in range(line - 1)]
    halo = lax.ppermute(edge, ("frm", "row", "sub"), pairs + [(b, a) for a, b in pairs])
    w_piece, w_msg = call(
        reorder_kernel,
        [vmem(w_own), order, edge],
        [piece, (message(rank, NF * cl), BF16)],
        in_specs=[whole, whole, anywhere],
    )
    w_msgs = [w_msg] + [row_shift(w_msg, shift) for shift in range(1, rows)]
    (early,) = call(
        functools.partial(first_early_kernel, cl),
        [w_msg, vmem(half_done)],
        [((rank, frames), F32)],
        cost=16 * NF * cl * frames * rank,
    )
    (spectra,) = call(
        functools.partial(other_spectra_kernel, rows),
        [halo, ahead, vmem(table)] + sig + [vmem(half_done), early],
        [pltpu.VMEM((NF, blocks, rows, cl, TAPS), BF16)],
        [
            pltpu.VMEM((rows, cl, frames + TAPS), BF16),
            pltpu.VMEM((((rows - 1) * blocks + 1) * cl, 2 * TAPS), BF16),
        ],
        in_specs=[whole] * (rows + 3) + [anywhere] * 2,
        limit=8,
        cost=2 * NF * chans * frames * 4 * TAPS,
        aliases={rows + 3: 0},
    )
    spectra = vmem(spectra)

    def products(places, activations, after):
        return call(
            functools.partial(products_kernel, places, rows, subs, cl),
            [activations, spectra] + after,
            [piece] * len(places),
            in_specs=[whole] * 2 + [anywhere] * len(after),
            cost=1 if after else 16 * NF * cl * frames * rank // subs * len(places),
        )

    def gathered(activations, h_gram, msgs):
        got = [sub_shift(m, dc) for m, (_, dc) in zip(msgs, others_of(rows, subs))]
        places = [(dx, 0) for dx in range(1, rows)] + [(0, dc) for dc in range(1, subs)]
        formed = products(places, activations, [])
        for_rows, for_cores = formed[: rows - 1], formed[rows - 1 :]
        from_cores = [sub_shift(m, dc + 1) for dc, m in enumerate(for_cores)]
        *outs, gram = call(
            functools.partial(core_kernel, rows - 1, rank),
            list(for_rows) + [h_gram] + got,
            [msg] * (rows - 1) + [((rank, rank), F32)],
        )
        from_rows = [row_shift(m, dx + 1) for dx, m in enumerate(outs)]
        (own,) = products([(0, 0)], activations, outs)
        (part,) = call(functools.partial(row_kernel, subs), [own, gram] + from_cores + from_rows, [msg])
        return [part] + [frm_shift(part, shift) for shift in reversed(range(1, frms))]

    activations, h_gram, *msgs = call(
        functools.partial(first_kernel, rows, subs, cl),
        w_msgs + [early, vmem(old), spectra],
        update_outs,
        [pltpu.VMEM((rank, frames), F32)],
        limit=8,
    )
    piled = [pltpu.VMEM((frms,) + msg[0], BF16)]
    w_piece, w_msg = call(
        functools.partial(update_kernel, frms),
        [w_piece] + gathered(activations, h_gram, msgs),
        [piece, msg],
        piled,
    )
    w_msgs = [w_msg] + [sub_shift(w_msg, dc) for dc in range(1, subs)]
    w_pieces = pltpu.VMEM((rows, subs, rank, size), BF16)
    (early,) = call(
        functools.partial(early_kernel, rows, subs, cl),
        w_msgs + [spectra],
        [((rank, frames), F32)],
        [w_pieces],
        cost=16 * NF * cl * frames * rank,
    )
    from_rows = [row_shift(w_msg, dx) for dx in range(1, rows)]
    *from_rows, early = lax.optimization_barrier((*from_rows, early))
    for base in from_rows:
        w_msgs += [base] + [sub_shift(base, dc) for dc in range(1, subs)]
    activations, h_gram, *msgs = call(
        functools.partial(later_kernel, rows, subs, cl),
        w_msgs + [early, activations, spectra],
        update_outs,
        [w_pieces, pltpu.VMEM((rank, frames), F32)],
        limit=8,
    )
    parts = gathered(activations, h_gram, msgs)
    activations, parts[0] = lax.optimization_barrier((activations, parts[0]))
    sides = [activations] + [row_shift(activations, shift) for shift in range(1, rows)]
    (part,) = call(
        functools.partial(last_kernel, frms), [w_piece, order] + parts, [((rank, NF * cl), F32)], piled
    )
    (wide,) = call(
        functools.partial(join_kernel, rows),
        sides,
        [pltpu.HBM((rank, window), F32)],
        [pltpu.SemaphoreType.DMA((rows,))],
        in_specs=[anywhere] * rows,
        out_specs=[anywhere],
    )
    (synergies,) = call(
        sum_kernel,
        [hbm(wide), part] + [sub_shift(part, dc) for dc in range(1, subs)],
        [pltpu.HBM((rank, NF * cl), F32)],
        [pltpu.VMEM((rank, NF * cl), F32), pltpu.SemaphoreType.DMA],
        in_specs=[anywhere] + [whole] * subs,
        out_specs=[anywhere],
    )
    return (synergies.T, wide)


def solution(mesh):
    placed = (P("row", ("grp", "frm", "sub")), P("row", None), P(None, ("grp", "frm", "sub")))
    return jax.shard_map(
        shards,
        mesh=mesh,
        in_specs=placed,
        out_specs=(P(("grp", "row"), None), P(None, ("grp", "frm", "sub"))),
        check_vma=False,
    )
```

```python
import functools
import math

import jax
import jax.numpy as jnp
import ml_dtypes
import numpy as np
from jax import lax
from jax.experimental import pallas as pl
from jax.experimental.pallas import tpu as pltpu
from jax.sharding import PartitionSpec as P

NF = 40
TAPS = 128
HALF = TAPS // 2
LANES = 128
CUTS = (8, 16, 24, 32, NF)
AHEAD = CUTS[0]
F32 = jnp.float32
BF16 = jnp.bfloat16
HIGH = lax.Precision.HIGHEST
NT = (((1,), (1,)), ((), ()))
MIB = 1024 * 1024


def wavelets():
    f = np.float32
    level = np.arange(NF, dtype=f) / f(NF - 1)
    freq = f(2.0) * np.power(f(12.0), level)
    sigma = f(7.0) / (f(2.0 * math.pi) * freq)
    times = (np.arange(TAPS, dtype=f) - f(HALF)) / f(50.0)
    env = np.exp(-(times[None, :] ** 2) / (f(2.0) * sigma[:, None] ** 2))
    scale = f(1.0) / np.sqrt(np.sum(env * env, axis=1))
    env = env * scale[:, None]
    phase = f(2.0 * math.pi) * freq[:, None] * times[None, :]
    return np.stack([env * np.cos(phase), env * np.sin(phase)]).astype(ml_dtypes.bfloat16)


def toeplitz():
    kernel = wavelets()
    table = np.zeros((NF, 2 * TAPS, 2 * TAPS), ml_dtypes.bfloat16)
    for at in range(TAPS):
        for part in range(2):
            table[:, at : at + TAPS, part * TAPS + at] = kernel[part]
    return table


def split_two(value):
    top = value.astype(BF16)
    return top, (value - top.astype(F32)).astype(BF16)


def message(rank, size):
    return (rank * -(-size // LANES) + rank // 2, LANES)


def pack(out_ref, main, gram):
    rank, size = main.shape
    half = rank // 2
    for at in range(0, size, LANES):
        line = at // LANES * rank
        width = min(LANES, size - at)
        out_ref[line : line + rank, :width] = main[:, at : at + width].astype(BF16)
    top, rest = split_two(gram)
    terms = [top[:half], top[half:], rest[:half], rest[half:]]
    line = out_ref.shape[0] - half
    for at, term in enumerate(terms):
        out_ref[line:, at * rank : (at + 1) * rank] = term


def body(value, rank, size):
    parts = []
    for at in range(0, size, LANES):
        line = at // LANES * rank
        parts.append(value[line : line + rank, : min(LANES, size - at)])
    return jnp.concatenate(parts, axis=1)


def gram_of(value, rank):
    last = value[value.shape[0] - rank // 2 :, :].astype(F32)
    total = last[:, : 2 * rank] + last[:, 2 * rank : 4 * rank]
    return jnp.concatenate([total[:, :rank], total[:, rank:]], axis=0)


def reorder_kernel(w_ref, order_ref, *refs):
    piece_ref, msg_ref = refs[-2:]
    w = w_ref[...]
    rank, size = piece_ref.shape
    gram = lax.dot_general(w, w, NT, precision=HIGH, preferred_element_type=F32)
    moved = jnp.dot(three_terms(w), order_ref[...], preferred_element_type=F32)
    whole = moved[:rank] + (moved[rank : 2 * rank] + moved[2 * rank :])
    for c in range(w.shape[1] // size):

        @pl.when(lax.axis_index("sub") == c)
        def _():
            piece_ref[...] = whole[:, c * size : (c + 1) * size]

    pack(msg_ref, whole, gram)


def three_terms(value):
    top = value.astype(BF16)
    rest = value - top.astype(F32)
    middle = rest.astype(BF16)
    return jnp.concatenate([top, middle, (rest - middle.astype(F32)).astype(BF16)], axis=0)


def edges_kernel(rows, sig_ref, *refs):
    got_refs, out_ref = refs[: rows - 1], refs[-1]
    cl, width = sig_ref.shape
    x_me = lax.axis_index("row")
    for at, ref in enumerate((sig_ref,) + tuple(got_refs)):

        @pl.when(x_me == 0)
        def _():
            out_ref[at * cl : (at + 1) * cl, :] = ref[:, :TAPS]

        @pl.when(x_me > 0)
        def _():
            out_ref[at * cl : (at + 1) * cl, :] = ref[:, width - TAPS :]


def cut_kernel(rows, frames, sig_hbm, tab_hbm, *refs):
    out_refs, (tab_ref, sems) = refs[:rows], refs[rows:]
    window, x_me = sig_hbm.shape[1], lax.axis_index("row")
    width = out_refs[0].shape[1]
    copies = []
    for shift in reversed(range(rows)):
        target = lax.rem(x_me + shift, rows)
        begin = pl.multiple_of(jnp.clip(target * frames - TAPS, 0, window - width), TAPS)
        copies.append(pltpu.make_async_copy(sig_hbm.at[:, pl.ds(begin, width)], out_refs[shift], sems.at[shift]))
    copies.append(pltpu.make_async_copy(tab_hbm.at[:AHEAD], tab_ref, sems.at[rows]))
    for copy in copies:
        copy.start()
    for copy in copies:
        copy.wait()


def pair_rows(s_ref, span, pair, x, cl):
    halves = [s_ref[span, blk, x].reshape(-1, TAPS) for blk in (2 * pair, 2 * pair + 1)]
    return jnp.concatenate(halves, axis=1)


def numerators(parts, s_ref, num_ref, cl):
    for pair in range(num_ref.shape[1] // (2 * TAPS)):
        terms = [
            jnp.dot(w, pair_rows(s_ref, slice(None), pair, x, cl), preferred_element_type=F32) for w, x in parts
        ]
        num_ref[:, 2 * TAPS * pair : 2 * TAPS * (pair + 1)] = functools.reduce(jnp.add, terms)


def crossed(low, s_ref, places, subs, cl):
    count = NF // subs
    acc = jnp.zeros((low.shape[0], len(places) * count * cl), F32)
    for pair in range(low.shape[1] // (2 * TAPS)):
        cols = slice(2 * TAPS * pair, 2 * TAPS * (pair + 1))
        parts = [pair_rows(s_ref, pl.ds(core * count, count), pair, x, cl) for x, core in places]
        acc = acc + lax.dot_general(
            low[:, cols], jnp.concatenate(parts, axis=0), NT, preferred_element_type=F32
        )
    return acc


def others_of(rows, subs):
    return [(dx, dc) for dx in range(1, rows) for dc in range(1, subs)]


def new_activations(old, gram, above, s_ref, h_out, h_gram_ref, msg_refs, rows, subs, cl):
    new = old * above / jnp.dot(gram, old, precision=HIGH, preferred_element_type=F32)
    h_out[...] = new
    h_gram = lax.dot_general(new, new, NT, precision=HIGH, preferred_element_type=F32)
    h_gram_ref[...] = h_gram
    size = NF // subs * cl
    x_me, c_me = lax.axis_index("row"), lax.axis_index("sub")
    for ref, (dx, dc) in zip(msg_refs, others_of(rows, subs)):
        target = (lax.rem(x_me + dx, rows), lax.rem(c_me + dc, subs))
        ref[:, :size] = crossed(new.astype(BF16), s_ref, [target], subs, cl)
        ref[:, size:] = h_gram


def products_kernel(places, rows, subs, cl, h_ref, s_ref, *refs):
    x_me, c_me = lax.axis_index("row"), lax.axis_index("sub")
    low = h_ref[...].astype(BF16)
    targets = [(lax.rem(x_me + dx, rows), lax.rem(c_me + dc, subs)) for dx, dc in places]
    acc = crossed(low, s_ref, targets, subs, cl)
    size = acc.shape[1] // len(places)
    for at, ref in enumerate(refs[len(refs) - len(places) :]):
        ref[...] = acc[:, at * size : (at + 1) * size]


def place_signal(source, target, rows, frames):
    x_me = lax.axis_index("row")
    width = source.shape[1]

    @pl.when(x_me == 0)
    def _():
        target[:, HALF:] = source[:, : frames + HALF]

    @pl.when(x_me == rows - 1)
    def _():
        target[:, : frames + HALF] = source[:, width - frames - HALF :]

    if rows > 2:

        @pl.when((x_me > 0) & (x_me < rows - 1))
        def _():
            target[...] = source[:, HALF : HALF + frames + TAPS]


def power_of(x_ref, table):
    co = jnp.dot(x_ref[...], table, preferred_element_type=F32)
    return (co[:, :TAPS] * co[:, :TAPS] + co[:, TAPS:] * co[:, TAPS:]).astype(BF16)


def table_at(f, ahead_ref, tab_ref):
    return ahead_ref[f] if f < AHEAD else tab_ref[f - AHEAD]


def own_spectra_kernel(rows, sig_ref, ahead_ref, w_hbm, h_hbm, order_hbm, tab_hbm, *refs):
    s_ref, w_ref, old_ref, order_ref, tab_ref, xp_scr, x_scr, sems, tab_sems = refs
    _, blocks, _, cl, _ = s_ref.shape
    frames = blocks * TAPS
    x_me = lax.axis_index("row")
    mine = pl.ds(pl.multiple_of(x_me * frames, TAPS), frames)

    table = [
        pltpu.make_async_copy(tab_hbm.at[begin:end], tab_ref.at[begin - AHEAD : end - AHEAD], tab_sems.at[at])
        for at, (begin, end) in enumerate(zip(CUTS, CUTS[1:]))
    ]
    later = [
        pltpu.make_async_copy(w_hbm, w_ref, sems.at[0]),
        pltpu.make_async_copy(order_hbm, order_ref, sems.at[1]),
        pltpu.make_async_copy(h_hbm.at[:, mine], old_ref, sems.at[2]),
    ]
    for copy in table:
        copy.start()
    place_signal(sig_ref, xp_scr, rows, frames)
    first = jnp.where(x_me == 0, 1, 0)
    for at in range(blocks - 1):
        begin = pl.multiple_of((first + at) * TAPS, TAPS)
        x_scr[at * cl : (at + 1) * cl, :] = xp_scr[:, pl.ds(begin, 2 * TAPS)]

    for f in range(NF):
        if f in CUTS:
            table[CUTS.index(f)].wait()
        if f == CUTS[1]:
            for copy in later:
                copy.start()
        power = power_of(x_scr, table_at(f, ahead_ref, tab_ref))
        s_ref[f, pl.ds(first, blocks - 1), x_me] = power.reshape(blocks - 1, cl, TAPS)
    for copy in later:
        copy.wait()


def other_spectra_kernel(rows, halo_ref, ahead_ref, tab_ref, *refs):
    sig_refs, (s_ref, xp_scr, x_scr) = refs[:rows], refs[-3:]
    _, blocks, _, cl, _ = s_ref.shape
    frames = blocks * TAPS
    x_me = lax.axis_index("row")
    owners = [lax.rem(x_me + rows - shift, rows) for shift in range(rows)]
    for shift in range(rows):
        place_signal(sig_refs[shift], xp_scr.at[owners[shift]], rows, frames)

    @pl.when(x_me == 0)
    def _():
        for at in range(rows):
            xp_scr[rows - 1 - at, :, :HALF] = halo_ref[at * cl : (at + 1) * cl, HALF:]

    @pl.when(x_me == rows - 1)
    def _():
        for at in range(rows):
            xp_scr[(rows - at) % rows, :, frames + HALF :] = halo_ref[at * cl : (at + 1) * cl, :HALF]

    outer = jnp.where(x_me == 0, 0, blocks - 1)
    begin = pl.multiple_of(outer * TAPS, TAPS)
    x_scr[:cl, :] = xp_scr[x_me, :, pl.ds(begin, 2 * TAPS)]
    for shift in range(1, rows):
        for blk in range(blocks):
            at = cl * (1 + (shift - 1) * blocks + blk)
            x_scr[at : at + cl, :] = xp_scr[owners[shift], :, blk * TAPS : (blk + 2) * TAPS]

    for f in range(NF):
        power = power_of(x_scr, table_at(f, ahead_ref, tab_ref))
        s_ref[f, outer, x_me] = power[:cl]
        for shift in range(1, rows):
            line = cl * (1 + (shift - 1) * blocks)
            s_ref[f, :, owners[shift]] = power[line : line + blocks * cl].reshape(blocks, cl, TAPS)


def outer_pair(pairs):
    return jnp.where(lax.axis_index("row") == 0, 0, pairs - 1)


def pair_columns(pair):
    return pl.ds(pl.multiple_of(pair * 2 * TAPS, 2 * TAPS), 2 * TAPS)


def first_early_kernel(cl, w_ref, s_ref, num_ref):
    rank, frames = num_ref.shape
    pairs = frames // (2 * TAPS)
    x_me = lax.axis_index("row")
    w = body(w_ref[...], rank, NF * cl)
    num_ref[:, pair_columns(outer_pair(pairs))] = jnp.zeros((rank, 2 * TAPS), F32)
    for at in range(pairs - 1):
        pair = at + jnp.where(x_me == 0, 1, 0)
        rows_of = pair_rows(s_ref, slice(None), pair, x_me, cl)
        num_ref[:, pair_columns(pair)] = jnp.dot(w, rows_of, preferred_element_type=F32)


def first_kernel(rows, subs, cl, *refs):
    refs = list(refs)
    w_refs = [refs.pop(0) for _ in range(rows)]
    early_ref, h_ref, s_ref, h_out, h_gram_ref = (refs.pop(0) for _ in range(5))
    msg_refs, num_scr = refs[:-1], refs[-1]
    rank, frames = h_ref.shape
    x_me = lax.axis_index("row")
    parts, gram = [], jnp.zeros(h_gram_ref.shape, F32)
    for shift, ref in enumerate(w_refs):
        parts.append((body(ref[...], rank, NF * cl), lax.rem(x_me + rows - shift, rows)))
        gram = gram + gram_of(ref[...], rank)
    if rows > 1:
        numerators(parts[1:], s_ref, num_scr, cl)
    else:
        num_scr[...] = jnp.zeros_like(num_scr)
    outer = outer_pair(frames // (2 * TAPS))
    num_scr[:, pair_columns(outer)] += jnp.dot(
        parts[0][0], pair_rows(s_ref, slice(None), outer, x_me, cl), preferred_element_type=F32
    )
    above = early_ref[...] + num_scr[...]
    new_activations(h_ref[...], gram, above, s_ref, h_out, h_gram_ref, msg_refs, rows, subs, cl)


def row_parts(rows, subs, cl, w_refs, w_scr, shifts):
    x_me, c_me = lax.axis_index("row"), lax.axis_index("sub")
    size = NF // subs * cl
    parts = []
    for line, dx in enumerate(shifts):
        for dc in range(subs):
            piece = body(w_refs[line * subs + dc][...], w_scr.shape[2], size)
            w_scr[line, lax.rem(c_me + subs - dc, subs)] = piece
        w = jnp.concatenate([w_scr[line, c] for c in range(subs)], axis=1)
        parts.append((w, lax.rem(x_me + rows - dx, rows)))
    return parts


def early_kernel(rows, subs, cl, *refs):
    w_refs, (s_ref, num_ref, w_scr) = refs[:subs], refs[subs:]
    numerators(row_parts(rows, subs, cl, w_refs, w_scr, [0]), s_ref, num_ref, cl)


def add_pieces(base_ref, pieces, s_ref, out_ref, rows, subs, cl):
    rank, frames = out_ref.shape
    count = NF // subs
    x_me, c_me = lax.axis_index("row"), lax.axis_index("sub")
    terms = []
    for ref, dx, dc in pieces:
        core = lax.rem(c_me + subs - dc, subs)
        terms.append((body(ref[...], rank, count * cl), lax.rem(x_me + rows - dx, rows), core))
    for pair in range(frames // (2 * TAPS)):
        cols = slice(2 * TAPS * pair, 2 * TAPS * (pair + 1))
        acc = base_ref[:, cols]
        for w, x, core in terms:
            spectra = pair_rows(s_ref, pl.ds(core * count, count), pair, x, cl)
            acc = acc + jnp.dot(w, spectra, preferred_element_type=F32)
        out_ref[:, cols] = acc


def middle_kernel(rows, subs, cl, *refs):
    w_refs, (base_ref, s_ref, out_ref) = refs[:-3], refs[-3:]
    pieces = [(ref, dx + 1, 0) for dx, ref in enumerate(w_refs)]
    add_pieces(base_ref, pieces, s_ref, out_ref, rows, subs, cl)


def later_kernel(rows, subs, cl, *refs):
    refs = list(refs)
    w_refs = [refs.pop(0) for _ in range(rows * subs)]
    middle_ref, h_ref, s_ref, h_out, h_gram_ref = (refs.pop(0) for _ in range(5))
    msg_refs, num_scr = refs[:-1], refs[-1]
    gram = jnp.zeros(h_gram_ref.shape, F32)
    for ref in w_refs:
        gram = gram + gram_of(ref[...], h_ref.shape[0])
    pieces = [(w_refs[dx * subs + dc], dx, dc) for dx in range(1, rows) for dc in range(1, subs)]
    add_pieces(middle_ref, pieces, s_ref, num_scr, rows, subs, cl)
    new_activations(h_ref[...], gram, num_scr[...], s_ref, h_out, h_gram_ref, msg_refs, rows, subs, cl)


def core_kernel(count, rank, *refs):
    own_refs, gram_ref, got_refs = refs[:count], refs[count], refs[count + 1 : -count - 1]
    out_refs, total_ref = refs[-count - 1 : -1], refs[-1]
    size = own_refs[0].shape[1]
    each = len(got_refs) // count
    gram = gram_ref[...]
    for ref in got_refs[:each]:
        gram = gram + ref[:, size:]
    total_ref[...] = gram
    for at in range(count):
        total = own_refs[at][...]
        for ref in got_refs[at * each : (at + 1) * each]:
            total = total + ref[:, :size]
        pack(out_refs[at], total, gram)


def row_kernel(subs, own_ref, gram_ref, *refs):
    core_refs, msg_refs, out_ref = refs[: subs - 1], refs[subs - 1 : -1], refs[-1]
    rank, size = own_ref.shape
    total, gram = own_ref[...], gram_ref[...]
    for ref in core_refs:
        total = total + ref[...]
    for ref in msg_refs:
        total = total + body(ref[...], rank, size).astype(F32)
        gram = gram + gram_of(ref[...], rank)
    pack(out_ref, total, gram)


def summed(z_me, count, msg_refs, scr, rank, size):
    for at, shift in enumerate([0, *reversed(range(1, count))]):
        scr[partner(z_me, shift, count)] = msg_refs[at][...]
    total, gram = body(scr[0], rank, size).astype(F32), gram_of(scr[0], rank)
    for at in range(1, count):
        total = total + body(scr[at], rank, size).astype(F32)
        gram = gram + gram_of(scr[at], rank)
    return total, gram


def partner(place, shift, count):
    if count & (count - 1):
        return (place + count - shift) % count
    return place ^ shift


def update_kernel(count, w_ref, *refs):
    msg_refs, (new_ref, out_ref, scr) = refs[:count], refs[count:]
    rank, size = new_ref.shape
    total, gram = summed(lax.axis_index("frm"), count, msg_refs, scr, rank, size)
    w = w_ref[...]
    new = w * total / jnp.dot(gram, w, precision=HIGH, preferred_element_type=F32)
    new_ref[...] = new
    pack(out_ref, new, lax.dot_general(new, new, NT, precision=HIGH, preferred_element_type=F32))


def last_kernel(count, w_ref, order_ref, *refs):
    msg_refs, (out_ref, scr) = refs[:count], refs[count:]
    rank, size = w_ref.shape
    total, gram = summed(lax.axis_index("frm"), count, msg_refs, scr, rank, size)
    w = w_ref[...]
    new = w * total / jnp.dot(gram, w, precision=HIGH, preferred_element_type=F32)
    terms = three_terms(new)
    for c in range(order_ref.shape[1] // size):

        @pl.when(lax.axis_index("sub") == c)
        def _():
            moved = lax.dot_general(
                terms, order_ref[:, c * size : (c + 1) * size], NT, preferred_element_type=F32
            )
            out_ref[...] = moved[:rank] + (moved[rank : 2 * rank] + moved[2 * rank :])


def join_kernel(rows, *refs):
    act_refs, (out_ref, sems) = refs[:rows], refs[rows:]
    frames = act_refs[0].shape[1]
    x_me = lax.axis_index("row")
    copies = []
    for shift in range(rows):
        begin = pl.multiple_of(lax.rem(x_me + rows - shift, rows) * frames, TAPS)
        copies.append(pltpu.make_async_copy(act_refs[shift], out_ref.at[:, pl.ds(begin, frames)], sems.at[shift]))
    for copy in copies:
        copy.start()
    for copy in copies:
        copy.wait()


def sum_kernel(_, *refs):
    parts, (out_ref, scr, sem) = refs[:-3], refs[-3:]
    total = parts[0][...]
    for part in parts[1:]:
        total = total + part[...]
    scr[...] = total
    copy = pltpu.make_async_copy(scr, out_ref, sem)
    copy.start()
    copy.wait()


def call(kernel, args, outs, scratch=(), in_specs=None, out_specs=None, limit=4, cost=None, aliases=None):
    whole = pl.BlockSpec(memory_space=pltpu.VMEM)
    if cost is not None:
        cost = pl.CostEstimate(flops=cost, bytes_accessed=0, transcendentals=0)
    return pl.pallas_call(
        kernel,
        out_shape=[jax.ShapeDtypeStruct(*out) if isinstance(out, tuple) else out for out in outs],
        in_specs=in_specs or [whole] * len(args),
        out_specs=out_specs or [whole] * len(outs),
        scratch_shapes=list(scratch),
        compiler_params=pltpu.CompilerParams(vmem_limit_bytes=limit * MIB),
        cost_estimate=cost,
        input_output_aliases=aliases or {},
    )(*args)


def reorder(cl):
    order = np.zeros((cl, NF, NF, cl), ml_dtypes.bfloat16)
    chans, freqs = np.meshgrid(np.arange(cl), np.arange(NF), indexing="ij")
    order[chans, freqs, freqs, chans] = 1
    return order.reshape(cl * NF, NF * cl)


def shards(signal, w_start, h_start):
    rows, subs, frms = (lax.axis_size(axis) for axis in ("row", "sub", "frm"))
    x_me = lax.axis_index("row")
    cl, window = signal.shape
    rank = w_start.shape[1]
    frames = window // rows
    blocks = frames // TAPS
    chans = rows * cl
    size = NF * cl // subs
    line = frms * subs
    width = frames + (TAPS if rows == 2 else 2 * TAPS)
    anywhere = pl.BlockSpec(memory_space=pl.ANY)
    whole = pl.BlockSpec(memory_space=pltpu.VMEM)

    def hbm(value):
        return pltpu.with_memory_space_constraint(value, pltpu.HBM)

    def vmem(value):
        return pltpu.with_memory_space_constraint(value, pltpu.VMEM)

    def row_shift(value, shift):
        return lax.ppermute(value, "row", [(i, (i + shift) % rows) for i in range(rows)])

    def sub_shift(value, shift):
        return lax.ppermute(value, "sub", [(i, (i + shift) % subs) for i in range(subs)])

    def frm_shift(value, shift):
        return lax.ppermute(value, "frm", [(partner(i, shift, frms), i) for i in range(frms)])

    def place(x, at):
        return (at // subs * rows + x) * subs + at % subs

    table, order = hbm(jnp.asarray(toeplitz())), jnp.asarray(reorder(cl))
    *cuts, ahead = call(
        functools.partial(cut_kernel, rows, frames),
        [hbm(signal), table],
        [((cl, width), BF16)] * rows + [pltpu.VMEM((AHEAD,) + table.shape[1:], BF16)],
        [pltpu.SemaphoreType.DMA((rows + 1,))],
        in_specs=[anywhere] * 2,
    )
    own_sig, *out_sigs = cuts
    ahead = vmem(ahead)
    sig = [own_sig] + [row_shift(part, shift + 1) for shift, part in enumerate(out_sigs)]
    msg = (message(rank, size), BF16)
    piece = ((rank, size), F32)
    update_outs = [((rank, frames), F32), ((rank, rank), F32)]
    update_outs += [((rank, size + rank), F32)] * ((rows - 1) * (subs - 1))
    half_done, w_own, old, order, table = call(
        functools.partial(own_spectra_kernel, rows),
        [own_sig, ahead, hbm(w_start.T), hbm(h_start), hbm(order), table],
        [
            pltpu.VMEM((NF, blocks, rows, cl, TAPS), BF16),
            pltpu.VMEM((rank, NF * cl), F32),
            pltpu.VMEM((rank, frames), F32),
            pltpu.VMEM(order.shape, BF16),
            pltpu.VMEM((NF - AHEAD,) + table.shape[1:], BF16),
        ],
        [
            pltpu.VMEM((cl, frames + TAPS), BF16),
            pltpu.VMEM(((blocks - 1) * cl, 2 * TAPS), BF16),
            pltpu.SemaphoreType.DMA((3,)),
            pltpu.SemaphoreType.DMA((len(CUTS) - 1,)),
        ],
        in_specs=[whole] * 2 + [anywhere] * 4,
        limit=8,
        cost=2 * NF * cl * frames * 4 * TAPS,
    )
    order = vmem(order)
    (edge,) = call(
        functools.partial(edges_kernel, rows),
        sig + [vmem(half_done)],
        [((chans, TAPS), BF16)],
        in_specs=[whole] * rows + [anywhere],
    )
    pairs = [(place(rows - 1, i), place(0, i + 1)) for i in range(line - 1)]
    halo = lax.ppermute(edge, ("frm", "row", "sub"), pairs + [(b, a) for a, b in pairs])
    w_piece, w_msg = call(
        reorder_kernel,
        [vmem(w_own), order, edge],
        [piece, (message(rank, NF * cl), BF16)],
        in_specs=[whole, whole, anywhere],
    )
    w_msgs = [w_msg] + [row_shift(w_msg, shift) for shift in range(1, rows)]
    (early,) = call(
        functools.partial(first_early_kernel, cl),
        [w_msg, vmem(half_done)],
        [((rank, frames), F32)],
        cost=16 * NF * cl * frames * rank,
    )
    (spectra,) = call(
        functools.partial(other_spectra_kernel, rows),
        [halo, ahead, vmem(table)] + sig + [vmem(half_done), early],
        [pltpu.VMEM((NF, blocks, rows, cl, TAPS), BF16)],
        [
            pltpu.VMEM((rows, cl, frames + TAPS), BF16),
            pltpu.VMEM((((rows - 1) * blocks + 1) * cl, 2 * TAPS), BF16),
        ],
        in_specs=[whole] * (rows + 3) + [anywhere] * 2,
        limit=8,
        cost=2 * NF * chans * frames * 4 * TAPS,
        aliases={rows + 3: 0},
    )
    spectra = vmem(spectra)

    def products(places, activations, after):
        return call(
            functools.partial(products_kernel, places, rows, subs, cl),
            [activations, spectra] + after,
            [piece] * len(places),
            in_specs=[whole] * 2 + [anywhere] * len(after),
            cost=1 if after else 16 * NF * cl * frames * rank // subs * len(places),
        )

    def gathered(activations, h_gram, msgs):
        got = [sub_shift(m, dc) for m, (_, dc) in zip(msgs, others_of(rows, subs))]
        places = [(dx, 0) for dx in range(1, rows)] + [(0, dc) for dc in range(1, subs)]
        formed = products(places, activations, [])
        for_rows, for_cores = formed[: rows - 1], formed[rows - 1 :]
        from_cores = [sub_shift(m, dc + 1) for dc, m in enumerate(for_cores)]
        *outs, gram = call(
            functools.partial(core_kernel, rows - 1, rank),
            list(for_rows) + [h_gram] + got,
            [msg] * (rows - 1) + [((rank, rank), F32)],
        )
        from_rows = [row_shift(m, dx + 1) for dx, m in enumerate(outs)]
        (own,) = products([(0, 0)], activations, outs)
        (part,) = call(functools.partial(row_kernel, subs), [own, gram] + from_cores + from_rows, [msg])
        return [part] + [frm_shift(part, shift) for shift in reversed(range(1, frms))]

    activations, h_gram, *msgs = call(
        functools.partial(first_kernel, rows, subs, cl),
        w_msgs + [early, vmem(old), spectra],
        update_outs,
        [pltpu.VMEM((rank, frames), F32)],
        limit=8,
    )
    piled = [pltpu.VMEM((frms,) + msg[0], BF16)]
    w_piece, w_msg = call(
        functools.partial(update_kernel, frms),
        [w_piece] + gathered(activations, h_gram, msgs),
        [piece, msg],
        piled,
    )
    w_msgs = [w_msg] + [sub_shift(w_msg, dc) for dc in range(1, subs)]
    w_pieces = pltpu.VMEM((1, subs, rank, size), BF16)
    (early,) = call(
        functools.partial(early_kernel, rows, subs, cl),
        w_msgs + [spectra],
        [((rank, frames), F32)],
        [w_pieces],
        cost=16 * NF * cl * frames * rank,
    )
    from_rows = [row_shift(w_msg, dx) for dx in range(1, rows)]
    *from_rows, early = lax.optimization_barrier((*from_rows, early))
    (middle,) = call(
        functools.partial(middle_kernel, rows, subs, cl),
        from_rows + [early, spectra],
        [((rank, frames), F32)],
        cost=16 * NF * cl * frames * rank // subs,
    )
    for base in from_rows:
        w_msgs += [base] + [sub_shift(base, dc) for dc in range(1, subs)]
    activations, h_gram, *msgs = call(
        functools.partial(later_kernel, rows, subs, cl),
        w_msgs + [middle, activations, spectra],
        update_outs,
        [pltpu.VMEM((rank, frames), F32)],
        limit=8,
    )
    parts = gathered(activations, h_gram, msgs)
    activations, parts[0] = lax.optimization_barrier((activations, parts[0]))
    sides = [activations] + [row_shift(activations, shift) for shift in range(1, rows)]
    (part,) = call(
        functools.partial(last_kernel, frms), [w_piece, order] + parts, [((rank, NF * cl), F32)], piled
    )
    (wide,) = call(
        functools.partial(join_kernel, rows),
        sides,
        [pltpu.HBM((rank, window), F32)],
        [pltpu.SemaphoreType.DMA((rows,))],
        in_specs=[anywhere] * rows,
        out_specs=[anywhere],
    )
    (synergies,) = call(
        sum_kernel,
        [hbm(wide), part] + [sub_shift(part, dc) for dc in range(1, subs)],
        [pltpu.HBM((rank, NF * cl), F32)],
        [pltpu.VMEM((rank, NF * cl), F32), pltpu.SemaphoreType.DMA],
        in_specs=[anywhere] + [whole] * subs,
        out_specs=[anywhere],
    )
    return (synergies.T, wide)


def solution(mesh):
    placed = (P("row", ("grp", "frm", "sub")), P("row", None), P(None, ("grp", "frm", "sub")))
    return jax.shard_map(
        shards,
        mesh=mesh,
        in_specs=placed,
        out_specs=(P(("grp", "row"), None), P(None, ("grp", "frm", "sub"))),
        check_vma=False,
    )
```

```python
import functools
import math

import jax
import jax.numpy as jnp
import ml_dtypes
import numpy as np
from jax import lax
from jax.experimental import pallas as pl
from jax.experimental.pallas import tpu as pltpu
from jax.sharding import PartitionSpec as P

NF = 40
TAPS = 128
HALF = TAPS // 2
LANES = 128
CUTS = (0, 2, 8, 16, 24, 32, NF)
F32 = jnp.float32
BF16 = jnp.bfloat16
HIGH = lax.Precision.HIGHEST
NT = (((1,), (1,)), ((), ()))
MIB = 1024 * 1024


def wavelets():
    f = np.float32
    level = np.arange(NF, dtype=f) / f(NF - 1)
    freq = f(2.0) * np.power(f(12.0), level)
    sigma = f(7.0) / (f(2.0 * math.pi) * freq)
    times = (np.arange(TAPS, dtype=f) - f(HALF)) / f(50.0)
    env = np.exp(-(times[None, :] ** 2) / (f(2.0) * sigma[:, None] ** 2))
    scale = f(1.0) / np.sqrt(np.sum(env * env, axis=1))
    env = env * scale[:, None]
    phase = f(2.0 * math.pi) * freq[:, None] * times[None, :]
    return np.stack([env * np.cos(phase), env * np.sin(phase)]).astype(ml_dtypes.bfloat16)


def toeplitz():
    kernel = wavelets()
    table = np.zeros((NF, 2 * TAPS, 2 * TAPS), ml_dtypes.bfloat16)
    for at in range(TAPS):
        for part in range(2):
            table[:, at : at + TAPS, part * TAPS + at] = kernel[part]
    return table


def split_two(value):
    top = value.astype(BF16)
    return top, (value - top.astype(F32)).astype(BF16)


def message(rank, size):
    return (rank * -(-size // LANES) + rank // 2, LANES)


def pack(out_ref, main, gram):
    rank, size = main.shape
    half = rank // 2
    for at in range(0, size, LANES):
        line = at // LANES * rank
        width = min(LANES, size - at)
        out_ref[line : line + rank, :width] = main[:, at : at + width].astype(BF16)
    top, rest = split_two(gram)
    terms = [top[:half], top[half:], rest[:half], rest[half:]]
    line = out_ref.shape[0] - half
    for at, term in enumerate(terms):
        out_ref[line:, at * rank : (at + 1) * rank] = term


def body(value, rank, size):
    parts = []
    for at in range(0, size, LANES):
        line = at // LANES * rank
        parts.append(value[line : line + rank, : min(LANES, size - at)])
    return jnp.concatenate(parts, axis=1)


def gram_of(value, rank):
    last = value[value.shape[0] - rank // 2 :, :].astype(F32)
    total = last[:, : 2 * rank] + last[:, 2 * rank : 4 * rank]
    return jnp.concatenate([total[:, :rank], total[:, rank:]], axis=0)


def reorder_kernel(w_ref, order_ref, *refs):
    piece_ref, msg_ref = refs[-2:]
    w = w_ref[...]
    rank, size = piece_ref.shape
    gram = lax.dot_general(w, w, NT, precision=HIGH, preferred_element_type=F32)
    moved = jnp.dot(three_terms(w), order_ref[...], preferred_element_type=F32)
    whole = moved[:rank] + (moved[rank : 2 * rank] + moved[2 * rank :])
    for c in range(w.shape[1] // size):

        @pl.when(lax.axis_index("sub") == c)
        def _():
            piece_ref[...] = whole[:, c * size : (c + 1) * size]

    pack(msg_ref, whole, gram)


def three_terms(value):
    top = value.astype(BF16)
    rest = value - top.astype(F32)
    middle = rest.astype(BF16)
    return jnp.concatenate([top, middle, (rest - middle.astype(F32)).astype(BF16)], axis=0)


def edges_kernel(rows, sig_ref, *refs):
    got_refs, out_ref = refs[: rows - 1], refs[-1]
    cl, width = sig_ref.shape
    x_me = lax.axis_index("row")
    for at, ref in enumerate((sig_ref,) + tuple(got_refs)):

        @pl.when(x_me == 0)
        def _():
            out_ref[at * cl : (at + 1) * cl, :] = ref[:, :TAPS]

        @pl.when(x_me > 0)
        def _():
            out_ref[at * cl : (at + 1) * cl, :] = ref[:, width - TAPS :]


def window_of(shift, rows, frames, width, window):
    target = lax.rem(lax.axis_index("row") + shift, rows)
    return pl.ds(pl.multiple_of(jnp.clip(target * frames - TAPS, 0, window - width), TAPS), width)


def cut_kernel(rows, frames, sig_hbm, *refs):
    out_refs, sems = refs[:-1], refs[-1]
    copies = []
    for at, ref in enumerate(out_refs):
        span = window_of(at + 1, rows, frames, ref.shape[1], sig_hbm.shape[1])
        copies.append(pltpu.make_async_copy(sig_hbm.at[:, span], ref, sems.at[at]))
    for copy in copies:
        copy.start()
    for copy in copies:
        copy.wait()


def pair_rows(s_ref, span, pair, x, cl):
    halves = [s_ref[span, blk, x].reshape(-1, TAPS) for blk in (2 * pair, 2 * pair + 1)]
    return jnp.concatenate(halves, axis=1)


def numerators(parts, s_ref, num_ref, cl):
    for pair in range(num_ref.shape[1] // (2 * TAPS)):
        terms = [
            jnp.dot(w, pair_rows(s_ref, slice(None), pair, x, cl), preferred_element_type=F32) for w, x in parts
        ]
        num_ref[:, 2 * TAPS * pair : 2 * TAPS * (pair + 1)] = functools.reduce(jnp.add, terms)


def crossed(low, s_ref, places, subs, cl):
    count = NF // subs
    acc = jnp.zeros((low.shape[0], len(places) * count * cl), F32)
    for pair in range(low.shape[1] // (2 * TAPS)):
        cols = slice(2 * TAPS * pair, 2 * TAPS * (pair + 1))
        parts = [pair_rows(s_ref, pl.ds(core * count, count), pair, x, cl) for x, core in places]
        acc = acc + lax.dot_general(
            low[:, cols], jnp.concatenate(parts, axis=0), NT, preferred_element_type=F32
        )
    return acc


def others_of(rows, subs):
    return [(dx, dc) for dx in range(1, rows) for dc in range(1, subs)]


def new_activations(old, gram, above, s_ref, h_out, h_gram_ref, msg_refs, rows, subs, cl):
    new = old * above / jnp.dot(gram, old, precision=HIGH, preferred_element_type=F32)
    h_out[...] = new
    h_gram = lax.dot_general(new, new, NT, precision=HIGH, preferred_element_type=F32)
    h_gram_ref[...] = h_gram
    size = NF // subs * cl
    x_me, c_me = lax.axis_index("row"), lax.axis_index("sub")
    for ref, (dx, dc) in zip(msg_refs, others_of(rows, subs)):
        target = (lax.rem(x_me + dx, rows), lax.rem(c_me + dc, subs))
        ref[:, :size] = crossed(new.astype(BF16), s_ref, [target], subs, cl)
        ref[:, size:] = h_gram


def products_kernel(places, rows, subs, cl, h_ref, s_ref, *refs):
    x_me, c_me = lax.axis_index("row"), lax.axis_index("sub")
    low = h_ref[...].astype(BF16)
    targets = [(lax.rem(x_me + dx, rows), lax.rem(c_me + dc, subs)) for dx, dc in places]
    acc = crossed(low, s_ref, targets, subs, cl)
    size = acc.shape[1] // len(places)
    for at, ref in enumerate(refs[len(refs) - len(places) :]):
        ref[...] = acc[:, at * size : (at + 1) * size]


def place_signal(source, target, rows, frames):
    x_me = lax.axis_index("row")
    width = source.shape[1]

    @pl.when(x_me == 0)
    def _():
        target[:, HALF:] = source[:, : frames + HALF]

    @pl.when(x_me == rows - 1)
    def _():
        target[:, : frames + HALF] = source[:, width - frames - HALF :]

    if rows > 2:

        @pl.when((x_me > 0) & (x_me < rows - 1))
        def _():
            target[...] = source[:, HALF : HALF + frames + TAPS]


def power_of(x_ref, table):
    co = jnp.dot(x_ref[...], table, preferred_element_type=F32)
    return (co[:, :TAPS] * co[:, :TAPS] + co[:, TAPS:] * co[:, TAPS:]).astype(BF16)


def own_spectra_kernel(rows, sig_hbm, w_hbm, h_hbm, order_hbm, tab_hbm, *refs):
    s_ref, sig_ref, w_ref, old_ref, order_ref, tab_ref, xp_scr, x_scr, sems, tab_sems = refs
    _, blocks, _, cl, _ = s_ref.shape
    frames = blocks * TAPS
    x_me = lax.axis_index("row")
    mine = pl.ds(pl.multiple_of(x_me * frames, TAPS), frames)

    table = [
        pltpu.make_async_copy(tab_hbm.at[begin:end], tab_ref.at[begin:end], tab_sems.at[at])
        for at, (begin, end) in enumerate(zip(CUTS, CUTS[1:]))
    ]
    later = [
        pltpu.make_async_copy(w_hbm, w_ref, sems.at[0]),
        pltpu.make_async_copy(order_hbm, order_ref, sems.at[1]),
        pltpu.make_async_copy(h_hbm.at[:, mine], old_ref, sems.at[2]),
    ]
    own_span = window_of(0, rows, frames, sig_ref.shape[1], sig_hbm.shape[1])
    own_copy = pltpu.make_async_copy(sig_hbm.at[:, own_span], sig_ref, sems.at[3])
    own_copy.start()
    for copy in table:
        copy.start()
    own_copy.wait()
    place_signal(sig_ref, xp_scr, rows, frames)
    first = jnp.where(x_me == 0, 1, 0)
    for at in range(blocks - 1):
        begin = pl.multiple_of((first + at) * TAPS, TAPS)
        x_scr[at * cl : (at + 1) * cl, :] = xp_scr[:, pl.ds(begin, 2 * TAPS)]

    for f in range(NF):
        if f in CUTS:
            table[CUTS.index(f)].wait()
        if f == CUTS[3]:
            for copy in later:
                copy.start()
        power = power_of(x_scr, tab_ref[f])
        s_ref[f, pl.ds(first, blocks - 1), x_me] = power.reshape(blocks - 1, cl, TAPS)
    for copy in later:
        copy.wait()


def other_spectra_kernel(rows, halo_ref, tab_ref, *refs):
    sig_refs, (s_ref, xp_scr, x_scr) = refs[:rows], refs[-3:]
    _, blocks, _, cl, _ = s_ref.shape
    frames = blocks * TAPS
    x_me = lax.axis_index("row")
    owners = [lax.rem(x_me + rows - shift, rows) for shift in range(rows)]
    for shift in range(rows):
        place_signal(sig_refs[shift], xp_scr.at[owners[shift]], rows, frames)

    @pl.when(x_me == 0)
    def _():
        for at in range(rows):
            xp_scr[rows - 1 - at, :, :HALF] = halo_ref[at * cl : (at + 1) * cl, HALF:]

    @pl.when(x_me == rows - 1)
    def _():
        for at in range(rows):
            xp_scr[(rows - at) % rows, :, frames + HALF :] = halo_ref[at * cl : (at + 1) * cl, :HALF]

    outer = jnp.where(x_me == 0, 0, blocks - 1)
    begin = pl.multiple_of(outer * TAPS, TAPS)
    x_scr[:cl, :] = xp_scr[x_me, :, pl.ds(begin, 2 * TAPS)]
    for shift in range(1, rows):
        for blk in range(blocks):
            at = cl * (1 + (shift - 1) * blocks + blk)
            x_scr[at : at + cl, :] = xp_scr[owners[shift], :, blk * TAPS : (blk + 2) * TAPS]

    for f in range(NF):
        power = power_of(x_scr, tab_ref[f])
        s_ref[f, outer, x_me] = power[:cl]
        for shift in range(1, rows):
            line = cl * (1 + (shift - 1) * blocks)
            s_ref[f, :, owners[shift]] = power[line : line + blocks * cl].reshape(blocks, cl, TAPS)


def outer_pair(pairs):
    return jnp.where(lax.axis_index("row") == 0, 0, pairs - 1)


def pair_columns(pair):
    return pl.ds(pl.multiple_of(pair * 2 * TAPS, 2 * TAPS), 2 * TAPS)


def first_early_kernel(cl, w_ref, s_ref, num_ref):
    rank, frames = num_ref.shape
    pairs = frames // (2 * TAPS)
    x_me = lax.axis_index("row")
    w = body(w_ref[...], rank, NF * cl)
    num_ref[:, pair_columns(outer_pair(pairs))] = jnp.zeros((rank, 2 * TAPS), F32)
    for at in range(pairs - 1):
        pair = at + jnp.where(x_me == 0, 1, 0)
        rows_of = pair_rows(s_ref, slice(None), pair, x_me, cl)
        num_ref[:, pair_columns(pair)] = jnp.dot(w, rows_of, preferred_element_type=F32)


def first_kernel(rows, subs, cl, *refs):
    refs = list(refs)
    w_refs = [refs.pop(0) for _ in range(rows)]
    early_ref, h_ref, s_ref, h_out, h_gram_ref = (refs.pop(0) for _ in range(5))
    msg_refs, num_scr = refs[:-1], refs[-1]
    rank, frames = h_ref.shape
    x_me = lax.axis_index("row")
    parts, gram = [], jnp.zeros(h_gram_ref.shape, F32)
    for shift, ref in enumerate(w_refs):
        parts.append((body(ref[...], rank, NF * cl), lax.rem(x_me + rows - shift, rows)))
        gram = gram + gram_of(ref[...], rank)
    if rows > 1:
        numerators(parts[1:], s_ref, num_scr, cl)
    else:
        num_scr[...] = jnp.zeros_like(num_scr)
    outer = outer_pair(frames // (2 * TAPS))
    num_scr[:, pair_columns(outer)] += jnp.dot(
        parts[0][0], pair_rows(s_ref, slice(None), outer, x_me, cl), preferred_element_type=F32
    )
    above = early_ref[...] + num_scr[...]
    new_activations(h_ref[...], gram, above, s_ref, h_out, h_gram_ref, msg_refs, rows, subs, cl)


def row_parts(rows, subs, cl, w_refs, w_scr, shifts):
    x_me, c_me = lax.axis_index("row"), lax.axis_index("sub")
    size = NF // subs * cl
    parts = []
    for line, dx in enumerate(shifts):
        for dc in range(subs):
            piece = body(w_refs[line * subs + dc][...], w_scr.shape[2], size)
            w_scr[line, lax.rem(c_me + subs - dc, subs)] = piece
        w = jnp.concatenate([w_scr[line, c] for c in range(subs)], axis=1)
        parts.append((w, lax.rem(x_me + rows - dx, rows)))
    return parts


def early_kernel(rows, subs, cl, *refs):
    w_refs, (s_ref, num_ref, w_scr) = refs[:subs], refs[subs:]
    numerators(row_parts(rows, subs, cl, w_refs, w_scr, [0]), s_ref, num_ref, cl)


def add_pieces(base_ref, pieces, s_ref, out_ref, rows, subs, cl):
    rank, frames = out_ref.shape
    count = NF // subs
    x_me, c_me = lax.axis_index("row"), lax.axis_index("sub")
    terms = []
    for ref, dx, dc in pieces:
        core = lax.rem(c_me + subs - dc, subs)
        terms.append((body(ref[...], rank, count * cl), lax.rem(x_me + rows - dx, rows), core))
    for pair in range(frames // (2 * TAPS)):
        cols = slice(2 * TAPS * pair, 2 * TAPS * (pair + 1))
        acc = base_ref[:, cols]
        for w, x, core in terms:
            spectra = pair_rows(s_ref, pl.ds(core * count, count), pair, x, cl)
            acc = acc + jnp.dot(w, spectra, preferred_element_type=F32)
        out_ref[:, cols] = acc


def middle_kernel(rows, subs, cl, *refs):
    w_refs, (base_ref, s_ref, out_ref) = refs[:-3], refs[-3:]
    pieces = [(ref, dx + 1, 0) for dx, ref in enumerate(w_refs)]
    add_pieces(base_ref, pieces, s_ref, out_ref, rows, subs, cl)


def later_kernel(rows, subs, cl, *refs):
    refs = list(refs)
    w_refs = [refs.pop(0) for _ in range(rows * subs)]
    middle_ref, h_ref, s_ref, h_out, h_gram_ref = (refs.pop(0) for _ in range(5))
    msg_refs, num_scr = refs[:-1], refs[-1]
    gram = jnp.zeros(h_gram_ref.shape, F32)
    for ref in w_refs:
        gram = gram + gram_of(ref[...], h_ref.shape[0])
    pieces = [(w_refs[dx * subs + dc], dx, dc) for dx in range(1, rows) for dc in range(1, subs)]
    add_pieces(middle_ref, pieces, s_ref, num_scr, rows, subs, cl)
    new_activations(h_ref[...], gram, num_scr[...], s_ref, h_out, h_gram_ref, msg_refs, rows, subs, cl)


def core_kernel(count, rank, *refs):
    own_refs, gram_ref, got_refs = refs[:count], refs[count], refs[count + 1 : -count - 1]
    out_refs, total_ref = refs[-count - 1 : -1], refs[-1]
    size = own_refs[0].shape[1]
    each = len(got_refs) // count
    gram = gram_ref[...]
    for ref in got_refs[:each]:
        gram = gram + ref[:, size:]
    total_ref[...] = gram
    for at in range(count):
        total = own_refs[at][...]
        for ref in got_refs[at * each : (at + 1) * each]:
            total = total + ref[:, :size]
        pack(out_refs[at], total, gram)


def row_kernel(subs, own_ref, gram_ref, *refs):
    core_refs, msg_refs, out_ref = refs[: subs - 1], refs[subs - 1 : -1], refs[-1]
    rank, size = own_ref.shape
    total, gram = own_ref[...], gram_ref[...]
    for ref in core_refs:
        total = total + ref[...]
    for ref in msg_refs:
        total = total + body(ref[...], rank, size).astype(F32)
        gram = gram + gram_of(ref[...], rank)
    pack(out_ref, total, gram)


def summed(z_me, count, msg_refs, scr, rank, size):
    for at, shift in enumerate([0, *reversed(range(1, count))]):
        scr[partner(z_me, shift, count)] = msg_refs[at][...]
    total, gram = body(scr[0], rank, size).astype(F32), gram_of(scr[0], rank)
    for at in range(1, count):
        total = total + body(scr[at], rank, size).astype(F32)
        gram = gram + gram_of(scr[at], rank)
    return total, gram


def partner(place, shift, count):
    if count & (count - 1):
        return (place + count - shift) % count
    return place ^ shift


def update_kernel(count, w_ref, *refs):
    msg_refs, (new_ref, out_ref, scr) = refs[:count], refs[count:]
    rank, size = new_ref.shape
    total, gram = summed(lax.axis_index("frm"), count, msg_refs, scr, rank, size)
    w = w_ref[...]
    new = w * total / jnp.dot(gram, w, precision=HIGH, preferred_element_type=F32)
    new_ref[...] = new
    pack(out_ref, new, lax.dot_general(new, new, NT, precision=HIGH, preferred_element_type=F32))


def last_kernel(count, w_ref, order_ref, *refs):
    msg_refs, (out_ref, scr) = refs[:count], refs[count:]
    rank, size = w_ref.shape
    total, gram = summed(lax.axis_index("frm"), count, msg_refs, scr, rank, size)
    w = w_ref[...]
    new = w * total / jnp.dot(gram, w, precision=HIGH, preferred_element_type=F32)
    terms = three_terms(new)
    for c in range(order_ref.shape[1] // size):

        @pl.when(lax.axis_index("sub") == c)
        def _():
            moved = lax.dot_general(
                terms, order_ref[:, c * size : (c + 1) * size], NT, preferred_element_type=F32
            )
            out_ref[...] = moved[:rank] + (moved[rank : 2 * rank] + moved[2 * rank :])


def join_kernel(rows, *refs):
    act_refs, (out_ref, sems) = refs[:rows], refs[rows:]
    frames = act_refs[0].shape[1]
    x_me = lax.axis_index("row")
    copies = []
    for shift in range(rows):
        begin = pl.multiple_of(lax.rem(x_me + rows - shift, rows) * frames, TAPS)
        copies.append(pltpu.make_async_copy(act_refs[shift], out_ref.at[:, pl.ds(begin, frames)], sems.at[shift]))
    for copy in copies:
        copy.start()
    for copy in copies:
        copy.wait()


def sum_kernel(_, *refs):
    parts, (out_ref, scr, sem) = refs[:-3], refs[-3:]
    total = parts[0][...]
    for part in parts[1:]:
        total = total + part[...]
    scr[...] = total
    copy = pltpu.make_async_copy(scr, out_ref, sem)
    copy.start()
    copy.wait()


def call(kernel, args, outs, scratch=(), in_specs=None, out_specs=None, limit=4, cost=None, aliases=None):
    whole = pl.BlockSpec(memory_space=pltpu.VMEM)
    if cost is not None:
        cost = pl.CostEstimate(flops=cost, bytes_accessed=0, transcendentals=0)
    return pl.pallas_call(
        kernel,
        out_shape=[jax.ShapeDtypeStruct(*out) if isinstance(out, tuple) else out for out in outs],
        in_specs=in_specs or [whole] * len(args),
        out_specs=out_specs or [whole] * len(outs),
        scratch_shapes=list(scratch),
        compiler_params=pltpu.CompilerParams(vmem_limit_bytes=limit * MIB),
        cost_estimate=cost,
        input_output_aliases=aliases or {},
    )(*args)


def reorder(cl):
    order = np.zeros((cl, NF, NF, cl), ml_dtypes.bfloat16)
    chans, freqs = np.meshgrid(np.arange(cl), np.arange(NF), indexing="ij")
    order[chans, freqs, freqs, chans] = 1
    return order.reshape(cl * NF, NF * cl)


def shards(signal, w_start, h_start):
    rows, subs, frms = (lax.axis_size(axis) for axis in ("row", "sub", "frm"))
    x_me = lax.axis_index("row")
    cl, window = signal.shape
    rank = w_start.shape[1]
    frames = window // rows
    blocks = frames // TAPS
    chans = rows * cl
    size = NF * cl // subs
    line = frms * subs
    width = frames + (TAPS if rows == 2 else 2 * TAPS)
    anywhere = pl.BlockSpec(memory_space=pl.ANY)
    whole = pl.BlockSpec(memory_space=pltpu.VMEM)

    def hbm(value):
        return pltpu.with_memory_space_constraint(value, pltpu.HBM)

    def vmem(value):
        return pltpu.with_memory_space_constraint(value, pltpu.VMEM)

    def row_shift(value, shift):
        return lax.ppermute(value, "row", [(i, (i + shift) % rows) for i in range(rows)])

    def sub_shift(value, shift):
        return lax.ppermute(value, "sub", [(i, (i + shift) % subs) for i in range(subs)])

    def frm_shift(value, shift):
        return lax.ppermute(value, "frm", [(partner(i, shift, frms), i) for i in range(frms)])

    def place(x, at):
        return (at // subs * rows + x) * subs + at % subs

    table, order = hbm(jnp.asarray(toeplitz())), jnp.asarray(reorder(cl))
    cuts = call(
        functools.partial(cut_kernel, rows, frames),
        [hbm(signal)],
        [((cl, width), BF16)] * (rows - 1),
        [pltpu.SemaphoreType.DMA((rows,))],
        in_specs=[anywhere],
    )
    sig = [row_shift(part, shift + 1) for shift, part in enumerate(cuts)]

    msg = (message(rank, size), BF16)
    piece = ((rank, size), F32)
    update_outs = [((rank, frames), F32), ((rank, rank), F32)]
    update_outs += [((rank, size + rank), F32)] * ((rows - 1) * (subs - 1))
    half_done, own_sig, w_own, old, order, table = call(
        functools.partial(own_spectra_kernel, rows),
        [hbm(signal), hbm(w_start.T), hbm(h_start), hbm(order), table],
        [
            pltpu.VMEM((NF, blocks, rows, cl, TAPS), BF16),
            pltpu.VMEM((cl, width), BF16),
            pltpu.VMEM((rank, NF * cl), F32),
            pltpu.VMEM((rank, frames), F32),
            pltpu.VMEM(order.shape, BF16),
            pltpu.VMEM(table.shape, BF16),
        ],
        [
            pltpu.VMEM((cl, frames + TAPS), BF16),
            pltpu.VMEM(((blocks - 1) * cl, 2 * TAPS), BF16),
            pltpu.SemaphoreType.DMA((4,)),
            pltpu.SemaphoreType.DMA((len(CUTS) - 1,)),
        ],
        in_specs=[anywhere] * 5,
        limit=8,
        cost=2 * NF * cl * frames * 4 * TAPS,
    )
    order, sig = vmem(order), [vmem(own_sig)] + sig
    (edge,) = call(
        functools.partial(edges_kernel, rows),
        sig + [vmem(half_done)],
        [((chans, TAPS), BF16)],
        in_specs=[whole] * rows + [anywhere],
    )
    pairs = [(place(rows - 1, i), place(0, i + 1)) for i in range(line - 1)]
    halo = lax.ppermute(edge, ("frm", "row", "sub"), pairs + [(b, a) for a, b in pairs])
    w_piece, w_msg = call(
        reorder_kernel,
        [vmem(w_own), order, edge],
        [piece, (message(rank, NF * cl), BF16)],
        in_specs=[whole, whole, anywhere],
    )
    w_msgs = [w_msg] + [row_shift(w_msg, shift) for shift in range(1, rows)]
    (early,) = call(
        functools.partial(first_early_kernel, cl),
        [w_msg, vmem(half_done)],
        [((rank, frames), F32)],
        cost=16 * NF * cl * frames * rank,
    )
    (spectra,) = call(
        functools.partial(other_spectra_kernel, rows),
        [halo, vmem(table)] + sig + [vmem(half_done), early],
        [pltpu.VMEM((NF, blocks, rows, cl, TAPS), BF16)],
        [
            pltpu.VMEM((rows, cl, frames + TAPS), BF16),
            pltpu.VMEM((((rows - 1) * blocks + 1) * cl, 2 * TAPS), BF16),
        ],
        in_specs=[whole] * (rows + 2) + [anywhere] * 2,
        limit=8,
        cost=2 * NF * chans * frames * 4 * TAPS,
        aliases={rows + 2: 0},
    )
    spectra = vmem(spectra)

    def products(places, activations, after):
        return call(
            functools.partial(products_kernel, places, rows, subs, cl),
            [activations, spectra] + after,
            [piece] * len(places),
            in_specs=[whole] * 2 + [anywhere] * len(after),
            cost=1 if after else 16 * NF * cl * frames * rank // subs * len(places),
        )

    def gathered(activations, h_gram, msgs):
        got = [sub_shift(m, dc) for m, (_, dc) in zip(msgs, others_of(rows, subs))]
        places = [(dx, 0) for dx in range(1, rows)] + [(0, dc) for dc in range(1, subs)]
        formed = products(places, activations, [])
        for_rows, for_cores = formed[: rows - 1], formed[rows - 1 :]
        from_cores = [sub_shift(m, dc + 1) for dc, m in enumerate(for_cores)]
        *outs, gram = call(
            functools.partial(core_kernel, rows - 1, rank),
            list(for_rows) + [h_gram] + got,
            [msg] * (rows - 1) + [((rank, rank), F32)],
        )
        from_rows = [row_shift(m, dx + 1) for dx, m in enumerate(outs)]
        (own,) = products([(0, 0)], activations, outs)
        (part,) = call(functools.partial(row_kernel, subs), [own, gram] + from_cores + from_rows, [msg])
        return [part] + [frm_shift(part, shift) for shift in reversed(range(1, frms))]

    activations, h_gram, *msgs = call(
        functools.partial(first_kernel, rows, subs, cl),
        w_msgs + [early, vmem(old), spectra],
        update_outs,
        [pltpu.VMEM((rank, frames), F32)],
        limit=8,
    )
    piled = [pltpu.VMEM((frms,) + msg[0], BF16)]
    w_piece, w_msg = call(
        functools.partial(update_kernel, frms),
        [w_piece] + gathered(activations, h_gram, msgs),
        [piece, msg],
        piled,
    )
    w_msgs = [w_msg] + [sub_shift(w_msg, dc) for dc in range(1, subs)]
    w_pieces = pltpu.VMEM((1, subs, rank, size), BF16)
    (early,) = call(
        functools.partial(early_kernel, rows, subs, cl),
        w_msgs + [spectra],
        [((rank, frames), F32)],
        [w_pieces],
        cost=16 * NF * cl * frames * rank,
    )
    from_rows = [row_shift(w_msg, dx) for dx in range(1, rows)]
    *from_rows, early = lax.optimization_barrier((*from_rows, early))
    (middle,) = call(
        functools.partial(middle_kernel, rows, subs, cl),
        from_rows + [early, spectra],
        [((rank, frames), F32)],
        cost=16 * NF * cl * frames * rank // subs,
    )
    for base in from_rows:
        w_msgs += [base] + [sub_shift(base, dc) for dc in range(1, subs)]
    activations, h_gram, *msgs = call(
        functools.partial(later_kernel, rows, subs, cl),
        w_msgs + [middle, activations, spectra],
        update_outs,
        [pltpu.VMEM((rank, frames), F32)],
        limit=8,
    )
    parts = gathered(activations, h_gram, msgs)
    activations, parts[0] = lax.optimization_barrier((activations, parts[0]))
    sides = [activations] + [row_shift(activations, shift) for shift in range(1, rows)]
    (part,) = call(
        functools.partial(last_kernel, frms), [w_piece, order] + parts, [((rank, NF * cl), F32)], piled
    )
    (wide,) = call(
        functools.partial(join_kernel, rows),
        sides,
        [pltpu.HBM((rank, window), F32)],
        [pltpu.SemaphoreType.DMA((rows,))],
        in_specs=[anywhere] * rows,
        out_specs=[anywhere],
    )
    (synergies,) = call(
        sum_kernel,
        [hbm(wide), part] + [sub_shift(part, dc) for dc in range(1, subs)],
        [pltpu.HBM((rank, NF * cl), F32)],
        [pltpu.VMEM((rank, NF * cl), F32), pltpu.SemaphoreType.DMA],
        in_specs=[anywhere] + [whole] * subs,
        out_specs=[anywhere],
    )
    return (synergies.T, wide)


def solution(mesh):
    placed = (P("row", ("grp", "frm", "sub")), P("row", None), P(None, ("grp", "frm", "sub")))
    return jax.shard_map(
        shards,
        mesh=mesh,
        in_specs=placed,
        out_specs=(P(("grp", "row"), None), P(None, ("grp", "frm", "sub"))),
        check_vma=False,
    )
```

```python
import functools
import math

import jax
import jax.numpy as jnp
import ml_dtypes
import numpy as np
from jax import lax
from jax.experimental import pallas as pl
from jax.experimental.pallas import tpu as pltpu
from jax.sharding import PartitionSpec as P

NF = 40
TAPS = 128
HALF = TAPS // 2
LANES = 128
CUTS = (4, 8, 16, 24, 32, NF)
AHEAD = CUTS[0]
F32 = jnp.float32
BF16 = jnp.bfloat16
HIGH = lax.Precision.HIGHEST
NT = (((1,), (1,)), ((), ()))
MIB = 1024 * 1024


def wavelets():
    f = np.float32
    level = np.arange(NF, dtype=f) / f(NF - 1)
    freq = f(2.0) * np.power(f(12.0), level)
    sigma = f(7.0) / (f(2.0 * math.pi) * freq)
    times = (np.arange(TAPS, dtype=f) - f(HALF)) / f(50.0)
    env = np.exp(-(times[None, :] ** 2) / (f(2.0) * sigma[:, None] ** 2))
    scale = f(1.0) / np.sqrt(np.sum(env * env, axis=1))
    env = env * scale[:, None]
    phase = f(2.0 * math.pi) * freq[:, None] * times[None, :]
    return np.stack([env * np.cos(phase), env * np.sin(phase)]).astype(ml_dtypes.bfloat16)


def toeplitz():
    kernel = wavelets()
    table = np.zeros((NF, 2 * TAPS, 2 * TAPS), ml_dtypes.bfloat16)
    for at in range(TAPS):
        for part in range(2):
            table[:, at : at + TAPS, part * TAPS + at] = kernel[part]
    return table


def split_two(value):
    top = value.astype(BF16)
    return top, (value - top.astype(F32)).astype(BF16)


def message(rank, size):
    return (rank * -(-size // LANES) + rank // 2, LANES)


def pack(out_ref, main, gram):
    rank, size = main.shape
    half = rank // 2
    for at in range(0, size, LANES):
        line = at // LANES * rank
        width = min(LANES, size - at)
        out_ref[line : line + rank, :width] = main[:, at : at + width].astype(BF16)
    top, rest = split_two(gram)
    terms = [top[:half], top[half:], rest[:half], rest[half:]]
    line = out_ref.shape[0] - half
    for at, term in enumerate(terms):
        out_ref[line:, at * rank : (at + 1) * rank] = term


def body(value, rank, size):
    parts = []
    for at in range(0, size, LANES):
        line = at // LANES * rank
        parts.append(value[line : line + rank, : min(LANES, size - at)])
    return jnp.concatenate(parts, axis=1)


def gram_of(value, rank):
    last = value[value.shape[0] - rank // 2 :, :].astype(F32)
    total = last[:, : 2 * rank] + last[:, 2 * rank : 4 * rank]
    return jnp.concatenate([total[:, :rank], total[:, rank:]], axis=0)


def reorder_kernel(w_ref, order_ref, *refs):
    piece_ref, msg_ref = refs[-2:]
    w = w_ref[...]
    rank, size = piece_ref.shape
    gram = lax.dot_general(w, w, NT, precision=HIGH, preferred_element_type=F32)
    moved = jnp.dot(three_terms(w), order_ref[...], preferred_element_type=F32)
    whole = moved[:rank] + (moved[rank : 2 * rank] + moved[2 * rank :])
    for c in range(w.shape[1] // size):

        @pl.when(lax.axis_index("sub") == c)
        def _():
            piece_ref[...] = whole[:, c * size : (c + 1) * size]

    pack(msg_ref, whole, gram)


def three_terms(value):
    top = value.astype(BF16)
    rest = value - top.astype(F32)
    middle = rest.astype(BF16)
    return jnp.concatenate([top, middle, (rest - middle.astype(F32)).astype(BF16)], axis=0)


def edges_kernel(rows, sig_ref, *refs):
    got_refs, out_ref = refs[: rows - 1], refs[-1]
    cl, width = sig_ref.shape
    x_me = lax.axis_index("row")
    for at, ref in enumerate((sig_ref,) + tuple(got_refs)):

        @pl.when(x_me == 0)
        def _():
            out_ref[at * cl : (at + 1) * cl, :] = ref[:, :TAPS]

        @pl.when(x_me > 0)
        def _():
            out_ref[at * cl : (at + 1) * cl, :] = ref[:, width - TAPS :]


def cut_kernel(rows, frames, sig_hbm, tab_hbm, *refs):
    out_refs, (tab_ref, sems) = refs[:rows], refs[rows:]
    window, x_me = sig_hbm.shape[1], lax.axis_index("row")
    width = out_refs[0].shape[1]
    copies = []
    for shift in reversed(range(rows)):
        target = lax.rem(x_me + shift, rows)
        begin = pl.multiple_of(jnp.clip(target * frames - TAPS, 0, window - width), TAPS)
        copies.append(pltpu.make_async_copy(sig_hbm.at[:, pl.ds(begin, width)], out_refs[shift], sems.at[shift]))
    copies.append(pltpu.make_async_copy(tab_hbm.at[:AHEAD], tab_ref, sems.at[rows]))
    for copy in copies:
        copy.start()
    for copy in copies:
        copy.wait()


def pair_rows(s_ref, span, pair, x, cl):
    halves = [s_ref[span, blk, x].reshape(-1, TAPS) for blk in (2 * pair, 2 * pair + 1)]
    return jnp.concatenate(halves, axis=1)


def numerators(parts, s_ref, num_ref, cl):
    for pair in range(num_ref.shape[1] // (2 * TAPS)):
        terms = [
            jnp.dot(w, pair_rows(s_ref, slice(None), pair, x, cl), preferred_element_type=F32) for w, x in parts
        ]
        num_ref[:, 2 * TAPS * pair : 2 * TAPS * (pair + 1)] = functools.reduce(jnp.add, terms)


def crossed(low, s_ref, places, subs, cl):
    count = NF // subs
    acc = jnp.zeros((low.shape[0], len(places) * count * cl), F32)
    for pair in range(low.shape[1] // (2 * TAPS)):
        cols = slice(2 * TAPS * pair, 2 * TAPS * (pair + 1))
        parts = [pair_rows(s_ref, pl.ds(core * count, count), pair, x, cl) for x, core in places]
        acc = acc + lax.dot_general(
            low[:, cols], jnp.concatenate(parts, axis=0), NT, preferred_element_type=F32
        )
    return acc


def others_of(rows, subs):
    return [(dx, dc) for dx in range(1, rows) for dc in range(1, subs)]


def new_activations(old, gram, above, s_ref, h_out, h_gram_ref, msg_refs, rows, subs, cl):
    new = old * above / jnp.dot(gram, old, precision=HIGH, preferred_element_type=F32)
    h_out[...] = new
    h_gram = lax.dot_general(new, new, NT, precision=HIGH, preferred_element_type=F32)
    h_gram_ref[...] = h_gram
    size = NF // subs * cl
    x_me, c_me = lax.axis_index("row"), lax.axis_index("sub")
    for ref, (dx, dc) in zip(msg_refs, others_of(rows, subs)):
        target = (lax.rem(x_me + dx, rows), lax.rem(c_me + dc, subs))
        ref[:, :size] = crossed(new.astype(BF16), s_ref, [target], subs, cl)
        ref[:, size:] = h_gram


def products_kernel(places, rows, subs, cl, h_ref, s_ref, *refs):
    x_me, c_me = lax.axis_index("row"), lax.axis_index("sub")
    low = h_ref[...].astype(BF16)
    targets = [(lax.rem(x_me + dx, rows), lax.rem(c_me + dc, subs)) for dx, dc in places]
    acc = crossed(low, s_ref, targets, subs, cl)
    size = acc.shape[1] // len(places)
    for at, ref in enumerate(refs[len(refs) - len(places) :]):
        ref[...] = acc[:, at * size : (at + 1) * size]


def place_signal(source, target, rows, frames):
    x_me = lax.axis_index("row")
    width = source.shape[1]

    @pl.when(x_me == 0)
    def _():
        target[:, HALF:] = source[:, : frames + HALF]

    @pl.when(x_me == rows - 1)
    def _():
        target[:, : frames + HALF] = source[:, width - frames - HALF :]

    if rows > 2:

        @pl.when((x_me > 0) & (x_me < rows - 1))
        def _():
            target[...] = source[:, HALF : HALF + frames + TAPS]


def power_of(x_ref, table):
    co = jnp.dot(x_ref[...], table, preferred_element_type=F32)
    return (co[:, :TAPS] * co[:, :TAPS] + co[:, TAPS:] * co[:, TAPS:]).astype(BF16)


def table_at(f, ahead_ref, tab_ref):
    return ahead_ref[f] if f < AHEAD else tab_ref[f - AHEAD]


def own_spectra_kernel(rows, sig_ref, ahead_ref, w_hbm, h_hbm, order_hbm, tab_hbm, *refs):
    s_ref, w_ref, old_ref, order_ref, tab_ref, xp_scr, x_scr, sems, tab_sems = refs
    _, blocks, _, cl, _ = s_ref.shape
    frames = blocks * TAPS
    x_me = lax.axis_index("row")
    mine = pl.ds(pl.multiple_of(x_me * frames, TAPS), frames)

    table = [
        pltpu.make_async_copy(tab_hbm.at[begin:end], tab_ref.at[begin - AHEAD : end - AHEAD], tab_sems.at[at])
        for at, (begin, end) in enumerate(zip(CUTS, CUTS[1:]))
    ]
    later = [
        pltpu.make_async_copy(w_hbm, w_ref, sems.at[0]),
        pltpu.make_async_copy(order_hbm, order_ref, sems.at[1]),
        pltpu.make_async_copy(h_hbm.at[:, mine], old_ref, sems.at[2]),
    ]
    for copy in table:
        copy.start()
    place_signal(sig_ref, xp_scr, rows, frames)
    first = jnp.where(x_me == 0, 1, 0)
    for at in range(blocks - 1):
        begin = pl.multiple_of((first + at) * TAPS, TAPS)
        x_scr[at * cl : (at + 1) * cl, :] = xp_scr[:, pl.ds(begin, 2 * TAPS)]

    for f in range(NF):
        if f in CUTS:
            table[CUTS.index(f)].wait()
        if f == CUTS[2]:
            for copy in later:
                copy.start()
        power = power_of(x_scr, table_at(f, ahead_ref, tab_ref))
        s_ref[f, pl.ds(first, blocks - 1), x_me] = power.reshape(blocks - 1, cl, TAPS)
    for copy in later:
        copy.wait()


def other_spectra_kernel(rows, halo_ref, ahead_ref, tab_ref, *refs):
    sig_refs, (s_ref, xp_scr, x_scr) = refs[:rows], refs[-3:]
    _, blocks, _, cl, _ = s_ref.shape
    frames = blocks * TAPS
    x_me = lax.axis_index("row")
    owners = [lax.rem(x_me + rows - shift, rows) for shift in range(rows)]
    for shift in range(rows):
        place_signal(sig_refs[shift], xp_scr.at[owners[shift]], rows, frames)

    @pl.when(x_me == 0)
    def _():
        for at in range(rows):
            xp_scr[rows - 1 - at, :, :HALF] = halo_ref[at * cl : (at + 1) * cl, HALF:]

    @pl.when(x_me == rows - 1)
    def _():
        for at in range(rows):
            xp_scr[(rows - at) % rows, :, frames + HALF :] = halo_ref[at * cl : (at + 1) * cl, :HALF]

    outer = jnp.where(x_me == 0, 0, blocks - 1)
    begin = pl.multiple_of(outer * TAPS, TAPS)
    x_scr[:cl, :] = xp_scr[x_me, :, pl.ds(begin, 2 * TAPS)]
    for shift in range(1, rows):
        for blk in range(blocks):
            at = cl * (1 + (shift - 1) * blocks + blk)
            x_scr[at : at + cl, :] = xp_scr[owners[shift], :, blk * TAPS : (blk + 2) * TAPS]

    for f in range(NF):
        power = power_of(x_scr, table_at(f, ahead_ref, tab_ref))
        s_ref[f, outer, x_me] = power[:cl]
        for shift in range(1, rows):
            line = cl * (1 + (shift - 1) * blocks)
            s_ref[f, :, owners[shift]] = power[line : line + blocks * cl].reshape(blocks, cl, TAPS)


def outer_pair(pairs):
    return jnp.where(lax.axis_index("row") == 0, 0, pairs - 1)


def pair_columns(pair):
    return pl.ds(pl.multiple_of(pair * 2 * TAPS, 2 * TAPS), 2 * TAPS)


def first_early_kernel(cl, w_ref, s_ref, num_ref):
    rank, frames = num_ref.shape
    pairs = frames // (2 * TAPS)
    x_me = lax.axis_index("row")
    w = body(w_ref[...], rank, NF * cl)
    num_ref[:, pair_columns(outer_pair(pairs))] = jnp.zeros((rank, 2 * TAPS), F32)
    for at in range(pairs - 1):
        pair = at + jnp.where(x_me == 0, 1, 0)
        rows_of = pair_rows(s_ref, slice(None), pair, x_me, cl)
        num_ref[:, pair_columns(pair)] = jnp.dot(w, rows_of, preferred_element_type=F32)


def first_kernel(rows, subs, cl, *refs):
    refs = list(refs)
    w_refs = [refs.pop(0) for _ in range(rows)]
    early_ref, h_ref, s_ref, h_out, h_gram_ref = (refs.pop(0) for _ in range(5))
    msg_refs, num_scr = refs[:-1], refs[-1]
    rank, frames = h_ref.shape
    x_me = lax.axis_index("row")
    parts, gram = [], jnp.zeros(h_gram_ref.shape, F32)
    for shift, ref in enumerate(w_refs):
        parts.append((body(ref[...], rank, NF * cl), lax.rem(x_me + rows - shift, rows)))
        gram = gram + gram_of(ref[...], rank)
    if rows > 1:
        numerators(parts[1:], s_ref, num_scr, cl)
    else:
        num_scr[...] = jnp.zeros_like(num_scr)
    outer = outer_pair(frames // (2 * TAPS))
    num_scr[:, pair_columns(outer)] += jnp.dot(
        parts[0][0], pair_rows(s_ref, slice(None), outer, x_me, cl), preferred_element_type=F32
    )
    above = early_ref[...] + num_scr[...]
    new_activations(h_ref[...], gram, above, s_ref, h_out, h_gram_ref, msg_refs, rows, subs, cl)


def row_parts(rows, subs, cl, w_refs, w_scr, shifts):
    x_me, c_me = lax.axis_index("row"), lax.axis_index("sub")
    size = NF // subs * cl
    parts = []
    for line, dx in enumerate(shifts):
        for dc in range(subs):
            piece = body(w_refs[line * subs + dc][...], w_scr.shape[2], size)
            w_scr[line, lax.rem(c_me + subs - dc, subs)] = piece
        w = jnp.concatenate([w_scr[line, c] for c in range(subs)], axis=1)
        parts.append((w, lax.rem(x_me + rows - dx, rows)))
    return parts


def early_kernel(rows, subs, cl, *refs):
    w_refs, (s_ref, num_ref, w_scr) = refs[:subs], refs[subs:]
    numerators(row_parts(rows, subs, cl, w_refs, w_scr, [0]), s_ref, num_ref, cl)


def add_pieces(base_ref, pieces, s_ref, out_ref, rows, subs, cl):
    rank, frames = out_ref.shape
    count = NF // subs
    x_me, c_me = lax.axis_index("row"), lax.axis_index("sub")
    terms = []
    for ref, dx, dc in pieces:
        core = lax.rem(c_me + subs - dc, subs)
        terms.append((body(ref[...], rank, count * cl), lax.rem(x_me + rows - dx, rows), core))
    for pair in range(frames // (2 * TAPS)):
        cols = slice(2 * TAPS * pair, 2 * TAPS * (pair + 1))
        acc = base_ref[:, cols]
        for w, x, core in terms:
            spectra = pair_rows(s_ref, pl.ds(core * count, count), pair, x, cl)
            acc = acc + jnp.dot(w, spectra, preferred_element_type=F32)
        out_ref[:, cols] = acc


def middle_kernel(rows, subs, cl, *refs):
    w_refs, (base_ref, s_ref, out_ref) = refs[:-3], refs[-3:]
    pieces = [(ref, dx + 1, 0) for dx, ref in enumerate(w_refs)]
    add_pieces(base_ref, pieces, s_ref, out_ref, rows, subs, cl)


def later_kernel(rows, subs, cl, *refs):
    refs = list(refs)
    w_refs = [refs.pop(0) for _ in range(rows * subs)]
    middle_ref, h_ref, s_ref, h_out, h_gram_ref = (refs.pop(0) for _ in range(5))
    msg_refs, num_scr = refs[:-1], refs[-1]
    gram = jnp.zeros(h_gram_ref.shape, F32)
    for ref in w_refs:
        gram = gram + gram_of(ref[...], h_ref.shape[0])
    pieces = [(w_refs[dx * subs + dc], dx, dc) for dx in range(1, rows) for dc in range(1, subs)]
    add_pieces(middle_ref, pieces, s_ref, num_scr, rows, subs, cl)
    new_activations(h_ref[...], gram, num_scr[...], s_ref, h_out, h_gram_ref, msg_refs, rows, subs, cl)


def core_kernel(count, rank, *refs):
    own_refs, gram_ref, got_refs = refs[:count], refs[count], refs[count + 1 : -count - 1]
    out_refs, total_ref = refs[-count - 1 : -1], refs[-1]
    size = own_refs[0].shape[1]
    each = len(got_refs) // count
    gram = gram_ref[...]
    for ref in got_refs[:each]:
        gram = gram + ref[:, size:]
    total_ref[...] = gram
    for at in range(count):
        total = own_refs[at][...]
        for ref in got_refs[at * each : (at + 1) * each]:
            total = total + ref[:, :size]
        pack(out_refs[at], total, gram)


def row_kernel(subs, own_ref, gram_ref, *refs):
    core_refs, msg_refs, out_ref = refs[: subs - 1], refs[subs - 1 : -1], refs[-1]
    rank, size = own_ref.shape
    total, gram = own_ref[...], gram_ref[...]
    for ref in core_refs:
        total = total + ref[...]
    for ref in msg_refs:
        total = total + body(ref[...], rank, size).astype(F32)
        gram = gram + gram_of(ref[...], rank)
    pack(out_ref, total, gram)


def summed(z_me, count, msg_refs, scr, rank, size):
    for at, shift in enumerate([0, *reversed(range(1, count))]):
        scr[partner(z_me, shift, count)] = msg_refs[at][...]
    total, gram = body(scr[0], rank, size).astype(F32), gram_of(scr[0], rank)
    for at in range(1, count):
        total = total + body(scr[at], rank, size).astype(F32)
        gram = gram + gram_of(scr[at], rank)
    return total, gram


def partner(place, shift, count):
    if count & (count - 1):
        return (place + count - shift) % count
    return place ^ shift


def update_kernel(count, w_ref, *refs):
    msg_refs, (new_ref, out_ref, scr) = refs[:count], refs[count:]
    rank, size = new_ref.shape
    total, gram = summed(lax.axis_index("frm"), count, msg_refs, scr, rank, size)
    w = w_ref[...]
    new = w * total / jnp.dot(gram, w, precision=HIGH, preferred_element_type=F32)
    new_ref[...] = new
    pack(out_ref, new, lax.dot_general(new, new, NT, precision=HIGH, preferred_element_type=F32))


def last_kernel(count, w_ref, order_ref, *refs):
    msg_refs, (out_ref, scr) = refs[:count], refs[count:]
    rank, size = w_ref.shape
    total, gram = summed(lax.axis_index("frm"), count, msg_refs, scr, rank, size)
    w = w_ref[...]
    new = w * total / jnp.dot(gram, w, precision=HIGH, preferred_element_type=F32)
    terms = three_terms(new)
    for c in range(order_ref.shape[1] // size):

        @pl.when(lax.axis_index("sub") == c)
        def _():
            moved = lax.dot_general(
                terms, order_ref[:, c * size : (c + 1) * size], NT, preferred_element_type=F32
            )
            out_ref[...] = moved[:rank] + (moved[rank : 2 * rank] + moved[2 * rank :])


def join_kernel(rows, *refs):
    act_refs, (out_ref, sems) = refs[:rows], refs[rows:]
    frames = act_refs[0].shape[1]
    x_me = lax.axis_index("row")
    copies = []
    for shift in range(rows):
        begin = pl.multiple_of(lax.rem(x_me + rows - shift, rows) * frames, TAPS)
        copies.append(pltpu.make_async_copy(act_refs[shift], out_ref.at[:, pl.ds(begin, frames)], sems.at[shift]))
    for copy in copies:
        copy.start()
    for copy in copies:
        copy.wait()


def sum_kernel(_, *refs):
    parts, (out_ref, scr, sems) = refs[:-3], refs[-3:]
    copies = []
    for at in range(0, scr.shape[0], 8):
        lines = slice(at, at + 8)
        total = parts[0][lines, :]
        for part in parts[1:]:
            total = total + part[lines, :]
        scr[lines, :] = total
        copies.append(pltpu.make_async_copy(scr.at[lines], out_ref.at[lines], sems.at[at // 8]))
        copies[-1].start()
    for copy in copies:
        copy.wait()


def call(kernel, args, outs, scratch=(), in_specs=None, out_specs=None, limit=4, cost=None, aliases=None):
    whole = pl.BlockSpec(memory_space=pltpu.VMEM)
    if cost is not None:
        cost = pl.CostEstimate(flops=cost, bytes_accessed=0, transcendentals=0)
    return pl.pallas_call(
        kernel,
        out_shape=[jax.ShapeDtypeStruct(*out) if isinstance(out, tuple) else out for out in outs],
        in_specs=in_specs or [whole] * len(args),
        out_specs=out_specs or [whole] * len(outs),
        scratch_shapes=list(scratch),
        compiler_params=pltpu.CompilerParams(vmem_limit_bytes=limit * MIB),
        cost_estimate=cost,
        input_output_aliases=aliases or {},
    )(*args)


def reorder(cl):
    order = np.zeros((cl, NF, NF, cl), ml_dtypes.bfloat16)
    chans, freqs = np.meshgrid(np.arange(cl), np.arange(NF), indexing="ij")
    order[chans, freqs, freqs, chans] = 1
    return order.reshape(cl * NF, NF * cl)


def shards(signal, w_start, h_start):
    rows, subs, frms = (lax.axis_size(axis) for axis in ("row", "sub", "frm"))
    x_me = lax.axis_index("row")
    cl, window = signal.shape
    rank = w_start.shape[1]
    frames = window // rows
    blocks = frames // TAPS
    chans = rows * cl
    size = NF * cl // subs
    line = frms * subs
    width = frames + (TAPS if rows == 2 else 2 * TAPS)
    anywhere = pl.BlockSpec(memory_space=pl.ANY)
    whole = pl.BlockSpec(memory_space=pltpu.VMEM)

    def hbm(value):
        return pltpu.with_memory_space_constraint(value, pltpu.HBM)

    def vmem(value):
        return pltpu.with_memory_space_constraint(value, pltpu.VMEM)

    def row_shift(value, shift):
        return lax.ppermute(value, "row", [(i, (i + shift) % rows) for i in range(rows)])

    def sub_shift(value, shift):
        return lax.ppermute(value, "sub", [(i, (i + shift) % subs) for i in range(subs)])

    def frm_shift(value, shift):
        return lax.ppermute(value, "frm", [(partner(i, shift, frms), i) for i in range(frms)])

    def place(x, at):
        return (at // subs * rows + x) * subs + at % subs

    table, order = hbm(jnp.asarray(toeplitz())), jnp.asarray(reorder(cl))
    *cuts, ahead = call(
        functools.partial(cut_kernel, rows, frames),
        [hbm(signal), table],
        [((cl, width), BF16)] * rows + [pltpu.VMEM((AHEAD,) + table.shape[1:], BF16)],
        [pltpu.SemaphoreType.DMA((rows + 1,))],
        in_specs=[anywhere] * 2,
    )
    own_sig, *out_sigs = cuts
    ahead = vmem(ahead)
    sig = [own_sig] + [row_shift(part, shift + 1) for shift, part in enumerate(out_sigs)]
    msg = (message(rank, size), BF16)
    piece = ((rank, size), F32)
    update_outs = [((rank, frames), F32), ((rank, rank), F32)]
    update_outs += [((rank, size + rank), F32)] * ((rows - 1) * (subs - 1))
    half_done, w_own, old, order, table = call(
        functools.partial(own_spectra_kernel, rows),
        [own_sig, ahead, hbm(w_start.T), hbm(h_start), hbm(order), table],
        [
            pltpu.VMEM((NF, blocks, rows, cl, TAPS), BF16),
            pltpu.VMEM((rank, NF * cl), F32),
            pltpu.VMEM((rank, frames), F32),
            pltpu.VMEM(order.shape, BF16),
            pltpu.VMEM((NF - AHEAD,) + table.shape[1:], BF16),
        ],
        [
            pltpu.VMEM((cl, frames + TAPS), BF16),
            pltpu.VMEM(((blocks - 1) * cl, 2 * TAPS), BF16),
            pltpu.SemaphoreType.DMA((3,)),
            pltpu.SemaphoreType.DMA((len(CUTS) - 1,)),
        ],
        in_specs=[whole] * 2 + [anywhere] * 4,
        limit=8,
        cost=2 * NF * cl * frames * 4 * TAPS,
    )
    order = vmem(order)
    (edge,) = call(
        functools.partial(edges_kernel, rows),
        sig + [vmem(half_done)],
        [((chans, TAPS), BF16)],
        in_specs=[whole] * rows + [anywhere],
    )
    pairs = [(place(rows - 1, i), place(0, i + 1)) for i in range(line - 1)]
    halo = lax.ppermute(edge, ("frm", "row", "sub"), pairs + [(b, a) for a, b in pairs])
    w_piece, w_msg = call(
        reorder_kernel,
        [vmem(w_own), order, edge],
        [piece, (message(rank, NF * cl), BF16)],
        in_specs=[whole, whole, anywhere],
    )
    w_msgs = [w_msg] + [row_shift(w_msg, shift) for shift in range(1, rows)]
    (early,) = call(
        functools.partial(first_early_kernel, cl),
        [w_msg, vmem(half_done)],
        [((rank, frames), F32)],
        cost=16 * NF * cl * frames * rank,
    )
    (spectra,) = call(
        functools.partial(other_spectra_kernel, rows),
        [halo, ahead, vmem(table)] + sig + [vmem(half_done), early],
        [pltpu.VMEM((NF, blocks, rows, cl, TAPS), BF16)],
        [
            pltpu.VMEM((rows, cl, frames + TAPS), BF16),
            pltpu.VMEM((((rows - 1) * blocks + 1) * cl, 2 * TAPS), BF16),
        ],
        in_specs=[whole] * (rows + 3) + [anywhere] * 2,
        limit=8,
        cost=2 * NF * chans * frames * 4 * TAPS,
        aliases={rows + 3: 0},
    )
    spectra = vmem(spectra)

    def products(places, activations, after):
        return call(
            functools.partial(products_kernel, places, rows, subs, cl),
            [activations, spectra] + after,
            [piece] * len(places),
            in_specs=[whole] * 2 + [anywhere] * len(after),
            cost=1 if after else 16 * NF * cl * frames * rank // subs * len(places),
        )

    def gathered(activations, h_gram, msgs):
        got = [sub_shift(m, dc) for m, (_, dc) in zip(msgs, others_of(rows, subs))]
        places = [(dx, 0) for dx in range(1, rows)] + [(0, dc) for dc in range(1, subs)]
        formed = products(places, activations, [])
        for_rows, for_cores = formed[: rows - 1], formed[rows - 1 :]
        from_cores = [sub_shift(m, dc + 1) for dc, m in enumerate(for_cores)]
        *outs, gram = call(
            functools.partial(core_kernel, rows - 1, rank),
            list(for_rows) + [h_gram] + got,
            [msg] * (rows - 1) + [((rank, rank), F32)],
        )
        from_rows = [row_shift(m, dx + 1) for dx, m in enumerate(outs)]
        (own,) = products([(0, 0)], activations, outs)
        (part,) = call(functools.partial(row_kernel, subs), [own, gram] + from_cores + from_rows, [msg])
        return [part] + [frm_shift(part, shift) for shift in reversed(range(1, frms))]

    activations, h_gram, *msgs = call(
        functools.partial(first_kernel, rows, subs, cl),
        w_msgs + [early, vmem(old), spectra],
        update_outs,
        [pltpu.VMEM((rank, frames), F32)],
        limit=8,
    )
    piled = [pltpu.VMEM((frms,) + msg[0], BF16)]
    w_piece, w_msg = call(
        functools.partial(update_kernel, frms),
        [w_piece] + gathered(activations, h_gram, msgs),
        [piece, msg],
        piled,
    )
    w_msgs = [w_msg] + [sub_shift(w_msg, dc) for dc in range(1, subs)]
    w_pieces = pltpu.VMEM((1, subs, rank, size), BF16)
    (early,) = call(
        functools.partial(early_kernel, rows, subs, cl),
        w_msgs + [spectra],
        [((rank, frames), F32)],
        [w_pieces],
        cost=16 * NF * cl * frames * rank,
    )
    from_rows = [row_shift(w_msg, dx) for dx in range(1, rows)]
    *from_rows, early = lax.optimization_barrier((*from_rows, early))
    (middle,) = call(
        functools.partial(middle_kernel, rows, subs, cl),
        from_rows + [early, spectra],
        [((rank, frames), F32)],
        cost=16 * NF * cl * frames * rank // subs,
    )
    for base in from_rows:
        w_msgs += [base] + [sub_shift(base, dc) for dc in range(1, subs)]
    activations, h_gram, *msgs = call(
        functools.partial(later_kernel, rows, subs, cl),
        w_msgs + [middle, activations, spectra],
        update_outs,
        [pltpu.VMEM((rank, frames), F32)],
        limit=8,
    )
    parts = gathered(activations, h_gram, msgs)
    activations, parts[0] = lax.optimization_barrier((activations, parts[0]))
    sides = [activations] + [row_shift(activations, shift) for shift in range(1, rows)]
    (part,) = call(
        functools.partial(last_kernel, frms), [w_piece, order] + parts, [((rank, NF * cl), F32)], piled
    )
    (wide,) = call(
        functools.partial(join_kernel, rows),
        sides,
        [pltpu.HBM((rank, window), F32)],
        [pltpu.SemaphoreType.DMA((rows,))],
        in_specs=[anywhere] * rows,
        out_specs=[anywhere],
    )
    (synergies,) = call(
        sum_kernel,
        [hbm(wide), part] + [sub_shift(part, dc) for dc in range(1, subs)],
        [pltpu.HBM((rank, NF * cl), F32)],
        [pltpu.VMEM((rank, NF * cl), F32), pltpu.SemaphoreType.DMA((rank // 8,))],
        in_specs=[anywhere] + [whole] * subs,
        out_specs=[anywhere],
    )
    return (synergies.T, wide)


def solution(mesh):
    placed = (P("row", ("grp", "frm", "sub")), P("row", None), P(None, ("grp", "frm", "sub")))
    return jax.shard_map(
        shards,
        mesh=mesh,
        in_specs=placed,
        out_specs=(P(("grp", "row"), None), P(None, ("grp", "frm", "sub"))),
        check_vma=False,
    )
```

```python
import functools
import math

import jax
import jax.numpy as jnp
import ml_dtypes
import numpy as np
from jax import lax
from jax.experimental import pallas as pl
from jax.experimental.pallas import tpu as pltpu
from jax.sharding import PartitionSpec as P

NF = 40
TAPS = 128
HALF = TAPS // 2
LANES = 128
CUTS = (4, 8, 16, 24, 32, NF)
AHEAD = CUTS[0]
F32 = jnp.float32
BF16 = jnp.bfloat16
HIGH = lax.Precision.HIGHEST
NT = (((1,), (1,)), ((), ()))
MIB = 1024 * 1024


def wavelets():
    f = np.float32
    level = np.arange(NF, dtype=f) / f(NF - 1)
    freq = f(2.0) * np.power(f(12.0), level)
    sigma = f(7.0) / (f(2.0 * math.pi) * freq)
    times = (np.arange(TAPS, dtype=f) - f(HALF)) / f(50.0)
    env = np.exp(-(times[None, :] ** 2) / (f(2.0) * sigma[:, None] ** 2))
    scale = f(1.0) / np.sqrt(np.sum(env * env, axis=1))
    env = env * scale[:, None]
    phase = f(2.0 * math.pi) * freq[:, None] * times[None, :]
    return np.stack([env * np.cos(phase), env * np.sin(phase)]).astype(ml_dtypes.bfloat16)


def toeplitz():
    kernel = wavelets()
    table = np.zeros((NF, 2 * TAPS, 2 * TAPS), ml_dtypes.bfloat16)
    for at in range(TAPS):
        for part in range(2):
            table[:, at : at + TAPS, part * TAPS + at] = kernel[part]
    return table


def split_two(value):
    top = value.astype(BF16)
    return top, (value - top.astype(F32)).astype(BF16)


def message(rank, size):
    return (rank * -(-size // LANES) + rank // 2, LANES)


def pack(out_ref, main, gram):
    rank, size = main.shape
    half = rank // 2
    for at in range(0, size, LANES):
        line = at // LANES * rank
        width = min(LANES, size - at)
        out_ref[line : line + rank, :width] = main[:, at : at + width].astype(BF16)
    top, rest = split_two(gram)
    terms = [top[:half], top[half:], rest[:half], rest[half:]]
    line = out_ref.shape[0] - half
    for at, term in enumerate(terms):
        out_ref[line:, at * rank : (at + 1) * rank] = term


def body(value, rank, size):
    parts = []
    for at in range(0, size, LANES):
        line = at // LANES * rank
        parts.append(value[line : line + rank, : min(LANES, size - at)])
    return jnp.concatenate(parts, axis=1)


def gram_of(value, rank):
    last = value[value.shape[0] - rank // 2 :, :].astype(F32)
    total = last[:, : 2 * rank] + last[:, 2 * rank : 4 * rank]
    return jnp.concatenate([total[:, :rank], total[:, rank:]], axis=0)


def reorder_kernel(w_ref, order_ref, *refs):
    piece_ref, msg_ref = refs[-2:]
    w = w_ref[...]
    rank, size = piece_ref.shape
    gram = lax.dot_general(w, w, NT, precision=HIGH, preferred_element_type=F32)
    moved = jnp.dot(three_terms(w), order_ref[...], preferred_element_type=F32)
    whole = moved[:rank] + (moved[rank : 2 * rank] + moved[2 * rank :])
    for c in range(w.shape[1] // size):

        @pl.when(lax.axis_index("sub") == c)
        def _():
            piece_ref[...] = whole[:, c * size : (c + 1) * size]

    pack(msg_ref, whole, gram)


def three_terms(value):
    top = value.astype(BF16)
    rest = value - top.astype(F32)
    middle = rest.astype(BF16)
    return jnp.concatenate([top, middle, (rest - middle.astype(F32)).astype(BF16)], axis=0)


def edges_kernel(rows, sig_ref, *refs):
    got_refs, out_ref = refs[: rows - 1], refs[-1]
    cl, width = sig_ref.shape
    x_me = lax.axis_index("row")
    for at, ref in enumerate((sig_ref,) + tuple(got_refs)):

        @pl.when(x_me == 0)
        def _():
            out_ref[at * cl : (at + 1) * cl, :] = ref[:, :TAPS]

        @pl.when(x_me > 0)
        def _():
            out_ref[at * cl : (at + 1) * cl, :] = ref[:, width - TAPS :]


def cut_kernel(rows, frames, sig_hbm, tab_hbm, *refs):
    out_refs, (tab_ref, sems) = refs[:rows], refs[rows:]
    window, x_me = sig_hbm.shape[1], lax.axis_index("row")
    width = out_refs[0].shape[1]
    copies = []
    for shift in reversed(range(rows)):
        target = lax.rem(x_me + shift, rows)
        begin = pl.multiple_of(jnp.clip(target * frames - TAPS, 0, window - width), TAPS)
        copies.append(pltpu.make_async_copy(sig_hbm.at[:, pl.ds(begin, width)], out_refs[shift], sems.at[shift]))
    copies.append(pltpu.make_async_copy(tab_hbm.at[:AHEAD], tab_ref, sems.at[rows]))
    for copy in copies:
        copy.start()
    for copy in copies:
        copy.wait()


def pair_rows(s_ref, span, pair, x, cl):
    halves = [s_ref[span, blk, x].reshape(-1, TAPS) for blk in (2 * pair, 2 * pair + 1)]
    return jnp.concatenate(halves, axis=1)


def numerators(parts, s_ref, num_ref, cl):
    for pair in range(num_ref.shape[1] // (2 * TAPS)):
        terms = [
            jnp.dot(w, pair_rows(s_ref, slice(None), pair, x, cl), preferred_element_type=F32) for w, x in parts
        ]
        num_ref[:, 2 * TAPS * pair : 2 * TAPS * (pair + 1)] = functools.reduce(jnp.add, terms)


def crossed(low, s_ref, places, subs, cl):
    count = NF // subs
    acc = jnp.zeros((low.shape[0], len(places) * count * cl), F32)
    for pair in range(low.shape[1] // (2 * TAPS)):
        cols = slice(2 * TAPS * pair, 2 * TAPS * (pair + 1))
        parts = [pair_rows(s_ref, pl.ds(core * count, count), pair, x, cl) for x, core in places]
        acc = acc + lax.dot_general(
            low[:, cols], jnp.concatenate(parts, axis=0), NT, preferred_element_type=F32
        )
    return acc


def others_of(rows, subs):
    return [(dx, dc) for dx in range(1, rows) for dc in range(1, subs)]


def two_term_dot(left, right):
    top, rest = split_two(left)
    right_top, right_rest = split_two(right)
    return jnp.dot(
        jnp.concatenate([top, rest, top], axis=1),
        jnp.concatenate([right_top, right_top, right_rest], axis=0),
        preferred_element_type=F32,
    )


def two_term_gram(value):
    rank = value.shape[0]
    both = jnp.concatenate(split_two(value), axis=0)
    full = lax.dot_general(both, both, NT, preferred_element_type=F32)
    return full[:rank, :rank] + (full[:rank, rank:] + full[rank:, :rank]) + full[rank:, rank:]


def new_activations(old, gram, above, s_ref, h_out, h_gram_ref, msg_refs, rows, subs, cl):
    new = old * above / two_term_dot(gram, old)
    h_out[...] = new
    h_gram = two_term_gram(new)
    h_gram_ref[...] = h_gram
    size = NF // subs * cl
    x_me, c_me = lax.axis_index("row"), lax.axis_index("sub")
    for ref, (dx, dc) in zip(msg_refs, others_of(rows, subs)):
        target = (lax.rem(x_me + dx, rows), lax.rem(c_me + dc, subs))
        ref[:, :size] = crossed(new.astype(BF16), s_ref, [target], subs, cl)
        ref[:, size:] = h_gram


def products_kernel(places, rows, subs, cl, h_ref, s_ref, *refs):
    x_me, c_me = lax.axis_index("row"), lax.axis_index("sub")
    low = h_ref[...].astype(BF16)
    targets = [(lax.rem(x_me + dx, rows), lax.rem(c_me + dc, subs)) for dx, dc in places]
    acc = crossed(low, s_ref, targets, subs, cl)
    size = acc.shape[1] // len(places)
    for at, ref in enumerate(refs[len(refs) - len(places) :]):
        ref[...] = acc[:, at * size : (at + 1) * size]


def place_signal(source, target, rows, frames):
    x_me = lax.axis_index("row")
    width = source.shape[1]

    @pl.when(x_me == 0)
    def _():
        target[:, HALF:] = source[:, : frames + HALF]

    @pl.when(x_me == rows - 1)
    def _():
        target[:, : frames + HALF] = source[:, width - frames - HALF :]

    if rows > 2:

        @pl.when((x_me > 0) & (x_me < rows - 1))
        def _():
            target[...] = source[:, HALF : HALF + frames + TAPS]


def power_of(x_ref, table):
    co = jnp.dot(x_ref[...], table, preferred_element_type=F32)
    return (co[:, :TAPS] * co[:, :TAPS] + co[:, TAPS:] * co[:, TAPS:]).astype(BF16)


def table_at(f, ahead_ref, tab_ref):
    return ahead_ref[f] if f < AHEAD else tab_ref[f - AHEAD]


def own_spectra_kernel(rows, sig_ref, ahead_ref, w_hbm, h_hbm, order_hbm, tab_hbm, *refs):
    s_ref, w_ref, old_ref, order_ref, tab_ref, xp_scr, x_scr, sems, tab_sems = refs
    _, blocks, _, cl, _ = s_ref.shape
    frames = blocks * TAPS
    x_me = lax.axis_index("row")
    mine = pl.ds(pl.multiple_of(x_me * frames, TAPS), frames)

    table = [
        pltpu.make_async_copy(tab_hbm.at[begin:end], tab_ref.at[begin - AHEAD : end - AHEAD], tab_sems.at[at])
        for at, (begin, end) in enumerate(zip(CUTS, CUTS[1:]))
    ]
    later = [
        pltpu.make_async_copy(w_hbm, w_ref, sems.at[0]),
        pltpu.make_async_copy(order_hbm, order_ref, sems.at[1]),
        pltpu.make_async_copy(h_hbm.at[:, mine], old_ref, sems.at[2]),
    ]
    for copy in table:
        copy.start()
    place_signal(sig_ref, xp_scr, rows, frames)
    first = jnp.where(x_me == 0, 1, 0)
    for at in range(blocks - 1):
        begin = pl.multiple_of((first + at) * TAPS, TAPS)
        x_scr[at * cl : (at + 1) * cl, :] = xp_scr[:, pl.ds(begin, 2 * TAPS)]

    for f in range(NF):
        if f in CUTS:
            table[CUTS.index(f)].wait()
        if f == CUTS[2]:
            for copy in later:
                copy.start()
        power = power_of(x_scr, table_at(f, ahead_ref, tab_ref))
        s_ref[f, pl.ds(first, blocks - 1), x_me] = power.reshape(blocks - 1, cl, TAPS)
    for copy in later:
        copy.wait()


def other_spectra_kernel(rows, halo_ref, ahead_ref, tab_ref, *refs):
    sig_refs, (s_ref, xp_scr, x_scr) = refs[:rows], refs[-3:]
    _, blocks, _, cl, _ = s_ref.shape
    frames = blocks * TAPS
    x_me = lax.axis_index("row")
    owners = [lax.rem(x_me + rows - shift, rows) for shift in range(rows)]
    for shift in range(rows):
        place_signal(sig_refs[shift], xp_scr.at[owners[shift]], rows, frames)

    @pl.when(x_me == 0)
    def _():
        for at in range(rows):
            xp_scr[rows - 1 - at, :, :HALF] = halo_ref[at * cl : (at + 1) * cl, HALF:]

    @pl.when(x_me == rows - 1)
    def _():
        for at in range(rows):
            xp_scr[(rows - at) % rows, :, frames + HALF :] = halo_ref[at * cl : (at + 1) * cl, :HALF]

    outer = jnp.where(x_me == 0, 0, blocks - 1)
    begin = pl.multiple_of(outer * TAPS, TAPS)
    x_scr[:cl, :] = xp_scr[x_me, :, pl.ds(begin, 2 * TAPS)]
    for shift in range(1, rows):
        for blk in range(blocks):
            at = cl * (1 + (shift - 1) * blocks + blk)
            x_scr[at : at + cl, :] = xp_scr[owners[shift], :, blk * TAPS : (blk + 2) * TAPS]

    for f in range(NF):
        power = power_of(x_scr, table_at(f, ahead_ref, tab_ref))
        s_ref[f, outer, x_me] = power[:cl]
        for shift in range(1, rows):
            line = cl * (1 + (shift - 1) * blocks)
            s_ref[f, :, owners[shift]] = power[line : line + blocks * cl].reshape(blocks, cl, TAPS)


def outer_pair(pairs):
    return jnp.where(lax.axis_index("row") == 0, 0, pairs - 1)


def pair_columns(pair):
    return pl.ds(pl.multiple_of(pair * 2 * TAPS, 2 * TAPS), 2 * TAPS)


def first_early_kernel(cl, w_ref, s_ref, num_ref):
    rank, frames = num_ref.shape
    pairs = frames // (2 * TAPS)
    x_me = lax.axis_index("row")
    w = body(w_ref[...], rank, NF * cl)
    num_ref[:, pair_columns(outer_pair(pairs))] = jnp.zeros((rank, 2 * TAPS), F32)
    for at in range(pairs - 1):
        pair = at + jnp.where(x_me == 0, 1, 0)
        rows_of = pair_rows(s_ref, slice(None), pair, x_me, cl)
        num_ref[:, pair_columns(pair)] = jnp.dot(w, rows_of, preferred_element_type=F32)


def first_kernel(rows, subs, cl, *refs):
    refs = list(refs)
    w_refs = [refs.pop(0) for _ in range(rows)]
    early_ref, h_ref, s_ref, h_out, h_gram_ref = (refs.pop(0) for _ in range(5))
    msg_refs, num_scr = refs[:-1], refs[-1]
    rank, frames = h_ref.shape
    x_me = lax.axis_index("row")
    parts, gram = [], jnp.zeros(h_gram_ref.shape, F32)
    for shift, ref in enumerate(w_refs):
        parts.append((body(ref[...], rank, NF * cl), lax.rem(x_me + rows - shift, rows)))
        gram = gram + gram_of(ref[...], rank)
    if rows > 1:
        numerators(parts[1:], s_ref, num_scr, cl)
    else:
        num_scr[...] = jnp.zeros_like(num_scr)
    outer = outer_pair(frames // (2 * TAPS))
    num_scr[:, pair_columns(outer)] += jnp.dot(
        parts[0][0], pair_rows(s_ref, slice(None), outer, x_me, cl), preferred_element_type=F32
    )
    above = early_ref[...] + num_scr[...]
    new_activations(h_ref[...], gram, above, s_ref, h_out, h_gram_ref, msg_refs, rows, subs, cl)


def row_parts(rows, subs, cl, w_refs, w_scr, shifts):
    x_me, c_me = lax.axis_index("row"), lax.axis_index("sub")
    size = NF // subs * cl
    parts = []
    for line, dx in enumerate(shifts):
        for dc in range(subs):
            piece = body(w_refs[line * subs + dc][...], w_scr.shape[2], size)
            w_scr[line, lax.rem(c_me + subs - dc, subs)] = piece
        w = jnp.concatenate([w_scr[line, c] for c in range(subs)], axis=1)
        parts.append((w, lax.rem(x_me + rows - dx, rows)))
    return parts


def early_kernel(rows, subs, cl, *refs):
    w_refs, (s_ref, num_ref, w_scr) = refs[:subs], refs[subs:]
    numerators(row_parts(rows, subs, cl, w_refs, w_scr, [0]), s_ref, num_ref, cl)


def add_pieces(base_ref, pieces, s_ref, out_ref, rows, subs, cl):
    rank, frames = out_ref.shape
    count = NF // subs
    x_me, c_me = lax.axis_index("row"), lax.axis_index("sub")
    terms = []
    for ref, dx, dc in pieces:
        core = lax.rem(c_me + subs - dc, subs)
        terms.append((body(ref[...], rank, count * cl), lax.rem(x_me + rows - dx, rows), core))
    for pair in range(frames // (2 * TAPS)):
        cols = slice(2 * TAPS * pair, 2 * TAPS * (pair + 1))
        acc = base_ref[:, cols]
        for w, x, core in terms:
            spectra = pair_rows(s_ref, pl.ds(core * count, count), pair, x, cl)
            acc = acc + jnp.dot(w, spectra, preferred_element_type=F32)
        out_ref[:, cols] = acc


def middle_kernel(rows, subs, cl, *refs):
    w_refs, (base_ref, s_ref, out_ref) = refs[:-3], refs[-3:]
    pieces = [(ref, dx + 1, 0) for dx, ref in enumerate(w_refs)]
    add_pieces(base_ref, pieces, s_ref, out_ref, rows, subs, cl)


def later_kernel(rows, subs, cl, *refs):
    refs = list(refs)
    w_refs = [refs.pop(0) for _ in range(rows * subs)]
    middle_ref, h_ref, s_ref, h_out, h_gram_ref = (refs.pop(0) for _ in range(5))
    msg_refs, num_scr = refs[:-1], refs[-1]
    gram = jnp.zeros(h_gram_ref.shape, F32)
    for ref in w_refs:
        gram = gram + gram_of(ref[...], h_ref.shape[0])
    pieces = [(w_refs[dx * subs + dc], dx, dc) for dx in range(1, rows) for dc in range(1, subs)]
    add_pieces(middle_ref, pieces, s_ref, num_scr, rows, subs, cl)
    new_activations(h_ref[...], gram, num_scr[...], s_ref, h_out, h_gram_ref, msg_refs, rows, subs, cl)


def core_kernel(count, rank, *refs):
    own_refs, gram_ref, got_refs = refs[:count], refs[count], refs[count + 1 : -count - 1]
    out_refs, total_ref = refs[-count - 1 : -1], refs[-1]
    size = own_refs[0].shape[1]
    each = len(got_refs) // count
    gram = gram_ref[...]
    for ref in got_refs[:each]:
        gram = gram + ref[:, size:]
    total_ref[...] = gram
    for at in range(count):
        total = own_refs[at][...]
        for ref in got_refs[at * each : (at + 1) * each]:
            total = total + ref[:, :size]
        pack(out_refs[at], total, gram)


def row_kernel(subs, own_ref, gram_ref, *refs):
    core_refs, msg_refs, out_ref = refs[: subs - 1], refs[subs - 1 : -1], refs[-1]
    rank, size = own_ref.shape
    total, gram = own_ref[...], gram_ref[...]
    for ref in core_refs:
        total = total + ref[...]
    for ref in msg_refs:
        total = total + body(ref[...], rank, size).astype(F32)
        gram = gram + gram_of(ref[...], rank)
    pack(out_ref, total, gram)


def summed(z_me, count, msg_refs, scr, rank, size):
    for at, shift in enumerate([0, *reversed(range(1, count))]):
        scr[partner(z_me, shift, count)] = msg_refs[at][...]
    total, gram = body(scr[0], rank, size).astype(F32), gram_of(scr[0], rank)
    for at in range(1, count):
        total = total + body(scr[at], rank, size).astype(F32)
        gram = gram + gram_of(scr[at], rank)
    return total, gram


def partner(place, shift, count):
    if count & (count - 1):
        return (place + count - shift) % count
    return place ^ shift


def update_kernel(count, w_ref, *refs):
    msg_refs, (new_ref, out_ref, scr) = refs[:count], refs[count:]
    rank, size = new_ref.shape
    total, gram = summed(lax.axis_index("frm"), count, msg_refs, scr, rank, size)
    w = w_ref[...]
    new = w * total / jnp.dot(gram, w, precision=HIGH, preferred_element_type=F32)
    new_ref[...] = new
    pack(out_ref, new, lax.dot_general(new, new, NT, precision=HIGH, preferred_element_type=F32))


def last_kernel(count, w_ref, order_ref, *refs):
    msg_refs, (out_ref, scr) = refs[:count], refs[count:]
    rank, size = w_ref.shape
    total, gram = summed(lax.axis_index("frm"), count, msg_refs, scr, rank, size)
    w = w_ref[...]
    new = w * total / jnp.dot(gram, w, precision=HIGH, preferred_element_type=F32)
    terms = three_terms(new)
    for c in range(order_ref.shape[1] // size):

        @pl.when(lax.axis_index("sub") == c)
        def _():
            moved = lax.dot_general(
                terms, order_ref[:, c * size : (c + 1) * size], NT, preferred_element_type=F32
            )
            out_ref[...] = moved[:rank] + (moved[rank : 2 * rank] + moved[2 * rank :])


def join_kernel(rows, *refs):
    act_refs, (out_ref, sems) = refs[:rows], refs[rows:]
    frames = act_refs[0].shape[1]
    x_me = lax.axis_index("row")
    copies = []
    for shift in range(rows):
        begin = pl.multiple_of(lax.rem(x_me + rows - shift, rows) * frames, TAPS)
        copies.append(pltpu.make_async_copy(act_refs[shift], out_ref.at[:, pl.ds(begin, frames)], sems.at[shift]))
    for copy in copies:
        copy.start()
    for copy in copies:
        copy.wait()


def sum_kernel(_, *refs):
    parts, (out_ref, scr, sems) = refs[:-3], refs[-3:]
    copies = []
    for at in range(0, scr.shape[0], 8):
        lines = slice(at, at + 8)
        total = parts[0][lines, :]
        for part in parts[1:]:
            total = total + part[lines, :]
        scr[lines, :] = total
        copies.append(pltpu.make_async_copy(scr.at[lines], out_ref.at[lines], sems.at[at // 8]))
        copies[-1].start()
    for copy in copies:
        copy.wait()


def call(kernel, args, outs, scratch=(), in_specs=None, out_specs=None, limit=4, cost=None, aliases=None):
    whole = pl.BlockSpec(memory_space=pltpu.VMEM)
    if cost is not None:
        cost = pl.CostEstimate(flops=cost, bytes_accessed=0, transcendentals=0)
    return pl.pallas_call(
        kernel,
        out_shape=[jax.ShapeDtypeStruct(*out) if isinstance(out, tuple) else out for out in outs],
        in_specs=in_specs or [whole] * len(args),
        out_specs=out_specs or [whole] * len(outs),
        scratch_shapes=list(scratch),
        compiler_params=pltpu.CompilerParams(vmem_limit_bytes=limit * MIB),
        cost_estimate=cost,
        input_output_aliases=aliases or {},
    )(*args)


def reorder(cl):
    order = np.zeros((cl, NF, NF, cl), ml_dtypes.bfloat16)
    chans, freqs = np.meshgrid(np.arange(cl), np.arange(NF), indexing="ij")
    order[chans, freqs, freqs, chans] = 1
    return order.reshape(cl * NF, NF * cl)


def shards(signal, w_start, h_start):
    rows, subs, frms = (lax.axis_size(axis) for axis in ("row", "sub", "frm"))
    x_me = lax.axis_index("row")
    cl, window = signal.shape
    rank = w_start.shape[1]
    frames = window // rows
    blocks = frames // TAPS
    chans = rows * cl
    size = NF * cl // subs
    line = frms * subs
    width = frames + (TAPS if rows == 2 else 2 * TAPS)
    anywhere = pl.BlockSpec(memory_space=pl.ANY)
    whole = pl.BlockSpec(memory_space=pltpu.VMEM)

    def hbm(value):
        return pltpu.with_memory_space_constraint(value, pltpu.HBM)

    def vmem(value):
        return pltpu.with_memory_space_constraint(value, pltpu.VMEM)

    def row_shift(value, shift):
        return lax.ppermute(value, "row", [(i, (i + shift) % rows) for i in range(rows)])

    def sub_shift(value, shift):
        return lax.ppermute(value, "sub", [(i, (i + shift) % subs) for i in range(subs)])

    def frm_shift(value, shift):
        return lax.ppermute(value, "frm", [(partner(i, shift, frms), i) for i in range(frms)])

    def place(x, at):
        return (at // subs * rows + x) * subs + at % subs

    table, order = hbm(jnp.asarray(toeplitz())), jnp.asarray(reorder(cl))
    *cuts, ahead = call(
        functools.partial(cut_kernel, rows, frames),
        [hbm(signal), table],
        [((cl, width), BF16)] * rows + [pltpu.VMEM((AHEAD,) + table.shape[1:], BF16)],
        [pltpu.SemaphoreType.DMA((rows + 1,))],
        in_specs=[anywhere] * 2,
    )
    own_sig, *out_sigs = cuts
    ahead = vmem(ahead)
    sig = [own_sig] + [row_shift(part, shift + 1) for shift, part in enumerate(out_sigs)]
    msg = (message(rank, size), BF16)
    piece = ((rank, size), F32)
    update_outs = [((rank, frames), F32), ((rank, rank), F32)]
    update_outs += [((rank, size + rank), F32)] * ((rows - 1) * (subs - 1))
    half_done, w_own, old, order, table = call(
        functools.partial(own_spectra_kernel, rows),
        [own_sig, ahead, hbm(w_start.T), hbm(h_start), hbm(order), table],
        [
            pltpu.VMEM((NF, blocks, rows, cl, TAPS), BF16),
            pltpu.VMEM((rank, NF * cl), F32),
            pltpu.VMEM((rank, frames), F32),
            pltpu.VMEM(order.shape, BF16),
            pltpu.VMEM((NF - AHEAD,) + table.shape[1:], BF16),
        ],
        [
            pltpu.VMEM((cl, frames + TAPS), BF16),
            pltpu.VMEM(((blocks - 1) * cl, 2 * TAPS), BF16),
            pltpu.SemaphoreType.DMA((3,)),
            pltpu.SemaphoreType.DMA((len(CUTS) - 1,)),
        ],
        in_specs=[whole] * 2 + [anywhere] * 4,
        limit=8,
        cost=2 * NF * cl * frames * 4 * TAPS,
    )
    order = vmem(order)
    (edge,) = call(
        functools.partial(edges_kernel, rows),
        sig + [vmem(half_done)],
        [((chans, TAPS), BF16)],
        in_specs=[whole] * rows + [anywhere],
    )
    pairs = [(place(rows - 1, i), place(0, i + 1)) for i in range(line - 1)]
    halo = lax.ppermute(edge, ("frm", "row", "sub"), pairs + [(b, a) for a, b in pairs])
    w_piece, w_msg = call(
        reorder_kernel,
        [vmem(w_own), order, edge],
        [piece, (message(rank, NF * cl), BF16)],
        in_specs=[whole, whole, anywhere],
    )
    w_msgs = [w_msg] + [row_shift(w_msg, shift) for shift in range(1, rows)]
    (early,) = call(
        functools.partial(first_early_kernel, cl),
        [w_msg, vmem(half_done)],
        [((rank, frames), F32)],
        cost=16 * NF * cl * frames * rank,
    )
    (spectra,) = call(
        functools.partial(other_spectra_kernel, rows),
        [halo, ahead, vmem(table)] + sig + [vmem(half_done), early],
        [pltpu.VMEM((NF, blocks, rows, cl, TAPS), BF16)],
        [
            pltpu.VMEM((rows, cl, frames + TAPS), BF16),
            pltpu.VMEM((((rows - 1) * blocks + 1) * cl, 2 * TAPS), BF16),
        ],
        in_specs=[whole] * (rows + 3) + [anywhere] * 2,
        limit=8,
        cost=2 * NF * chans * frames * 4 * TAPS,
        aliases={rows + 3: 0},
    )
    spectra = vmem(spectra)

    def products(places, activations, after):
        return call(
            functools.partial(products_kernel, places, rows, subs, cl),
            [activations, spectra] + after,
            [piece] * len(places),
            in_specs=[whole] * 2 + [anywhere] * len(after),
            cost=1 if after else 16 * NF * cl * frames * rank // subs * len(places),
        )

    def gathered(activations, h_gram, msgs):
        got = [sub_shift(m, dc) for m, (_, dc) in zip(msgs, others_of(rows, subs))]
        places = [(dx, 0) for dx in range(1, rows)] + [(0, dc) for dc in range(1, subs)]
        formed = products(places, activations, [])
        for_rows, for_cores = formed[: rows - 1], formed[rows - 1 :]
        from_cores = [sub_shift(m, dc + 1) for dc, m in enumerate(for_cores)]
        *outs, gram = call(
            functools.partial(core_kernel, rows - 1, rank),
            list(for_rows) + [h_gram] + got,
            [msg] * (rows - 1) + [((rank, rank), F32)],
        )
        from_rows = [row_shift(m, dx + 1) for dx, m in enumerate(outs)]
        (own,) = products([(0, 0)], activations, outs)
        (part,) = call(functools.partial(row_kernel, subs), [own, gram] + from_cores + from_rows, [msg])
        return [part] + [frm_shift(part, shift) for shift in reversed(range(1, frms))]

    activations, h_gram, *msgs = call(
        functools.partial(first_kernel, rows, subs, cl),
        w_msgs + [early, vmem(old), spectra],
        update_outs,
        [pltpu.VMEM((rank, frames), F32)],
        limit=8,
    )
    piled = [pltpu.VMEM((frms,) + msg[0], BF16)]
    w_piece, w_msg = call(
        functools.partial(update_kernel, frms),
        [w_piece] + gathered(activations, h_gram, msgs),
        [piece, msg],
        piled,
    )
    w_msgs = [w_msg] + [sub_shift(w_msg, dc) for dc in range(1, subs)]
    w_pieces = pltpu.VMEM((1, subs, rank, size), BF16)
    (early,) = call(
        functools.partial(early_kernel, rows, subs, cl),
        w_msgs + [spectra],
        [((rank, frames), F32)],
        [w_pieces],
        cost=16 * NF * cl * frames * rank,
    )
    from_rows = [row_shift(w_msg, dx) for dx in range(1, rows)]
    *from_rows, early = lax.optimization_barrier((*from_rows, early))
    (middle,) = call(
        functools.partial(middle_kernel, rows, subs, cl),
        from_rows + [early, spectra],
        [((rank, frames), F32)],
        cost=16 * NF * cl * frames * rank // subs,
    )
    for base in from_rows:
        w_msgs += [base] + [sub_shift(base, dc) for dc in range(1, subs)]
    activations, h_gram, *msgs = call(
        functools.partial(later_kernel, rows, subs, cl),
        w_msgs + [middle, activations, spectra],
        update_outs,
        [pltpu.VMEM((rank, frames), F32)],
        limit=8,
    )
    parts = gathered(activations, h_gram, msgs)
    activations, parts[0] = lax.optimization_barrier((activations, parts[0]))
    sides = [activations] + [row_shift(activations, shift) for shift in range(1, rows)]
    (part,) = call(
        functools.partial(last_kernel, frms), [w_piece, order] + parts, [((rank, NF * cl), F32)], piled
    )
    (wide,) = call(
        functools.partial(join_kernel, rows),
        sides,
        [pltpu.HBM((rank, window), F32)],
        [pltpu.SemaphoreType.DMA((rows,))],
        in_specs=[anywhere] * rows,
        out_specs=[anywhere],
    )
    (synergies,) = call(
        sum_kernel,
        [hbm(wide), part] + [sub_shift(part, dc) for dc in range(1, subs)],
        [pltpu.HBM((rank, NF * cl), F32)],
        [pltpu.VMEM((rank, NF * cl), F32), pltpu.SemaphoreType.DMA((rank // 8,))],
        in_specs=[anywhere] + [whole] * subs,
        out_specs=[anywhere],
    )
    return (synergies.T, wide)


def solution(mesh):
    placed = (P("row", ("grp", "frm", "sub")), P("row", None), P(None, ("grp", "frm", "sub")))
    return jax.shard_map(
        shards,
        mesh=mesh,
        in_specs=placed,
        out_specs=(P(("grp", "row"), None), P(None, ("grp", "frm", "sub"))),
        check_vma=False,
    )
```

```python
import functools
import math

import jax
import jax.numpy as jnp
import ml_dtypes
import numpy as np
from jax import lax
from jax.experimental import pallas as pl
from jax.experimental.pallas import tpu as pltpu
from jax.sharding import PartitionSpec as P

NF = 40
TAPS = 128
HALF = TAPS // 2
LANES = 128
CUTS = (4, 8, 16, 24, 32, NF)
AHEAD = CUTS[0]
F32 = jnp.float32
BF16 = jnp.bfloat16
NT = (((1,), (1,)), ((), ()))
MIB = 1024 * 1024


def wavelets():
    f = np.float32
    level = np.arange(NF, dtype=f) / f(NF - 1)
    freq = f(2.0) * np.power(f(12.0), level)
    sigma = f(7.0) / (f(2.0 * math.pi) * freq)
    times = (np.arange(TAPS, dtype=f) - f(HALF)) / f(50.0)
    env = np.exp(-(times[None, :] ** 2) / (f(2.0) * sigma[:, None] ** 2))
    scale = f(1.0) / np.sqrt(np.sum(env * env, axis=1))
    env = env * scale[:, None]
    phase = f(2.0 * math.pi) * freq[:, None] * times[None, :]
    return np.stack([env * np.cos(phase), env * np.sin(phase)]).astype(ml_dtypes.bfloat16)


def toeplitz():
    kernel = wavelets()
    table = np.zeros((NF, 2 * TAPS, 2 * TAPS), ml_dtypes.bfloat16)
    for at in range(TAPS):
        for part in range(2):
            table[:, at : at + TAPS, part * TAPS + at] = kernel[part]
    return table


def split_two(value):
    top = value.astype(BF16)
    return top, (value - top.astype(F32)).astype(BF16)


def message(rank, size):
    return (rank * -(-size // LANES) + rank // 2, LANES)


def pack(out_ref, main, gram):
    rank, size = main.shape
    half = rank // 2
    for at in range(0, size, LANES):
        line = at // LANES * rank
        width = min(LANES, size - at)
        out_ref[line : line + rank, :width] = main[:, at : at + width].astype(BF16)
    top, rest = split_two(gram)
    terms = [top[:half], top[half:], rest[:half], rest[half:]]
    line = out_ref.shape[0] - half
    for at, term in enumerate(terms):
        out_ref[line:, at * rank : (at + 1) * rank] = term


def body(value, rank, size):
    parts = []
    for at in range(0, size, LANES):
        line = at // LANES * rank
        parts.append(value[line : line + rank, : min(LANES, size - at)])
    return jnp.concatenate(parts, axis=1)


def gram_of(value, rank):
    last = value[value.shape[0] - rank // 2 :, :].astype(F32)
    total = last[:, : 2 * rank] + last[:, 2 * rank : 4 * rank]
    return jnp.concatenate([total[:, :rank], total[:, rank:]], axis=0)


def reorder_kernel(w_ref, order_ref, *refs):
    piece_ref, msg_ref = refs[-2:]
    w = w_ref[...]
    rank, size = piece_ref.shape
    gram = two_term_gram(w)
    moved = jnp.dot(three_terms(w), order_ref[...], preferred_element_type=F32)
    whole = moved[:rank] + (moved[rank : 2 * rank] + moved[2 * rank :])
    for c in range(w.shape[1] // size):

        @pl.when(lax.axis_index("sub") == c)
        def _():
            piece_ref[...] = whole[:, c * size : (c + 1) * size]

    pack(msg_ref, whole, gram)


def three_terms(value):
    top = value.astype(BF16)
    rest = value - top.astype(F32)
    middle = rest.astype(BF16)
    return jnp.concatenate([top, middle, (rest - middle.astype(F32)).astype(BF16)], axis=0)


def edges_kernel(rows, sig_ref, *refs):
    got_refs, out_ref = refs[: rows - 1], refs[-1]
    cl, width = sig_ref.shape
    x_me = lax.axis_index("row")
    for at, ref in enumerate((sig_ref,) + tuple(got_refs)):

        @pl.when(x_me == 0)
        def _():
            out_ref[at * cl : (at + 1) * cl, :] = ref[:, :TAPS]

        @pl.when(x_me > 0)
        def _():
            out_ref[at * cl : (at + 1) * cl, :] = ref[:, width - TAPS :]


def cut_kernel(rows, frames, sig_hbm, tab_hbm, *refs):
    out_refs, (tab_ref, sems) = refs[:rows], refs[rows:]
    window, x_me = sig_hbm.shape[1], lax.axis_index("row")
    width = out_refs[0].shape[1]
    copies = []
    for shift in reversed(range(rows)):
        target = lax.rem(x_me + shift, rows)
        begin = pl.multiple_of(jnp.clip(target * frames - TAPS, 0, window - width), TAPS)
        copies.append(pltpu.make_async_copy(sig_hbm.at[:, pl.ds(begin, width)], out_refs[shift], sems.at[shift]))
    copies.append(pltpu.make_async_copy(tab_hbm.at[:AHEAD], tab_ref, sems.at[rows]))
    for copy in copies:
        copy.start()
    for copy in copies:
        copy.wait()


def pair_rows(s_ref, span, pair, x, cl):
    halves = [s_ref[span, blk, x].reshape(-1, TAPS) for blk in (2 * pair, 2 * pair + 1)]
    return jnp.concatenate(halves, axis=1)


def numerators(parts, s_ref, num_ref, cl):
    for pair in range(num_ref.shape[1] // (2 * TAPS)):
        terms = [
            jnp.dot(w, pair_rows(s_ref, slice(None), pair, x, cl), preferred_element_type=F32) for w, x in parts
        ]
        num_ref[:, 2 * TAPS * pair : 2 * TAPS * (pair + 1)] = functools.reduce(jnp.add, terms)


def crossed(low, s_ref, places, subs, cl):
    count = NF // subs
    acc = jnp.zeros((low.shape[0], len(places) * count * cl), F32)
    for pair in range(low.shape[1] // (2 * TAPS)):
        cols = slice(2 * TAPS * pair, 2 * TAPS * (pair + 1))
        parts = [pair_rows(s_ref, pl.ds(core * count, count), pair, x, cl) for x, core in places]
        acc = acc + lax.dot_general(
            low[:, cols], jnp.concatenate(parts, axis=0), NT, preferred_element_type=F32
        )
    return acc


def others_of(rows, subs):
    return [(dx, dc) for dx in range(1, rows) for dc in range(1, subs)]


def two_term_dot(left, right):
    top, rest = split_two(left)
    right_top, right_rest = split_two(right)
    return jnp.dot(
        jnp.concatenate([top, rest, top], axis=1),
        jnp.concatenate([right_top, right_top, right_rest], axis=0),
        preferred_element_type=F32,
    )


def two_term_gram(value):
    rank = value.shape[0]
    both = jnp.concatenate(split_two(value), axis=0)
    full = lax.dot_general(both, both, NT, preferred_element_type=F32)
    return full[:rank, :rank] + (full[:rank, rank:] + full[rank:, :rank]) + full[rank:, rank:]


def new_activations(old, gram, above, s_ref, h_out, h_gram_ref, msg_refs, rows, subs, cl):
    new = old * above / two_term_dot(gram, old)
    h_out[...] = new
    h_gram = two_term_gram(new)
    h_gram_ref[...] = h_gram
    size = NF // subs * cl
    x_me, c_me = lax.axis_index("row"), lax.axis_index("sub")
    for ref, (dx, dc) in zip(msg_refs, others_of(rows, subs)):
        target = (lax.rem(x_me + dx, rows), lax.rem(c_me + dc, subs))
        ref[:, :size] = crossed(new.astype(BF16), s_ref, [target], subs, cl)
        ref[:, size:] = h_gram


def products_kernel(places, rows, subs, cl, h_ref, s_ref, *refs):
    x_me, c_me = lax.axis_index("row"), lax.axis_index("sub")
    low = h_ref[...].astype(BF16)
    targets = [(lax.rem(x_me + dx, rows), lax.rem(c_me + dc, subs)) for dx, dc in places]
    acc = crossed(low, s_ref, targets, subs, cl)
    size = acc.shape[1] // len(places)
    for at, ref in enumerate(refs[len(refs) - len(places) :]):
        ref[...] = acc[:, at * size : (at + 1) * size]


def place_signal(source, target, rows, frames):
    x_me = lax.axis_index("row")
    width = source.shape[1]

    @pl.when(x_me == 0)
    def _():
        target[:, HALF:] = source[:, : frames + HALF]

    @pl.when(x_me == rows - 1)
    def _():
        target[:, : frames + HALF] = source[:, width - frames - HALF :]

    if rows > 2:

        @pl.when((x_me > 0) & (x_me < rows - 1))
        def _():
            target[...] = source[:, HALF : HALF + frames + TAPS]


def power_of(x_ref, table):
    co = jnp.dot(x_ref[...], table, preferred_element_type=F32)
    return (co[:, :TAPS] * co[:, :TAPS] + co[:, TAPS:] * co[:, TAPS:]).astype(BF16)


def table_at(f, ahead_ref, tab_ref):
    return ahead_ref[f] if f < AHEAD else tab_ref[f - AHEAD]


def own_spectra_kernel(rows, sig_ref, ahead_ref, w_hbm, h_hbm, order_hbm, tab_hbm, *refs):
    s_ref, w_ref, old_ref, order_ref, tab_ref, xp_scr, x_scr, sems, tab_sems = refs
    _, blocks, _, cl, _ = s_ref.shape
    frames = blocks * TAPS
    x_me = lax.axis_index("row")
    mine = pl.ds(pl.multiple_of(x_me * frames, TAPS), frames)

    table = [
        pltpu.make_async_copy(tab_hbm.at[begin:end], tab_ref.at[begin - AHEAD : end - AHEAD], tab_sems.at[at])
        for at, (begin, end) in enumerate(zip(CUTS, CUTS[1:]))
    ]
    later = [
        pltpu.make_async_copy(w_hbm, w_ref, sems.at[0]),
        pltpu.make_async_copy(order_hbm, order_ref, sems.at[1]),
        pltpu.make_async_copy(h_hbm.at[:, mine], old_ref, sems.at[2]),
    ]
    for copy in table:
        copy.start()
    place_signal(sig_ref, xp_scr, rows, frames)
    first = jnp.where(x_me == 0, 1, 0)
    for at in range(blocks - 1):
        begin = pl.multiple_of((first + at) * TAPS, TAPS)
        x_scr[at * cl : (at + 1) * cl, :] = xp_scr[:, pl.ds(begin, 2 * TAPS)]

    for f in range(NF):
        if f in CUTS:
            table[CUTS.index(f)].wait()
        if f == CUTS[2]:
            for copy in later:
                copy.start()
        power = power_of(x_scr, table_at(f, ahead_ref, tab_ref))
        s_ref[f, pl.ds(first, blocks - 1), x_me] = power.reshape(blocks - 1, cl, TAPS)
    for copy in later:
        copy.wait()


def other_spectra_kernel(rows, halo_ref, ahead_ref, tab_ref, *refs):
    sig_refs, (s_ref, xp_scr, x_scr) = refs[:rows], refs[-3:]
    _, blocks, _, cl, _ = s_ref.shape
    frames = blocks * TAPS
    x_me = lax.axis_index("row")
    owners = [lax.rem(x_me + rows - shift, rows) for shift in range(rows)]
    for shift in range(rows):
        place_signal(sig_refs[shift], xp_scr.at[owners[shift]], rows, frames)

    @pl.when(x_me == 0)
    def _():
        for at in range(rows):
            xp_scr[rows - 1 - at, :, :HALF] = halo_ref[at * cl : (at + 1) * cl, HALF:]

    @pl.when(x_me == rows - 1)
    def _():
        for at in range(rows):
            xp_scr[(rows - at) % rows, :, frames + HALF :] = halo_ref[at * cl : (at + 1) * cl, :HALF]

    outer = jnp.where(x_me == 0, 0, blocks - 1)
    begin = pl.multiple_of(outer * TAPS, TAPS)
    x_scr[:cl, :] = xp_scr[x_me, :, pl.ds(begin, 2 * TAPS)]
    for shift in range(1, rows):
        for blk in range(blocks):
            at = cl * (1 + (shift - 1) * blocks + blk)
            x_scr[at : at + cl, :] = xp_scr[owners[shift], :, blk * TAPS : (blk + 2) * TAPS]

    for f in range(NF):
        power = power_of(x_scr, table_at(f, ahead_ref, tab_ref))
        s_ref[f, outer, x_me] = power[:cl]
        for shift in range(1, rows):
            line = cl * (1 + (shift - 1) * blocks)
            s_ref[f, :, owners[shift]] = power[line : line + blocks * cl].reshape(blocks, cl, TAPS)


def outer_pair(pairs):
    return jnp.where(lax.axis_index("row") == 0, 0, pairs - 1)


def pair_columns(pair):
    return pl.ds(pl.multiple_of(pair * 2 * TAPS, 2 * TAPS), 2 * TAPS)


def first_early_kernel(cl, w_ref, s_ref, num_ref):
    rank, frames = num_ref.shape
    pairs = frames // (2 * TAPS)
    x_me = lax.axis_index("row")
    w = body(w_ref[...], rank, NF * cl)
    num_ref[:, pair_columns(outer_pair(pairs))] = jnp.zeros((rank, 2 * TAPS), F32)
    for at in range(pairs - 1):
        pair = at + jnp.where(x_me == 0, 1, 0)
        rows_of = pair_rows(s_ref, slice(None), pair, x_me, cl)
        num_ref[:, pair_columns(pair)] = jnp.dot(w, rows_of, preferred_element_type=F32)


def first_kernel(rows, subs, cl, *refs):
    refs = list(refs)
    w_refs = [refs.pop(0) for _ in range(rows)]
    early_ref, h_ref, s_ref, h_out, h_gram_ref = (refs.pop(0) for _ in range(5))
    msg_refs, num_scr = refs[:-1], refs[-1]
    rank, frames = h_ref.shape
    x_me = lax.axis_index("row")
    parts, gram = [], jnp.zeros(h_gram_ref.shape, F32)
    for shift, ref in enumerate(w_refs):
        parts.append((body(ref[...], rank, NF * cl), lax.rem(x_me + rows - shift, rows)))
        gram = gram + gram_of(ref[...], rank)
    if rows > 1:
        numerators(parts[1:], s_ref, num_scr, cl)
    else:
        num_scr[...] = jnp.zeros_like(num_scr)
    outer = outer_pair(frames // (2 * TAPS))
    num_scr[:, pair_columns(outer)] += jnp.dot(
        parts[0][0], pair_rows(s_ref, slice(None), outer, x_me, cl), preferred_element_type=F32
    )
    above = early_ref[...] + num_scr[...]
    new_activations(h_ref[...], gram, above, s_ref, h_out, h_gram_ref, msg_refs, rows, subs, cl)


def row_parts(rows, subs, cl, w_refs, w_scr, shifts):
    x_me, c_me = lax.axis_index("row"), lax.axis_index("sub")
    size = NF // subs * cl
    parts = []
    for line, dx in enumerate(shifts):
        for dc in range(subs):
            piece = body(w_refs[line * subs + dc][...], w_scr.shape[2], size)
            w_scr[line, lax.rem(c_me + subs - dc, subs)] = piece
        w = jnp.concatenate([w_scr[line, c] for c in range(subs)], axis=1)
        parts.append((w, lax.rem(x_me + rows - dx, rows)))
    return parts


def early_kernel(rows, subs, cl, *refs):
    w_refs, (s_ref, num_ref, w_scr) = refs[:subs], refs[subs:]
    numerators(row_parts(rows, subs, cl, w_refs, w_scr, [0]), s_ref, num_ref, cl)


def add_pieces(base_ref, pieces, s_ref, out_ref, rows, subs, cl):
    rank, frames = out_ref.shape
    count = NF // subs
    x_me, c_me = lax.axis_index("row"), lax.axis_index("sub")
    terms = []
    for ref, dx, dc in pieces:
        core = lax.rem(c_me + subs - dc, subs)
        terms.append((body(ref[...], rank, count * cl), lax.rem(x_me + rows - dx, rows), core))
    for pair in range(frames // (2 * TAPS)):
        cols = slice(2 * TAPS * pair, 2 * TAPS * (pair + 1))
        acc = base_ref[:, cols]
        for w, x, core in terms:
            spectra = pair_rows(s_ref, pl.ds(core * count, count), pair, x, cl)
            acc = acc + jnp.dot(w, spectra, preferred_element_type=F32)
        out_ref[:, cols] = acc


def middle_kernel(rows, subs, cl, *refs):
    w_refs, (base_ref, s_ref, out_ref) = refs[:-3], refs[-3:]
    pieces = [(ref, dx + 1, 0) for dx, ref in enumerate(w_refs)]
    add_pieces(base_ref, pieces, s_ref, out_ref, rows, subs, cl)


def later_kernel(rows, subs, cl, *refs):
    refs = list(refs)
    w_refs = [refs.pop(0) for _ in range(rows * subs)]
    middle_ref, h_ref, s_ref, h_out, h_gram_ref = (refs.pop(0) for _ in range(5))
    msg_refs, num_scr = refs[:-1], refs[-1]
    gram = jnp.zeros(h_gram_ref.shape, F32)
    for ref in w_refs:
        gram = gram + gram_of(ref[...], h_ref.shape[0])
    pieces = [(w_refs[dx * subs + dc], dx, dc) for dx in range(1, rows) for dc in range(1, subs)]
    add_pieces(middle_ref, pieces, s_ref, num_scr, rows, subs, cl)
    new_activations(h_ref[...], gram, num_scr[...], s_ref, h_out, h_gram_ref, msg_refs, rows, subs, cl)


def core_kernel(count, rank, *refs):
    own_refs, gram_ref, got_refs = refs[:count], refs[count], refs[count + 1 : -count - 1]
    out_refs, total_ref = refs[-count - 1 : -1], refs[-1]
    size = own_refs[0].shape[1]
    each = len(got_refs) // count
    gram = gram_ref[...]
    for ref in got_refs[:each]:
        gram = gram + ref[:, size:]
    total_ref[...] = gram
    for at in range(count):
        total = own_refs[at][...]
        for ref in got_refs[at * each : (at + 1) * each]:
            total = total + ref[:, :size]
        pack(out_refs[at], total, gram)


def row_kernel(subs, own_ref, gram_ref, *refs):
    core_refs, msg_refs, out_ref = refs[: subs - 1], refs[subs - 1 : -1], refs[-1]
    rank, size = own_ref.shape
    total, gram = own_ref[...], gram_ref[...]
    for ref in core_refs:
        total = total + ref[...]
    for ref in msg_refs:
        total = total + body(ref[...], rank, size).astype(F32)
        gram = gram + gram_of(ref[...], rank)
    pack(out_ref, total, gram)


def summed(z_me, count, msg_refs, scr, rank, size):
    for at, shift in enumerate([0, *reversed(range(1, count))]):
        scr[partner(z_me, shift, count)] = msg_refs[at][...]
    total, gram = body(scr[0], rank, size).astype(F32), gram_of(scr[0], rank)
    for at in range(1, count):
        total = total + body(scr[at], rank, size).astype(F32)
        gram = gram + gram_of(scr[at], rank)
    return total, gram


def partner(place, shift, count):
    if count & (count - 1):
        return (place + count - shift) % count
    return place ^ shift


def update_kernel(count, w_ref, *refs):
    msg_refs, (new_ref, out_ref, scr) = refs[:count], refs[count:]
    rank, size = new_ref.shape
    total, gram = summed(lax.axis_index("frm"), count, msg_refs, scr, rank, size)
    w = w_ref[...]
    new = w * total / two_term_dot(gram, w)
    new_ref[...] = new
    pack(out_ref, new, two_term_gram(new))


def last_kernel(count, w_ref, order_ref, *refs):
    msg_refs, (out_ref, scr) = refs[:count], refs[count:]
    rank, size = w_ref.shape
    total, gram = summed(lax.axis_index("frm"), count, msg_refs, scr, rank, size)
    w = w_ref[...]
    new = w * total / two_term_dot(gram, w)
    terms = three_terms(new)
    for c in range(order_ref.shape[1] // size):

        @pl.when(lax.axis_index("sub") == c)
        def _():
            moved = lax.dot_general(
                terms, order_ref[:, c * size : (c + 1) * size], NT, preferred_element_type=F32
            )
            out_ref[...] = moved[:rank] + (moved[rank : 2 * rank] + moved[2 * rank :])


def join_kernel(rows, *refs):
    act_refs, (out_ref, sems) = refs[:rows], refs[rows:]
    frames = act_refs[0].shape[1]
    x_me = lax.axis_index("row")
    copies = []
    for shift in range(rows):
        begin = pl.multiple_of(lax.rem(x_me + rows - shift, rows) * frames, TAPS)
        copies.append(pltpu.make_async_copy(act_refs[shift], out_ref.at[:, pl.ds(begin, frames)], sems.at[shift]))
    for copy in copies:
        copy.start()
    for copy in copies:
        copy.wait()


def sum_kernel(_, *refs):
    parts, (out_ref, scr, sems) = refs[:-3], refs[-3:]
    copies = []
    for at in range(0, scr.shape[0], 8):
        lines = slice(at, at + 8)
        total = parts[0][lines, :]
        for part in parts[1:]:
            total = total + part[lines, :]
        scr[lines, :] = total
        copies.append(pltpu.make_async_copy(scr.at[lines], out_ref.at[lines], sems.at[at // 8]))
        copies[-1].start()
    for copy in copies:
        copy.wait()


def call(kernel, args, outs, scratch=(), in_specs=None, out_specs=None, limit=4, cost=None, aliases=None):
    whole = pl.BlockSpec(memory_space=pltpu.VMEM)
    if cost is not None:
        cost = pl.CostEstimate(flops=cost, bytes_accessed=0, transcendentals=0)
    return pl.pallas_call(
        kernel,
        out_shape=[jax.ShapeDtypeStruct(*out) if isinstance(out, tuple) else out for out in outs],
        in_specs=in_specs or [whole] * len(args),
        out_specs=out_specs or [whole] * len(outs),
        scratch_shapes=list(scratch),
        compiler_params=pltpu.CompilerParams(vmem_limit_bytes=limit * MIB),
        cost_estimate=cost,
        input_output_aliases=aliases or {},
    )(*args)


def reorder(cl):
    order = np.zeros((cl, NF, NF, cl), ml_dtypes.bfloat16)
    chans, freqs = np.meshgrid(np.arange(cl), np.arange(NF), indexing="ij")
    order[chans, freqs, freqs, chans] = 1
    return order.reshape(cl * NF, NF * cl)


def shards(signal, w_start, h_start):
    rows, subs, frms = (lax.axis_size(axis) for axis in ("row", "sub", "frm"))
    x_me = lax.axis_index("row")
    cl, window = signal.shape
    rank = w_start.shape[1]
    frames = window // rows
    blocks = frames // TAPS
    chans = rows * cl
    size = NF * cl // subs
    line = frms * subs
    width = frames + (TAPS if rows == 2 else 2 * TAPS)
    anywhere = pl.BlockSpec(memory_space=pl.ANY)
    whole = pl.BlockSpec(memory_space=pltpu.VMEM)

    def hbm(value):
        return pltpu.with_memory_space_constraint(value, pltpu.HBM)

    def vmem(value):
        return pltpu.with_memory_space_constraint(value, pltpu.VMEM)

    def row_shift(value, shift):
        return lax.ppermute(value, "row", [(i, (i + shift) % rows) for i in range(rows)])

    def sub_shift(value, shift):
        return lax.ppermute(value, "sub", [(i, (i + shift) % subs) for i in range(subs)])

    def frm_shift(value, shift):
        return lax.ppermute(value, "frm", [(partner(i, shift, frms), i) for i in range(frms)])

    def place(x, at):
        return (at // subs * rows + x) * subs + at % subs

    table, order = hbm(jnp.asarray(toeplitz())), jnp.asarray(reorder(cl))
    *cuts, ahead = call(
        functools.partial(cut_kernel, rows, frames),
        [hbm(signal), table],
        [((cl, width), BF16)] * rows + [pltpu.VMEM((AHEAD,) + table.shape[1:], BF16)],
        [pltpu.SemaphoreType.DMA((rows + 1,))],
        in_specs=[anywhere] * 2,
    )
    own_sig, *out_sigs = cuts
    ahead = vmem(ahead)
    sig = [own_sig] + [row_shift(part, shift + 1) for shift, part in enumerate(out_sigs)]
    msg = (message(rank, size), BF16)
    piece = ((rank, size), F32)
    update_outs = [((rank, frames), F32), ((rank, rank), F32)]
    update_outs += [((rank, size + rank), F32)] * ((rows - 1) * (subs - 1))
    half_done, w_own, old, order, table = call(
        functools.partial(own_spectra_kernel, rows),
        [own_sig, ahead, hbm(w_start.T), hbm(h_start), hbm(order), table],
        [
            pltpu.VMEM((NF, blocks, rows, cl, TAPS), BF16),
            pltpu.VMEM((rank, NF * cl), F32),
            pltpu.VMEM((rank, frames), F32),
            pltpu.VMEM(order.shape, BF16),
            pltpu.VMEM((NF - AHEAD,) + table.shape[1:], BF16),
        ],
        [
            pltpu.VMEM((cl, frames + TAPS), BF16),
            pltpu.VMEM(((blocks - 1) * cl, 2 * TAPS), BF16),
            pltpu.SemaphoreType.DMA((3,)),
            pltpu.SemaphoreType.DMA((len(CUTS) - 1,)),
        ],
        in_specs=[whole] * 2 + [anywhere] * 4,
        limit=8,
        cost=2 * NF * cl * frames * 4 * TAPS,
    )
    order = vmem(order)
    (edge,) = call(
        functools.partial(edges_kernel, rows),
        sig + [vmem(half_done)],
        [((chans, TAPS), BF16)],
        in_specs=[whole] * rows + [anywhere],
    )
    pairs = [(place(rows - 1, i), place(0, i + 1)) for i in range(line - 1)]
    halo = lax.ppermute(edge, ("frm", "row", "sub"), pairs + [(b, a) for a, b in pairs])
    w_piece, w_msg = call(
        reorder_kernel,
        [vmem(w_own), order, edge],
        [piece, (message(rank, NF * cl), BF16)],
        in_specs=[whole, whole, anywhere],
    )
    w_msgs = [w_msg] + [row_shift(w_msg, shift) for shift in range(1, rows)]
    (early,) = call(
        functools.partial(first_early_kernel, cl),
        [w_msg, vmem(half_done)],
        [((rank, frames), F32)],
        cost=16 * NF * cl * frames * rank,
    )
    (spectra,) = call(
        functools.partial(other_spectra_kernel, rows),
        [halo, ahead, vmem(table)] + sig + [vmem(half_done), early],
        [pltpu.VMEM((NF, blocks, rows, cl, TAPS), BF16)],
        [
            pltpu.VMEM((rows, cl, frames + TAPS), BF16),
            pltpu.VMEM((((rows - 1) * blocks + 1) * cl, 2 * TAPS), BF16),
        ],
        in_specs=[whole] * (rows + 3) + [anywhere] * 2,
        limit=8,
        cost=2 * NF * chans * frames * 4 * TAPS,
        aliases={rows + 3: 0},
    )
    spectra = vmem(spectra)

    def products(places, activations, after):
        return call(
            functools.partial(products_kernel, places, rows, subs, cl),
            [activations, spectra] + after,
            [piece] * len(places),
            in_specs=[whole] * 2 + [anywhere] * len(after),
            cost=1 if after else 16 * NF * cl * frames * rank // subs * len(places),
        )

    def gathered(activations, h_gram, msgs):
        got = [sub_shift(m, dc) for m, (_, dc) in zip(msgs, others_of(rows, subs))]
        places = [(dx, 0) for dx in range(1, rows)] + [(0, dc) for dc in range(1, subs)]
        formed = products(places, activations, [])
        for_rows, for_cores = formed[: rows - 1], formed[rows - 1 :]
        from_cores = [sub_shift(m, dc + 1) for dc, m in enumerate(for_cores)]
        *outs, gram = call(
            functools.partial(core_kernel, rows - 1, rank),
            list(for_rows) + [h_gram] + got,
            [msg] * (rows - 1) + [((rank, rank), F32)],
        )
        from_rows = [row_shift(m, dx + 1) for dx, m in enumerate(outs)]
        (own,) = products([(0, 0)], activations, outs)
        (part,) = call(functools.partial(row_kernel, subs), [own, gram] + from_cores + from_rows, [msg])
        return [part] + [frm_shift(part, shift) for shift in reversed(range(1, frms))]

    activations, h_gram, *msgs = call(
        functools.partial(first_kernel, rows, subs, cl),
        w_msgs + [early, vmem(old), spectra],
        update_outs,
        [pltpu.VMEM((rank, frames), F32)],
        limit=8,
    )
    piled = [pltpu.VMEM((frms,) + msg[0], BF16)]
    w_piece, w_msg = call(
        functools.partial(update_kernel, frms),
        [w_piece] + gathered(activations, h_gram, msgs),
        [piece, msg],
        piled,
    )
    w_msgs = [w_msg] + [sub_shift(w_msg, dc) for dc in range(1, subs)]
    w_pieces = pltpu.VMEM((1, subs, rank, size), BF16)
    (early,) = call(
        functools.partial(early_kernel, rows, subs, cl),
        w_msgs + [spectra],
        [((rank, frames), F32)],
        [w_pieces],
        cost=16 * NF * cl * frames * rank,
    )
    from_rows = [row_shift(w_msg, dx) for dx in range(1, rows)]
    *from_rows, early = lax.optimization_barrier((*from_rows, early))
    (middle,) = call(
        functools.partial(middle_kernel, rows, subs, cl),
        from_rows + [early, spectra],
        [((rank, frames), F32)],
        cost=16 * NF * cl * frames * rank // subs,
    )
    for base in from_rows:
        w_msgs += [base] + [sub_shift(base, dc) for dc in range(1, subs)]
    activations, h_gram, *msgs = call(
        functools.partial(later_kernel, rows, subs, cl),
        w_msgs + [middle, activations, spectra],
        update_outs,
        [pltpu.VMEM((rank, frames), F32)],
        limit=8,
    )
    parts = gathered(activations, h_gram, msgs)
    activations, parts[0] = lax.optimization_barrier((activations, parts[0]))
    sides = [activations] + [row_shift(activations, shift) for shift in range(1, rows)]
    (part,) = call(
        functools.partial(last_kernel, frms), [w_piece, order] + parts, [((rank, NF * cl), F32)], piled
    )
    (wide,) = call(
        functools.partial(join_kernel, rows),
        sides,
        [pltpu.HBM((rank, window), F32)],
        [pltpu.SemaphoreType.DMA((rows,))],
        in_specs=[anywhere] * rows,
        out_specs=[anywhere],
    )
    (synergies,) = call(
        sum_kernel,
        [hbm(wide), part] + [sub_shift(part, dc) for dc in range(1, subs)],
        [pltpu.HBM((rank, NF * cl), F32)],
        [pltpu.VMEM((rank, NF * cl), F32), pltpu.SemaphoreType.DMA((rank // 8,))],
        in_specs=[anywhere] + [whole] * subs,
        out_specs=[anywhere],
    )
    return (synergies.T, wide)


def solution(mesh):
    placed = (P("row", ("grp", "frm", "sub")), P("row", None), P(None, ("grp", "frm", "sub")))
    return jax.shard_map(
        shards,
        mesh=mesh,
        in_specs=placed,
        out_specs=(P(("grp", "row"), None), P(None, ("grp", "frm", "sub"))),
        check_vma=False,
    )
```
